32 devices in a mesh: dp: 32 (over z, y, x, core).
Axes of the slice: x: 2, y: 2, z: 4, core: 2. Of those that a mesh axis runs over, the one named last changes fastest.
Arguments:
- tokens: bfloat16 [32768, 768], P('dp'), may hold values from -6 to 6
- lengths: int32 [128, 5], P('dp'), may hold values from 0 to 197, as said below
- attn_gain: bfloat16 [768], P('dp'), may hold values from 0.25 to 1.75
- attn_shift: bfloat16 [768], P('dp'), may hold values from -1.25 to 1.25
- query_weight: bfloat16 [768, 768], P('dp'), may hold values from -0.21875 to 0.21875
- query_bias: bfloat16 [768], P('dp'), may hold values from -1.25 to 1.25
- key_weight: bfloat16 [768, 768], P('dp'), may hold values from -0.21875 to 0.21875
- value_weight: bfloat16 [768, 768], P('dp'), may hold values from -0.21875 to 0.21875
- value_bias: bfloat16 [768], P('dp'), may hold values from -1.25 to 1.25
- out_weight: bfloat16 [768, 768], P('dp'), may hold values from -0.875 to 0.875
- out_bias: bfloat16 [768], P('dp'), may hold values from -1.25 to 1.25
- mlp_gain: bfloat16 [768], P('dp'), may hold values from 0.25 to 1.75
- mlp_shift: bfloat16 [768], P('dp'), may hold values from -1.25 to 1.25
- up_weight: bfloat16 [768, 3072], P('dp'), may hold values from -0.21875 to 0.21875
- up_bias: bfloat16 [3072], P('dp'), may hold values from -1.25 to 1.25
- down_weight: bfloat16 [3072, 768], P('dp'), may hold values from -0.109375 to 0.109375
- down_bias: bfloat16 [768], P('dp'), may hold values from -1.25 to 1.25
- grad_out: bfloat16 [32768, 768], P('dp'), may hold values from -6 to 6
Outputs:
- block_out: bfloat16 [32768, 768], P('dp')
- grad_tokens: bfloat16 [32768, 768], P('dp')
- grad_attn_gain: float32 [768], P('dp')
- grad_attn_shift: float32 [768], P('dp')
- grad_query_weight: float32 [768, 768], P('dp')
- grad_query_bias: float32 [768], P('dp')
- grad_key_weight: float32 [768, 768], P('dp')
- grad_value_weight: float32 [768, 768], P('dp')
- grad_value_bias: float32 [768], P('dp')
- grad_out_weight: float32 [768, 768], P('dp')
- grad_out_bias: float32 [768], P('dp')
- grad_mlp_gain: float32 [768], P('dp')
- grad_mlp_shift: float32 [768], P('dp')
- grad_up_weight: float32 [768, 3072], P('dp')
- grad_up_bias: float32 [3072], P('dp')
- grad_down_weight: float32 [3072, 768], P('dp')
- grad_down_bias: float32 [768], P('dp')
The draws below stay inside these ranges and needn't reach their ends.
Inputs may be any that keep to these rules, and one draw needn't show every extreme that they name: `lengths`: row t lists the images packed into the t-th block of 256 rows, in order: either one image of 197 tokens followed by one of 50, or one to 5 images of 50 tokens; remaining entries are 0, and the rows after the images are padding. Images never cross a block's end.
All inputs are finite; a program needn't handle non-finite values.
Results may differ from the reference program's by a relative error of at most 0.013.
Values may be sent and summed in bfloat16 or wider, within the bound.
No kernel may reach another device: no remote copies, remote signals or barrier semaphores. Data moves between devices by JAX's collectives and lax.ppermute only.
A program may use at most 192 MiB of HBM per device.

```python
import jax
import jax.numpy as jnp
from jax import lax

D = 768
FF = 3072
HEADS = 12
HEAD_DIM = 64
TILE = 256
SMALL_LEN = 50
BIG_LEN = 197
SLOTS = 5
TILES_DEV = 4
TILES = 128
TOKENS = 32768


def draw_lengths(key, part):
    key = jax.random.fold_in(key, 11)
    tile_kind = jax.random.randint(key, (TILES,), 0, 8)
    tile_kind = tile_kind.at[0].set(0)
    image_count = jnp.where(tile_kind == 0, 2, jnp.minimum(tile_kind, SLOTS))
    slot_index = jnp.arange(SLOTS, dtype=jnp.int32)
    small_rows = jnp.where(slot_index[None, :] < image_count[:, None], SMALL_LEN, 0)
    leading = jnp.where(tile_kind == 0, BIG_LEN, SMALL_LEN)
    return small_rows.at[:, 0].set(leading).astype(jnp.int32)


def strengthened(array, stream_key, source, target, blocks, factor):
    def block_of(dim):
        return (jnp.arange(array.shape[dim]) // (array.shape[dim] // blocks)).reshape((-1,) + (1,) * (array.ndim - 1 - dim))

    one_side = jax.random.permutation(stream_key, blocks)[block_of(target)]
    far = (block_of(target) + blocks // 2) % blocks
    return jnp.where((block_of(source) == one_side) | (block_of(source) == far), factor * array, array)


def block_levels(stream_key, shape, shards, least, high):
    factor_of = 1.0
    for position, shards_of in shards:
        heights = jax.random.uniform(jax.random.fold_in(jax.random.fold_in(stream_key, 6), position), (shards_of,), jnp.float32, least / len(shards), high / len(shards))
        factor_of = factor_of * jnp.repeat(jnp.exp(heights), shape[position] // shards_of).reshape((-1,) + (1,) * (len(shape) - 1 - position))
    return factor_of


def gaussian(own_key, shape, deviation, bound, cuts=(), kind=jnp.bfloat16):
    array = jax.random.normal(own_key, shape, jnp.float32) * deviation
    if len(cuts) > 0:
        array = block_levels(own_key, shape, cuts, -0.22, 0.18) * array
    return jnp.clip(array, min=-bound, max=bound).astype(kind)


def noise_with(own_key, dims, spread, limit, cuts, heavy, kind=jnp.bfloat16):
    drawn = spread * jax.random.normal(own_key, dims, jnp.float32)
    if cuts:
        drawn = drawn * block_levels(own_key, dims, cuts, -0.22, 0.18)
    return jnp.clip(strengthened(drawn, jax.random.fold_in(own_key, 3), *heavy), -limit, limit).astype(kind)


def setup_inputs(seed: int = 0) -> dict:
    keys = jax.random.split(jax.random.key(seed), 19)
    tokens = gaussian(keys[0], (TOKENS, D), 1.0, 6.0, ((0, 32),))
    lengths = draw_lengths(jax.random.fold_in(keys[18], 71), 0)
    attn_gain = jnp.clip(1.0 + 0.15 * jax.random.normal(keys[2], (D,), jnp.float32), 0.25, 1.75).astype(jnp.bfloat16)
    attn_shift = gaussian(keys[3], (D,), 0.2, 1.25, ((0, 32),))
    query_weight = gaussian(keys[4], (D, D), D ** -0.5, 0.21875, ((0, 32),))
    query_bias = gaussian(keys[5], (D,), 0.2, 1.25, ((0, 32),))
    key_weight = gaussian(keys[6], (D, D), D ** -0.5, 0.21875, ((0, 32),))
    value_weight = gaussian(keys[7], (D, D), D ** -0.5, 0.21875, ((0, 32),))
    value_bias = gaussian(keys[8], (D,), 0.2, 1.25, ((0, 32),))
    out_weight = gaussian(keys[9], (D, D), (D // 16) ** -0.5, 0.875, ((0, 32),))
    out_bias = gaussian(keys[10], (D,), 0.2, 1.25, ((0, 32),))
    mlp_gain = jnp.clip(1.0 + 0.15 * jax.random.normal(keys[11], (D,), jnp.float32), 0.25, 1.75).astype(jnp.bfloat16)
    mlp_shift = gaussian(keys[12], (D,), 0.2, 1.25, ((0, 32),))
    up_weight = gaussian(keys[13], (D, FF), D ** -0.5, 0.21875, ((0, 32),))
    up_bias = gaussian(keys[14], (FF,), 0.2, 1.25, ((0, 32),))
    down_weight = gaussian(keys[15], (FF, D), FF ** -0.5, 0.109375, ((0, 32),))
    down_bias = gaussian(keys[16], (D,), 0.2, 1.25, ((0, 32),))
    grad_out = noise_with(keys[17], (TOKENS, D), 1.0, 6.0, ((0, 32),), (0, 1, 32, 2.75))
    return dict(tokens=tokens, lengths=lengths, attn_gain=attn_gain, attn_shift=attn_shift, query_weight=query_weight, query_bias=query_bias, key_weight=key_weight, value_weight=value_weight, value_bias=value_bias, out_weight=out_weight, out_bias=out_bias, mlp_gain=mlp_gain, mlp_shift=mlp_shift, up_weight=up_weight, up_bias=up_bias, down_weight=down_weight, down_bias=down_bias, grad_out=grad_out)


epsilon = 1e-06
masked_score = -1e+30

@jax.custom_vjp
def low(v):
    return lax.optimization_barrier(v.astype(jnp.bfloat16)).astype(jnp.float32)

@jax.custom_vjp
def low_back(v):
    return v

def low_keep(v):
    return (low(v), None)

def low_pass(kept, grad):
    return (grad,)

def back_keep(v):
    return (v, None)

def back_low(kept, grad):
    return (low(grad),)
low.defvjp(low_keep, low_pass)
low_back.defvjp(back_keep, back_low)

def segment_ids(lengths, block_rows):
    bounds = jnp.cumsum(lengths, axis=1).astype(jnp.int32)
    row_index = jnp.arange(block_rows, dtype=jnp.int32)
    return lax.optimization_barrier(jnp.sum((row_index[None, :, None] >= bounds[:, None, :]).astype(jnp.int32), axis=2)).astype(jnp.int32)

def layer_norm(rows, gain, shift):
    centered = rows - lax.optimization_barrier(jnp.mean(rows, axis=-1, keepdims=True))
    inverse = lax.rsqrt(lax.optimization_barrier(jnp.mean(centered * centered, axis=-1, keepdims=True)) + epsilon)
    return centered * inverse * gain + shift

def highest(left, right):
    return jnp.dot(left, right, precision=lax.Precision.HIGHEST, preferred_element_type=jnp.float32)

def attend_group(packed):
    queries, key_rows, value_rows, segment = packed
    scores = jnp.einsum('tqhd,tkhd->thqk', queries, key_rows, precision=lax.Precision.HIGHEST) * HEAD_DIM ** (-0.5)
    scores = low_back(scores)
    same_image = (segment[:, :, None] == segment[:, None, :])[:, None]
    probs = jax.nn.softmax(jnp.where(same_image, scores, masked_score), axis=-1)
    return jnp.einsum('thqk,tkhd->tqhd', low(probs), value_rows, precision=lax.Precision.HIGHEST)

def forward(rows_in, segment, attn_gain, attn_shift, query_weight, query_bias, key_weight, value_weight, value_bias, out_weight, out_bias, mlp_gain, mlp_shift, up_weight, up_bias, down_weight, down_bias):
    normed_one = low(layer_norm(rows_in, attn_gain, attn_shift))
    queries = low_back(low(highest(normed_one, query_weight) + query_bias))
    key_rows = low_back(low(highest(normed_one, key_weight)))
    value_rows = low_back(low(highest(normed_one, value_weight) + value_bias))
    grouped = (TILES // TILES_DEV, TILES_DEV, TILE, HEADS, HEAD_DIM)
    packed = (queries.reshape(grouped), key_rows.reshape(grouped), value_rows.reshape(grouped), segment.reshape(grouped[:3]))
    mixed = lax.map(jax.checkpoint(attend_group), packed)
    mixed = low_back(low(mixed.reshape(TOKENS, D)))
    resid = rows_in + low_back(highest(mixed, out_weight) + out_bias)
    normed_two = low(layer_norm(resid, mlp_gain, mlp_shift))
    up_pre = low_back(highest(normed_two, up_weight) + up_bias)
    activated = low(jax.nn.gelu(up_pre))
    return resid + low_back(highest(activated, down_weight) + down_bias)

def reference(tokens, lengths, attn_gain, attn_shift, query_weight, query_bias, key_weight, value_weight, value_bias, out_weight, out_bias, mlp_gain, mlp_shift, up_weight, up_bias, down_weight, down_bias, grad_out):
    segment = segment_ids(lengths, TILE)
    valid = (segment < SLOTS).astype(jnp.float32).reshape(TOKENS, 1)

    def run_block(rows_in, *params):
        return forward(rows_in, segment, *params)
    inputs = (tokens, attn_gain, attn_shift, query_weight, query_bias, key_weight, value_weight, value_bias, out_weight, out_bias, mlp_gain, mlp_shift, up_weight, up_bias, down_weight, down_bias)
    floats = tuple((member.astype(jnp.float32) for member in inputs))
    block_out, pull_back = jax.vjp(run_block, *floats)
    grads = pull_back(grad_out.astype(jnp.float32) * valid)
    return (block_out.astype(jnp.bfloat16), grads[0].astype(jnp.bfloat16), grads[1], grads[2], grads[3], grads[4], grads[5], grads[6], grads[7], grads[8], grads[9], grads[10], grads[11], grads[12], grads[13], grads[14], grads[15])
```

```python
import jax
import jax.numpy as jnp
from jax import lax
from jax.experimental import pallas as pl
from jax.experimental.pallas import tpu as pltpu
from jax.sharding import PartitionSpec as P

HEADS = 12
HEAD_DIM = 64
PAIRS = 6
LANES = 128
EPS = 1e-06
MASKED = -1e30
SCALE = HEAD_DIM**-0.5
GELU_C = 0.7978845608028654
GELU_A = 0.044715
VMEM = 56 * 1024 * 1024
F32 = jnp.float32
BF16 = jnp.bfloat16


def dot_nn(left, right):
    return lax.dot_general(left, right, (((1,), (0,)), ((), ())), preferred_element_type=F32)


def dot_nt(left, right):
    return lax.dot_general(left, right, (((1,), (1,)), ((), ())), preferred_element_type=F32)


def dot_tn(left, right):
    return lax.dot_general(left, right, (((0,), (0,)), ((), ())), preferred_element_type=F32)


def normalize(rows):
    centered = rows - jnp.mean(rows, axis=-1, keepdims=True)
    inverse = lax.rsqrt(jnp.mean(centered * centered, axis=-1, keepdims=True) + EPS)
    return centered * inverse, inverse


def norm_back(grads, gain, hat, inverse):
    scaled = grads * gain
    mean = jnp.mean(scaled, axis=-1, keepdims=True)
    mean_hat = jnp.mean(scaled * hat, axis=-1, keepdims=True)
    return inverse * (scaled - mean - hat * mean_hat)


def column_sum(rows):
    return jnp.sum(rows, axis=0, keepdims=True)


def segments(lengths_ref, tile, slots, rows, axis):
    shape = (rows, 1) if axis == 0 else (1, rows)
    index = lax.broadcasted_iota(jnp.int32, shape, axis)
    segment = jnp.zeros(shape, jnp.int32)
    bound = 0
    for slot in range(slots):
        bound = bound + lengths_ref[tile, slot]
        segment = segment + (index >= bound).astype(jnp.int32)
    return segment


def mask_bias(lengths_ref, tile, slots, rows):
    same = segments(lengths_ref, tile, slots, rows, 0) == segments(lengths_ref, tile, slots, rows, 1)
    return jnp.where(same, 0.0, MASKED).astype(F32)


def half_of(pair, side):
    lane = lax.broadcasted_iota(jnp.int32, pair.shape, 1)
    keep = lane < HEAD_DIM if side == 0 else lane >= HEAD_DIM
    return jnp.where(keep, pair, jnp.zeros_like(pair))


def attention_forward(lengths_ref, x_ref, grad_ref, vec_ref, wq_ref, wk_ref, wv_ref, wo_ref,
                      n1_ref, q_ref, k_ref, v_ref, mixed_ref, lse_ref, resid_ref, n2_ref, cot_ref, dsum_ref):
    tile = pl.program_id(0)
    rows = x_ref.shape[0]
    slots = lengths_ref.shape[1]
    x = x_ref[...].astype(F32)
    hat, _ = normalize(x)
    n1 = (hat * vec_ref[0:1, :] + vec_ref[1:2, :]).astype(BF16)
    n1_ref[...] = n1
    q_ref[...] = (dot_nn(n1, wq_ref[...]) + vec_ref[2:3, :]).astype(BF16) * jnp.asarray(SCALE, BF16)
    k_ref[...] = dot_nn(n1, wk_ref[...]).astype(BF16)
    v_ref[...] = (dot_nn(n1, wv_ref[...]) + vec_ref[3:4, :]).astype(BF16)
    bias = mask_bias(lengths_ref, tile, slots, rows)
    lane = lax.broadcasted_iota(jnp.int32, (rows, LANES), 1)
    lse = jnp.zeros((rows, LANES), F32)
    for pair in range(PAIRS):
        cols = pl.ds(pair * LANES, LANES)
        qp, kp, vp = q_ref[:, cols], k_ref[:, cols], v_ref[:, cols]
        total = None
        for side in range(2):
            scores = dot_nt(half_of(qp, side), kp) + bias
            top = jnp.max(scores, axis=-1, keepdims=True)
            weights = jnp.exp(scores - top)
            sums = jnp.sum(weights, axis=-1, keepdims=True)
            probs = (weights * (1.0 / sums)).astype(BF16)
            part = dot_nn(probs, half_of(vp, side))
            total = part if total is None else total + part
            lse = jnp.where(lane == 2 * pair + side, top + jnp.log(sums), lse)
        mixed_ref[:, cols] = total.astype(BF16)
    lse_ref[...] = lse
    resid = x + (dot_nn(mixed_ref[...], wo_ref[...]) + vec_ref[4:5, :])
    resid_ref[...] = resid
    hat_two, _ = normalize(resid)
    n2_ref[...] = (hat_two * vec_ref[5:6, :] + vec_ref[6:7, :]).astype(BF16)
    valid = segments(lengths_ref, tile, slots, rows, 0) < slots
    cot = jnp.where(valid, grad_ref[...].astype(F32), 0.0)
    cot_ref[...] = cot.astype(BF16)

    @pl.when(tile == 0)
    def _():
        dsum_ref[...] = jnp.zeros_like(dsum_ref)

    dsum_ref[0:1, :] += column_sum(cot)


def mlp_up(n2_ref, cot_ref, wup_ref, bup_ref, act_ref, slope_ref, dwd_ref):
    pre = dot_nn(n2_ref[...], wup_ref[...]) + bup_ref[...]
    square = pre * pre
    tanh = jnp.tanh(pre * (GELU_C + (GELU_C * GELU_A) * square))
    half = 0.5 + 0.5 * tanh
    act = (pre * half).astype(BF16)
    inner = GELU_C + (3.0 * GELU_C * GELU_A) * square
    slope_ref[...] = (half + (0.5 * pre) * (1.0 - tanh * tanh) * inner).astype(BF16)
    act_ref[...] = act
    dwd_ref[...] = dot_tn(act, cot_ref[...]).astype(BF16)


def mlp_down(n2_ref, cot_ref, resid_ref, vec_ref, act_ref, slope_ref, wup_ref, wdown_ref,
             out_ref, gresid_ref, gattn_ref, dwu_ref, dbu_ref, dsum_ref, out_acc, grad_acc):
    step = pl.program_id(0)

    @pl.when(step == 0)
    def _():
        out_acc[...] = jnp.zeros_like(out_acc)
        grad_acc[...] = jnp.zeros_like(grad_acc)

    cot = cot_ref[...]
    wdown = wdown_ref[...]
    grad_up = (dot_nt(cot, wdown) * slope_ref[...].astype(F32)).astype(BF16)
    dbu_ref[...] = column_sum(grad_up.astype(F32))
    dwu_ref[...] = dot_tn(n2_ref[...], grad_up).astype(BF16)
    out_acc[...] += dot_nn(act_ref[...], wdown)
    grad_acc[...] += dot_nt(grad_up, wup_ref[...])

    @pl.when(step == pl.num_programs(0) - 1)
    def _():
        block = 256
        dsum_ref[...] = jnp.zeros_like(dsum_ref)

        @pl.loop(0, cot_ref.shape[0] // block)
        def _(index):
            at = pl.ds(pl.multiple_of(index * block, block), block)
            resid = resid_ref[at, :]
            out_ref[at, :] = (resid + (out_acc[at, :] + vec_ref[7:8, :])).astype(BF16)
            hat, inverse = normalize(resid)
            grad_two = grad_acc[at, :]
            gresid = cot_ref[at, :].astype(F32) + norm_back(grad_two, vec_ref[5:6, :], hat, inverse)
            gresid_ref[at, :] = gresid
            gattn = gresid.astype(BF16)
            gattn_ref[at, :] = gattn
            dsum_ref[0:1, :] += column_sum(gattn.astype(F32))
            dsum_ref[1:2, :] += column_sum(grad_two * hat)
            dsum_ref[2:3, :] += column_sum(grad_two)


def attention_backward(lengths_ref, q_ref, k_ref, v_ref, lse_ref, gattn_ref, wo_ref,
                       dq_ref, dk_ref, dv_ref, dsum_ref, gmix_ref):
    tile = pl.program_id(0)
    rows = q_ref.shape[0]
    gmix_ref[...] = dot_nt(gattn_ref[...], wo_ref[...]).astype(BF16)
    bias = mask_bias(lengths_ref, tile, lengths_ref.shape[1], rows)
    for pair in range(PAIRS):
        cols = pl.ds(pair * LANES, LANES)
        qp, kp, vp, gp = q_ref[:, cols], k_ref[:, cols], v_ref[:, cols], gmix_ref[:, cols]
        dq = dk = dv = None
        for side in range(2):
            head = 2 * pair + side
            qh, kh, gh = half_of(qp, side), half_of(kp, side), half_of(gp, side)
            probs = jnp.exp(dot_nt(qh, kp) + bias - lse_ref[:, head : head + 1])
            grad_probs = dot_nt(gh, vp)
            dot = jnp.sum(probs * grad_probs, axis=-1, keepdims=True)
            grad_scores = (probs * (grad_probs - dot)).astype(BF16)
            one_q = dot_nn(grad_scores, kh)
            one_k = dot_tn(grad_scores, qh)
            one_v = dot_tn(probs.astype(BF16), gh)
            dq = one_q if dq is None else dq + one_q
            dk = one_k if dk is None else dk + one_k
            dv = one_v if dv is None else dv + one_v
        dq_ref[:, cols] = (dq * SCALE).astype(BF16)
        dk_ref[:, cols] = dk.astype(BF16)
        dv_ref[:, cols] = dv.astype(BF16)

    @pl.when(tile == 0)
    def _():
        dsum_ref[...] = jnp.zeros_like(dsum_ref)

    dsum_ref[0:1, :] += column_sum(dq_ref[...].astype(F32))
    dsum_ref[1:2, :] += column_sum(dv_ref[...].astype(F32))


def weight_grads(n1_ref, mixed_ref, dq_ref, dk_ref, dv_ref, gattn_ref, wq_out, wk_out, wv_out, wo_out):
    n1 = n1_ref[...]
    wq_out[...] = dot_tn(n1, dq_ref[...]).astype(BF16)
    wk_out[...] = dot_tn(n1, dk_ref[...]).astype(BF16)
    wv_out[...] = dot_tn(n1, dv_ref[...]).astype(BF16)
    wo_out[...] = dot_tn(mixed_ref[...], gattn_ref[...]).astype(BF16)


def tokens_backward(x_ref, gresid_ref, vec_ref, dq_ref, dk_ref, dv_ref, wq_ref, wk_ref, wv_ref, gtok_ref, dsum_ref):
    grad_one = dot_nt(dq_ref[...], wq_ref[...]) + dot_nt(dk_ref[...], wk_ref[...]) + dot_nt(dv_ref[...], wv_ref[...])
    hat, inverse = normalize(x_ref[...].astype(F32))
    gtok_ref[...] = (gresid_ref[...] + norm_back(grad_one, vec_ref[0:1, :], hat, inverse)).astype(BF16)

    @pl.when(pl.program_id(0) == 0)
    def _():
        dsum_ref[...] = jnp.zeros_like(dsum_ref)

    dsum_ref[0:1, :] += column_sum(grad_one * hat)
    dsum_ref[1:2, :] += column_sum(grad_one)


def rows_spec(block, width):
    return pl.BlockSpec((block, width), lambda i: (i, 0))


def cols_spec(height, block):
    return pl.BlockSpec((height, block), lambda i: (0, i))


def whole_spec(shape):
    return pl.BlockSpec(shape, lambda i: (0,) * len(shape), pipeline_mode=pl.Buffered(1))


def kept_spec(shape):
    return pl.BlockSpec(shape, lambda i: (0,) * len(shape))


SMEM = pl.BlockSpec(memory_space=pltpu.SMEM)


def call(kernel, grid, ins, outs, scratch, name, flops, *args):
    out_specs = tuple(spec for spec, _ in outs)
    out_shape = tuple(shape for _, shape in outs)
    moved = sum(a.size * a.dtype.itemsize for a in args) + sum(s.size * s.dtype.itemsize for s in out_shape)
    return pl.pallas_call(
        kernel,
        grid=grid,
        in_specs=ins,
        out_specs=out_specs,
        out_shape=out_shape,
        scratch_shapes=scratch,
        compiler_params=pltpu.CompilerParams(vmem_limit_bytes=VMEM, dimension_semantics=("arbitrary",) * len(grid)),
        cost_estimate=pl.CostEstimate(flops=flops, bytes_accessed=moved, transcendentals=0),
        name=name,
    )(*args)


def shaped(*shape, dtype=BF16):
    return jax.ShapeDtypeStruct(shape, dtype)


def body(tokens, lengths, attn_gain, attn_shift, query_weight, query_bias, key_weight, value_weight, value_bias,
         out_weight, out_bias, mlp_gain, mlp_shift, up_weight, up_bias, down_weight, down_bias, grad_out):
    count = lax.axis_size("dp")
    rows, width = tokens.shape
    tiles = lengths.shape[0]
    tile = rows // tiles
    hidden = up_bias.shape[0] * count
    own = width // count
    folds = hidden // width
    vectors = (attn_gain, attn_shift, query_bias, value_bias, out_bias, mlp_gain, mlp_shift, down_bias)
    flat = jnp.concatenate(vectors + (up_bias,))
    packed = jnp.concatenate(
        (
            query_weight,
            key_weight,
            value_weight,
            out_weight,
            up_weight.reshape(own, folds, width).transpose(1, 0, 2).reshape(own * folds, width),
            down_weight,
            jnp.pad(flat.reshape(1, -1), ((0, 7), (0, width - flat.size))),
        ),
        axis=0,
    )
    whole = lax.all_gather(packed, "dp", axis=0, tiled=True).reshape(count, -1, width)

    def part(index):
        return whole[:, index * own : (index + 1) * own, :].reshape(width, width)

    wq, wk, wv, wo = (part(index) for index in range(4))
    wup = whole[:, 4 * own : (4 + folds) * own, :].reshape(count, folds, own, width).transpose(0, 2, 1, 3)
    wup = wup.reshape(width, hidden)
    wdown = whole[:, (4 + folds) * own : (4 + 2 * folds) * own, :].reshape(hidden, width)
    last = whole[:, (4 + 2 * folds) * own, : flat.size].astype(F32)
    vec = last[:, : 8 * own].reshape(count, 8, own).transpose(1, 0, 2).reshape(8, width)
    bup = last[:, 8 * own :].reshape(1, hidden)

    tile_rows = rows_spec(tile, width)
    square = whole_spec((width, width))
    vec_spec = whole_spec((8, width))
    sums = (kept_spec((8, width)), shaped(8, width, dtype=F32))
    low_rows = (tile_rows, shaped(rows, width))
    high_rows = (tile_rows, shaped(rows, width, dtype=F32))
    lse_spec = rows_spec(tile, LANES)
    mac = 2 * rows * width * width
    n1, q, k, v, mixed, lse, resid, n2, cot, sum_down = call(
        attention_forward, (tiles,), [SMEM, tile_rows, tile_rows, vec_spec, square, square, square, square],
        [low_rows] * 5 + [(lse_spec, shaped(rows, LANES, dtype=F32)), high_rows, low_rows, low_rows, sums],
        [], "attention_forward", 6 * mac, lengths, tokens, grad_out, vec, wq, wk, wv, wo)
    block = min(384, hidden)
    steps = hidden // block
    full_rows = whole_spec((rows, width))
    act, slope, d_down = call(
        mlp_up, (steps,), [full_rows, full_rows, cols_spec(width, block), cols_spec(1, block)],
        [(cols_spec(rows, block), shaped(rows, hidden))] * 2 + [(rows_spec(block, width), shaped(hidden, width))],
        [], "mlp_up", 2 * folds * mac, n2, cot, wup, bup)
    out, gresid, gattn, d_up, sum_up, sum_two = call(
        mlp_down, (steps,),
        [full_rows, full_rows, full_rows, vec_spec, cols_spec(rows, block), cols_spec(rows, block),
         cols_spec(width, block), rows_spec(block, width)],
        [(kept_spec((rows, width)), shaped(rows, width)), (kept_spec((rows, width)), shaped(rows, width, dtype=F32)),
         (kept_spec((rows, width)), shaped(rows, width)), (cols_spec(width, block), shaped(width, hidden)),
         (cols_spec(1, block), shaped(1, hidden, dtype=F32)), sums],
        [pltpu.VMEM((rows, width), F32), pltpu.VMEM((rows, width), F32)],
        "mlp_down", 4 * folds * mac, n2, cot, resid, vec, act, slope, wup, wdown)
    dq, dk, dv, sum_qv = call(
        attention_backward, (tiles,), [SMEM, tile_rows, tile_rows, tile_rows, lse_spec, tile_rows, square],
        [low_rows] * 3 + [sums], [pltpu.VMEM((tile, width), BF16)],
        "attention_backward", 4 * mac, lengths, q, k, v, lse, gattn, wo)
    side = width // 2
    d_q, d_k, d_v, d_o = call(
        weight_grads, (2,), [full_rows] * 2 + [cols_spec(rows, side)] * 4,
        [(cols_spec(width, side), shaped(width, width))] * 4, [],
        "weight_grads", 4 * mac, n1, mixed, dq, dk, dv, gattn)
    gtok, sum_one = call(
        tokens_backward, (tiles,),
        [tile_rows, tile_rows, vec_spec, tile_rows, tile_rows, tile_rows, square, square, square],
        [low_rows, sums], [], "tokens_backward", 3 * mac, tokens, gresid, vec, dq, dk, dv, wq, wk, wv)

    vec_grads = jnp.concatenate(
        (sum_one[0:2], sum_qv[0:2], sum_two[0:3], sum_down[0:1]), axis=0)
    vec_grads = vec_grads.reshape(8, count, own).transpose(1, 0, 2).reshape(count, 8 * own)
    flat_grads = jnp.concatenate((vec_grads, sum_up.reshape(count, folds * own)), axis=1).astype(BF16)
    flat_grads = jnp.pad(flat_grads.reshape(count, 1, -1), ((0, 0), (0, 7), (0, width - flat.size)))
    grads = jnp.concatenate(
        (
            d_q.reshape(count, own, width),
            d_k.reshape(count, own, width),
            d_v.reshape(count, own, width),
            d_o.reshape(count, own, width),
            d_up.reshape(count, own, folds, width).transpose(0, 2, 1, 3).reshape(count, folds * own, width),
            d_down.reshape(count, folds * own, width),
            flat_grads,
        ),
        axis=1,
    )
    share = lax.psum_scatter(grads.reshape(-1, width), "dp", scatter_dimension=0, tiled=True).astype(F32)
    g_q, g_k, g_v, g_o = (share[index * own : (index + 1) * own] for index in range(4))
    g_up = share[4 * own : (4 + folds) * own].reshape(folds, own, width).transpose(1, 0, 2).reshape(own, hidden)
    g_down = share[(4 + folds) * own : (4 + 2 * folds) * own]
    g_vec = share[(4 + 2 * folds) * own]
    g_gain, g_shift, g_qb, g_vb, g_ob, g_mg, g_ms, g_db = (g_vec[index * own : (index + 1) * own] for index in range(8))
    g_ub = g_vec[8 * own : 8 * own + folds * own]
    return (out, gtok, g_gain, g_shift, g_q, g_qb, g_k, g_v, g_vb, g_o, g_ob, g_mg, g_ms, g_up, g_ub, g_down, g_db)


def solution(mesh):
    rows, flat = P("dp", None), P("dp")
    return jax.shard_map(
        body,
        mesh=mesh,
        in_specs=(rows, rows, flat, flat, rows, flat, rows, rows, flat, rows, flat, flat, flat, rows, flat, rows, flat, rows),
        out_specs=(rows, rows, flat, flat, rows, flat, rows, rows, flat, rows, flat, flat, flat, rows, flat, rows, flat),
        check_vma=False,
    )
```

```python
import functools

import jax
import jax.numpy as jnp
from jax import lax
from jax.experimental import pallas as pl
from jax.experimental.pallas import tpu as pltpu
from jax.sharding import PartitionSpec as P

HEADS = 12
HEAD_DIM = 64
PAIRS = 6
LANES = 128
CHIPS = 16
EPS = 1e-06
MASKED = -1e30
SCALE = HEAD_DIM**-0.5
GELU_C = 0.7978845608028654
GELU_A = 0.044715
VMEM = 56 * 1024 * 1024
F32 = jnp.float32
BF16 = jnp.bfloat16


def dot_nn(left, right):
    return lax.dot_general(left, right, (((1,), (0,)), ((), ())), preferred_element_type=F32)


def dot_nt(left, right):
    return lax.dot_general(left, right, (((1,), (1,)), ((), ())), preferred_element_type=F32)


def dot_tn(left, right):
    return lax.dot_general(left, right, (((0,), (0,)), ((), ())), preferred_element_type=F32)


def normalize(rows):
    centered = rows - jnp.mean(rows, axis=-1, keepdims=True)
    inverse = lax.rsqrt(jnp.mean(centered * centered, axis=-1, keepdims=True) + EPS)
    return centered * inverse, inverse


def norm_back(grads, gain, hat, inverse):
    scaled = grads * gain
    mean = jnp.mean(scaled, axis=-1, keepdims=True)
    mean_hat = jnp.mean(scaled * hat, axis=-1, keepdims=True)
    return inverse * (scaled - mean - hat * mean_hat)


def column_sum(rows):
    return jnp.sum(rows, axis=0, keepdims=True)


def segments(lengths_ref, tile, slots, rows, axis):
    shape = (rows, 1) if axis == 0 else (1, rows)
    index = lax.broadcasted_iota(jnp.int32, shape, axis)
    segment = jnp.zeros(shape, jnp.int32)
    bound = 0
    for slot in range(slots):
        bound = bound + lengths_ref[tile, slot]
        segment = segment + (index >= bound).astype(jnp.int32)
    return segment


def mask_bias(lengths_ref, tile, slots, rows):
    same = segments(lengths_ref, tile, slots, rows, 0) == segments(lengths_ref, tile, slots, rows, 1)
    return jnp.where(same, 0.0, MASKED).astype(F32)


def half_of(pair, side):
    lane = lax.broadcasted_iota(jnp.int32, pair.shape, 1)
    keep = lane < HEAD_DIM if side == 0 else lane >= HEAD_DIM
    return jnp.where(keep, pair, jnp.zeros_like(pair))


def fetch_weights(me, sources, weight_refs, parts_ref, sem):
    core, chip = me & 1, me >> 1
    side = sources[0].shape[2]
    each = weight_refs[0].shape[0] // CHIPS
    for index, source in enumerate(sources):
        half = core if index < 4 else 1 - core
        cols = pl.ds(pl.multiple_of(half * side, LANES), side)
        for layer in range(4):
            owner = chip ^ (4 * layer + index % 4)
            rows = pl.ds(pl.multiple_of(owner * each, 16), each)
            for number, ref in enumerate(weight_refs):
                pltpu.make_async_copy(
                    source.at[layer, pl.ds(number * each, each), :], ref.at[rows, cols], sem.at[number]
                ).start()
            pltpu.make_async_copy(
                source.at[layer, pl.ds(3 * each, 16), :], parts_ref.at[2 * owner + half], sem.at[3]
            ).start()


def project(me_ref, x_ref, *refs):
    sources = refs[:8]
    n1_ref, q_ref, k_ref, v_ref, wq_ref, wk_ref, wv_ref, vec_ref, bup_ref, parts_ref, sem = refs[8:]
    weights = (wq_ref, wk_ref, wv_ref)

    @pl.when(pl.program_id(0) == 0)
    def _():
        fetch_weights(me_ref[0], sources, weights, parts_ref, sem)
        for number, ref in enumerate(weights + (parts_ref,)):
            pltpu.make_async_copy(ref, ref, sem.at[number]).wait()
        count, _, side = parts_ref.shape
        parts = [parts_ref[device].astype(F32) for device in range(count)]
        group = count // 2
        vec_ref[...] = jnp.concatenate((sum(parts[:group]), sum(parts[group:])), axis=1)
        blocks = bup_ref.shape[1] // side
        group = count // blocks
        for block in range(blocks):
            rows = sum(parts[block * group : (block + 1) * group])
            bup_ref[:, block * side : (block + 1) * side] = rows[8:9]

    project_rows(x_ref, vec_ref, wq_ref, wk_ref, wv_ref, n1_ref, q_ref, k_ref, v_ref)


def project_rows(x_ref, vec_ref, wq_ref, wk_ref, wv_ref, n1_ref, q_ref, k_ref, v_ref):
    hat, _ = normalize(x_ref[...].astype(F32))
    n1 = (hat * vec_ref[0:1, :] + vec_ref[1:2, :]).astype(BF16)
    n1_ref[...] = n1
    q_ref[...] = (dot_nn(n1, wq_ref[...]) + vec_ref[2:3, :]).astype(BF16) * jnp.asarray(SCALE, BF16)
    k_ref[...] = dot_nn(n1, wk_ref[...]).astype(BF16)
    v_ref[...] = (dot_nn(n1, wv_ref[...]) + vec_ref[3:4, :]).astype(BF16)


def attention_forward(lengths_ref, grad_ref, q_ref, k_ref, v_ref, mixed_ref, lse_ref, cot_ref, dsum_ref):
    tile = pl.program_id(0)
    rows = q_ref.shape[0]
    slots = lengths_ref.shape[1]
    bias = mask_bias(lengths_ref, tile, slots, rows)
    lane = lax.broadcasted_iota(jnp.int32, (rows, LANES), 1)
    lse = jnp.zeros((rows, LANES), F32)
    for pair in range(PAIRS):
        cols = pl.ds(pair * LANES, LANES)
        qp, kp, vp = q_ref[:, cols], k_ref[:, cols], v_ref[:, cols]
        total = None
        for side in range(2):
            scores = dot_nt(half_of(qp, side), kp) + bias
            top = jnp.max(scores, axis=-1, keepdims=True)
            weights = jnp.exp(scores - top)
            sums = jnp.sum(weights, axis=-1, keepdims=True)
            probs = (weights * (1.0 / sums)).astype(BF16)
            part = dot_nn(probs, half_of(vp, side))
            total = part if total is None else total + part
            lse = jnp.where(lane == 2 * pair + side, top + jnp.log(sums), lse)
        mixed_ref[:, cols] = total.astype(BF16)
    lse_ref[...] = lse
    valid = segments(lengths_ref, tile, slots, rows, 0) < slots
    cot = jnp.where(valid, grad_ref[...].astype(F32), 0.0)
    cot_ref[...] = cot.astype(BF16)

    @pl.when(tile == 0)
    def _():
        dsum_ref[...] = jnp.zeros_like(dsum_ref)

    dsum_ref[0:1, :] += column_sum(cot)


def up_block(ref):
    return ref[...].reshape(-1, ref.shape[-1])


def down_block(ref):
    return jnp.concatenate([ref[:, half].reshape(-1, ref.shape[-1]) for half in range(2)], axis=1)


def mlp_up(me_ref, x_ref, mixed_ref, vec_ref, wo_ref, cot_ref, wup_ref, bup_ref,
           resid_ref, n2_ref, act_ref, slope_ref, send_ref, keep_ref):
    step = pl.program_id(0)
    me = me_ref[0]

    @pl.when(step == 0)
    def _():
        weight = down_block(wo_ref)
        block = 256

        @pl.loop(0, x_ref.shape[0] // block)
        def _(index):
            at = pl.ds(pl.multiple_of(index * block, block), block)
            resid = x_ref[at, :].astype(F32) + (dot_nn(mixed_ref[at, :], weight) + vec_ref[4:5, :])
            resid_ref[at, :] = resid
            hat, _ = normalize(resid)
            n2_ref[at, :] = (hat * vec_ref[5:6, :] + vec_ref[6:7, :]).astype(BF16)

    pre = dot_nn(n2_ref[...], up_block(wup_ref)) + bup_ref[...]
    square = pre * pre
    tanh = jnp.tanh(pre * (GELU_C + (GELU_C * GELU_A) * square))
    half = 0.5 + 0.5 * tanh
    act = (pre * half).astype(BF16)
    inner = GELU_C + (3.0 * GELU_C * GELU_A) * square
    slope_ref[...] = (half + (0.5 * pre) * (1.0 - tanh * tanh) * inner).astype(BF16)
    act_ref[...] = act
    grad_weight = dot_tn(act, cot_ref[...])
    first = (me & 1) == 0
    side = send_ref.shape[3]
    low, high = grad_weight[:, :side], grad_weight[:, side:]
    keep = jnp.where(first, low, high).astype(BF16)
    send = jnp.where(first, high, low).astype(BF16)
    deep = send_ref.shape[2]
    chips = keep.shape[0] // deep
    for index in range(chips):
        chip = (step * chips + index) ^ (me >> 1)
        keep_ref[chip & 3, chip >> 2] = keep[index * deep : (index + 1) * deep]
        send_ref[chip & 3, chip >> 2] = send[index * deep : (index + 1) * deep]


def spread(me, rows, put):
    layer, plane = me >> 3, (me >> 1) & 3
    each = rows.shape[0] // CHIPS
    for chip in range(CHIPS):
        put((chip & 3) ^ plane, (chip >> 2) ^ layer, rows[chip * each : (chip + 1) * each].astype(BF16))


def mlp_down(me_ref, n2_ref, cot_ref, resid_ref, vec_ref, mixed_ref, act_ref, slope_ref, wup_ref, wdown_ref,
             out_ref, gresid_ref, gattn_ref, send_ref, keep_ref, dbu_ref, dsum_ref, out_acc, grad_acc):
    step = pl.program_id(0)
    steps = pl.num_programs(0)
    me = me_ref[0]
    half_steps = steps // 2

    @pl.when(step == 0)
    def _():
        out_acc[...] = jnp.zeros_like(out_acc)
        grad_acc[...] = jnp.zeros_like(grad_acc)

    cot = cot_ref[...]
    wdown = down_block(wdown_ref)
    grad_up = (dot_nt(cot, wdown) * slope_ref[...].astype(F32)).astype(BF16)
    dbu_ref[...] = column_sum(grad_up.astype(F32))
    grad_weight = dot_tn(n2_ref[...], grad_up)
    each = grad_weight.shape[0] // CHIPS

    def put_in(ref, fold, rows):
        base = pl.multiple_of(fold * each, 16)

        def put(plane, layer, piece):
            ref[plane, layer, pl.ds(base, each), :] = piece

        spread(me, rows, put)

    @pl.when(step < half_steps)
    def _():
        put_in(send_ref, step, grad_weight)

    @pl.when(step >= half_steps)
    def _():
        put_in(keep_ref, step - half_steps, grad_weight)

    out_acc[...] += dot_nn(act_ref[...], wdown)
    grad_acc[...] += dot_nt(grad_up, up_block(wup_ref))

    @pl.when(step == steps - 1)
    def _():
        block = 256
        dsum_ref[...] = jnp.zeros_like(dsum_ref)

        @pl.loop(0, cot_ref.shape[0] // block)
        def _(index):
            at = pl.ds(pl.multiple_of(index * block, block), block)
            resid = resid_ref[at, :]
            out_ref[at, :] = (resid + (out_acc[at, :] + vec_ref[7:8, :])).astype(BF16)
            hat, inverse = normalize(resid)
            grad_two = grad_acc[at, :]
            gresid = cot_ref[at, :].astype(F32) + norm_back(grad_two, vec_ref[5:6, :], hat, inverse)
            gresid_ref[at, :] = gresid
            gattn = gresid.astype(BF16)
            gattn_ref[at, :] = gattn
            dsum_ref[0:1, :] += column_sum(gattn.astype(F32))
            dsum_ref[1:2, :] += column_sum(grad_two * hat)
            dsum_ref[2:3, :] += column_sum(grad_two)

        side = send_ref.shape[3]
        grad_out = dot_tn(mixed_ref[...], gattn_ref[...])
        first = (me & 1) == 0
        low, high = grad_out[:, :side], grad_out[:, side:]
        put_in(send_ref, half_steps, jnp.where(first, high, low))
        put_in(keep_ref, half_steps, jnp.where(first, low, high))


def attention_backward(lengths_ref, q_ref, k_ref, v_ref, lse_ref, gattn_ref, wo_ref,
                       dq_ref, dk_ref, dv_ref, dsum_ref, gmix_ref):
    tile = pl.program_id(0)
    rows = q_ref.shape[0]
    gmix_ref[...] = dot_nt(gattn_ref[...], down_block(wo_ref)).astype(BF16)
    bias = mask_bias(lengths_ref, tile, lengths_ref.shape[1], rows)
    for pair in range(PAIRS):
        cols = pl.ds(pair * LANES, LANES)
        qp, kp, vp, gp = q_ref[:, cols], k_ref[:, cols], v_ref[:, cols], gmix_ref[:, cols]
        dq = dk = dv = None
        for side in range(2):
            head = 2 * pair + side
            qh, kh, gh = half_of(qp, side), half_of(kp, side), half_of(gp, side)
            probs = jnp.exp(dot_nt(qh, kp) + bias - lse_ref[:, head : head + 1])
            grad_probs = dot_nt(gh, vp)
            dot = jnp.sum(probs * grad_probs, axis=-1, keepdims=True)
            grad_scores = (probs * (grad_probs - dot)).astype(BF16)
            one_q = dot_nn(grad_scores, kh)
            one_k = dot_tn(grad_scores, qh)
            one_v = dot_tn(probs.astype(BF16), gh)
            dq = one_q if dq is None else dq + one_q
            dk = one_k if dk is None else dk + one_k
            dv = one_v if dv is None else dv + one_v
        dq_ref[:, cols] = (dq * SCALE).astype(BF16)
        dk_ref[:, cols] = dk.astype(BF16)
        dv_ref[:, cols] = dv.astype(BF16)

    @pl.when(tile == 0)
    def _():
        dsum_ref[...] = jnp.zeros_like(dsum_ref)

    dsum_ref[0:1, :] += column_sum(dq_ref[...].astype(F32))
    dsum_ref[1:2, :] += column_sum(dv_ref[...].astype(F32))


def weight_grads(me_ref, n1_ref, dq_ref, dk_ref, dv_ref, sum_one_ref, sum_qv_ref, sum_two_ref, sum_down_ref,
                 sum_up_ref, send_ref, keep_ref):
    step = pl.program_id(0)
    me = me_ref[0]
    n1 = n1_ref[...]
    results = [dot_tn(n1, ref[...]) for ref in (dq_ref, dk_ref, dv_ref)]
    each = n1.shape[1] // CHIPS
    side = send_ref.shape[3]
    vecs = jnp.concatenate((sum_one_ref[0:2], sum_qv_ref[0:2], sum_two_ref[0:3], sum_down_ref[0:1]), axis=0)

    def put_in(ref):
        for number, result in enumerate(results):
            def put(plane, layer, rows):
                ref[plane, layer, number * each : (number + 1) * each, :] = rows

            spread(me, result, put)
        for chip in range(CHIPS):
            half = chip // (CHIPS // 2)
            block = chip * (sum_up_ref.shape[1] // side) // CHIPS
            last = jnp.broadcast_to(sum_up_ref[:, block * side : (block + 1) * side], (8, side))
            rows = jnp.concatenate((vecs[:, half * side : (half + 1) * side], last), axis=0)
            ref[(chip & 3) ^ ((me >> 1) & 3), (chip >> 2) ^ (me >> 3), 3 * each :, :] = rows.astype(BF16)

    @pl.when(step == 0)
    def _():
        put_in(send_ref)

    @pl.when(step == 1)
    def _():
        put_in(keep_ref)


def tokens_backward(x_ref, gresid_ref, vec_ref, dq_ref, dk_ref, dv_ref, wq_ref, wk_ref, wv_ref, gtok_ref, dsum_ref):
    grad_one = dot_nt(dq_ref[...], wq_ref[...]) + dot_nt(dk_ref[...], wk_ref[...]) + dot_nt(dv_ref[...], wv_ref[...])
    hat, inverse = normalize(x_ref[...].astype(F32))
    gtok_ref[...] = (gresid_ref[...] + norm_back(grad_one, vec_ref[0:1, :], hat, inverse)).astype(BF16)

    @pl.when(pl.program_id(0) == 0)
    def _():
        dsum_ref[...] = jnp.zeros_like(dsum_ref)

    dsum_ref[0:1, :] += column_sum(grad_one * hat)
    dsum_ref[1:2, :] += column_sum(grad_one)


def rows_spec(block, width):
    return pl.BlockSpec((block, width), lambda i, *me: (i, 0))


def cols_spec(height, block):
    return pl.BlockSpec((height, block), lambda i, *me: (0, i))


def whole_spec(shape):
    return pl.BlockSpec(shape, lambda *i: (0,) * len(shape), pipeline_mode=pl.Buffered(1))


def kept_spec(shape):
    return pl.BlockSpec(shape, lambda *i: (0,) * len(shape))


SMEM = pl.BlockSpec(memory_space=pltpu.SMEM)


def call(kernel, grid, ins, outs, scratch, name, flops, *args):
    out_specs = tuple(spec for spec, _ in outs)
    out_shape = tuple(shape for _, shape in outs)
    return pl.pallas_call(
        kernel,
        grid=grid,
        in_specs=ins,
        out_specs=out_specs,
        out_shape=out_shape,
        scratch_shapes=scratch,
        compiler_params=pltpu.CompilerParams(vmem_limit_bytes=VMEM, dimension_semantics=("arbitrary",) * len(grid)),
        name=name,
    )(*args)


def call_with(me, kernel, steps, ins, outs, scratch, name, flops, *args):
    out_shape = tuple(shape for _, shape in outs)
    return pl.pallas_call(
        kernel,
        grid_spec=pltpu.PrefetchScalarGridSpec(
            num_scalar_prefetch=1, grid=(steps,), in_specs=ins, out_specs=tuple(spec for spec, _ in outs),
            scratch_shapes=scratch),
        out_shape=out_shape,
        compiler_params=pltpu.CompilerParams(vmem_limit_bytes=VMEM, dimension_semantics=("arbitrary",)),
        name=name,
    )(me, *args)


def shaped(*shape, dtype=BF16):
    return jax.ShapeDtypeStruct(shape, dtype)


def flipped(count, change):
    pairs = []
    for source in range(count):
        core, chip = source & 1, source >> 1
        core, chip = change(core, chip)
        pairs.append((source, 2 * chip + core))
    return pairs


def swap(array, change):
    return lax.ppermute(array, "dp", flipped(lax.axis_size("dp"), change))


def other_core(core, chip):
    return core ^ 1, chip


def other_plane(distance):
    return lambda core, chip: (core, chip ^ distance)


def other_layer(distance):
    return lambda core, chip: (core, chip ^ (4 * distance))


def split_shards(core_ref, q_ref, k_ref, v_ref, o_ref, u_ref, d_ref, keep_ref, send_ref):
    own, width = q_ref.shape
    side = width // 2
    first = core_ref[0] == 0

    def put(index, low, high):
        keep_ref[index] = jnp.where(first, low, high).astype(BF16)
        send_ref[index] = jnp.where(first, high, low).astype(BF16)

    for index, ref in enumerate((q_ref, k_ref, v_ref, o_ref)):
        rows = ref[...].astype(F32)
        put(index, rows[:, :side], rows[:, side:])
    up = u_ref[...].astype(F32)
    folds = up.shape[1] // width
    for part in range(folds):
        low = part * side
        high = (folds + part) * side
        put(4 + part, up[:, low : low + side], up[:, high : high + side])
    down = d_ref[...].astype(F32)
    for part in range(folds):
        rows = down[part * own : (part + 1) * own]
        put(4 + folds + part, rows[:, :side], rows[:, side:])


def join_shards(me_ref, keep_ref, take_ref, *refs):
    vectors, (near_ref, far_ref) = refs[:-2], refs[-2:]
    me = me_ref[0]
    first = (me & 1) == 0
    parts, own, side = keep_ref.shape
    folds = (parts - 4) // 2
    keep = keep_ref[...].astype(F32)
    take = take_ref[...].astype(F32)

    def joined(index):
        low = jnp.where(first, keep[index], take[index])
        high = jnp.where(first, take[index], keep[index])
        return jnp.concatenate((low, high), axis=0).astype(BF16)

    for index in range(3):
        near_ref[2 * own * index : 2 * own * (index + 1), :] = joined(index)
    for index in range(folds):
        far_ref[2 * own * index : 2 * own * (index + 1), :] = joined(4 + index)
    base = 2 * folds * own
    near = keep[4 + folds :].reshape(folds * own, side)
    other = take[4 + folds :].reshape(folds * own, side)
    far_ref[base : base + folds * own, :] = jnp.where(first, near, other).astype(BF16)
    far_ref[base + folds * own : 2 * base, :] = jnp.where(first, other, near).astype(BF16)
    far_ref[2 * base :, :] = joined(3)
    rows = []
    for ref in vectors:
        flat = ref[...].astype(F32).reshape(1, -1)
        rows.append(jnp.concatenate((flat, jnp.zeros((1, side - flat.shape[1]), F32)), axis=1))
    rows.append(jnp.zeros((16 - len(rows), side), F32))
    rows = jnp.concatenate(rows, axis=0)
    short = pltpu.roll(rows, own * lax.rem(me, side // own), 1)
    long = pltpu.roll(rows, folds * own * lax.rem(me, side // (folds * own)), 1)
    index = lax.broadcasted_iota(jnp.int32, rows.shape, 0)
    near_ref[6 * own :, :] = jnp.where(index < 8, short, long).astype(BF16)


def across_layers(shard):
    return jnp.stack([shard] + [swap(shard, other_layer(distance)) for distance in (1, 2, 3)])


def after(arrays, *others):
    return lax.optimization_barrier((arrays, others))[0]


def small_call(kernel, args, outs, name, scratch=(), ins=None):
    return pl.pallas_call(
        kernel,
        in_specs=ins,
        out_specs=tuple(spec for spec, _ in outs),
        out_shape=tuple(shape for _, shape in outs),
        scratch_shapes=list(scratch),
        compiler_params=pltpu.CompilerParams(vmem_limit_bytes=VMEM),
        name=name,
    )(*args)


VMEM_SPEC = pl.BlockSpec(memory_space=pltpu.VMEM)
ANY_SPEC = pl.BlockSpec(memory_space=pl.ANY)


def gather_by_hand(me, weights, vectors):
    count = lax.axis_size("dp")
    own, width = weights[0].shape
    side = width // 2
    folds = weights[5].shape[0] // own
    halves = (VMEM_SPEC, shaped(4 + 2 * folds, own, side))
    keep, send = small_call(split_shards, (me & 1, *weights), [halves, halves], "split_shards", ins=[SMEM] + [VMEM_SPEC] * 6)
    take = swap(send, other_core)
    near, far = small_call(
        join_shards, (me, keep, take, *vectors),
        [(VMEM_SPEC, shaped(6 * own + 16, side)), (VMEM_SPEC, shaped((4 * folds + 2) * own, side))], "join_shards",
        ins=[SMEM] + [VMEM_SPEC] * (2 + len(vectors)))
    far = lax.all_gather(far, "dp", axis=0, tiled=True).reshape(count // 2, 2, (4 * folds + 2) * own, side)
    near = across_layers(near)
    near = [near] + [swap(near, other_plane(distance)) for distance in (1, 2, 3)]
    return near + [swap(piece, other_core) for piece in near], far


def gather_plain(weights, vectors):
    squares, up_weight, down_weight = weights[:4], weights[4], weights[5]
    count = lax.axis_size("dp")
    own, width = squares[0].shape
    folds = down_weight.shape[0] // own
    hidden = up_weight.shape[1]
    side = width // 2
    flat = jnp.concatenate(vectors)
    packed = jnp.concatenate(
        (
            *squares,
            up_weight.reshape(own, folds, width).transpose(1, 0, 2).reshape(own * folds, width),
            down_weight,
            jnp.pad(flat.reshape(1, -1), ((0, 7), (0, width - flat.size))),
        ),
        axis=0,
    )
    whole = lax.all_gather(packed, "dp", axis=0, tiled=True).reshape(count, -1, width)
    square_all = [whole[:, index * own : (index + 1) * own, :].reshape(width, width) for index in range(4)]
    wup = whole[:, 4 * own : (4 + folds) * own, :].reshape(count, folds, own, width).transpose(0, 2, 1, 3)
    wup = wup.reshape(CHIPS, width // CHIPS, 2, folds, side).transpose(0, 2, 3, 1, 4).reshape(CHIPS, 2, -1, side)
    wdown = whole[:, (4 + folds) * own : (4 + 2 * folds) * own, :]
    wdown = wdown.reshape(CHIPS, hidden // CHIPS, 2, side).transpose(0, 2, 1, 3)
    last = whole[:, (4 + 2 * folds) * own, : flat.size].astype(F32)
    vec = last[:, : 8 * own].reshape(count, 8, own).transpose(1, 0, 2).reshape(8, width)
    bup = last[:, 8 * own :].reshape(1, hidden)
    wo = square_all[3].reshape(CHIPS, width // CHIPS, 2, side).transpose(0, 2, 1, 3)
    return (*square_all[:3], jnp.concatenate((wup, wdown, wo), axis=2), jnp.pad(vec, ((0, 8), (0, 0))), bup)


def merge_planes(keep_ref, take_ref, own_ref, *send_refs):
    for plane in range(4):
        whole = keep_ref[plane].astype(F32) + take_ref[plane].astype(F32)
        if plane == 0:
            own_ref[...] = whole
        else:
            send_refs[plane - 1][...] = whole.astype(BF16)


def merge_layers(own_ref, a_ref, b_ref, c_ref, rest_ref, *send_refs):
    for layer in range(4):
        whole = own_ref[layer] + a_ref[layer].astype(F32) + b_ref[layer].astype(F32) + c_ref[layer].astype(F32)
        if layer == 0:
            rest_ref[...] = whole
        else:
            send_refs[layer - 1][...] = whole.astype(BF16)


def merge_last(parts, core_ref, rest_ref, a_ref, b_ref, c_ref, keep_ref, send_ref, *flat_refs):
    whole = rest_ref[...] + a_ref[...].astype(F32) + b_ref[...].astype(F32) + c_ref[...].astype(F32)
    first = core_ref[0] == 0
    base = 0
    at = 0
    for size in parts:
        low = whole[base : base + size]
        high = whole[base + size : base + 2 * size]
        keep_ref[at : at + size, :] = jnp.where(first, low, high)
        send_ref[at : at + size, :] = jnp.where(first, high, low)
        base += 2 * size
        at += size
    if flat_refs:
        flat_refs[0][...] = whole[base:]


def finish_hidden(core_ref, keep_ref, take_ref, down_ref, up_ref, out_ref):
    first = core_ref[0] == 0
    keep, take = keep_ref[...], take_ref[...]
    left, right = jnp.where(first, keep, take), jnp.where(first, take, keep)
    side = keep.shape[1]
    deep = down_ref.shape[0]
    down_ref[:, :side] = left[:deep]
    down_ref[:, side:] = right[:deep]
    own, hidden = up_ref.shape
    folds = hidden // (2 * side)
    for fold in range(folds):
        rows = slice(deep + fold * own, deep + (fold + 1) * own)
        up_ref[:, fold * side : (fold + 1) * side] = left[rows]
        up_ref[:, (folds + fold) * side : (folds + fold + 1) * side] = right[rows]
    rows = slice(deep + folds * own, deep + (folds + 1) * own)
    out_ref[:, :side] = left[rows]
    out_ref[:, side:] = right[rows]


def finish_square(me_ref, keep_ref, take_ref, flat_ref, *refs):
    me = me_ref[0]
    first = (me & 1) == 0
    keep, take = keep_ref[...], take_ref[...]
    left, right = jnp.where(first, keep, take), jnp.where(first, take, keep)
    side = keep.shape[1]
    own = refs[0].shape[0]
    for number, ref in enumerate(refs[:3]):
        ref[:, :side] = left[number * own : (number + 1) * own]
        ref[:, side:] = right[number * own : (number + 1) * own]
    flat = flat_ref[...]
    long = refs[-1].shape[0]
    short_turn = lax.rem(side - own * lax.rem(me, side // own), side)
    long_turn = lax.rem(side - long * lax.rem(me, side // long), side)
    short = pltpu.roll(flat, short_turn, 1)
    for number, ref in enumerate(refs[3:-1]):
        ref[...] = short[number, :own]
    refs[-1][...] = pltpu.roll(flat, long_turn, 1)[8, :long]


def scatter_core(send):
    return swap(send, other_core)


def scatter_planes(keep, take):
    planes, layers, rows, side = keep.shape
    block = pl.BlockSpec((planes, 1, rows, side), lambda i: (0, i, 0, 0))
    out = pl.BlockSpec((1, rows, side), lambda i: (i, 0, 0))
    own, *sends = call(
        merge_planes, (layers,), [block, block],
        [(out, shaped(layers, rows, side, dtype=F32))] + [(out, shaped(layers, rows, side))] * 3, [], "merge_planes", 0,
        keep, take)
    return [own] + [swap(piece, other_plane(r + 1)) for r, piece in enumerate(sends)]


def scatter_layers(pieces):
    rows, side = pieces[0].shape[1:]
    rest, *sends = small_call(
        merge_layers, pieces, [(VMEM_SPEC, shaped(rows, side, dtype=F32))] + [(VMEM_SPEC, shaped(rows, side))] * 3,
        "merge_layers", ins=[VMEM_SPEC] * 4)
    return [rest] + [swap(piece, other_layer(r + 1)) for r, piece in enumerate(sends)]


def scatter_last(core, pieces, parts):
    rows, side = pieces[0].shape
    half = sum(parts)
    outs = [(VMEM_SPEC, shaped(half, side, dtype=F32))] * 2
    if rows > 2 * half:
        outs.append((VMEM_SPEC, shaped(rows - 2 * half, side, dtype=F32)))
    return small_call(
        functools.partial(merge_last, parts), (core, *pieces), outs, "merge_last", ins=[SMEM] + [VMEM_SPEC] * 4)


def reduce_plain(down_pair, up_pair, square_pair, flat):
    def whole(pair):
        return jnp.stack(pair).transpose(2, 1, 3, 0, 4)

    def squares(rows, parts, each):
        side = rows.shape[-1]
        return rows.reshape(CHIPS, parts, each, 2 * side).transpose(1, 0, 2, 3).reshape(parts, CHIPS * each, 2 * side)

    def scattered(array, axis):
        return lax.psum_scatter(array, "dp", scatter_dimension=axis, tiled=True).astype(F32)

    down, up, square = whole(down_pair), whole(up_pair), whole(square_pair)
    layers, planes, deep, _, side = down.shape
    each = up.shape[2] - deep
    folds = deep // each
    out = squares(up[:, :, deep:], 1, each)
    up = up[:, :, :deep].reshape(CHIPS, folds, each, 2, side).transpose(0, 2, 3, 1, 4)
    square = squares(square[:, :, : 3 * each], 3, each)
    return (
        scattered(down.reshape(CHIPS * deep, 2 * side), 0),
        scattered(up.reshape(CHIPS * each, 2 * folds * side), 0),
        *scattered(jnp.concatenate((square, out), axis=0), 1),
        lax.psum_scatter(flat, "dp", scatter_dimension=0, tiled=True).reshape(-1),
    )


def body(tokens, lengths, attn_gain, attn_shift, query_weight, query_bias, key_weight, value_weight, value_bias,
         out_weight, out_bias, mlp_gain, mlp_shift, up_weight, up_bias, down_weight, down_bias, grad_out):
    count = lax.axis_size("dp")
    rows, width = tokens.shape
    tiles = lengths.shape[0]
    tile = rows // tiles
    hidden = up_bias.shape[0] * count
    own = width // count
    folds = hidden // width
    vectors = (attn_gain, attn_shift, query_bias, value_bias, out_bias, mlp_gain, mlp_shift, down_bias, up_bias)
    by_hand = count == 2 * CHIPS
    me = lax.axis_index("dp").astype(jnp.int32).reshape(1) if by_hand else jnp.zeros((1,), jnp.int32)
    core = me & 1
    weights = (query_weight, key_weight, value_weight, out_weight, up_weight, down_weight)

    tile_rows = rows_spec(tile, width)
    square = whole_spec((width, width))
    vec_spec = whole_spec((16, width))
    sums = (kept_spec((8, width)), shaped(8, width, dtype=F32))
    low_rows = (tile_rows, shaped(rows, width))
    lse_spec = rows_spec(tile, LANES)
    mac = 2 * rows * width * width
    kept_square = (kept_spec((width, width)), shaped(width, width))
    side = width // 2
    if by_hand:
        near, far = gather_by_hand(me, weights, vectors)
        n1, q, k, v, wq, wk, wv, vec, bup = call_with(
            me, project, tiles, [rows_spec(tile, width)] + [ANY_SPEC] * 8,
            [low_rows] * 4 + [kept_square] * 3
            + [(kept_spec((16, width)), shaped(16, width, dtype=F32)), (kept_spec((1, hidden)), shaped(1, hidden, dtype=F32))],
            [pltpu.VMEM((count, 16, side), BF16), pltpu.SemaphoreType.DMA((4,))], "project", 3 * mac, tokens, *near)
    else:
        wq, wk, wv, far, vec, bup = gather_plain(weights, vectors)
        n1, q, k, v = call(
            project_rows, (tiles,), [tile_rows, vec_spec, square, square, square], [low_rows] * 4,
            [], "project", 3 * mac, tokens, vec, wq, wk, wv)
    mixed, lse, cot, sum_down = call(
        attention_forward, (tiles,), [SMEM, tile_rows, tile_rows, tile_rows, tile_rows],
        [low_rows, (lse_spec, shaped(rows, LANES, dtype=F32)), low_rows, sums],
        [], "attention_forward", mac, lengths, grad_out, q, k, v)

    steps = hidden // side
    each = width // CHIPS
    deep = hidden // CHIPS
    full_rows = whole_spec((rows, width))
    kept_low = (kept_spec((rows, width)), shaped(rows, width))
    kept_high = (kept_spec((rows, width)), shaped(rows, width, dtype=F32))

    def pair_of(count):
        return (kept_spec((4, CHIPS // 4, count, side)), shaped(4, CHIPS // 4, count, side))

    def up_spec(at):
        return pl.BlockSpec(
            (CHIPS, 1, each, side), lambda i, me: (0, at(i, me) // folds, lax.rem(at(i, me), folds), 0))

    def down_spec(at):
        return pl.BlockSpec((side // deep, 2, deep, side), lambda i, me: (at(i, me), 0, 1, 0))

    out_spec = pl.BlockSpec((CHIPS, 2, each, side), lambda *i: (0, 0, 2 * folds, 0), pipeline_mode=pl.Buffered(1))

    def hidden_spec(height, at):
        return pl.BlockSpec((height, side), lambda i, me: (0, at(i, me)))

    def in_turn(i, me):
        return i

    def send_first(i, me):
        return ((i // folds) ^ 1 ^ (me[0] & 1)) * folds + lax.rem(i, folds)

    hidden_rows = (hidden_spec(rows, in_turn), shaped(rows, hidden))
    resid, n2, act, slope, down_send, down_keep = call_with(
        me, mlp_up, steps,
        [full_rows, full_rows, vec_spec, out_spec, full_rows, up_spec(in_turn), hidden_spec(1, in_turn)],
        [kept_high, kept_low, hidden_rows, hidden_rows, pair_of(deep), pair_of(deep)],
        [], "mlp_up", 2 * folds * mac, tokens, mixed, vec, far, cot, far, bup)

    out, gresid, gattn, up_send, up_keep, sum_up, sum_two = call_with(
        me, mlp_down, steps,
        [full_rows, full_rows, full_rows, vec_spec, full_rows, hidden_spec(rows, send_first),
         hidden_spec(rows, send_first), up_spec(send_first), down_spec(send_first)],
        [kept_low, kept_high, kept_low, pair_of(deep + each), pair_of(deep + each),
         (hidden_spec(1, send_first), shaped(1, hidden, dtype=F32)), sums],
        [pltpu.VMEM((rows, width), F32), pltpu.VMEM((rows, width), F32)],
        "mlp_down", 4 * folds * mac, n2, cot, resid, vec, mixed, act, slope, far, far)
    if by_hand:
        down_take = after(scatter_core(down_send), gattn)
        down_planes = scatter_planes(down_keep, down_take)
        up_take = scatter_core(up_send)
        gattn = after(gattn, down_planes[0])
    dq, dk, dv, sum_qv = call(
        attention_backward, (tiles,), [SMEM, tile_rows, tile_rows, tile_rows, lse_spec, tile_rows, out_spec],
        [low_rows] * 3 + [sums], [pltpu.VMEM((tile, width), BF16)],
        "attention_backward", 4 * mac, lengths, q, k, v, lse, gattn, far)
    if by_hand:
        up_take, down_planes = after((up_take, down_planes), dq)
        down_layers = scatter_layers(down_planes)
        up_planes = scatter_planes(up_keep, up_take)
        gresid = after(gresid, down_layers[0], up_planes[0])
    gtok, sum_one = call(
        tokens_backward, (tiles,),
        [tile_rows, tile_rows, vec_spec, tile_rows, tile_rows, tile_rows, square, square, square],
        [low_rows, sums], [], "tokens_backward", 3 * mac, tokens, gresid, vec, dq, dk, dv, wq, wk, wv)
    if by_hand:
        up_planes, down_layers = after((up_planes, down_layers), sum_one)
        up_layers = scatter_layers(up_planes)
        down_keep, down_send = scatter_last(core, down_layers, (folds * own,))
        n1 = after(n1, up_layers[0], down_keep)

    half_cols = pl.BlockSpec((rows, side), lambda i, me: (0, (me[0] & 1) ^ 1 ^ i))
    sum_spec = whole_spec((8, width))
    square_send, square_keep = call_with(
        me, weight_grads, 2, [full_rows] + [half_cols] * 3 + [sum_spec] * 4 + [whole_spec((1, hidden))],
        [pair_of(3 * each + 16)] * 2, [],
        "weight_grads", 3 * mac, n1, dq, dk, dv, sum_one, sum_qv, sum_two, sum_down, sum_up)
    if by_hand:
        square_take = scatter_core(square_send)
        up_layers = after(up_layers, square_send)
        up_keep, up_send = scatter_last(core, up_layers, (own,) * (folds + 1))
        hidden_keep = jnp.concatenate((down_keep, up_keep), axis=0)
        hidden_take = scatter_core(jnp.concatenate((down_send, up_send), axis=0))
        square_planes = scatter_planes(square_keep, square_take)
        hidden_take = after(hidden_take, square_planes[0])
        g_down, g_up, g_o = small_call(
            finish_hidden, (core, hidden_keep, hidden_take),
            [(VMEM_SPEC, shaped(folds * own, width, dtype=F32)), (VMEM_SPEC, shaped(own, hidden, dtype=F32)),
             (VMEM_SPEC, shaped(own, width, dtype=F32))], "finish_hidden", ins=[SMEM] + [VMEM_SPEC] * 2)
        square_layers = scatter_layers(square_planes)
        square_keep, square_send, flat = scatter_last(core, square_layers, (own,) * 3)
        square_take = scatter_core(square_send)
        g_q, g_k, g_v, *g_flat, g_ub = small_call(
            finish_square, (me, square_keep, square_take, flat),
            [(VMEM_SPEC, shaped(own, width, dtype=F32))] * 3 + [(VMEM_SPEC, shaped(own, dtype=F32))] * 8
            + [(VMEM_SPEC, shaped(folds * own, dtype=F32))], "finish_square", ins=[SMEM] + [VMEM_SPEC] * 3)
    else:
        flat = jnp.concatenate((sum_one[0:2], sum_qv[0:2], sum_two[0:3], sum_down[0:1]), axis=0)
        flat = flat.reshape(8, count, own).transpose(1, 0, 2).reshape(count, 8 * own)
        flat = jnp.concatenate((flat, sum_up.reshape(count, folds * own)), axis=1)
        g_down, g_up, g_q, g_k, g_v, g_o, flat = reduce_plain(
            (down_keep, down_send), (up_keep, up_send), (square_keep, square_send), flat)
        g_flat = [flat[index * own : (index + 1) * own] for index in range(8)]
        g_ub = flat[8 * own :]
    g_gain, g_shift, g_qb, g_vb, g_ob, g_mg, g_ms, g_db = g_flat
    return (out, gtok, g_gain, g_shift, g_q, g_qb, g_k, g_v, g_vb, g_o, g_ob, g_mg, g_ms, g_up, g_ub, g_down, g_db)


def solution(mesh):
    rows, flat = P("dp", None), P("dp")
    return jax.shard_map(
        body,
        mesh=mesh,
        in_specs=(rows, rows, flat, flat, rows, flat, rows, rows, flat, rows, flat, flat, flat, rows, flat, rows, flat, rows),
        out_specs=(rows, rows, flat, flat, rows, flat, rows, rows, flat, rows, flat, flat, flat, rows, flat, rows, flat),
        check_vma=False,
    )
```

```python
import functools

import jax
import jax.numpy as jnp
from jax import lax
from jax.experimental import pallas as pl
from jax.experimental.pallas import tpu as pltpu
from jax.sharding import PartitionSpec as P

HEADS = 12
HEAD_DIM = 64
PAIRS = 6
LANES = 128
CHIPS = 16
MERGE_STEPS = 2
LONG = 10**11
SHORT = 6 * 10**9
EPS = 1e-06
MASKED = -1e30
SCALE = HEAD_DIM**-0.5
GELU_C = 0.7978845608028654
GELU_A = 0.044715
VMEM = 64 * 1024 * 1024 - 65536
F32 = jnp.float32
BF16 = jnp.bfloat16


def dot_nn(left, right):
    return lax.dot_general(left, right, (((1,), (0,)), ((), ())), preferred_element_type=F32)


def dot_nt(left, right):
    return lax.dot_general(left, right, (((1,), (1,)), ((), ())), preferred_element_type=F32)


def dot_tn(left, right):
    return lax.dot_general(left, right, (((0,), (0,)), ((), ())), preferred_element_type=F32)


def normalize(rows):
    centered = rows - jnp.mean(rows, axis=-1, keepdims=True)
    inverse = lax.rsqrt(jnp.mean(centered * centered, axis=-1, keepdims=True) + EPS)
    return centered * inverse, inverse


def norm_back(grads, gain, hat, inverse):
    scaled = grads * gain
    mean = jnp.mean(scaled, axis=-1, keepdims=True)
    mean_hat = jnp.mean(scaled * hat, axis=-1, keepdims=True)
    return inverse * (scaled - mean - hat * mean_hat)


def column_sum(rows):
    return jnp.sum(rows, axis=0, keepdims=True)


def segments(lengths_ref, tile, slots, rows, axis):
    shape = (rows, 1) if axis == 0 else (1, rows)
    index = lax.broadcasted_iota(jnp.int32, shape, axis)
    segment = jnp.zeros(shape, jnp.int32)
    bound = 0
    for slot in range(slots):
        bound = bound + lengths_ref[tile, slot]
        segment = segment + (index >= bound).astype(jnp.int32)
    return segment


def mask_bias(lengths_ref, tile, slots, rows):
    same = segments(lengths_ref, tile, slots, rows, 0) == segments(lengths_ref, tile, slots, rows, 1)
    return jnp.where(same, 0.0, MASKED).astype(F32)


def half_of(pair, side):
    lane = lax.broadcasted_iota(jnp.int32, pair.shape, 1)
    keep = lane < HEAD_DIM if side == 0 else lane >= HEAD_DIM
    return jnp.where(keep, pair, jnp.zeros_like(pair))


def fetch_weights(me, sources, weight_refs, parts_ref, sem):
    core, chip = me & 1, me >> 1
    side = sources[0].shape[2]
    each = weight_refs[0].shape[0] // CHIPS
    for index, source in enumerate(sources):
        half = core if index < 4 else 1 - core
        cols = pl.ds(pl.multiple_of(half * side, LANES), side)
        for layer in range(4):
            owner = chip ^ (4 * layer + index % 4)
            rows = pl.ds(pl.multiple_of(owner * each, 16), each)
            for number, ref in enumerate(weight_refs):
                pltpu.make_async_copy(
                    source.at[layer, pl.ds(number * each, each), :], ref.at[rows, cols], sem.at[number]
                ).start()
            pltpu.make_async_copy(
                source.at[layer, pl.ds(4 * each, 16), :], parts_ref.at[2 * owner + half], sem.at[4]
            ).start()


def project(me_ref, x_ref, *refs):
    sources = refs[:8]
    n1_ref, q_ref, k_ref, v_ref, wq_ref, wk_ref, wv_ref, wo_ref, vec_ref, bup_ref, parts_ref, sem = refs[8:]
    weights = (wq_ref, wk_ref, wv_ref, wo_ref)

    @pl.when(pl.program_id(0) == 0)
    def _():
        fetch_weights(me_ref[0], sources, weights, parts_ref, sem)
        for number, ref in enumerate(weights + (parts_ref,)):
            pltpu.make_async_copy(ref, ref, sem.at[number]).wait()
        count, _, side = parts_ref.shape
        parts = [parts_ref[device].astype(F32) for device in range(count)]
        group = count // 2
        vec_ref[...] = jnp.concatenate((sum(parts[:group]), sum(parts[group:])), axis=1)
        blocks = bup_ref.shape[1] // side
        group = count // blocks
        for block in range(blocks):
            rows = sum(parts[block * group : (block + 1) * group])
            bup_ref[:, block * side : (block + 1) * side] = rows[8:9]

    project_rows(x_ref, vec_ref, wq_ref, wk_ref, wv_ref, n1_ref, q_ref, k_ref, v_ref)


def project_rows(x_ref, vec_ref, wq_ref, wk_ref, wv_ref, n1_ref, q_ref, k_ref, v_ref):
    hat, _ = normalize(x_ref[...].astype(F32))
    n1 = (hat * vec_ref[0:1, :] + vec_ref[1:2, :]).astype(BF16)
    n1_ref[...] = n1
    q_ref[...] = (dot_nn(n1, wq_ref[...]) + vec_ref[2:3, :]).astype(BF16) * jnp.asarray(SCALE, BF16)
    k_ref[...] = dot_nn(n1, wk_ref[...]).astype(BF16)
    v_ref[...] = (dot_nn(n1, wv_ref[...]) + vec_ref[3:4, :]).astype(BF16)


def attention_forward(lengths_ref, x_ref, grad_ref, vec_ref, q_ref, k_ref, v_ref, wo_ref,
                      mixed_ref, lse_ref, resid_ref, n2_ref, cot_ref, dsum_ref):
    tile = pl.program_id(0)
    rows = q_ref.shape[0]
    slots = lengths_ref.shape[1]
    bias = mask_bias(lengths_ref, tile, slots, rows)
    lane = lax.broadcasted_iota(jnp.int32, (rows, LANES), 1)
    lse = jnp.zeros((rows, LANES), F32)

    def at(pair):
        return pl.ds(pair * LANES, LANES)

    def scores_of(pair):
        qp, kp = q_ref[:, at(pair)], k_ref[:, at(pair)]
        return [dot_nt(half_of(qp, side), kp) for side in range(2)]

    def softmax_of(scores):
        scores = scores + bias
        top = jnp.max(scores, axis=-1, keepdims=True)
        weights = jnp.exp(scores - top)
        sums = jnp.sum(weights, axis=-1, keepdims=True)
        return (weights * (1.0 / sums)).astype(BF16), top + jnp.log(sums)

    raw = {}
    probs = {}
    for turn in range(PAIRS + 2):
        if turn < PAIRS:
            raw[turn] = scores_of(turn)
        if 0 <= turn - 1 < PAIRS:
            both = [softmax_of(scores) for scores in raw.pop(turn - 1)]
            for side in range(2):
                lse = jnp.where(lane == 2 * (turn - 1) + side, both[side][1], lse)
            probs[turn - 1] = [pair[0] for pair in both]
        if turn >= 2:
            vp = v_ref[:, at(turn - 2)]
            parts = [dot_nn(probs[turn - 2][side], half_of(vp, side)) for side in range(2)]
            mixed_ref[:, at(turn - 2)] = (parts[0] + parts[1]).astype(BF16)
    lse_ref[...] = lse
    resid = x_ref[...].astype(F32) + (dot_nn(mixed_ref[...], wo_ref[...]) + vec_ref[4:5, :])
    resid_ref[...] = resid
    hat, _ = normalize(resid)
    n2_ref[...] = (hat * vec_ref[5:6, :] + vec_ref[6:7, :]).astype(BF16)
    valid = segments(lengths_ref, tile, slots, rows, 0) < slots
    cot = jnp.where(valid, grad_ref[...].astype(F32), 0.0)
    cot_ref[...] = cot.astype(BF16)

    @pl.when(tile == 0)
    def _():
        dsum_ref[...] = jnp.zeros_like(dsum_ref)

    dsum_ref[0:1, :] += column_sum(cot)


def flat_rows(ref):
    return ref[...].reshape(-1, ref.shape[-1])


def spread(me, rows, put):
    layer, plane = me >> 3, (me >> 1) & 3
    each = rows.shape[0] // CHIPS
    for chip in range(CHIPS):
        put((chip & 3) ^ plane, (chip >> 2) ^ layer, rows[chip * each : (chip + 1) * each].astype(BF16))


def mlp(me_ref, n2_ref, cot_ref, resid_ref, vec_ref, bup_ref, wup_ref, wdown_ref,
        out_ref, gtwo_ref, down_send_ref, down_keep_ref, up_send_ref, up_keep_ref, dbu_ref, acc, act_ref, gup_ref):
    step = pl.program_id(0)
    steps = pl.num_programs(0)
    me = me_ref[0]
    block = 256
    chunks = [slice(start, start + block) for start in range(0, n2_ref.shape[0], block)]

    @pl.when(step == 0)
    def _():
        gtwo_ref[...] = jnp.zeros_like(gtwo_ref)
        acc[...] = resid_ref[...] + vec_ref[7:8, :]

    wup = flat_rows(wup_ref)
    wdown = flat_rows(wdown_ref)
    sums = jnp.zeros_like(dbu_ref)
    for at in chunks:
        pre = dot_nn(n2_ref[at, :], wup) + bup_ref[...]
        grad_act = dot_nt(cot_ref[at, :], wdown)
        square = pre * pre
        tanh = jnp.tanh(pre * (GELU_C + (GELU_C * GELU_A) * square))
        half = 0.5 + 0.5 * tanh
        inner = GELU_C + (3.0 * GELU_C * GELU_A) * square
        act_ref[at, :] = (pre * half).astype(BF16)
        gup = (grad_act * (half + (0.5 * pre) * (1.0 - tanh * tanh) * inner)).astype(BF16)
        gup_ref[at, :] = gup
        sums = sums + column_sum(gup.astype(F32))
    dbu_ref[...] = sums
    for at in chunks:
        acc[at, :] += dot_nn(act_ref[at, :], wdown)
        gtwo_ref[at, :] += dot_nt(gup_ref[at, :], wup)

    grad_down = dot_tn(act_ref[...], cot_ref[...])
    first = (me & 1) == 0
    plane = (me >> 1) & 3
    deep = down_send_ref.shape[2]
    for index in range(4):
        low = grad_down[2 * deep * index : 2 * deep * index + deep]
        high = grad_down[2 * deep * index + deep : 2 * deep * (index + 1)]
        down_keep_ref[0, index ^ plane] = jnp.where(first, low, high).astype(BF16)
        down_send_ref[0, index ^ plane] = jnp.where(first, high, low).astype(BF16)

    grad_up = dot_tn(n2_ref[...], gup_ref[...])

    def put_in(ref):
        def put(plane, layer, piece):
            ref[0, layer, plane] = piece

        spread(me, grad_up, put)

    @pl.when(step < steps // 2)
    def _():
        put_in(up_send_ref)

    @pl.when(step >= steps // 2)
    def _():
        put_in(up_keep_ref)

    @pl.when(step == steps - 1)
    def _():
        out_ref[...] = acc[...].astype(BF16)


def attention_backward(lengths_ref, q_ref, k_ref, v_ref, lse_ref, cot_ref, resid_ref, gtwo_ref, vec_ref, wo_ref,
                       grads_ref, gresid_ref, dsum_ref, gmix_ref):
    tile = pl.program_id(0)
    rows = q_ref.shape[0]

    @pl.when(tile == 0)
    def _():
        dsum_ref[...] = jnp.zeros_like(dsum_ref)

    hat, inverse = normalize(resid_ref[...])
    grad_two = gtwo_ref[...]
    gresid = cot_ref[...].astype(F32) + norm_back(grad_two, vec_ref[5:6, :], hat, inverse)
    gresid_ref[...] = gresid
    gattn = gresid.astype(BF16)
    grads_ref[3] = gattn
    dsum_ref[2:3, :] += column_sum(gattn.astype(F32))
    dsum_ref[3:4, :] += column_sum(grad_two * hat)
    dsum_ref[4:5, :] += column_sum(grad_two)
    gmix_ref[...] = dot_nt(gattn, wo_ref[...]).astype(BF16)
    bias = mask_bias(lengths_ref, tile, lengths_ref.shape[1], rows)

    def load(pair):
        cols = pl.ds(pair * LANES, LANES)
        return q_ref[:, cols], k_ref[:, cols], v_ref[:, cols], gmix_ref[:, cols]

    def products_of(pair):
        qp, kp, vp, gp = load(pair)
        return [(dot_nt(half_of(qp, side), kp), dot_nt(half_of(gp, side), vp)) for side in range(2)]

    def softmax_back(pair, products):
        results = []
        for side, (scores, grad_probs) in enumerate(products):
            head = 2 * pair + side
            probs = jnp.exp(scores + bias - lse_ref[:, head : head + 1])
            weighted = probs * grad_probs
            dot = jnp.sum(weighted, axis=-1, keepdims=True)
            results.append((probs.astype(BF16), (weighted - probs * dot).astype(BF16)))
        return results

    def store(pair, results):
        qp, kp, vp, gp = load(pair)
        dq = sum(dot_nn(results[side][1], half_of(kp, side)) for side in range(2))
        dk = sum(dot_tn(results[side][1], half_of(qp, side)) for side in range(2))
        dv = sum(dot_tn(results[side][0], half_of(gp, side)) for side in range(2))
        cols = pl.ds(pair * LANES, LANES)
        grads_ref[0, :, cols] = (dq * SCALE).astype(BF16)
        grads_ref[1, :, cols] = dk.astype(BF16)
        grads_ref[2, :, cols] = dv.astype(BF16)

    raw = {}
    done = {}
    for turn in range(PAIRS + 2):
        if turn < PAIRS:
            raw[turn] = products_of(turn)
        if 0 <= turn - 1 < PAIRS:
            done[turn - 1] = softmax_back(turn - 1, raw.pop(turn - 1))
        if turn >= 2:
            store(turn - 2, done.pop(turn - 2))

    dsum_ref[0:1, :] += column_sum(grads_ref[0].astype(F32))
    dsum_ref[1:2, :] += column_sum(grads_ref[2].astype(F32))


def projections_backward(me_ref, x_ref, gresid_ref, vec_ref, grads_ref, wq_ref, wk_ref, wv_ref, n1_ref, mixed_ref,
                         columns_ref, sum_back_ref, sum_down_ref, sum_up_ref,
                         gtok_ref, dsum_ref, send_ref, keep_ref):
    step = pl.program_id(0)
    tiles = pl.num_programs(0) - 4
    me = me_ref[0]
    first = (me & 1) == 0
    side = send_ref.shape[3]
    each = wq_ref.shape[0] // CHIPS

    @pl.when(step == 0)
    def _():
        dsum_ref[...] = jnp.zeros_like(dsum_ref)

    @pl.when(step < tiles)
    def _():
        grad_one = dot_nt(grads_ref[0], wq_ref[...]) + dot_nt(grads_ref[1], wk_ref[...]) + dot_nt(grads_ref[2], wv_ref[...])
        hat, inverse = normalize(x_ref[...].astype(F32))
        gtok_ref[...] = (gresid_ref[...] + norm_back(grad_one, vec_ref[0:1, :], hat, inverse)).astype(BF16)
        dsum_ref[0:1, :] += column_sum(grad_one * hat)
        dsum_ref[1:2, :] += column_sum(grad_one)

    def run(left, number):
        result = dot_tn(left, columns_ref[0])
        low, high = result[:, :side], result[:, side:]
        rows_at = pl.ds(pl.multiple_of(number * each, 16), each)

        def put_send(plane, layer, rows):
            send_ref[layer, plane, rows_at, :] = rows

        def put_keep(plane, layer, rows):
            keep_ref[layer, plane, rows_at, :] = rows

        spread(me, jnp.where(first, high, low), put_send)
        spread(me, jnp.where(first, low, high), put_keep)

    @pl.when((step >= tiles) & (step < tiles + 3))
    def _():
        run(n1_ref[...], step - tiles)

    @pl.when(step == tiles + 3)
    def _():
        run(mixed_ref[...], 3)
        vecs = jnp.concatenate((dsum_ref[0:2], sum_back_ref[0:5], sum_down_ref[0:1]), axis=0)
        for chip in range(CHIPS):
            half = chip // (CHIPS // 2)
            block = chip * (sum_up_ref.shape[1] // side) // CHIPS
            last = jnp.broadcast_to(sum_up_ref[:, block * side : (block + 1) * side], (8, side))
            rows = jnp.concatenate((vecs[:, half * side : (half + 1) * side], last), axis=0).astype(BF16)
            at = ((chip >> 2) ^ (me >> 3), (chip & 3) ^ ((me >> 1) & 3))
            send_ref[at[0], at[1], 4 * each :, :] = rows
            keep_ref[at[0], at[1], 4 * each :, :] = rows


def rows_spec(block, width):
    return pl.BlockSpec((block, width), lambda i, *me: (i, 0))


def cols_spec(height, block):
    return pl.BlockSpec((height, block), lambda i, *me: (0, i))


def whole_spec(shape):
    return pl.BlockSpec(shape, lambda *i: (0,) * len(shape), pipeline_mode=pl.Buffered(1))


def kept_spec(shape):
    return pl.BlockSpec(shape, lambda *i: (0,) * len(shape))


SMEM = pl.BlockSpec(memory_space=pltpu.SMEM)


def cost(flops):
    return pl.CostEstimate(flops=flops, bytes_accessed=1, transcendentals=0)


def call(kernel, grid, ins, outs, scratch, name, flops, *args):
    out_specs = tuple(spec for spec, _ in outs)
    out_shape = tuple(shape for _, shape in outs)
    return pl.pallas_call(
        kernel,
        grid=grid,
        in_specs=ins,
        out_specs=out_specs,
        out_shape=out_shape,
        scratch_shapes=scratch,
        compiler_params=pltpu.CompilerParams(vmem_limit_bytes=VMEM, dimension_semantics=("arbitrary",) * len(grid)),
        cost_estimate=cost(flops),
        name=name,
    )(*args)


def call_with(me, kernel, steps, ins, outs, scratch, name, flops, *args):
    out_shape = tuple(shape for _, shape in outs)
    return pl.pallas_call(
        kernel,
        grid_spec=pltpu.PrefetchScalarGridSpec(
            num_scalar_prefetch=1, grid=(steps,), in_specs=ins, out_specs=tuple(spec for spec, _ in outs),
            scratch_shapes=scratch),
        out_shape=out_shape,
        compiler_params=pltpu.CompilerParams(vmem_limit_bytes=VMEM, dimension_semantics=("arbitrary",)),
        cost_estimate=cost(0),
        name=name,
    )(me, *args)


def shaped(*shape, dtype=BF16):
    return jax.ShapeDtypeStruct(shape, dtype)


def flipped(count, change):
    pairs = []
    for source in range(count):
        core, chip = source & 1, source >> 1
        core, chip = change(core, chip)
        pairs.append((source, 2 * chip + core))
    return pairs


def swap(array, change):
    return lax.ppermute(array, "dp", flipped(lax.axis_size("dp"), change))


def other_core(core, chip):
    return core ^ 1, chip


def first_plane(core, chip):
    return core, chip ^ (1 + core)


def second_plane(core, chip):
    return core, chip ^ (2 - core)


def other_plane(distance):
    return lambda core, chip: (core, chip ^ distance)


def other_layer(distance):
    return lambda core, chip: (core, chip ^ (4 * distance))


def split_shards(core_ref, q_ref, k_ref, v_ref, o_ref, u_ref, keep_ref, send_ref):
    width = q_ref.shape[1]
    side = width // 2
    first = core_ref[0] == 0

    def put(index, low, high):
        keep_ref[index] = jnp.where(first, low, high).astype(BF16)
        send_ref[index] = jnp.where(first, high, low).astype(BF16)

    for index, ref in enumerate((q_ref, k_ref, v_ref, o_ref)):
        rows = ref[...].astype(F32)
        put(index, rows[:, :side], rows[:, side:])
    up = u_ref[...].astype(F32)
    folds = up.shape[1] // width
    for part in range(folds):
        low = part * side
        high = (folds + part) * side
        put(4 + part, up[:, low : low + side], up[:, high : high + side])


def join_shards(me_ref, keep_ref, take_ref, down_ref, *refs):
    vectors, (near_ref, far_ref) = refs[:-2], refs[-2:]
    me = me_ref[0]
    first = (me & 1) == 0
    parts, own, side = keep_ref.shape
    folds = parts - 4
    keep = keep_ref[...].astype(F32)
    take = take_ref[...].astype(F32)

    def joined(index):
        low = jnp.where(first, keep[index], take[index])
        high = jnp.where(first, take[index], keep[index])
        return jnp.concatenate((low, high), axis=0).astype(BF16)

    for index in range(4):
        near_ref[2 * own * index : 2 * own * (index + 1), :] = joined(index)
    for index in range(folds):
        far_ref[2 * own * (index // 2) : 2 * own * (index // 2 + 1), side * (index % 2) : side * (index % 2 + 1)] = joined(4 + index)
    far_ref[folds * own :, :] = down_ref[...]
    rows = []
    for ref in vectors:
        flat = ref[...].astype(F32).reshape(1, -1)
        rows.append(jnp.concatenate((flat, jnp.zeros((1, side - flat.shape[1]), F32)), axis=1))
    rows.append(jnp.zeros((16 - len(rows), side), F32))
    rows = jnp.concatenate(rows, axis=0)
    short = pltpu.roll(rows, own * lax.rem(me, side // own), 1)
    long = pltpu.roll(rows, folds * own * lax.rem(me, side // (folds * own)), 1)
    index = lax.broadcasted_iota(jnp.int32, rows.shape, 0)
    near_ref[8 * own :, :] = jnp.where(index < 8, short, long).astype(BF16)


def across_layers(shard):
    return jnp.stack([shard] + [swap(shard, other_layer(distance)) for distance in (1, 2, 3)])


def after(arrays, *others):
    return lax.optimization_barrier((arrays, others))[0]


def small_call(kernel, args, outs, name, scratch=(), ins=None, flops=0):
    return pl.pallas_call(
        kernel,
        in_specs=ins,
        out_specs=tuple(spec for spec, _ in outs),
        out_shape=tuple(shape for _, shape in outs),
        scratch_shapes=list(scratch),
        compiler_params=pltpu.CompilerParams(vmem_limit_bytes=VMEM),
        cost_estimate=cost(flops),
        name=name,
    )(*args)


VMEM_SPEC = pl.BlockSpec(memory_space=pltpu.VMEM)
ANY_SPEC = pl.BlockSpec(memory_space=pl.ANY)


def gather_by_hand(me, weights, vectors):
    count = lax.axis_size("dp")
    own, width = weights[0].shape
    side = width // 2
    deep = weights[5].shape[0]
    folds = deep // own
    halves = (VMEM_SPEC, shaped(4 + folds, own, side))
    keep, send = small_call(
        split_shards, (me & 1, *weights[:5]), [halves, halves], "split_shards", ins=[SMEM] + [VMEM_SPEC] * 5)
    take = swap(send, other_core)
    near, far = small_call(
        join_shards, (me, keep, take, weights[5], *vectors),
        [(VMEM_SPEC, shaped(8 * own + 16, side)), (VMEM_SPEC, shaped(2 * deep, width))], "join_shards",
        ins=[SMEM] + [VMEM_SPEC] * (3 + len(vectors)))
    far = lax.all_gather(far, "dp", axis=0, tiled=True).reshape(count // 2, 2, 2 * deep, width)
    near = across_layers(near)
    near = [near] + [swap(near, other_plane(distance)) for distance in (1, 2, 3)]
    return near + [swap(piece, other_core) for piece in near], far


def gather_plain(weights, vectors):
    squares, up_weight, down_weight = weights[:4], weights[4], weights[5]
    count = lax.axis_size("dp")
    own, width = squares[0].shape
    folds = down_weight.shape[0] // own
    hidden = up_weight.shape[1]
    flat = jnp.concatenate(vectors)
    packed = jnp.concatenate(
        (
            *squares,
            up_weight.reshape(own, folds, width).transpose(1, 0, 2).reshape(own * folds, width),
            down_weight,
            jnp.pad(flat.reshape(1, -1), ((0, 7), (0, width - flat.size))),
        ),
        axis=0,
    )
    whole = lax.all_gather(packed, "dp", axis=0, tiled=True).reshape(count, -1, width)
    square_all = [whole[:, index * own : (index + 1) * own, :].reshape(width, width) for index in range(4)]
    wup = whole[:, 4 * own : (4 + folds) * own, :].reshape(count, folds, own, width).transpose(0, 2, 1, 3)
    wup = wup.reshape(CHIPS, width // CHIPS, 2, folds // 2, width).transpose(0, 2, 3, 1, 4).reshape(CHIPS, 2, -1, width)
    wdown = whole[:, (4 + folds) * own : (4 + 2 * folds) * own, :]
    wdown = wdown.reshape(CHIPS, 2, -1, width)
    last = whole[:, (4 + 2 * folds) * own, : flat.size].astype(F32)
    vec = last[:, : 8 * own].reshape(count, 8, own).transpose(1, 0, 2).reshape(8, width)
    bup = last[:, 8 * own :].reshape(1, hidden)
    return (*square_all, jnp.concatenate((wup, wdown), axis=2), jnp.pad(vec, ((0, 8), (0, 0))), bup)


def merge_core(core_ref, keep_ref, take_ref, own_ref, send_ref):
    core = core_ref[0]

    def whole(plane):
        return (keep_ref[:, plane].astype(F32) + take_ref[:, plane].astype(F32)).astype(BF16)

    own_ref[:, 0] = whole(0)
    own_ref[:, 1] = whole(2 - core)
    send_ref[:, 0] = whole(1 + core)
    send_ref[:, 1] = whole(3)


def merge_first(*refs):
    pairs, rest_ref, send_ref = refs[:-2], refs[-2], refs[-1]
    base = 0
    for own_ref, take_ref in zip(pairs[::2], pairs[1::2]):
        for part in range(own_ref.shape[0]):
            at = slice(base, base + own_ref.shape[3])
            rest_ref[:, at, :] = own_ref[part, :, 0].astype(F32) + take_ref[part, :, 0].astype(F32)
            send_ref[:, at, :] = (own_ref[part, :, 1].astype(F32) + take_ref[part, :, 1].astype(F32)).astype(BF16)
            base += own_ref.shape[3]


def merge_second(own_ref, take_ref, rest_ref, *send_refs):
    for layer in range(4):
        whole = own_ref[layer] + take_ref[layer].astype(F32)
        if layer == 0:
            rest_ref[...] = whole
        else:
            send_refs[layer - 1][...] = whole.astype(BF16)


def merge_last(deep, core_ref, rest_ref, a_ref, b_ref, c_ref, *refs):
    whole = rest_ref[...] + a_ref[...].astype(F32) + b_ref[...].astype(F32) + c_ref[...].astype(F32)
    first = core_ref[0] == 0
    if deep:
        refs[0][...] = whole[:deep]
        refs = refs[1:]
    keep_ref, send_ref = refs[:2]
    parts, own, _ = keep_ref.shape
    for part in range(parts):
        low = whole[deep + 2 * own * part : deep + 2 * own * part + own]
        high = whole[deep + 2 * own * part + own : deep + 2 * own * (part + 1)]
        keep_ref[part] = jnp.where(first, low, high)
        send_ref[part] = jnp.where(first, high, low)
    if not deep:
        refs[2][...] = whole[2 * own * parts :]


def finish(me_ref, up_keep_ref, up_take_ref, keep_ref, take_ref, flat_ref, up_ref, *refs):
    me = me_ref[0]
    first = (me & 1) == 0
    side = keep_ref.shape[2]
    width = 2 * side
    squares, flats = refs[:4], refs[4:]
    own = up_ref.shape[0]
    for number, ref in enumerate(squares):
        keep, take = keep_ref[number], take_ref[number]
        ref[:, :side] = jnp.where(first, keep, take)
        ref[:, side:] = jnp.where(first, take, keep)
    parts = up_keep_ref.shape[0]
    for part in range(parts):
        keep, take = up_keep_ref[part], up_take_ref[part]
        up_ref[:, part * width : (part + 1) * width] = jnp.where(first, keep, take)
        up_ref[:, (parts + part) * width : (parts + part + 1) * width] = jnp.where(first, take, keep)
    flat = flat_ref[...]
    long = flats[-1].shape[0]
    short_turn = lax.rem(side - own * lax.rem(me, side // own), side)
    long_turn = lax.rem(side - long * lax.rem(me, side // long), side)
    short = pltpu.roll(flat, short_turn, 1)
    for number, ref in enumerate(flats[:-1]):
        ref[...] = short[number, :own]
    flats[-1][...] = pltpu.roll(flat, long_turn, 1)[8, :long]


def scatter_core(send):
    return swap(send, other_core)


def scatter_first(core, keep, take):
    shape = keep.shape
    planes, rows, side = shape[-3:]
    keep, take = keep.reshape(-1, planes, rows, side), take.reshape(-1, planes, rows, side)
    count = keep.shape[0]
    steps = MERGE_STEPS
    block = pl.BlockSpec((count // steps, planes, rows, side), lambda i: (i, 0, 0, 0))
    half = (pl.BlockSpec((count // steps, 2, rows, side), lambda i: (i, 0, 0, 0)), shaped(count, 2, rows, side))
    own, send = call(merge_core, (steps,), [SMEM, block, block], [half, half], [], "merge_core", 0, core, keep, take)
    parts = (-1, CHIPS // 4, 2, rows, side)
    return own.reshape(parts), swap(send, first_plane).reshape(parts)


def scatter_second(*pairs):
    _, count, _, _, side = pairs[0].shape
    rows = sum(piece.shape[0] * piece.shape[3] for piece in pairs[::2])
    steps = MERGE_STEPS
    ins = [pl.BlockSpec((piece.shape[0], count // steps, *piece.shape[2:]), lambda i: (0, i, 0, 0, 0)) for piece in pairs]
    out = pl.BlockSpec((count // steps, rows, side), lambda i: (i, 0, 0))
    rest, send = call(
        merge_first, (steps,), ins, [(out, shaped(count, rows, side, dtype=F32)), (out, shaped(count, rows, side))], [],
        "merge_first", LONG, *pairs)
    return rest, swap(send, second_plane)


def scatter_layers(own, take):
    _, rows, side = own.shape
    out = shaped(rows, side)
    rest, *sends = small_call(
        merge_second, (own, take), [(VMEM_SPEC, shaped(rows, side, dtype=F32))] + [(VMEM_SPEC, out)] * 3,
        "merge_second", ins=[VMEM_SPEC] * 2)
    return [rest] + [swap(piece, other_layer(r + 1)) for r, piece in enumerate(sends)]


def scatter_last(core, pieces, own, parts, deep):
    rows, side = pieces[0].shape
    outs = [(VMEM_SPEC, shaped(parts, own, side, dtype=F32))] * 2
    if deep:
        outs = [(VMEM_SPEC, shaped(deep, side, dtype=F32))] + outs
    else:
        outs.append((VMEM_SPEC, shaped(rows - 2 * own * parts, side, dtype=F32)))
    return small_call(
        functools.partial(merge_last, deep), (core, *pieces), outs, "merge_last", ins=[SMEM] + [VMEM_SPEC] * 4, flops=SHORT if deep else 0)


def reduce_plain(down_pair, up_pair, square_pair, flat):
    def scattered(array, axis):
        return lax.psum_scatter(array, "dp", scatter_dimension=axis, tiled=True).astype(F32)

    deep, width = down_pair[0].shape[2:]
    down = jnp.stack(down_pair).transpose(1, 2, 0, 3, 4).reshape(-1, width)
    up = jnp.stack(up_pair)
    folds, each = up.shape[1], up.shape[4]
    up = up.transpose(2, 3, 4, 0, 1, 5).reshape(CHIPS * each, 2 * folds * width)
    square = jnp.stack(square_pair).transpose(1, 2, 3, 0, 4)[:, :, : 4 * each]
    square = square.reshape(CHIPS, 4, each, width).transpose(1, 0, 2, 3).reshape(4, CHIPS * each, width)
    return (
        scattered(down, 0),
        scattered(up, 0),
        *scattered(square, 1),
        lax.psum_scatter(flat, "dp", scatter_dimension=0, tiled=True).reshape(-1),
    )


def body(tokens, lengths, attn_gain, attn_shift, query_weight, query_bias, key_weight, value_weight, value_bias,
         out_weight, out_bias, mlp_gain, mlp_shift, up_weight, up_bias, down_weight, down_bias, grad_out):
    count = lax.axis_size("dp")
    rows, width = tokens.shape
    tiles = lengths.shape[0]
    tile = rows // tiles
    hidden = up_bias.shape[0] * count
    own = width // count
    folds = hidden // width
    vectors = (attn_gain, attn_shift, query_bias, value_bias, out_bias, mlp_gain, mlp_shift, down_bias, up_bias)
    by_hand = count == 2 * CHIPS
    me = lax.axis_index("dp").astype(jnp.int32).reshape(1) if by_hand else jnp.zeros((1,), jnp.int32)
    core = me & 1
    weights = (query_weight, key_weight, value_weight, out_weight, up_weight, down_weight)

    tile_rows = rows_spec(tile, width)
    square = whole_spec((width, width))
    vec_spec = whole_spec((16, width))
    sums = (kept_spec((8, width)), shaped(8, width, dtype=F32))
    low_rows = (tile_rows, shaped(rows, width))
    lse_spec = rows_spec(tile, LANES)
    mac = 2 * rows * width * width
    kept_square = (kept_spec((width, width)), shaped(width, width))
    kept_vec = (kept_spec((16, width)), shaped(16, width, dtype=F32))
    kept_hidden = (kept_spec((1, hidden)), shaped(1, hidden, dtype=F32))
    side = width // 2
    if by_hand:
        near, far = gather_by_hand(me, weights, vectors)
        n1, q, k, v, wq, wk, wv, wo, vec, bup = call_with(
            me, project, tiles, [tile_rows] + [ANY_SPEC] * 8, [low_rows] * 4 + [kept_square] * 4 + [kept_vec, kept_hidden],
            [pltpu.VMEM((count, 16, side), BF16), pltpu.SemaphoreType.DMA((5,))], "project", 0, tokens, *near)
    else:
        wq, wk, wv, wo, far, vec, bup = gather_plain(weights, vectors)
        n1, q, k, v = call(
            project_rows, (tiles,), [tile_rows, vec_spec, square, square, square], [low_rows] * 4,
            [], "project", 0, tokens, vec, wq, wk, wv)
    high_rows = (tile_rows, shaped(rows, width, dtype=F32))
    mixed, lse, resid, n2, cot, sum_down = call(
        attention_forward, (tiles,), [SMEM, tile_rows, tile_rows, vec_spec, tile_rows, tile_rows, tile_rows, square],
        [low_rows, (lse_spec, shaped(rows, LANES, dtype=F32)), high_rows, low_rows, low_rows, sums],
        [], "attention_forward", 0, lengths, tokens, grad_out, vec, q, k, v, wo)

    halves = folds // 2
    each = width // CHIPS
    deep = hidden // (2 * CHIPS)
    full_rows = whole_spec((rows, width))
    kept_low = (kept_spec((rows, width)), shaped(rows, width))
    kept_high = (kept_spec((rows, width)), shaped(rows, width, dtype=F32))

    def turn(i, me):
        return ((i // halves) ^ 1 ^ (me[0] & 1)) * halves + lax.rem(i, halves)

    up_spec = pl.BlockSpec((CHIPS, 1, each, width), lambda i, me: (0, turn(i, me) // halves, lax.rem(turn(i, me), halves), 0))
    down_spec = pl.BlockSpec((width // (2 * deep), 2, deep, width), lambda i, me: (turn(i, me), 0, 1, 0))
    hidden_spec = pl.BlockSpec((1, width), lambda i, me: (0, turn(i, me)))
    down_pair = (pl.BlockSpec((1, 4, deep, width), lambda i, me: (turn(i, me) ^ (me[0] >> 3), 0, 0, 0)), shaped(4, 4, deep, width))
    part = (1, CHIPS // 4, 4, each, width)
    up_shape = shaped(halves, *part[1:])
    out, gtwo, down_send, down_keep, up_send, up_keep, sum_up = call_with(
        me, mlp, folds,
        [full_rows, full_rows, full_rows, vec_spec, hidden_spec, up_spec, down_spec],
        [kept_low, kept_high, down_pair, down_pair,
         (pl.BlockSpec(part, lambda i, me: (jnp.minimum(i, halves - 1), 0, 0, 0, 0)), up_shape),
         (pl.BlockSpec(part, lambda i, me: (jnp.maximum(i - halves, 0), 0, 0, 0, 0)), up_shape),
         (hidden_spec, shaped(1, hidden, dtype=F32))],
        [pltpu.VMEM((rows, width), F32), pltpu.VMEM((rows, width), BF16), pltpu.VMEM((rows, width), BF16)],
        "mlp", 6 * folds * mac, n2, cot, resid, vec, bup, far, far)
    if by_hand:
        down_first = scatter_first(core, down_keep, scatter_core(down_send))
        up_first = scatter_first(core, up_keep, scatter_core(up_send))
        gtwo = after(gtwo, down_first[0], up_first[0])
    grads_spec = pl.BlockSpec((4, tile, width), lambda i, *me: (0, i, 0))
    grads, gresid, sum_back = call(
        attention_backward, (tiles,),
        [SMEM, tile_rows, tile_rows, tile_rows, lse_spec, tile_rows, tile_rows, tile_rows, vec_spec, square],
        [(grads_spec, shaped(4, rows, width)), high_rows, sums], [pltpu.VMEM((tile, width), BF16)],
        "attention_backward", 0, lengths, q, k, v, lse, cot, resid, gtwo, vec, wo)
    if by_hand:
        down_first, up_first = after((down_first, up_first), grads)
        hidden_second = scatter_second(*down_first, *up_first)
        gresid = after(gresid, hidden_second[0])
    sum_spec = whole_spec((8, width))
    pair_shape = (CHIPS // 4, 4, 4 * each + 16, side)
    tile_at = pl.BlockSpec((tile, width), lambda i, me: (jnp.minimum(i, tiles - 1), 0))
    tile_grads = pl.BlockSpec((4, tile, width), lambda i, me: (0, jnp.minimum(i, tiles - 1), 0))
    columns = pl.BlockSpec((1, rows, width), lambda i, me: (jnp.maximum(i - tiles, 0), 0, 0))
    gtok, sum_one, square_send, square_keep = call_with(
        me, projections_backward, tiles + 4,
        [tile_at, tile_at, vec_spec, tile_grads, square, square, square, full_rows, full_rows, columns, sum_spec, sum_spec,
         whole_spec((1, hidden))],
        [(tile_at, shaped(rows, width)), sums] + [(kept_spec(pair_shape), shaped(*pair_shape))] * 2, [],
        "projections_backward", 7 * mac,
        tokens, gresid, vec, grads, wq, wk, wv, n1, mixed, grads, sum_back, sum_down, sum_up)
    if by_hand:
        square_send = after(square_send, hidden_second[1])
        square_take = scatter_core(square_send)
        hidden_layers = scatter_layers(*hidden_second)
        square_keep = after(square_keep, hidden_layers[0])
        square_first = scatter_first(core, square_keep, square_take)
        square_second = scatter_second(*square_first)
        hidden_layers = after(hidden_layers, square_second[0])
        g_down, up_keep, up_send = scatter_last(core, hidden_layers, own, halves, deep)
        up_take = scatter_core(up_send)
        square_second = after(square_second, g_down)
        square_layers = scatter_layers(*square_second)
        square_keep, square_send, flat = scatter_last(core, square_layers, own, 4, 0)
        square_take = scatter_core(square_send)
        outs = [(VMEM_SPEC, shaped(own, hidden, dtype=F32))] + [(VMEM_SPEC, shaped(own, width, dtype=F32))] * 4
        outs += [(VMEM_SPEC, shaped(own, dtype=F32))] * 8 + [(VMEM_SPEC, shaped(folds * own, dtype=F32))]
        g_up, g_q, g_k, g_v, g_o, *g_flat, g_ub = small_call(
            finish, (me, up_keep, up_take, square_keep, square_take, flat), outs, "finish", ins=[SMEM] + [VMEM_SPEC] * 5)
    else:
        flat = jnp.concatenate((sum_one[0:2], sum_back[0:5], sum_down[0:1]), axis=0)
        flat = flat.reshape(8, count, own).transpose(1, 0, 2).reshape(count, 8 * own)
        flat = jnp.concatenate((flat, sum_up.reshape(count, folds * own)), axis=1)
        g_down, g_up, g_q, g_k, g_v, g_o, flat = reduce_plain(
            (down_keep, down_send), (up_keep, up_send), (square_keep, square_send), flat)
        g_flat = [flat[index * own : (index + 1) * own] for index in range(8)]
        g_ub = flat[8 * own :]
    g_gain, g_shift, g_qb, g_vb, g_ob, g_mg, g_ms, g_db = g_flat
    return (out, gtok, g_gain, g_shift, g_q, g_qb, g_k, g_v, g_vb, g_o, g_ob, g_mg, g_ms, g_up, g_ub, g_down, g_db)


def solution(mesh):
    rows, flat = P("dp", None), P("dp")
    return jax.shard_map(
        body,
        mesh=mesh,
        in_specs=(rows, rows, flat, flat, rows, flat, rows, rows, flat, rows, flat, flat, flat, rows, flat, rows, flat, rows),
        out_specs=(rows, rows, flat, flat, rows, flat, rows, rows, flat, rows, flat, flat, flat, rows, flat, rows, flat),
        check_vma=False,
    )
```

```python
import functools

import jax
import jax.numpy as jnp
from jax import lax
from jax.experimental import pallas as pl
from jax.experimental.pallas import tpu as pltpu
from jax.sharding import PartitionSpec as P

HEADS = 12
HEAD_DIM = 64
PAIRS = 6
LANES = 128
CHIPS = 16
MERGE_STEPS = 2
LONG = 10**11
SHORT = 6 * 10**9
EPS = 1e-06
MASKED = -1e30
SCALE = HEAD_DIM**-0.5
GELU_C = 0.7978845608028654
GELU_A = 0.044715
VMEM = 64 * 1024 * 1024 - 65536
F32 = jnp.float32
BF16 = jnp.bfloat16


def dot_nn(left, right):
    return lax.dot_general(left, right, (((1,), (0,)), ((), ())), preferred_element_type=F32)


def dot_nt(left, right):
    return lax.dot_general(left, right, (((1,), (1,)), ((), ())), preferred_element_type=F32)


def dot_tn(left, right):
    return lax.dot_general(left, right, (((0,), (0,)), ((), ())), preferred_element_type=F32)


def normalize(rows):
    centered = rows - jnp.mean(rows, axis=-1, keepdims=True)
    inverse = lax.rsqrt(jnp.mean(centered * centered, axis=-1, keepdims=True) + EPS)
    return centered * inverse, inverse


def norm_back(grads, gain, hat, inverse):
    scaled = grads * gain
    mean = jnp.mean(scaled, axis=-1, keepdims=True)
    mean_hat = jnp.mean(scaled * hat, axis=-1, keepdims=True)
    return inverse * (scaled - mean - hat * mean_hat)


def column_sum(rows):
    return jnp.sum(rows, axis=0, keepdims=True)


def segments(lengths_ref, tile, slots, rows, axis):
    shape = (rows, 1) if axis == 0 else (1, rows)
    index = lax.broadcasted_iota(jnp.int32, shape, axis)
    segment = jnp.zeros(shape, jnp.int32)
    bound = 0
    for slot in range(slots):
        bound = bound + lengths_ref[tile, slot]
        segment = segment + (index >= bound).astype(jnp.int32)
    return segment


def mask_bias(lengths_ref, tile, slots, rows):
    same = segments(lengths_ref, tile, slots, rows, 0) == segments(lengths_ref, tile, slots, rows, 1)
    return jnp.where(same, 0.0, MASKED).astype(F32)


def half_of(pair, side):
    lane = lax.broadcasted_iota(jnp.int32, pair.shape, 1)
    keep = lane < HEAD_DIM if side == 0 else lane >= HEAD_DIM
    return jnp.where(keep, pair, jnp.zeros_like(pair))


def fetch_weights(me, sources, weight_refs, parts_ref, sem):
    core, chip = me & 1, me >> 1
    side = sources[0].shape[2]
    each = weight_refs[0].shape[0] // CHIPS
    for index, source in enumerate(sources):
        half = core if index < 4 else 1 - core
        cols = pl.ds(pl.multiple_of(half * side, LANES), side)
        for layer in range(4):
            owner = chip ^ (4 * layer + index % 4)
            rows = pl.ds(pl.multiple_of(owner * each, 16), each)
            for number, ref in enumerate(weight_refs):
                pltpu.make_async_copy(
                    source.at[layer, pl.ds(number * each, each), :], ref.at[rows, cols], sem.at[number]
                ).start()
            pltpu.make_async_copy(
                source.at[layer, pl.ds(4 * each, 16), :], parts_ref.at[2 * owner + half], sem.at[4]
            ).start()


def project(me_ref, lengths_ref, x_ref, grad_ref, *refs):
    sources = refs[:8]
    n1_ref, q_ref, k_ref, v_ref, cot_ref, dsum_ref = refs[8:14]
    wq_ref, wk_ref, wv_ref, wo_ref, vec_ref, bup_ref, parts_ref, sem = refs[14:]
    weights = (wq_ref, wk_ref, wv_ref, wo_ref)
    core = me_ref[0] & 1

    @pl.when(pl.program_id(0) == 0)
    def _():
        fetch_weights(me_ref[0], sources, weights, parts_ref, sem)
        for number, ref in enumerate(weights + (parts_ref,)):
            pltpu.make_async_copy(ref, ref, sem.at[number]).wait()
        count, _, side = parts_ref.shape
        group = count // 2
        halves = [sum(parts_ref[half * group + index].astype(F32) for index in range(group)) for half in range(2)]
        vec_ref[...] = jnp.concatenate(halves, axis=1)
        blocks = bup_ref.shape[1] // side
        group = CHIPS // blocks
        for block in range(blocks):
            rows = sum(parts_ref[2 * (block * group + index) + core].astype(F32) for index in range(group))
            bup_ref[:, block * side : (block + 1) * side] = rows[8:9]

    project_rows(lengths_ref, x_ref, grad_ref, vec_ref, wq_ref, wk_ref, wv_ref, n1_ref, q_ref, k_ref, v_ref, cot_ref, dsum_ref)


def project_rows(lengths_ref, x_ref, grad_ref, vec_ref, wq_ref, wk_ref, wv_ref,
                 n1_ref, q_ref, k_ref, v_ref, cot_ref, dsum_ref):
    tile = pl.program_id(0)
    rows = x_ref.shape[0]
    slots = lengths_ref.shape[1]
    hat, _ = normalize(x_ref[...].astype(F32))
    n1 = (hat * vec_ref[0:1, :] + vec_ref[1:2, :]).astype(BF16)
    n1_ref[...] = n1
    q_ref[...] = (dot_nn(n1, wq_ref[...]) + vec_ref[2:3, :]).astype(BF16) * jnp.asarray(SCALE, BF16)
    k_ref[...] = dot_nn(n1, wk_ref[...]).astype(BF16)
    v_ref[...] = (dot_nn(n1, wv_ref[...]) + vec_ref[3:4, :]).astype(BF16)
    valid = segments(lengths_ref, tile, slots, rows, 0) < slots
    cot = jnp.where(valid, grad_ref[...].astype(F32), 0.0)
    cot_ref[...] = cot.astype(BF16)

    @pl.when(tile == 0)
    def _():
        dsum_ref[...] = jnp.zeros_like(dsum_ref)

    dsum_ref[0:1, :] += column_sum(cot)


def attention_forward(lengths_ref, x_ref, vec_ref, q_ref, k_ref, v_ref, wo_ref, mixed_ref, lse_ref, resid_ref, n2_ref):
    tile = pl.program_id(0)
    rows = q_ref.shape[0]
    slots = lengths_ref.shape[1]
    bias = mask_bias(lengths_ref, tile, slots, rows)
    lane = lax.broadcasted_iota(jnp.int32, (rows, LANES), 1)
    lse = jnp.zeros((rows, LANES), F32)

    def at(pair):
        return pl.ds(pair * LANES, LANES)

    def scores_of(pair):
        qp, kp = q_ref[:, at(pair)], k_ref[:, at(pair)]
        return [dot_nt(half_of(qp, side), kp) for side in range(2)]

    def softmax_of(scores):
        scores = scores + bias
        top = jnp.max(scores, axis=-1, keepdims=True)
        weights = jnp.exp(scores - top)
        sums = jnp.sum(weights, axis=-1, keepdims=True)
        return (weights * (1.0 / sums)).astype(BF16), top + jnp.log(sums)

    raw = {}
    probs = {}
    for turn in range(PAIRS + 2):
        if turn < PAIRS:
            raw[turn] = scores_of(turn)
        if 0 <= turn - 1 < PAIRS:
            both = [softmax_of(scores) for scores in raw.pop(turn - 1)]
            for side in range(2):
                lse = jnp.where(lane == 2 * (turn - 1) + side, both[side][1], lse)
            probs[turn - 1] = [pair[0] for pair in both]
        if turn >= 2:
            vp = v_ref[:, at(turn - 2)]
            parts = [dot_nn(probs[turn - 2][side], half_of(vp, side)) for side in range(2)]
            mixed_ref[:, at(turn - 2)] = (parts[0] + parts[1]).astype(BF16)
    lse_ref[...] = lse
    resid = x_ref[...].astype(F32) + (dot_nn(mixed_ref[...], wo_ref[...]) + vec_ref[4:5, :])
    resid_ref[...] = resid
    hat, _ = normalize(resid)
    n2_ref[...] = (hat * vec_ref[5:6, :] + vec_ref[6:7, :]).astype(BF16)


def flat_rows(ref):
    return ref[...].reshape(-1, ref.shape[-1])


def spread(me, rows, put):
    layer, plane = me >> 3, (me >> 1) & 3
    each = rows.shape[0] // CHIPS
    for chip in range(CHIPS):
        put((chip & 3) ^ plane, (chip >> 2) ^ layer, rows[chip * each : (chip + 1) * each].astype(BF16))


def mlp(sets, me_ref, *refs):
    n2_hbm, cot_hbm = refs[:sets], refs[sets : 2 * sets]
    bup_ref, wup_ref, wdown_ref = refs[2 * sets : 2 * sets + 3]
    refs = refs[2 * sets + 3 :]
    out_hbm, gtwo_hbm, refs = refs[:sets], refs[sets : 2 * sets], refs[2 * sets :]
    down_own, down_send, up_own, up_send, dbu_ref = refs[:5]
    n2_ref, cot_ref, acc, gacc, act_ref, gup_ref, low_ref, gdown_ref, gupw_ref, in_sem, out_sem, grad_sem = refs[5:]
    step = pl.program_id(0)
    last = pl.num_programs(0) - 1
    me = me_ref[0]
    rows = n2_ref.shape[0] // sets

    def rows_of(index):
        return pl.ds(pl.multiple_of(index * rows, rows), rows)

    @pl.when(step == 0)
    def _():
        for index in range(sets):
            at = pl.ds(index * rows, rows)
            pltpu.make_async_copy(n2_hbm[index], n2_ref.at[at, :], in_sem.at[0, index]).start()
            pltpu.make_async_copy(cot_hbm[index], cot_ref.at[at, :], in_sem.at[1, index]).start()

    wup = flat_rows(wup_ref)
    wdown = flat_rows(wdown_ref)
    dbu_ref[...] = jnp.zeros_like(dbu_ref)

    @pl.loop(0, sets)
    def _(index):
        at = rows_of(index)

        @pl.when(step == 0)
        def _():
            pltpu.make_async_copy(n2_ref.at[at, :], n2_ref.at[at, :], in_sem.at[0, index]).wait()
            pltpu.make_async_copy(cot_ref.at[at, :], cot_ref.at[at, :], in_sem.at[1, index]).wait()

        pre = dot_nn(n2_ref[at, :], wup) + bup_ref[...]
        grad_act = dot_nt(cot_ref[at, :], wdown)
        square = pre * pre
        tanh = jnp.tanh(pre * (GELU_C + (GELU_C * GELU_A) * square))
        half = 0.5 + 0.5 * tanh
        inner = GELU_C + (3.0 * GELU_C * GELU_A) * square
        act_ref[at, :] = (pre * half).astype(BF16)
        gup = (grad_act * (half + (0.5 * pre) * (1.0 - tanh * tanh) * inner)).astype(BF16)
        gup_ref[at, :] = gup
        dbu_ref[...] += column_sum(gup.astype(F32))

    @pl.when(step == 0)
    def _():
        @pl.loop(0, sets)
        def _(index):
            at = rows_of(index)
            acc[at, :] = dot_nn(act_ref[at, :], wdown)
            gacc[at, :] = dot_nt(gup_ref[at, :], wup)

    @pl.when((step > 0) & (step < last))
    def _():
        @pl.loop(0, sets)
        def _(index):
            at = rows_of(index)
            acc[at, :] += dot_nn(act_ref[at, :], wdown)
            gacc[at, :] += dot_nt(gup_ref[at, :], wup)

    def results():
        for index in range(sets):
            at = pl.ds(index * rows, rows)
            yield pltpu.make_async_copy(low_ref.at[0, at, :], out_hbm[index], out_sem.at[0, index])
            source = low_ref.at[1, at, :] if index else gacc.at[at, :]
            yield pltpu.make_async_copy(source, gtwo_hbm[index], out_sem.at[1, index])

    @pl.when(step == last)
    def _():
        @pl.loop(0, sets)
        def _(index):
            at = rows_of(index)
            low_ref[0, at, :] = (acc[at, :] + dot_nn(act_ref[at, :], wdown)).astype(BF16)
            total = gacc[at, :] + dot_nt(gup_ref[at, :], wup)
            gacc[at, :] = total
            low_ref[1, at, :] = total.astype(BF16)

        for copy in results():
            copy.start()

    slot = lax.rem(step, 2)
    gdown_ref[slot] = dot_tn(act_ref[...], cot_ref[...]).astype(BF16)
    deep = down_own.shape[2]
    count = gdown_ref.shape[1] // deep
    for index in range(count):
        chip = step * count + index
        source = gdown_ref.at[slot, pl.ds(index * deep, deep), :]
        keep_or_send(me, chip & 3, (chip >> 2) ^ (me >> 3), source, down_own, down_send, grad_sem, 0)

    gupw_ref[slot] = dot_tn(n2_ref[...], gup_ref[...]).astype(BF16)
    each = gupw_ref.shape[1] // CHIPS
    for chip in range(CHIPS):
        source = gupw_ref.at[slot, pl.ds(chip * each, each), :]
        keep_or_send(
            me, chip & 3, (chip >> 2) ^ (me >> 3), source, up_own.at[step], up_send.at[step], grad_sem, 2)

    @pl.when(step == last)
    def _():
        for copy in results():
            copy.wait()
        for number, ref in enumerate((down_own, down_send, up_own, up_send)):
            pltpu.make_async_copy(ref, ref, grad_sem.at[number]).wait()


def keep_or_send(me, plane, layer, source, own_ref, send_ref, sem, number):
    core = me & 1
    relative = plane ^ ((me >> 1) & 3)
    mine = (relative == 0) | (relative == 2 - core)

    @pl.when(mine)
    def _():
        pltpu.make_async_copy(source, own_ref.at[layer, jnp.where(relative == 0, 0, 1)], sem.at[number]).start()

    @pl.when(jnp.logical_not(mine))
    def _():
        pltpu.make_async_copy(source, send_ref.at[layer, jnp.where(relative == 3, 1, 0)], sem.at[number + 1]).start()


def add_rows(resid_ref, vec_ref, a_ref, b_ref, out_ref):
    total = resid_ref[...] + (a_ref[...].astype(F32) + b_ref[...].astype(F32) + vec_ref[7:8, :])
    out_ref[...] = total.astype(BF16)


def attention_backward(lengths_ref, q_ref, k_ref, v_ref, lse_ref, cot_ref, resid_ref, gtwo_ref, gother_ref, vec_ref, wo_ref,
                       grads_ref, gresid_ref, dsum_ref, gmix_ref):
    tile = pl.program_id(0)
    rows = q_ref.shape[0]

    @pl.when(tile == 0)
    def _():
        dsum_ref[...] = jnp.zeros_like(dsum_ref)

    hat, inverse = normalize(resid_ref[...])
    grad_two = gtwo_ref[...] + gother_ref[...].astype(F32)
    gresid = cot_ref[...].astype(F32) + norm_back(grad_two, vec_ref[5:6, :], hat, inverse)
    gresid_ref[...] = gresid
    gattn = gresid.astype(BF16)
    grads_ref[3] = gattn
    dsum_ref[2:3, :] += column_sum(gattn.astype(F32))
    dsum_ref[3:4, :] += column_sum(grad_two * hat)
    dsum_ref[4:5, :] += column_sum(grad_two)
    gmix_ref[...] = dot_nt(gattn, wo_ref[...]).astype(BF16)
    bias = mask_bias(lengths_ref, tile, lengths_ref.shape[1], rows)

    def load(pair):
        cols = pl.ds(pair * LANES, LANES)
        return q_ref[:, cols], k_ref[:, cols], v_ref[:, cols], gmix_ref[:, cols]

    def products_of(pair):
        qp, kp, vp, gp = load(pair)
        return [(dot_nt(half_of(qp, side), kp), dot_nt(half_of(gp, side), vp)) for side in range(2)]

    def softmax_back(pair, products):
        results = []
        for side, (scores, grad_probs) in enumerate(products):
            head = 2 * pair + side
            probs = jnp.exp(scores + bias - lse_ref[:, head : head + 1])
            weighted = probs * grad_probs
            dot = jnp.sum(weighted, axis=-1, keepdims=True)
            results.append((probs.astype(BF16), (weighted - probs * dot).astype(BF16)))
        return results

    def store(pair, results):
        qp, kp, vp, gp = load(pair)
        dq = sum(dot_nn(results[side][1], half_of(kp, side)) for side in range(2))
        dk = sum(dot_tn(results[side][1], half_of(qp, side)) for side in range(2))
        dv = sum(dot_tn(results[side][0], half_of(gp, side)) for side in range(2))
        cols = pl.ds(pair * LANES, LANES)
        grads_ref[0, :, cols] = (dq * SCALE).astype(BF16)
        grads_ref[1, :, cols] = dk.astype(BF16)
        grads_ref[2, :, cols] = dv.astype(BF16)

    raw = {}
    done = {}
    for turn in range(PAIRS + 2):
        if turn < PAIRS:
            raw[turn] = products_of(turn)
        if 0 <= turn - 1 < PAIRS:
            done[turn - 1] = softmax_back(turn - 1, raw.pop(turn - 1))
        if turn >= 2:
            store(turn - 2, done.pop(turn - 2))

    dsum_ref[0:1, :] += column_sum(grads_ref[0].astype(F32))
    dsum_ref[1:2, :] += column_sum(grads_ref[2].astype(F32))


def projections_backward(me_ref, x_ref, gresid_ref, vec_ref, grads_ref, wq_ref, wk_ref, wv_ref, n1_ref, mixed_ref,
                         columns_ref, sum_back_ref, sum_down_ref, sum_up_ref,
                         gtok_ref, dsum_ref, send_ref, keep_ref):
    step = pl.program_id(0)
    tiles = pl.num_programs(0) - 4
    me = me_ref[0]
    first = (me & 1) == 0
    side = send_ref.shape[3]
    each = wq_ref.shape[0] // CHIPS

    @pl.when(step == 0)
    def _():
        dsum_ref[...] = jnp.zeros_like(dsum_ref)

    @pl.when(step < tiles)
    def _():
        grad_one = dot_nt(grads_ref[0], wq_ref[...]) + dot_nt(grads_ref[1], wk_ref[...]) + dot_nt(grads_ref[2], wv_ref[...])
        hat, inverse = normalize(x_ref[...].astype(F32))
        gtok_ref[...] = (gresid_ref[...] + norm_back(grad_one, vec_ref[0:1, :], hat, inverse)).astype(BF16)
        dsum_ref[0:1, :] += column_sum(grad_one * hat)
        dsum_ref[1:2, :] += column_sum(grad_one)

    def run(left, number):
        result = dot_tn(left, columns_ref[0])
        low, high = result[:, :side], result[:, side:]
        rows_at = pl.ds(pl.multiple_of(number * each, 16), each)

        def put_send(plane, layer, rows):
            send_ref[layer, plane, rows_at, :] = rows

        def put_keep(plane, layer, rows):
            keep_ref[layer, plane, rows_at, :] = rows

        spread(me, jnp.where(first, high, low), put_send)
        spread(me, jnp.where(first, low, high), put_keep)

    @pl.when((step >= tiles) & (step < tiles + 3))
    def _():
        run(n1_ref[...], step - tiles)

    @pl.when(step == tiles + 3)
    def _():
        run(mixed_ref[...], 3)
        vecs = jnp.concatenate((dsum_ref[0:2], sum_back_ref[0:5], sum_down_ref[0:1]), axis=0)
        for chip in range(CHIPS):
            half = chip // (CHIPS // 2)
            block = chip * (sum_up_ref.shape[1] // side) // CHIPS
            last = jnp.broadcast_to(sum_up_ref[:, block * side : (block + 1) * side], (8, side))
            short = vecs[:, half * side : (half + 1) * side]
            at = ((chip >> 2) ^ (me >> 3), (chip & 3) ^ ((me >> 1) & 3))
            keep_ref[at[0], at[1], 4 * each :, :] = jnp.concatenate((short, last), axis=0).astype(BF16)
            send_ref[at[0], at[1], 4 * each :, :] = jnp.concatenate((short, jnp.zeros_like(last)), axis=0).astype(BF16)


def rows_spec(block, width):
    return pl.BlockSpec((block, width), lambda i, *me: (i, 0))


def cols_spec(height, block):
    return pl.BlockSpec((height, block), lambda i, *me: (0, i))


def whole_spec(shape):
    return pl.BlockSpec(shape, lambda *i: (0,) * len(shape), pipeline_mode=pl.Buffered(1))


def kept_spec(shape):
    return pl.BlockSpec(shape, lambda *i: (0,) * len(shape))


SMEM = pl.BlockSpec(memory_space=pltpu.SMEM)


def cost(flops):
    return pl.CostEstimate(flops=flops, bytes_accessed=1, transcendentals=0)


def call(kernel, grid, ins, outs, scratch, name, flops, *args):
    out_specs = tuple(spec for spec, _ in outs)
    out_shape = tuple(shape for _, shape in outs)
    return pl.pallas_call(
        kernel,
        grid=grid,
        in_specs=ins,
        out_specs=out_specs,
        out_shape=out_shape,
        scratch_shapes=scratch,
        compiler_params=pltpu.CompilerParams(vmem_limit_bytes=VMEM, dimension_semantics=("arbitrary",) * len(grid)),
        cost_estimate=cost(flops),
        name=name,
    )(*args)


def call_with(me, kernel, steps, ins, outs, scratch, name, flops, *args):
    out_shape = tuple(shape for _, shape in outs)
    return pl.pallas_call(
        kernel,
        grid_spec=pltpu.PrefetchScalarGridSpec(
            num_scalar_prefetch=1, grid=(steps,), in_specs=ins, out_specs=tuple(spec for spec, _ in outs),
            scratch_shapes=scratch),
        out_shape=out_shape,
        compiler_params=pltpu.CompilerParams(vmem_limit_bytes=VMEM, dimension_semantics=("arbitrary",)),
        cost_estimate=cost(0),
        name=name,
    )(me, *args)


def shaped(*shape, dtype=BF16):
    return jax.ShapeDtypeStruct(shape, dtype)


def flipped(count, change):
    pairs = []
    for source in range(count):
        core, chip = source & 1, source >> 1
        core, chip = change(core, chip)
        pairs.append((source, 2 * chip + core))
    return pairs


def swap(array, change):
    return lax.ppermute(array, "dp", flipped(lax.axis_size("dp"), change))


def other_core(core, chip):
    return core ^ 1, chip


def first_plane(core, chip):
    return core, chip ^ (1 + core)


def second_plane(core, chip):
    return core, chip ^ (2 - core)


def other_plane(distance):
    return lambda core, chip: (core, chip ^ distance)


def other_layer(distance):
    return lambda core, chip: (core, chip ^ (4 * distance))


def split_shards(core_ref, q_ref, k_ref, v_ref, o_ref, u_ref, keep_ref, send_ref):
    width = q_ref.shape[1]
    side = width // 2
    first = core_ref[0] == 0

    def put(index, low, high):
        keep_ref[index] = jnp.where(first, low, high).astype(BF16)
        send_ref[index] = jnp.where(first, high, low).astype(BF16)

    for index, ref in enumerate((q_ref, k_ref, v_ref, o_ref)):
        rows = ref[...].astype(F32)
        put(index, rows[:, :side], rows[:, side:])
    up = u_ref[...].astype(F32)
    hidden = up.shape[1]
    deep = hidden // (2 * CHIPS)
    halves = [
        jnp.concatenate([up[:, start : start + deep] for start in range(half * deep, hidden, 2 * deep)], axis=1)
        for half in range(2)
    ]
    for part in range(hidden // width):
        at = slice(part * side, (part + 1) * side)
        put(4 + part, halves[0][:, at], halves[1][:, at])


def join_shards(me_ref, keep_ref, take_ref, down_ref, *refs):
    vectors, (near_ref, far_ref) = refs[:-2], refs[-2:]
    me = me_ref[0]
    first = (me & 1) == 0
    parts, own, side = keep_ref.shape
    folds = parts - 4
    keep = keep_ref[...].astype(F32)
    take = take_ref[...].astype(F32)

    def joined(index):
        low = jnp.where(first, keep[index], take[index])
        high = jnp.where(first, take[index], keep[index])
        return jnp.concatenate((low, high), axis=0).astype(BF16)

    for index in range(4):
        near_ref[2 * own * index : 2 * own * (index + 1), :] = joined(index)
    for index in range(folds):
        far_ref[2 * own * (index // 2) : 2 * own * (index // 2 + 1), side * (index % 2) : side * (index % 2 + 1)] = joined(4 + index)
    far_ref[folds * own :, :] = down_ref[...]
    rows = []
    for ref in vectors:
        flat = ref[...].astype(F32).reshape(1, -1)
        rows.append(jnp.concatenate((flat, jnp.zeros((1, side - flat.shape[1]), F32)), axis=1))
    rows.append(jnp.zeros((16 - len(rows), side), F32))
    rows = jnp.concatenate(rows, axis=0)
    short = pltpu.roll(rows, own * lax.rem(me, side // own), 1)
    long = pltpu.roll(rows, folds * own * lax.rem(me >> 1, side // (folds * own)), 1)
    index = lax.broadcasted_iota(jnp.int32, rows.shape, 0)
    near_ref[8 * own :, :] = jnp.where(index < 8, short, long).astype(BF16)


def across_layers(shard):
    return jnp.stack([shard] + [swap(shard, other_layer(distance)) for distance in (1, 2, 3)])


def after(arrays, *others):
    return lax.optimization_barrier((arrays, others))[0]


def small_call(kernel, args, outs, name, scratch=(), ins=None, flops=0):
    return pl.pallas_call(
        kernel,
        in_specs=ins,
        out_specs=tuple(spec for spec, _ in outs),
        out_shape=tuple(shape for _, shape in outs),
        scratch_shapes=list(scratch),
        compiler_params=pltpu.CompilerParams(vmem_limit_bytes=VMEM),
        cost_estimate=cost(flops),
        name=name,
    )(*args)


VMEM_SPEC = pl.BlockSpec(memory_space=pltpu.VMEM)
ANY_SPEC = pl.BlockSpec(memory_space=pl.ANY)


def gather_by_hand(me, weights, vectors):
    count = lax.axis_size("dp")
    own, width = weights[0].shape
    side = width // 2
    deep = weights[5].shape[0]
    folds = deep // own
    halves = (VMEM_SPEC, shaped(4 + folds, own, side))
    keep, send = small_call(
        split_shards, (me & 1, *weights[:5]), [halves, halves], "split_shards", ins=[SMEM] + [VMEM_SPEC] * 5)
    take = swap(send, other_core)
    near, far = small_call(
        join_shards, (me, keep, take, weights[5], *vectors),
        [(VMEM_SPEC, shaped(8 * own + 16, side)), (VMEM_SPEC, shaped(2 * deep, width))], "join_shards",
        ins=[SMEM] + [VMEM_SPEC] * (3 + len(vectors)))
    far = lax.all_gather(far, "dp", axis=0, tiled=True).reshape(count // 2, 2, 2 * deep, width)
    near = across_layers(near)
    near = [near] + [swap(near, other_plane(distance)) for distance in (1, 2, 3)]
    return near + [swap(piece, other_core) for piece in near], far


def gather_plain(weights, vectors):
    squares, up_weight, down_weight = weights[:4], weights[4], weights[5]
    count = lax.axis_size("dp")
    own, width = squares[0].shape
    folds = down_weight.shape[0] // own
    hidden = up_weight.shape[1]
    flat = jnp.concatenate(vectors)
    packed = jnp.concatenate(
        (
            *squares,
            up_weight.reshape(own, folds, width).transpose(1, 0, 2).reshape(own * folds, width),
            down_weight,
            jnp.pad(flat.reshape(1, -1), ((0, 7), (0, width - flat.size))),
        ),
        axis=0,
    )
    whole = lax.all_gather(packed, "dp", axis=0, tiled=True).reshape(count, -1, width)
    square_all = [whole[:, index * own : (index + 1) * own, :].reshape(width, width) for index in range(4)]
    wup = whole[:, 4 * own : (4 + folds) * own, :].reshape(count, folds, own, width).transpose(0, 2, 1, 3)
    wup = wup.reshape(CHIPS, width // CHIPS, 2, CHIPS // 2, 2, -1).transpose(0, 4, 2, 1, 3, 5).reshape(CHIPS, 2, -1, width)
    wdown = whole[:, (4 + folds) * own : (4 + 2 * folds) * own, :]
    wdown = wdown.reshape(CHIPS, 2, -1, width)
    last = whole[:, (4 + 2 * folds) * own, : flat.size].astype(F32)
    vec = last[:, : 8 * own].reshape(count, 8, own).transpose(1, 0, 2).reshape(8, width)
    bup = last[:, 8 * own :].reshape(CHIPS, 2, -1).transpose(1, 0, 2).reshape(2, 1, -1)
    return (*square_all, jnp.concatenate((wup, wdown), axis=2), jnp.pad(vec, ((0, 8), (0, 0))), bup)


def merge_core(core_ref, keep_ref, take_ref, own_ref, send_ref):
    core = core_ref[0]

    def whole(plane):
        return (keep_ref[:, plane].astype(F32) + take_ref[:, plane].astype(F32)).astype(BF16)

    own_ref[:, 0] = whole(0)
    own_ref[:, 1] = whole(2 - core)
    send_ref[:, 0] = whole(1 + core)
    send_ref[:, 1] = whole(3)


def merge_first(*refs):
    pairs, rest_ref, send_ref = refs[:-2], refs[-2], refs[-1]
    base = 0
    for own_ref, take_ref in zip(pairs[::2], pairs[1::2]):
        for part in range(own_ref.shape[0]):
            at = slice(base, base + own_ref.shape[3])
            rest_ref[:, at, :] = own_ref[part, :, 0].astype(F32) + take_ref[part, :, 0].astype(F32)
            send_ref[:, at, :] = (own_ref[part, :, 1].astype(F32) + take_ref[part, :, 1].astype(F32)).astype(BF16)
            base += own_ref.shape[3]


def merge_second(own_ref, take_ref, rest_ref, *send_refs):
    for layer in range(4):
        whole = own_ref[layer] + take_ref[layer].astype(F32)
        if layer == 0:
            rest_ref[...] = whole
        else:
            send_refs[layer - 1][...] = whole.astype(BF16)


def merge_last(deep, core_ref, rest_ref, a_ref, b_ref, c_ref, *refs):
    whole = rest_ref[...] + a_ref[...].astype(F32) + b_ref[...].astype(F32) + c_ref[...].astype(F32)
    first = core_ref[0] == 0
    if deep:
        refs[0][...] = whole[:deep]
        refs = refs[1:]
    keep_ref, send_ref = refs[:2]
    parts, own, _ = keep_ref.shape
    for part in range(parts):
        low = whole[deep + 2 * own * part : deep + 2 * own * part + own]
        high = whole[deep + 2 * own * part + own : deep + 2 * own * (part + 1)]
        keep_ref[part] = jnp.where(first, low, high)
        send_ref[part] = jnp.where(first, high, low)
    if not deep:
        refs[2][...] = whole[2 * own * parts :]


def finish(me_ref, up_keep_ref, up_take_ref, keep_ref, take_ref, flat_ref, up_ref, *refs):
    me = me_ref[0]
    first = (me & 1) == 0
    side = keep_ref.shape[2]
    width = 2 * side
    squares, flats = refs[:4], refs[4:]
    own = up_ref.shape[0]
    for number, ref in enumerate(squares):
        keep, take = keep_ref[number], take_ref[number]
        ref[:, :side] = jnp.where(first, keep, take)
        ref[:, side:] = jnp.where(first, take, keep)
    parts = up_keep_ref.shape[0]
    deep = parts * width // CHIPS
    for part in range(parts):
        keep, take = up_keep_ref[part], up_take_ref[part]
        low, high = jnp.where(first, keep, take), jnp.where(first, take, keep)
        pieces = []
        for start in range(0, width, deep):
            pieces += [low[:, start : start + deep], high[:, start : start + deep]]
        up_ref[:, 2 * width * part : 2 * width * (part + 1)] = jnp.concatenate(pieces, axis=1)
    flat = flat_ref[...]
    long = flats[-1].shape[0]
    short_turn = lax.rem(side - own * lax.rem(me, side // own), side)
    long_turn = lax.rem(side - long * lax.rem(me >> 1, side // long), side)
    short = pltpu.roll(flat, short_turn, 1)
    for number, ref in enumerate(flats[:-1]):
        ref[...] = short[number, :own]
    flats[-1][...] = pltpu.roll(flat, long_turn, 1)[8, :long]


def scatter_core(send):
    return swap(send, other_core)


def scatter_first(core, keep, take):
    shape = keep.shape
    planes, rows, side = shape[-3:]
    keep, take = keep.reshape(-1, planes, rows, side), take.reshape(-1, planes, rows, side)
    count = keep.shape[0]
    steps = MERGE_STEPS
    block = pl.BlockSpec((count // steps, planes, rows, side), lambda i: (i, 0, 0, 0))
    half = (pl.BlockSpec((count // steps, 2, rows, side), lambda i: (i, 0, 0, 0)), shaped(count, 2, rows, side))
    own, send = call(merge_core, (steps,), [SMEM, block, block], [half, half], [], "merge_core", 0, core, keep, take)
    parts = (-1, CHIPS // 4, 2, rows, side)
    return own.reshape(parts), swap(send, first_plane).reshape(parts)


def scatter_second(*pairs):
    _, count, _, _, side = pairs[0].shape
    rows = sum(piece.shape[0] * piece.shape[3] for piece in pairs[::2])
    steps = MERGE_STEPS
    ins = [pl.BlockSpec((piece.shape[0], count // steps, *piece.shape[2:]), lambda i: (0, i, 0, 0, 0)) for piece in pairs]
    out = pl.BlockSpec((count // steps, rows, side), lambda i: (i, 0, 0))
    rest, send = call(
        merge_first, (steps,), ins, [(out, shaped(count, rows, side, dtype=F32)), (out, shaped(count, rows, side))], [],
        "merge_first", LONG, *pairs)
    return rest, swap(send, second_plane)


def scatter_layers(own, take):
    _, rows, side = own.shape
    out = shaped(rows, side)
    rest, *sends = small_call(
        merge_second, (own, take), [(VMEM_SPEC, shaped(rows, side, dtype=F32))] + [(VMEM_SPEC, out)] * 3,
        "merge_second", ins=[VMEM_SPEC] * 2)
    return [rest] + [swap(piece, other_layer(r + 1)) for r, piece in enumerate(sends)]


def scatter_last(core, pieces, own, parts, deep):
    rows, side = pieces[0].shape
    outs = [(VMEM_SPEC, shaped(parts, own, side, dtype=F32))] * 2
    if deep:
        outs = [(VMEM_SPEC, shaped(deep, side, dtype=F32))] + outs
    else:
        outs.append((VMEM_SPEC, shaped(rows - 2 * own * parts, side, dtype=F32)))
    return small_call(
        functools.partial(merge_last, deep), (core, *pieces), outs, "merge_last", ins=[SMEM] + [VMEM_SPEC] * 4, flops=SHORT if deep else 0)


def reduce_plain(down_pairs, up_pairs, square_pair, flat):
    def scattered(array, axis):
        return lax.psum_scatter(array, "dp", scatter_dimension=axis, tiled=True).astype(F32)

    def planes(own, send, core):
        order = (own[..., 0, :, :], send[..., 0, :, :], own[..., 1, :, :], send[..., 1, :, :])
        if core == 1:
            order = (order[0], order[2], order[1], order[3])
        return jnp.stack(order, axis=-3)

    down = jnp.stack([planes(*pair, core) for core, pair in enumerate(down_pairs)])
    up = jnp.stack([planes(*pair, core) for core, pair in enumerate(up_pairs)])
    width = down.shape[-1]
    each = up.shape[4]
    down = down.transpose(1, 2, 0, 3, 4).reshape(-1, width)
    up = up.reshape(2, 2, CHIPS, each, CHIPS // 2, -1).transpose(2, 3, 1, 4, 0, 5).reshape(CHIPS * each, -1)
    square = jnp.stack(square_pair).transpose(1, 2, 3, 0, 4)[:, :, : 4 * each]
    square = square.reshape(CHIPS, 4, each, width).transpose(1, 0, 2, 3).reshape(4, CHIPS * each, width)
    return (
        scattered(down, 0),
        scattered(up, 0),
        *scattered(square, 1),
        lax.psum_scatter(flat, "dp", scatter_dimension=0, tiled=True).reshape(-1),
    )


def body(tokens, lengths, attn_gain, attn_shift, query_weight, query_bias, key_weight, value_weight, value_bias,
         out_weight, out_bias, mlp_gain, mlp_shift, up_weight, up_bias, down_weight, down_bias, grad_out):
    count = lax.axis_size("dp")
    rows, width = tokens.shape
    tiles = lengths.shape[0]
    tile = rows // tiles
    hidden = up_bias.shape[0] * count
    own = width // count
    folds = hidden // width
    vectors = (attn_gain, attn_shift, query_bias, value_bias, out_bias, mlp_gain, mlp_shift, down_bias, up_bias)
    by_hand = count == 2 * CHIPS
    me = lax.axis_index("dp").astype(jnp.int32).reshape(1) if by_hand else jnp.zeros((1,), jnp.int32)
    core = me & 1
    weights = (query_weight, key_weight, value_weight, out_weight, up_weight, down_weight)

    tile_rows = rows_spec(tile, width)
    square = whole_spec((width, width))
    vec_spec = whole_spec((16, width))
    sums = (kept_spec((8, width)), shaped(8, width, dtype=F32))
    low_rows = (tile_rows, shaped(rows, width))
    lse_spec = rows_spec(tile, LANES)
    mac = 2 * rows * width * width
    kept_square = (kept_spec((width, width)), shaped(width, width))
    kept_vec = (kept_spec((16, width)), shaped(16, width, dtype=F32))
    kept_hidden = (kept_spec((1, hidden // 2)), shaped(1, hidden // 2, dtype=F32))
    side = width // 2
    lengths_spec = SMEM
    rows_outs = [low_rows] * 5 + [sums]
    if by_hand:
        near, far = gather_by_hand(me, weights, vectors)
        n1, q, k, v, cot, sum_down, wq, wk, wv, wo, vec, bup = call_with(
            me, project, tiles, [lengths_spec, tile_rows, tile_rows] + [ANY_SPEC] * 8,
            rows_outs + [kept_square] * 4 + [kept_vec, kept_hidden],
            [pltpu.VMEM((count, 16, side), BF16), pltpu.SemaphoreType.DMA((5,))], "project", 0,
            lengths, tokens, grad_out, *near)
        cot_other = swap(cot, other_core)
    else:
        wq, wk, wv, wo, far, vec, bup = gather_plain(weights, vectors)
        n1, q, k, v, cot, sum_down = call(
            project_rows, (tiles,), [lengths_spec, tile_rows, tile_rows, vec_spec, square, square, square], rows_outs,
            [], "project", 0, lengths, tokens, grad_out, vec, wq, wk, wv)
    high_rows = (tile_rows, shaped(rows, width, dtype=F32))
    mixed, lse, resid, n2 = call(
        attention_forward, (tiles,), [SMEM, tile_rows, vec_spec, tile_rows, tile_rows, tile_rows, square],
        [low_rows, (lse_spec, shaped(rows, LANES, dtype=F32)), high_rows, low_rows],
        [], "attention_forward", 0, lengths, tokens, vec, q, k, v, wo)

    each = width // CHIPS
    deep = hidden // (2 * CHIPS)
    blocks = hidden // (2 * width)
    full_rows = whole_spec((rows, width))
    up_spec = pl.BlockSpec((CHIPS, 1, each, width), lambda i, me: (0, me[0] & 1, i, 0))
    down_spec = pl.BlockSpec((CHIPS // 2, 1, deep, width), lambda i, me: (i, me[0] & 1, 1, 0))
    hidden_spec = pl.BlockSpec((1, width), lambda i, me: (0, i))
    low_out, high_out = (ANY_SPEC, shaped(rows, width)), (ANY_SPEC, shaped(rows, width, dtype=F32))
    down_part = (ANY_SPEC, shaped(4, 2, deep, width))
    up_part = (ANY_SPEC, shaped(blocks, 4, 2, each, width))

    def run_mlp(me, tokens_of, bup):
        sets = len(tokens_of[0])
        low, high = pltpu.VMEM((sets * rows, width), BF16), pltpu.VMEM((sets * rows, width), F32)
        weight = pltpu.VMEM((2, width, width), BF16)
        dma = pltpu.SemaphoreType.DMA((2, sets))
        return call_with(
            me, functools.partial(mlp, sets), blocks, [ANY_SPEC] * (2 * sets) + [hidden_spec, up_spec, down_spec],
            [low_out] * sets + [high_out] + [low_out] * (sets - 1) + [down_part] * 2 + [up_part] * 2
            + [(hidden_spec, shaped(1, hidden // 2, dtype=F32))],
            [low, low, high, high, low, low, pltpu.VMEM((2, sets * rows, width), BF16), weight, weight, dma, dma,
             pltpu.SemaphoreType.DMA((4,))],
            "mlp", 0, *tokens_of[0], *tokens_of[1], bup, far, far)

    if by_hand:
        cot_other = after(cot_other, mixed)
        n2_other = swap(n2, other_core)
        out_own, out_other, gtwo, gtwo_other, down_own, down_send, up_own, up_send, sum_up = run_mlp(
            me, ((n2, n2_other), (cot, cot_other)), bup)
        gtwo_take = swap(gtwo_other, other_core)
        out_take = swap(out_other, other_core)
        parts = (-1, CHIPS // 4, 2)
        down_first = [piece.reshape(*parts, deep, width) for piece in (down_own, swap(down_send, first_plane))]
        up_first = [piece.reshape(*parts, each, width) for piece in (up_own, swap(up_send, first_plane))]
    else:
        runs = [run_mlp(me + half, ((n2,), (cot,)), bup[half]) for half in range(2)]
        (out_own, gtwo), (out_take, gtwo_take) = ((run[0], run[1]) for run in runs)
        gtwo_take = gtwo_take.astype(BF16)
        sum_up = jnp.concatenate([run[6] for run in runs], axis=1)
    grads_spec = pl.BlockSpec((4, tile, width), lambda i, *me: (0, i, 0))
    grads, gresid, sum_back = call(
        attention_backward, (tiles,),
        [SMEM, tile_rows, tile_rows, tile_rows, lse_spec, tile_rows, tile_rows, tile_rows, tile_rows, vec_spec, square],
        [(grads_spec, shaped(4, rows, width)), high_rows, sums], [pltpu.VMEM((tile, width), BF16)],
        "attention_backward", 0, lengths, q, k, v, lse, cot, resid, gtwo, gtwo_take, vec, wo)
    if by_hand:
        down_first, up_first = after((down_first, up_first), grads)
        hidden_second = scatter_second(*down_first, *up_first)
        gresid = after(gresid, hidden_second[0])
    sum_spec = whole_spec((8, width))
    pair_shape = (CHIPS // 4, 4, 4 * each + 16, side)
    tile_at = pl.BlockSpec((tile, width), lambda i, me: (jnp.minimum(i, tiles - 1), 0))
    tile_grads = pl.BlockSpec((4, tile, width), lambda i, me: (0, jnp.minimum(i, tiles - 1), 0))
    columns = pl.BlockSpec((1, rows, width), lambda i, me: (jnp.maximum(i - tiles, 0), 0, 0))
    gtok, sum_one, square_send, square_keep = call_with(
        me, projections_backward, tiles + 4,
        [tile_at, tile_at, vec_spec, tile_grads, square, square, square, full_rows, full_rows, columns, sum_spec, sum_spec,
         whole_spec((1, sum_up.shape[1]))],
        [(tile_at, shaped(rows, width)), sums] + [(kept_spec(pair_shape), shaped(*pair_shape))] * 2, [],
        "projections_backward", 7 * mac,
        tokens, gresid, vec, grads, wq, wk, wv, n1, mixed, grads, sum_back, sum_down, sum_up)
    if by_hand:
        square_send = after(square_send, hidden_second[1])
        square_take = scatter_core(square_send)
        hidden_layers = scatter_layers(*hidden_second)
        square_keep = after(square_keep, hidden_layers[0])
        square_first = scatter_first(core, square_keep, square_take)
        resid = after(resid, square_first[0])
        (out,) = call(
            add_rows, (tiles,), [tile_rows, vec_spec, tile_rows, tile_rows], [low_rows], [], "add_rows", 0,
            resid, vec, out_own, out_take)
        square_first = after(square_first, out)
        square_second = scatter_second(*square_first)
        hidden_layers = after(hidden_layers, square_second[0])
        g_down, up_keep, up_send = scatter_last(core, hidden_layers, own, blocks, deep)
        up_take = scatter_core(up_send)
        square_second = after(square_second, g_down)
        square_layers = scatter_layers(*square_second)
        square_keep, square_send, flat = scatter_last(core, square_layers, own, 4, 0)
        square_take = scatter_core(square_send)
        outs = [(VMEM_SPEC, shaped(own, hidden, dtype=F32))] + [(VMEM_SPEC, shaped(own, width, dtype=F32))] * 4
        outs += [(VMEM_SPEC, shaped(own, dtype=F32))] * 8 + [(VMEM_SPEC, shaped(folds * own, dtype=F32))]
        g_up, g_q, g_k, g_v, g_o, *g_flat, g_ub = small_call(
            finish, (me, up_keep, up_take, square_keep, square_take, flat), outs, "finish", ins=[SMEM] + [VMEM_SPEC] * 5)
    else:
        flat = jnp.concatenate((sum_one[0:2], sum_back[0:5], sum_down[0:1]), axis=0)
        flat = flat.reshape(8, count, own).transpose(1, 0, 2).reshape(count, 8 * own)
        hidden_sums = sum_up.reshape(2, CHIPS, deep).transpose(1, 0, 2).reshape(count, folds * own)
        flat = jnp.concatenate((flat, hidden_sums), axis=1)
        g_down, g_up, g_q, g_k, g_v, g_o, flat = reduce_plain(
            [run[2:4] for run in runs], [run[4:6] for run in runs], (square_keep, square_send), flat)
        (out,) = call(
            add_rows, (tiles,), [tile_rows, vec_spec, tile_rows, tile_rows], [low_rows], [], "add_rows", 0,
            resid, vec, out_own, out_take)
        g_flat = [flat[index * own : (index + 1) * own] for index in range(8)]
        g_ub = flat[8 * own :]
    g_gain, g_shift, g_qb, g_vb, g_ob, g_mg, g_ms, g_db = g_flat
    return (out, gtok, g_gain, g_shift, g_q, g_qb, g_k, g_v, g_vb, g_o, g_ob, g_mg, g_ms, g_up, g_ub, g_down, g_db)


def solution(mesh):
    rows, flat = P("dp", None), P("dp")
    return jax.shard_map(
        body,
        mesh=mesh,
        in_specs=(rows, rows, flat, flat, rows, flat, rows, rows, flat, rows, flat, flat, flat, rows, flat, rows, flat, rows),
        out_specs=(rows, rows, flat, flat, rows, flat, rows, rows, flat, rows, flat, flat, flat, rows, flat, rows, flat),
        check_vma=False,
    )
```

```python
import functools

import jax
import jax.numpy as jnp
from jax import lax
from jax.experimental import pallas as pl
from jax.experimental.pallas import tpu as pltpu
from jax.sharding import PartitionSpec as P

HEADS = 12
HEAD_DIM = 64
PAIRS = 6
LANES = 128
CHIPS = 16
MERGE_STEPS = 2
LONG = 10**11
SHORT = 6 * 10**9
MIDDLE = 115 * 10**8
EPS = 1e-06
MASKED = -1e30
SCALE = HEAD_DIM**-0.5
GELU_C = 0.7978845608028654
GELU_A = 0.044715
VMEM = 64 * 1024 * 1024 - 65536
F32 = jnp.float32
BF16 = jnp.bfloat16


def dot_nn(left, right):
    return lax.dot_general(left, right, (((1,), (0,)), ((), ())), preferred_element_type=F32)


def dot_nt(left, right):
    return lax.dot_general(left, right, (((1,), (1,)), ((), ())), preferred_element_type=F32)


def dot_tn(left, right):
    return lax.dot_general(left, right, (((0,), (0,)), ((), ())), preferred_element_type=F32)


def normalize(rows):
    centered = rows - jnp.mean(rows, axis=-1, keepdims=True)
    inverse = lax.rsqrt(jnp.mean(centered * centered, axis=-1, keepdims=True) + EPS)
    return centered * inverse, inverse


def norm_back(grads, gain, hat, inverse):
    scaled = grads * gain
    mean = jnp.mean(scaled, axis=-1, keepdims=True)
    mean_hat = jnp.mean(scaled * hat, axis=-1, keepdims=True)
    return inverse * (scaled - mean - hat * mean_hat)


def column_sum(rows):
    return jnp.sum(rows, axis=0, keepdims=True)


def segments(lengths_ref, tile, slots, rows, axis):
    shape = (rows, 1) if axis == 0 else (1, rows)
    index = lax.broadcasted_iota(jnp.int32, shape, axis)
    segment = jnp.zeros(shape, jnp.int32)
    bound = 0
    for slot in range(slots):
        bound = bound + lengths_ref[tile, slot]
        segment = segment + (index >= bound).astype(jnp.int32)
    return segment


def mask_bias(lengths_ref, tile, slots, rows):
    same = segments(lengths_ref, tile, slots, rows, 0) == segments(lengths_ref, tile, slots, rows, 1)
    return jnp.where(same, 0.0, MASKED).astype(F32)


def half_of(pair, side):
    lane = lax.broadcasted_iota(jnp.int32, pair.shape, 1)
    keep = lane < HEAD_DIM if side == 0 else lane >= HEAD_DIM
    return jnp.where(keep, pair, jnp.zeros_like(pair))


def fetch_weights(me, sources, weight_refs, parts_ref, sem):
    core, chip = me & 1, me >> 1
    side = sources[0].shape[2]
    each = weight_refs[0].shape[0] // CHIPS
    for index, source in enumerate(sources):
        half = core if index < 4 else 1 - core
        cols = pl.ds(pl.multiple_of(half * side, LANES), side)
        for layer in range(4):
            owner = chip ^ (4 * layer + (0, 1 + half, 2 - half, 3)[index % 4])
            rows = pl.ds(pl.multiple_of(owner * each, 16), each)
            for number, ref in enumerate(weight_refs):
                pltpu.make_async_copy(
                    source.at[layer, pl.ds(number * each, each), :], ref.at[rows, cols], sem.at[number]
                ).start()
            pltpu.make_async_copy(
                source.at[layer, pl.ds(4 * each, 16), :], parts_ref.at[2 * owner + half], sem.at[4]
            ).start()


def project(me_ref, x_ref, *refs):
    sources = refs[:8]
    n1_ref, q_ref, k_ref, v_ref = refs[8:12]
    wq_ref, wk_ref, wv_ref, wo_ref, vec_ref, bup_ref, parts_ref, sem = refs[12:]
    weights = (wq_ref, wk_ref, wv_ref, wo_ref)
    core = me_ref[0] & 1

    @pl.when(pl.program_id(0) == 0)
    def _():
        fetch_weights(me_ref[0], sources, weights, parts_ref, sem)
        for number, ref in enumerate(weights + (parts_ref,)):
            pltpu.make_async_copy(ref, ref, sem.at[number]).wait()
        count, _, side = parts_ref.shape
        group = count // 2
        halves = [sum(parts_ref[half * group + index].astype(F32) for index in range(group)) for half in range(2)]
        vec_ref[...] = jnp.concatenate(halves, axis=1)
        blocks = bup_ref.shape[1] // side
        group = CHIPS // blocks
        for block in range(blocks):
            rows = sum(parts_ref[2 * (block * group + index) + core].astype(F32) for index in range(group))
            bup_ref[:, block * side : (block + 1) * side] = rows[8:9]

    project_rows(x_ref, vec_ref, wq_ref, wk_ref, wv_ref, n1_ref, q_ref, k_ref, v_ref)


def project_rows(x_ref, vec_ref, wq_ref, wk_ref, wv_ref, n1_ref, q_ref, k_ref, v_ref):
    hat, _ = normalize(x_ref[...].astype(F32))
    n1 = (hat * vec_ref[0:1, :] + vec_ref[1:2, :]).astype(BF16)
    n1_ref[...] = n1
    q_ref[...] = (dot_nn(n1, wq_ref[...]) + vec_ref[2:3, :]).astype(BF16) * jnp.asarray(SCALE, BF16)
    k_ref[...] = dot_nn(n1, wk_ref[...]).astype(BF16)
    v_ref[...] = (dot_nn(n1, wv_ref[...]) + vec_ref[3:4, :]).astype(BF16)


def mask_grads(lengths_ref, grad_ref, cot_ref, dsum_ref):
    tile = pl.program_id(0)
    slots = lengths_ref.shape[1]
    valid = segments(lengths_ref, tile, slots, grad_ref.shape[0], 0) < slots
    cot = jnp.where(valid, grad_ref[...].astype(F32), 0.0)
    cot_ref[...] = cot.astype(BF16)

    @pl.when(tile == 0)
    def _():
        dsum_ref[...] = jnp.zeros_like(dsum_ref)

    dsum_ref[0:1, :] += column_sum(cot)


def attention_forward(lengths_ref, x_ref, vec_ref, q_ref, k_ref, v_ref, wo_ref, mixed_ref, lse_ref, resid_ref, n2_ref):
    tile = pl.program_id(0)
    rows = q_ref.shape[0]
    slots = lengths_ref.shape[1]
    bias = mask_bias(lengths_ref, tile, slots, rows)
    lane = lax.broadcasted_iota(jnp.int32, (rows, LANES), 1)
    lse = jnp.zeros((rows, LANES), F32)

    def at(pair):
        return pl.ds(pair * LANES, LANES)

    def scores_of(pair):
        qp, kp = q_ref[:, at(pair)], k_ref[:, at(pair)]
        return [dot_nt(half_of(qp, side), kp) for side in range(2)]

    def softmax_of(scores):
        scores = scores + bias
        top = jnp.max(scores, axis=-1, keepdims=True)
        weights = jnp.exp(scores - top)
        sums = jnp.sum(weights, axis=-1, keepdims=True)
        return (weights * (1.0 / sums)).astype(BF16), top + jnp.log(sums)

    raw = {}
    probs = {}
    for turn in range(PAIRS + 2):
        if turn < PAIRS:
            raw[turn] = scores_of(turn)
        if 0 <= turn - 1 < PAIRS:
            both = [softmax_of(scores) for scores in raw.pop(turn - 1)]
            for side in range(2):
                lse = jnp.where(lane == 2 * (turn - 1) + side, both[side][1], lse)
            probs[turn - 1] = [pair[0] for pair in both]
        if turn >= 2:
            vp = v_ref[:, at(turn - 2)]
            parts = [dot_nn(probs[turn - 2][side], half_of(vp, side)) for side in range(2)]
            mixed_ref[:, at(turn - 2)] = (parts[0] + parts[1]).astype(BF16)
    lse_ref[...] = lse
    resid = x_ref[...].astype(F32) + (dot_nn(mixed_ref[...], wo_ref[...]) + vec_ref[4:5, :])
    resid_ref[...] = resid
    hat, _ = normalize(resid)
    n2_ref[...] = (hat * vec_ref[5:6, :] + vec_ref[6:7, :]).astype(BF16)


def flat_rows(ref):
    return ref[...].reshape(-1, ref.shape[-1])


def spread(me, rows, put):
    layer, plane = me >> 3, (me >> 1) & 3
    each = rows.shape[0] // CHIPS
    for chip in range(CHIPS):
        put((chip & 3) ^ plane, (chip >> 2) ^ layer, rows[chip * each : (chip + 1) * each].astype(BF16))


def mlp(sets, me_ref, *refs):
    n2_hbm, cot_hbm = refs[:sets], refs[sets : 2 * sets]
    bup_ref, wup_ref, wdown_ref = refs[2 * sets : 2 * sets + 3]
    refs = refs[2 * sets + 3 :]
    act_hbm, gtwo_hbm, refs = refs[:sets], refs[sets : 2 * sets], refs[2 * sets :]
    down_own, down_send, up_own, up_send, dbu_ref = refs[:5]
    n2_ref, cot_ref, gacc, act_ref, gup_ref, low_ref, gdown_ref, gupw_ref, in_sem, act_sem, out_sem, grad_sem = refs[5:]
    step = pl.program_id(0)
    last = pl.num_programs(0) - 1
    me = me_ref[0]
    rows = n2_ref.shape[0] // sets

    def rows_of(index):
        return pl.ds(pl.multiple_of(index * rows, rows), rows)

    @pl.when(step == 0)
    def _():
        for index in range(sets):
            at = pl.ds(index * rows, rows)
            pltpu.make_async_copy(n2_hbm[index], n2_ref.at[at, :], in_sem.at[0, index]).start()
            pltpu.make_async_copy(cot_hbm[index], cot_ref.at[at, :], in_sem.at[1, index]).start()

    wup = flat_rows(wup_ref)
    wdown = flat_rows(wdown_ref)
    dbu_ref[...] = jnp.zeros_like(dbu_ref)
    slot = lax.rem(step, 2)
    width = n2_ref.shape[1]

    @pl.loop(0, sets)
    def _(index):
        at = rows_of(index)

        @pl.when(step == 0)
        def _():
            pltpu.make_async_copy(n2_ref.at[at, :], n2_ref.at[at, :], in_sem.at[0, index]).wait()
            pltpu.make_async_copy(cot_ref.at[at, :], cot_ref.at[at, :], in_sem.at[1, index]).wait()

        pre = dot_nn(n2_ref[at, :], wup) + bup_ref[...]
        grad_act = dot_nt(cot_ref[at, :], wdown)
        square = pre * pre
        tanh = jnp.tanh(pre * (GELU_C + (GELU_C * GELU_A) * square))
        half = 0.5 + 0.5 * tanh
        inner = GELU_C + (3.0 * GELU_C * GELU_A) * square
        act_ref[slot, at, :] = (pre * half).astype(BF16)
        gup = (grad_act * (half + (0.5 * pre) * (1.0 - tanh * tanh) * inner)).astype(BF16)
        gup_ref[at, :] = gup
        dbu_ref[...] += column_sum(gup.astype(F32))

    @pl.when(step == 0)
    def _():
        @pl.loop(0, sets)
        def _(index):
            at = rows_of(index)
            gacc[at, :] = dot_nt(gup_ref[at, :], wup)

    @pl.when((step > 0) & (step < last))
    def _():
        @pl.loop(0, sets)
        def _(index):
            at = rows_of(index)
            gacc[at, :] += dot_nt(gup_ref[at, :], wup)

    def results():
        for index in range(sets):
            at = pl.ds(index * rows, rows)
            source = low_ref.at[at, :] if index else gacc.at[at, :]
            yield pltpu.make_async_copy(source, gtwo_hbm[index], out_sem.at[index])

    def activations(number):
        for index in range(sets):
            source = act_ref.at[number, pl.ds(index * rows, rows), :]
            cols = pl.ds(number * width, width)
            yield pltpu.make_async_copy(source, act_hbm[index].at[:, cols], act_sem.at[number, index])

    for number in range(act_ref.shape[0]):

        @pl.when(step == number)
        def _():
            for copy in activations(number):
                copy.start()

    @pl.when(step == last)
    def _():
        @pl.loop(0, sets)
        def _(index):
            at = rows_of(index)
            total = gacc[at, :] + dot_nt(gup_ref[at, :], wup)
            gacc[at, :] = total
            low_ref[at, :] = total.astype(BF16)

        for copy in results():
            copy.start()

    gdown_ref[slot] = dot_tn(act_ref[slot], cot_ref[...]).astype(BF16)
    deep = down_own.shape[2]
    count = gdown_ref.shape[1] // deep
    for index in range(count):
        chip = step * count + index
        source = gdown_ref.at[slot, pl.ds(index * deep, deep), :]
        keep_or_send(me, chip & 3, (chip >> 2) ^ (me >> 3), source, down_own, down_send, grad_sem, 0)

    gupw_ref[slot] = dot_tn(n2_ref[...], gup_ref[...]).astype(BF16)
    each = gupw_ref.shape[1] // CHIPS
    for chip in range(CHIPS):
        source = gupw_ref.at[slot, pl.ds(chip * each, each), :]
        keep_or_send(
            me, chip & 3, (chip >> 2) ^ (me >> 3), source, up_own.at[step], up_send.at[step], grad_sem, 2)

    @pl.when(step == last)
    def _():
        for copy in results():
            copy.wait()
        for number in range(act_ref.shape[0]):
            for copy in activations(number):
                copy.wait()
        for number, ref in enumerate((down_own, down_send, up_own, up_send)):
            pltpu.make_async_copy(ref, ref, grad_sem.at[number]).wait()


def keep_or_send(me, plane, layer, source, own_ref, send_ref, sem, number):
    core = me & 1
    relative = plane ^ ((me >> 1) & 3)
    mine = (relative == 0) | (relative == 2 - core)

    @pl.when(mine)
    def _():
        pltpu.make_async_copy(source, own_ref.at[layer, jnp.where(relative == 0, 0, 1)], sem.at[number]).start()

    @pl.when(jnp.logical_not(mine))
    def _():
        pltpu.make_async_copy(source, send_ref.at[layer, jnp.where(relative == 3, 1, 0)], sem.at[number + 1]).start()


def mlp_out_other(me_ref, act_ref, wdown_ref, out_ref):
    out_ref[...] = dot_nn(act_ref[...], flat_rows(wdown_ref)).astype(BF16)


def mlp_out_own(me_ref, resid_ref, vec_ref, act_ref, take_ref, wdown_ref, out_ref):
    half = dot_nn(act_ref[...], flat_rows(wdown_ref)) + take_ref[...].astype(F32)
    out_ref[...] = (resid_ref[...] + (half + vec_ref[7:8, :])).astype(BF16)


def attention_backward(lengths_ref, q_ref, k_ref, v_ref, lse_ref, cot_ref, resid_ref, gtwo_ref, gother_ref, vec_ref, wo_ref,
                       grads_ref, gresid_ref, dsum_ref, gmix_ref):
    tile = pl.program_id(0)
    rows = q_ref.shape[0]

    @pl.when(tile == 0)
    def _():
        dsum_ref[...] = jnp.zeros_like(dsum_ref)

    hat, inverse = normalize(resid_ref[...])
    grad_two = gtwo_ref[...] + gother_ref[...].astype(F32)
    gresid = cot_ref[...].astype(F32) + norm_back(grad_two, vec_ref[5:6, :], hat, inverse)
    gresid_ref[...] = gresid
    gattn = gresid.astype(BF16)
    grads_ref[3] = gattn
    dsum_ref[2:3, :] += column_sum(gattn.astype(F32))
    dsum_ref[3:4, :] += column_sum(grad_two * hat)
    dsum_ref[4:5, :] += column_sum(grad_two)
    gmix_ref[...] = dot_nt(gattn, wo_ref[...]).astype(BF16)
    bias = mask_bias(lengths_ref, tile, lengths_ref.shape[1], rows)

    def load(pair):
        cols = pl.ds(pair * LANES, LANES)
        return q_ref[:, cols], k_ref[:, cols], v_ref[:, cols], gmix_ref[:, cols]

    def products_of(pair):
        qp, kp, vp, gp = load(pair)
        return [(dot_nt(half_of(qp, side), kp), dot_nt(half_of(gp, side), vp)) for side in range(2)]

    def softmax_back(pair, products):
        results = []
        for side, (scores, grad_probs) in enumerate(products):
            head = 2 * pair + side
            probs = jnp.exp(scores + bias - lse_ref[:, head : head + 1])
            weighted = probs * grad_probs
            dot = jnp.sum(weighted, axis=-1, keepdims=True)
            results.append((probs.astype(BF16), (weighted - probs * dot).astype(BF16)))
        return results

    def store(pair, results):
        qp, kp, vp, gp = load(pair)
        dq = sum(dot_nn(results[side][1], half_of(kp, side)) for side in range(2))
        dk = sum(dot_tn(results[side][1], half_of(qp, side)) for side in range(2))
        dv = sum(dot_tn(results[side][0], half_of(gp, side)) for side in range(2))
        cols = pl.ds(pair * LANES, LANES)
        grads_ref[0, :, cols] = (dq * SCALE).astype(BF16)
        grads_ref[1, :, cols] = dk.astype(BF16)
        grads_ref[2, :, cols] = dv.astype(BF16)

    raw = {}
    done = {}
    for turn in range(PAIRS + 2):
        if turn < PAIRS:
            raw[turn] = products_of(turn)
        if 0 <= turn - 1 < PAIRS:
            done[turn - 1] = softmax_back(turn - 1, raw.pop(turn - 1))
        if turn >= 2:
            store(turn - 2, done.pop(turn - 2))

    dsum_ref[0:1, :] += column_sum(grads_ref[0].astype(F32))
    dsum_ref[1:2, :] += column_sum(grads_ref[2].astype(F32))


def weight_grads(me_ref, n1_ref, mixed_ref, columns_ref, sum_back_ref, sum_down_ref, sum_up_ref, send_ref, keep_ref):
    step = pl.program_id(0)
    me = me_ref[0]
    first = (me & 1) == 0
    side = send_ref.shape[3]
    each = n1_ref.shape[1] // CHIPS

    def run(left, number):
        result = dot_tn(left, columns_ref[0])
        low, high = result[:, :side], result[:, side:]
        rows_at = pl.ds(pl.multiple_of(number * each, 16), each)

        def put_send(plane, layer, rows):
            send_ref[layer, plane, rows_at, :] = rows

        def put_keep(plane, layer, rows):
            keep_ref[layer, plane, rows_at, :] = rows

        spread(me, jnp.where(first, high, low), put_send)
        spread(me, jnp.where(first, low, high), put_keep)

    @pl.when(step < 3)
    def _():
        run(n1_ref[...], step)

    @pl.when(step == 3)
    def _():
        run(mixed_ref[...], 3)
        nothing = jnp.zeros((2, n1_ref.shape[1]), F32)
        vecs = jnp.concatenate((nothing, sum_back_ref[0:5], sum_down_ref[0:1]), axis=0)
        for chip in range(CHIPS):
            half = chip // (CHIPS // 2)
            block = chip * (sum_up_ref.shape[1] // side) // CHIPS
            last = jnp.broadcast_to(sum_up_ref[:, block * side : (block + 1) * side], (8, side))
            short = vecs[:, half * side : (half + 1) * side]
            at = ((chip >> 2) ^ (me >> 3), (chip & 3) ^ ((me >> 1) & 3))
            keep_ref[at[0], at[1], 4 * each :, :] = jnp.concatenate((short, last), axis=0).astype(BF16)
            send_ref[at[0], at[1], 4 * each :, :] = jnp.concatenate((short, jnp.zeros_like(last)), axis=0).astype(BF16)


def tokens_backward(x_ref, gresid_ref, vec_ref, grads_ref, wq_ref, wk_ref, wv_ref, gtok_ref, dsum_ref):
    @pl.when(pl.program_id(0) == 0)
    def _():
        dsum_ref[...] = jnp.zeros_like(dsum_ref)

    grad_one = dot_nt(grads_ref[0], wq_ref[...]) + dot_nt(grads_ref[1], wk_ref[...]) + dot_nt(grads_ref[2], wv_ref[...])
    hat, inverse = normalize(x_ref[...].astype(F32))
    gtok_ref[...] = (gresid_ref[...] + norm_back(grad_one, vec_ref[0:1, :], hat, inverse)).astype(BF16)
    dsum_ref[0:1, :] += column_sum(grad_one * hat)
    dsum_ref[1:2, :] += column_sum(grad_one)


def rows_spec(block, width):
    return pl.BlockSpec((block, width), lambda i, *me: (i, 0))


def cols_spec(height, block):
    return pl.BlockSpec((height, block), lambda i, *me: (0, i))


def whole_spec(shape):
    return pl.BlockSpec(shape, lambda *i: (0,) * len(shape), pipeline_mode=pl.Buffered(1))


def kept_spec(shape):
    return pl.BlockSpec(shape, lambda *i: (0,) * len(shape))


SMEM = pl.BlockSpec(memory_space=pltpu.SMEM)


def cost(flops):
    return pl.CostEstimate(flops=flops, bytes_accessed=1, transcendentals=0)


def call(kernel, grid, ins, outs, scratch, name, flops, *args):
    out_specs = tuple(spec for spec, _ in outs)
    out_shape = tuple(shape for _, shape in outs)
    return pl.pallas_call(
        kernel,
        grid=grid,
        in_specs=ins,
        out_specs=out_specs,
        out_shape=out_shape,
        scratch_shapes=scratch,
        compiler_params=pltpu.CompilerParams(vmem_limit_bytes=VMEM, dimension_semantics=("arbitrary",) * len(grid)),
        cost_estimate=cost(flops),
        name=name,
    )(*args)


def call_with(me, kernel, steps, ins, outs, scratch, name, flops, *args):
    out_shape = tuple(shape for _, shape in outs)
    return pl.pallas_call(
        kernel,
        grid_spec=pltpu.PrefetchScalarGridSpec(
            num_scalar_prefetch=1, grid=(steps,), in_specs=ins, out_specs=tuple(spec for spec, _ in outs),
            scratch_shapes=scratch),
        out_shape=out_shape,
        compiler_params=pltpu.CompilerParams(vmem_limit_bytes=VMEM, dimension_semantics=("arbitrary",)),
        cost_estimate=cost(0),
        name=name,
    )(me, *args)


def shaped(*shape, dtype=BF16):
    return jax.ShapeDtypeStruct(shape, dtype)


def flipped(count, change):
    pairs = []
    for source in range(count):
        core, chip = source & 1, source >> 1
        core, chip = change(core, chip)
        pairs.append((source, 2 * chip + core))
    return pairs


def swap(array, change):
    return lax.ppermute(array, "dp", flipped(lax.axis_size("dp"), change))


def other_core(core, chip):
    return core ^ 1, chip


def first_plane(core, chip):
    return core, chip ^ (1 + core)


def second_plane(core, chip):
    return core, chip ^ (2 - core)


def other_plane(distance):
    return lambda core, chip: (core, chip ^ distance)


def other_layer(distance):
    return lambda core, chip: (core, chip ^ (4 * distance))


def split_shards(core_ref, q_ref, k_ref, v_ref, o_ref, u_ref, keep_ref, send_ref):
    width = q_ref.shape[1]
    side = width // 2
    first = core_ref[0] == 0

    def put(index, low, high):
        keep_ref[index] = jnp.where(first, low, high).astype(BF16)
        send_ref[index] = jnp.where(first, high, low).astype(BF16)

    for index, ref in enumerate((q_ref, k_ref, v_ref, o_ref)):
        rows = ref[...].astype(F32)
        put(index, rows[:, :side], rows[:, side:])
    up = u_ref[...].astype(F32)
    hidden = up.shape[1]
    deep = hidden // (2 * CHIPS)
    halves = [
        jnp.concatenate([up[:, start : start + deep] for start in range(half * deep, hidden, 2 * deep)], axis=1)
        for half in range(2)
    ]
    for part in range(hidden // width):
        at = slice(part * side, (part + 1) * side)
        put(4 + part, halves[0][:, at], halves[1][:, at])


def join_shards(me_ref, keep_ref, take_ref, down_ref, *refs):
    vectors, (near_ref, far_ref) = refs[:-2], refs[-2:]
    me = me_ref[0]
    first = (me & 1) == 0
    parts, own, side = keep_ref.shape
    folds = parts - 4
    keep = keep_ref[...].astype(F32)
    take = take_ref[...].astype(F32)

    def joined(index):
        low = jnp.where(first, keep[index], take[index])
        high = jnp.where(first, take[index], keep[index])
        return jnp.concatenate((low, high), axis=0).astype(BF16)

    for index in range(4):
        near_ref[2 * own * index : 2 * own * (index + 1), :] = joined(index)
    for index in range(folds):
        far_ref[2 * own * (index // 2) : 2 * own * (index // 2 + 1), side * (index % 2) : side * (index % 2 + 1)] = joined(4 + index)
    far_ref[folds * own :, :] = down_ref[...]
    rows = []
    for ref in vectors:
        flat = ref[...].astype(F32).reshape(1, -1)
        rows.append(jnp.concatenate((flat, jnp.zeros((1, side - flat.shape[1]), F32)), axis=1))
    rows.append(jnp.zeros((16 - len(rows), side), F32))
    rows = jnp.concatenate(rows, axis=0)
    short = pltpu.roll(rows, own * lax.rem(me, side // own), 1)
    long = pltpu.roll(rows, folds * own * lax.rem(me >> 1, side // (folds * own)), 1)
    index = lax.broadcasted_iota(jnp.int32, rows.shape, 0)
    near_ref[8 * own :, :] = jnp.where(index < 8, short, long).astype(BF16)


def across_layers(shard):
    return jnp.stack([shard] + [swap(shard, other_layer(distance)) for distance in (1, 2, 3)])


def after(arrays, *others):
    return lax.optimization_barrier((arrays, others))[0]


def small_call(kernel, args, outs, name, scratch=(), ins=None, flops=0):
    return pl.pallas_call(
        kernel,
        in_specs=ins,
        out_specs=tuple(spec for spec, _ in outs),
        out_shape=tuple(shape for _, shape in outs),
        scratch_shapes=list(scratch),
        compiler_params=pltpu.CompilerParams(vmem_limit_bytes=VMEM),
        cost_estimate=cost(flops),
        name=name,
    )(*args)


VMEM_SPEC = pl.BlockSpec(memory_space=pltpu.VMEM)
ANY_SPEC = pl.BlockSpec(memory_space=pl.ANY)


def gather_by_hand(me, weights, vectors, masked):
    count = lax.axis_size("dp")
    own, width = weights[0].shape
    side = width // 2
    deep = weights[5].shape[0]
    folds = deep // own
    halves = (VMEM_SPEC, shaped(4 + folds, own, side))
    keep, send = small_call(
        split_shards, (me & 1, *weights[:5]), [halves, halves], "split_shards", ins=[SMEM] + [VMEM_SPEC] * 5)
    take = swap(send, other_core)
    near, far = small_call(
        join_shards, (me, keep, take, weights[5], *vectors),
        [(VMEM_SPEC, shaped(8 * own + 16, side)), (VMEM_SPEC, shaped(2 * deep, width))], "join_shards",
        ins=[SMEM] + [VMEM_SPEC] * (3 + len(vectors)))
    far = lax.all_gather(far, "dp", axis=0, tiled=True).reshape(count // 2, 2, 2 * deep, width)
    near = across_layers(near)
    cot, sum_down = masked(near)
    far_plane = after(swap(near, first_plane), cot)
    near = [near, far_plane, swap(near, second_plane), swap(far_plane, second_plane)]
    return near + [swap(piece, other_core) for piece in near], far, cot, sum_down


def gather_plain(weights, vectors):
    squares, up_weight, down_weight = weights[:4], weights[4], weights[5]
    count = lax.axis_size("dp")
    own, width = squares[0].shape
    folds = down_weight.shape[0] // own
    hidden = up_weight.shape[1]
    flat = jnp.concatenate(vectors)
    packed = jnp.concatenate(
        (
            *squares,
            up_weight.reshape(own, folds, width).transpose(1, 0, 2).reshape(own * folds, width),
            down_weight,
            jnp.pad(flat.reshape(1, -1), ((0, 7), (0, width - flat.size))),
        ),
        axis=0,
    )
    whole = lax.all_gather(packed, "dp", axis=0, tiled=True).reshape(count, -1, width)
    square_all = [whole[:, index * own : (index + 1) * own, :].reshape(width, width) for index in range(4)]
    wup = whole[:, 4 * own : (4 + folds) * own, :].reshape(count, folds, own, width).transpose(0, 2, 1, 3)
    wup = wup.reshape(CHIPS, width // CHIPS, 2, CHIPS // 2, 2, -1).transpose(0, 4, 2, 1, 3, 5).reshape(CHIPS, 2, -1, width)
    wdown = whole[:, (4 + folds) * own : (4 + 2 * folds) * own, :]
    wdown = wdown.reshape(CHIPS, 2, -1, width)
    last = whole[:, (4 + 2 * folds) * own, : flat.size].astype(F32)
    vec = last[:, : 8 * own].reshape(count, 8, own).transpose(1, 0, 2).reshape(8, width)
    bup = last[:, 8 * own :].reshape(CHIPS, 2, -1).transpose(1, 0, 2).reshape(2, 1, -1)
    return (*square_all, jnp.concatenate((wup, wdown), axis=2), jnp.pad(vec, ((0, 8), (0, 0))), bup)


def merge_core(core_ref, keep_ref, take_ref, own_ref, send_ref):
    core = core_ref[0]

    def whole(plane):
        return (keep_ref[:, plane].astype(F32) + take_ref[:, plane].astype(F32)).astype(BF16)

    own_ref[:, 0] = whole(0)
    own_ref[:, 1] = whole(2 - core)
    send_ref[:, 0] = whole(1 + core)
    send_ref[:, 1] = whole(3)


def merge_first(*refs):
    pairs, rest_ref, send_ref = refs[:-2], refs[-2], refs[-1]
    base = 0
    for own_ref, take_ref in zip(pairs[::2], pairs[1::2]):
        for part in range(own_ref.shape[0]):
            at = slice(base, base + own_ref.shape[3])
            rest_ref[:, at, :] = own_ref[part, :, 0].astype(F32) + take_ref[part, :, 0].astype(F32)
            send_ref[:, at, :] = (own_ref[part, :, 1].astype(F32) + take_ref[part, :, 1].astype(F32)).astype(BF16)
            base += own_ref.shape[3]


def merge_second(own_ref, take_ref, rest_ref, *send_refs):
    for layer in range(4):
        whole = own_ref[layer] + take_ref[layer].astype(F32)
        if layer == 0:
            rest_ref[...] = whole
        else:
            send_refs[layer - 1][...] = whole.astype(BF16)


def merge_last(deep, core_ref, rest_ref, a_ref, b_ref, c_ref, *refs):
    whole = rest_ref[...] + a_ref[...].astype(F32) + b_ref[...].astype(F32) + c_ref[...].astype(F32)
    first = core_ref[0] == 0
    if deep:
        refs[0][...] = whole[:deep]
        refs = refs[1:]
    keep_ref, send_ref = refs[:2]
    parts, own, _ = keep_ref.shape
    for part in range(parts):
        low = whole[deep + 2 * own * part : deep + 2 * own * part + own]
        high = whole[deep + 2 * own * part + own : deep + 2 * own * (part + 1)]
        keep_ref[part] = jnp.where(first, low, high)
        send_ref[part] = jnp.where(first, high, low)
    if not deep:
        refs[2][...] = whole[2 * own * parts :]


def finish(me_ref, up_keep_ref, up_take_ref, keep_ref, take_ref, flat_ref, late_ref, up_ref, *refs):
    me = me_ref[0]
    first = (me & 1) == 0
    side = keep_ref.shape[2]
    width = 2 * side
    squares, flats = refs[:4], refs[4:]
    own = up_ref.shape[0]
    for number, ref in enumerate(squares):
        keep, take = keep_ref[number], take_ref[number]
        ref[:, :side] = jnp.where(first, keep, take)
        ref[:, side:] = jnp.where(first, take, keep)
    parts = up_keep_ref.shape[0]
    deep = parts * width // CHIPS
    for part in range(parts):
        keep, take = up_keep_ref[part], up_take_ref[part]
        low, high = jnp.where(first, keep, take), jnp.where(first, take, keep)
        pieces = []
        for start in range(0, width, deep):
            pieces += [low[:, start : start + deep], high[:, start : start + deep]]
        up_ref[:, 2 * width * part : 2 * width * (part + 1)] = jnp.concatenate(pieces, axis=1)
    late = jnp.where(me < side // own, late_ref[0:2, :side], late_ref[0:2, side:])
    flat = jnp.concatenate((late, flat_ref[2:]), axis=0)
    long = flats[-1].shape[0]
    short_turn = lax.rem(side - own * lax.rem(me, side // own), side)
    long_turn = lax.rem(side - long * lax.rem(me >> 1, side // long), side)
    short = pltpu.roll(flat, short_turn, 1)
    for number, ref in enumerate(flats[:-1]):
        ref[...] = short[number, :own]
    flats[-1][...] = pltpu.roll(flat, long_turn, 1)[8, :long]


def fenced(function, *args):
    kinds = jax.eval_shape(function, *args)

    def nothing(*_):
        return jax.tree.map(lambda kind: jnp.zeros(kind.shape, kind.dtype), kinds)

    return lax.cond(lax.axis_index("dp") < lax.axis_size("dp"), function, nothing, *args)


def scatter_core(send):
    return swap(send, other_core)


def merge_core_of(core, keep, take):
    shape = keep.shape
    planes, rows, side = shape[-3:]
    keep, take = keep.reshape(-1, planes, rows, side), take.reshape(-1, planes, rows, side)
    count = keep.shape[0]
    steps = MERGE_STEPS
    block = pl.BlockSpec((count // steps, planes, rows, side), lambda i: (i, 0, 0, 0))
    half = (pl.BlockSpec((count // steps, 2, rows, side), lambda i: (i, 0, 0, 0)), shaped(count, 2, rows, side))
    own, send = call(merge_core, (steps,), [SMEM, block, block], [half, half], [], "merge_core", 0, core, keep, take)
    return own.reshape(-1, CHIPS // 4, 2, rows, side), send


def scatter_second(*pairs):
    _, count, _, _, side = pairs[0].shape
    rows = sum(piece.shape[0] * piece.shape[3] for piece in pairs[::2])
    steps = MERGE_STEPS
    ins = [pl.BlockSpec((piece.shape[0], count // steps, *piece.shape[2:]), lambda i: (0, i, 0, 0, 0)) for piece in pairs]
    out = pl.BlockSpec((count // steps, rows, side), lambda i: (i, 0, 0))
    rest, send = call(
        merge_first, (steps,), ins, [(out, shaped(count, rows, side, dtype=F32)), (out, shaped(count, rows, side))], [],
        "merge_first", 0, *pairs)
    return rest, swap(send, second_plane)


def scatter_layers(own, take):
    _, rows, side = own.shape
    out = shaped(rows, side)
    rest, *sends = small_call(
        merge_second, (own, take), [(VMEM_SPEC, shaped(rows, side, dtype=F32))] + [(VMEM_SPEC, out)] * 3,
        "merge_second", ins=[VMEM_SPEC] * 2)
    return [rest] + [swap(piece, other_layer(r + 1)) for r, piece in enumerate(sends)]


def scatter_last(core, pieces, own, parts, deep):
    rows, side = pieces[0].shape
    outs = [(VMEM_SPEC, shaped(parts, own, side, dtype=F32))] * 2
    if deep:
        outs = [(VMEM_SPEC, shaped(deep, side, dtype=F32))] + outs
    else:
        outs.append((VMEM_SPEC, shaped(rows - 2 * own * parts, side, dtype=F32)))
    return small_call(
        functools.partial(merge_last, deep), (core, *pieces), outs, "merge_last", ins=[SMEM] + [VMEM_SPEC] * 4, flops=SHORT if deep else 0)


def reduce_plain(down_pairs, up_pairs, square_pair, flat):
    def scattered(array, axis):
        return lax.psum_scatter(array, "dp", scatter_dimension=axis, tiled=True).astype(F32)

    def planes(own, send, core):
        order = (own[..., 0, :, :], send[..., 0, :, :], own[..., 1, :, :], send[..., 1, :, :])
        if core == 1:
            order = (order[0], order[2], order[1], order[3])
        return jnp.stack(order, axis=-3)

    down = jnp.stack([planes(*pair, core) for core, pair in enumerate(down_pairs)])
    up = jnp.stack([planes(*pair, core) for core, pair in enumerate(up_pairs)])
    width = down.shape[-1]
    each = up.shape[4]
    down = down.transpose(1, 2, 0, 3, 4).reshape(-1, width)
    up = up.reshape(2, 2, CHIPS, each, CHIPS // 2, -1).transpose(2, 3, 1, 4, 0, 5).reshape(CHIPS * each, -1)
    square = jnp.stack(square_pair).transpose(1, 2, 3, 0, 4)[:, :, : 4 * each]
    square = square.reshape(CHIPS, 4, each, width).transpose(1, 0, 2, 3).reshape(4, CHIPS * each, width)
    return (
        scattered(down, 0),
        scattered(up, 0),
        *scattered(square, 1),
        lax.psum_scatter(flat, "dp", scatter_dimension=0, tiled=True).reshape(-1),
    )


def body(tokens, lengths, attn_gain, attn_shift, query_weight, query_bias, key_weight, value_weight, value_bias,
         out_weight, out_bias, mlp_gain, mlp_shift, up_weight, up_bias, down_weight, down_bias, grad_out):
    count = lax.axis_size("dp")
    rows, width = tokens.shape
    tiles = lengths.shape[0]
    tile = rows // tiles
    hidden = up_bias.shape[0] * count
    own = width // count
    folds = hidden // width
    vectors = (attn_gain, attn_shift, query_bias, value_bias, out_bias, mlp_gain, mlp_shift, down_bias, up_bias)
    by_hand = count == 2 * CHIPS
    me = lax.axis_index("dp").astype(jnp.int32).reshape(1) if by_hand else jnp.zeros((1,), jnp.int32)
    core = me & 1
    weights = (query_weight, key_weight, value_weight, out_weight, up_weight, down_weight)

    tile_rows = rows_spec(tile, width)
    square = whole_spec((width, width))
    vec_spec = whole_spec((16, width))
    sums = (kept_spec((8, width)), shaped(8, width, dtype=F32))
    low_rows = (tile_rows, shaped(rows, width))
    lse_spec = rows_spec(tile, LANES)
    mac = 2 * rows * width * width
    kept_square = (kept_spec((width, width)), shaped(width, width))
    kept_vec = (kept_spec((16, width)), shaped(16, width, dtype=F32))
    kept_hidden = (kept_spec((1, hidden // 2)), shaped(1, hidden // 2, dtype=F32))
    side = width // 2

    def masked(*earlier):
        return call(
            mask_grads, (tiles,), [SMEM, tile_rows], [low_rows, sums], [], "mask_grads", 0,
            lengths, after(grad_out, *earlier))

    if by_hand:
        near, far, cot, sum_down = gather_by_hand(me, weights, vectors, masked)
        n1, q, k, v, wq, wk, wv, wo, vec, bup = call_with(
            me, project, tiles, [tile_rows] + [ANY_SPEC] * 8, [low_rows] * 4 + [kept_square] * 4 + [kept_vec, kept_hidden],
            [pltpu.VMEM((count, 16, side), BF16), pltpu.SemaphoreType.DMA((5,))], "project", 0, tokens, *near)
        cot_other = swap(cot, other_core)
    else:
        wq, wk, wv, wo, far, vec, bup = gather_plain(weights, vectors)
        cot, sum_down = masked()
        n1, q, k, v = call(
            project_rows, (tiles,), [tile_rows, vec_spec, square, square, square], [low_rows] * 4,
            [], "project", 0, tokens, vec, wq, wk, wv)
    high_rows = (tile_rows, shaped(rows, width, dtype=F32))
    mixed, lse, resid, n2 = call(
        attention_forward, (tiles,), [SMEM, tile_rows, vec_spec, tile_rows, tile_rows, tile_rows, square],
        [low_rows, (lse_spec, shaped(rows, LANES, dtype=F32)), high_rows, low_rows],
        [], "attention_forward", 0, lengths, tokens, vec, q, k, v, wo)

    each = width // CHIPS
    deep = hidden // (2 * CHIPS)
    blocks = hidden // (2 * width)
    full_rows = whole_spec((rows, width))
    up_spec = pl.BlockSpec((CHIPS, 1, each, width), lambda i, me: (0, me[0] & 1, i, 0))
    down_spec = pl.BlockSpec((CHIPS // 2, 1, deep, width), lambda i, me: (i, me[0] & 1, 1, 0))
    hidden_spec = pl.BlockSpec((1, width), lambda i, me: (0, i))
    low_out, high_out = (ANY_SPEC, shaped(rows, width)), (ANY_SPEC, shaped(rows, width, dtype=F32))
    act_out = (ANY_SPEC, shaped(rows, blocks * width))
    down_part = (ANY_SPEC, shaped(4, 2, deep, width))
    up_part = (ANY_SPEC, shaped(blocks, 4, 2, each, width))

    act_spec = pl.BlockSpec((tile, blocks * width), lambda i, *me: (i, 0))
    wide_spec = pl.BlockSpec(
        (CHIPS, 1, deep, width), lambda i, me: (0, me[0] & 1, 1, 0), pipeline_mode=pl.Buffered(1))

    def run_mlp(me, tokens_of, bup):
        sets = len(tokens_of[0])
        low, high = pltpu.VMEM((sets * rows, width), BF16), pltpu.VMEM((sets * rows, width), F32)
        weight = pltpu.VMEM((2, width, width), BF16)
        dma = pltpu.SemaphoreType.DMA((2, sets))
        return call_with(
            me, functools.partial(mlp, sets), blocks, [ANY_SPEC] * (2 * sets) + [hidden_spec, up_spec, down_spec],
            [act_out] * sets + [high_out] + [low_out] * (sets - 1) + [down_part] * 2 + [up_part] * 2
            + [(hidden_spec, shaped(1, hidden // 2, dtype=F32))],
            [low, low, high, pltpu.VMEM((blocks, sets * rows, width), BF16), low, low, weight, weight, dma,
             pltpu.SemaphoreType.DMA((blocks, sets)), pltpu.SemaphoreType.DMA((sets,)), pltpu.SemaphoreType.DMA((4,))],
            "mlp", 0, *tokens_of[0], *tokens_of[1], bup, far, far)

    if by_hand:
        cot_other = after(cot_other, mixed)
        n2_other = swap(n2, other_core)
        act_own, act_other, gtwo, gtwo_other, down_own, down_send, up_own, up_send, sum_up = run_mlp(
            me, ((n2, n2_other), (cot, cot_other)), bup)
        gtwo_take = swap(gtwo_other, other_core)
        parts = (-1, CHIPS // 4, 2)
        down_first = [piece.reshape(*parts, deep, width) for piece in (down_own, swap(down_send, first_plane))]
        up_first = [piece.reshape(*parts, each, width) for piece in (up_own, swap(up_send, first_plane))]
    else:
        runs = [run_mlp(me + half, ((n2,), (cot,)), bup[half]) for half in range(2)]
        (act_own, gtwo), (act_other, gtwo_take) = ((run[0], run[1]) for run in runs)
        gtwo_take = gtwo_take.astype(BF16)
        sum_up = jnp.concatenate([run[6] for run in runs], axis=1)
    grads_spec = pl.BlockSpec((4, tile, width), lambda i, *me: (0, i, 0))
    grads, gresid, sum_back = call(
        attention_backward, (tiles,),
        [SMEM, tile_rows, tile_rows, tile_rows, lse_spec, tile_rows, tile_rows, tile_rows, tile_rows, vec_spec, square],
        [(grads_spec, shaped(4, rows, width)), high_rows, sums], [pltpu.VMEM((tile, width), BF16)],
        "attention_backward", 0, lengths, q, k, v, lse, cot, resid, gtwo, gtwo_take, vec, wo)
    sum_spec = whole_spec((8, width))
    pair_shape = (CHIPS // 4, 4, 4 * each + 16, side)
    columns = pl.BlockSpec((1, rows, width), lambda i, me: (i, 0, 0))

    def run_weights(grads):
        return call_with(
            me, weight_grads, 4, [full_rows] * 2 + [columns, sum_spec, sum_spec, whole_spec((1, sum_up.shape[1]))],
            [(kept_spec(pair_shape), shaped(*pair_shape))] * 2, [], "weight_grads", 0,
            n1, mixed, grads, sum_back, sum_down, sum_up)

    def run_tokens(gresid):
        return call(
            tokens_backward, (tiles,), [tile_rows, tile_rows, vec_spec, grads_spec, square, square, square],
            [low_rows, sums], [], "tokens_backward", MIDDLE, tokens, gresid, vec, grads, wq, wk, wv)

    if by_hand:
        (out_other,) = call_with(
            me, mlp_out_other, tiles, [act_spec, wide_spec], [low_rows], [], "mlp_out_other", 0, after(act_other, grads), far)
        down_first, up_first = after((down_first, up_first), out_other)
        hidden_rest, hidden_take = scatter_second(*down_first, *up_first)

        def weights_of_chip(grads):
            square_send, square_keep = run_weights(grads)
            return merge_core_of(core, square_keep, scatter_core(square_send))

        square_own, square_send = fenced(weights_of_chip, after(grads, hidden_rest))
        square_take = swap(square_send, first_plane).reshape(square_own.shape)
        hidden_rest, hidden_take = after((hidden_rest, hidden_take), square_own)
        hidden_layers = scatter_layers(hidden_rest, hidden_take)
        gtok, late = run_tokens(after(gresid, hidden_layers[0]))
        square_take = after(square_take, late)
        late = late + swap(late, other_core)
        square_second = scatter_second(square_own, square_take)
        late = after(late, square_second[0])
        out_take = after(swap(out_other, other_core), square_second[0])
        (out,) = call_with(
            me, mlp_out_own, tiles, [tile_rows, vec_spec, act_spec, tile_rows, wide_spec], [low_rows], [],
            "mlp_out_own", 0, resid, vec, act_own, out_take, far)
        late = late + after(swap(late, other_layer(1)), out)
        hidden_layers = after(hidden_layers, late)
        g_down, up_keep, up_send = scatter_last(core, hidden_layers, own, blocks, deep)
        up_take = scatter_core(up_send)
        late = late + after(swap(late, other_layer(2)), g_down)
        square_second = after(square_second, g_down, late)
        square_layers = scatter_layers(*square_second)
        late = late + after(swap(late, other_plane(1)), square_layers[0])
        late = late + swap(late, other_plane(2))
        square_layers = after(square_layers, late)
        square_keep, square_send, flat = scatter_last(core, square_layers, own, 4, 0)
        square_take = scatter_core(square_send)
        outs = [(VMEM_SPEC, shaped(own, hidden, dtype=F32))] + [(VMEM_SPEC, shaped(own, width, dtype=F32))] * 4
        outs += [(VMEM_SPEC, shaped(own, dtype=F32))] * 8 + [(VMEM_SPEC, shaped(folds * own, dtype=F32))]
        g_up, g_q, g_k, g_v, g_o, *g_flat, g_ub = small_call(
            finish, (me, up_keep, up_take, square_keep, square_take, flat, late), outs, "finish",
            ins=[SMEM] + [VMEM_SPEC] * 6)
    else:
        square_send, square_keep = run_weights(grads)
        gtok, sum_one = run_tokens(gresid)
        flat = jnp.concatenate((sum_one[0:2], sum_back[0:5], sum_down[0:1]), axis=0)
        flat = flat.reshape(8, count, own).transpose(1, 0, 2).reshape(count, 8 * own)
        hidden_sums = sum_up.reshape(2, CHIPS, deep).transpose(1, 0, 2).reshape(count, folds * own)
        flat = jnp.concatenate((flat, hidden_sums), axis=1)
        g_down, g_up, g_q, g_k, g_v, g_o, flat = reduce_plain(
            [run[2:4] for run in runs], [run[4:6] for run in runs], (square_keep, square_send), flat)
        (out_other,) = call_with(
            me + 1, mlp_out_other, tiles, [act_spec, wide_spec], [low_rows], [], "mlp_out_other", 0, act_other, far)
        (out,) = call_with(
            me, mlp_out_own, tiles, [tile_rows, vec_spec, act_spec, tile_rows, wide_spec], [low_rows], [],
            "mlp_out_own", 0, resid, vec, act_own, out_other, far)
        g_flat = [flat[index * own : (index + 1) * own] for index in range(8)]
        g_ub = flat[8 * own :]
    g_gain, g_shift, g_qb, g_vb, g_ob, g_mg, g_ms, g_db = g_flat
    return (out, gtok, g_gain, g_shift, g_q, g_qb, g_k, g_v, g_vb, g_o, g_ob, g_mg, g_ms, g_up, g_ub, g_down, g_db)


def solution(mesh):
    rows, flat = P("dp", None), P("dp")
    return jax.shard_map(
        body,
        mesh=mesh,
        in_specs=(rows, rows, flat, flat, rows, flat, rows, rows, flat, rows, flat, flat, flat, rows, flat, rows, flat, rows),
        out_specs=(rows, rows, flat, flat, rows, flat, rows, rows, flat, rows, flat, flat, flat, rows, flat, rows, flat),
        check_vma=False,
    )
```

```python
import functools

import jax
import jax.numpy as jnp
from jax import lax
from jax.experimental import pallas as pl
from jax.experimental.pallas import tpu as pltpu
from jax.sharding import PartitionSpec as P

HEADS = 12
HEAD_DIM = 64
PAIRS = 6
LANES = 128
CHIPS = 16
MERGE_STEPS = 2
LONG = 10**11
SHORT = 6 * 10**9
MIDDLE = 115 * 10**8
EPS = 1e-06
MASKED = -1e30
SCALE = HEAD_DIM**-0.5
GELU_C = 0.7978845608028654
GELU_A = 0.044715
VMEM = 64 * 1024 * 1024 - 65536
F32 = jnp.float32
BF16 = jnp.bfloat16


def dot_nn(left, right):
    return lax.dot_general(left, right, (((1,), (0,)), ((), ())), preferred_element_type=F32)


def dot_nt(left, right):
    return lax.dot_general(left, right, (((1,), (1,)), ((), ())), preferred_element_type=F32)


def dot_tn(left, right):
    return lax.dot_general(left, right, (((0,), (0,)), ((), ())), preferred_element_type=F32)


def normalize(rows):
    centered = rows - jnp.mean(rows, axis=-1, keepdims=True)
    inverse = lax.rsqrt(jnp.mean(centered * centered, axis=-1, keepdims=True) + EPS)
    return centered * inverse, inverse


def norm_back(grads, gain, hat, inverse):
    scaled = grads * gain
    mean = jnp.mean(scaled, axis=-1, keepdims=True)
    mean_hat = jnp.mean(scaled * hat, axis=-1, keepdims=True)
    return inverse * (scaled - mean - hat * mean_hat)


def column_sum(rows):
    return jnp.sum(rows, axis=0, keepdims=True)


def segments(lengths_ref, tile, slots, rows, axis):
    shape = (rows, 1) if axis == 0 else (1, rows)
    index = lax.broadcasted_iota(jnp.int32, shape, axis)
    segment = jnp.zeros(shape, jnp.int32)
    bound = 0
    for slot in range(slots):
        bound = bound + lengths_ref[tile, slot]
        segment = segment + (index >= bound).astype(jnp.int32)
    return segment


def mask_bias(lengths_ref, tile, slots, rows):
    same = segments(lengths_ref, tile, slots, rows, 0) == segments(lengths_ref, tile, slots, rows, 1)
    return jnp.where(same, 0.0, MASKED).astype(F32)


def half_of(pair, side):
    lane = lax.broadcasted_iota(jnp.int32, pair.shape, 1)
    keep = lane < HEAD_DIM if side == 0 else lane >= HEAD_DIM
    return jnp.where(keep, pair, jnp.zeros_like(pair))


def fetch_weights(me, sources, weight_refs, parts_ref, sem):
    core, chip = me & 1, me >> 1
    side = sources[0].shape[2]
    each = weight_refs[0].shape[0] // CHIPS
    for index, source in enumerate(sources):
        half = core if index < 4 else 1 - core
        cols = pl.ds(pl.multiple_of(half * side, LANES), side)
        for layer in range(4):
            owner = chip ^ (4 * layer + (0, 1 + half, 2 - half, 3)[index % 4])
            rows = pl.ds(pl.multiple_of(owner * each, 16), each)
            for number, ref in enumerate(weight_refs):
                pltpu.make_async_copy(
                    source.at[layer, pl.ds(number * each, each), :], ref.at[rows, cols], sem.at[number]
                ).start()
            pltpu.make_async_copy(
                source.at[layer, pl.ds(4 * each, 16), :], parts_ref.at[2 * owner + half], sem.at[4]
            ).start()


def project(me_ref, x_ref, *refs):
    sources = refs[:8]
    n1_ref, q_ref, k_ref, v_ref = refs[8:12]
    wq_ref, wk_ref, wv_ref, wo_ref, vec_ref, bup_ref, parts_ref, sem = refs[12:]
    weights = (wq_ref, wk_ref, wv_ref, wo_ref)
    core = me_ref[0] & 1

    @pl.when(pl.program_id(0) == 0)
    def _():
        fetch_weights(me_ref[0], sources, weights, parts_ref, sem)
        for number, ref in enumerate(weights + (parts_ref,)):
            pltpu.make_async_copy(ref, ref, sem.at[number]).wait()
        count, _, side = parts_ref.shape
        group = count // 2
        halves = [sum(parts_ref[half * group + index].astype(F32) for index in range(group)) for half in range(2)]
        vec_ref[...] = jnp.concatenate(halves, axis=1)
        blocks = bup_ref.shape[1] // side
        group = CHIPS // blocks
        for block in range(blocks):
            rows = sum(parts_ref[2 * (block * group + index) + core].astype(F32) for index in range(group))
            bup_ref[:, block * side : (block + 1) * side] = rows[8:9]

    project_rows(x_ref, vec_ref, wq_ref, wk_ref, wv_ref, n1_ref, q_ref, k_ref, v_ref)


def project_rows(x_ref, vec_ref, wq_ref, wk_ref, wv_ref, n1_ref, q_ref, k_ref, v_ref):
    hat, _ = normalize(x_ref[...].astype(F32))
    n1 = (hat * vec_ref[0:1, :] + vec_ref[1:2, :]).astype(BF16)
    n1_ref[...] = n1
    q_ref[...] = (dot_nn(n1, wq_ref[...]) + vec_ref[2:3, :]).astype(BF16) * jnp.asarray(SCALE, BF16)
    k_ref[...] = dot_nn(n1, wk_ref[...]).astype(BF16)
    v_ref[...] = (dot_nn(n1, wv_ref[...]) + vec_ref[3:4, :]).astype(BF16)


def mask_grads(lengths_ref, grad_ref, cot_ref, dsum_ref):
    tile = pl.program_id(0)
    slots = lengths_ref.shape[1]
    valid = segments(lengths_ref, tile, slots, grad_ref.shape[0], 0) < slots
    cot = jnp.where(valid, grad_ref[...].astype(F32), 0.0)
    cot_ref[...] = cot.astype(BF16)

    @pl.when(tile == 0)
    def _():
        dsum_ref[...] = jnp.zeros_like(dsum_ref)

    dsum_ref[0:1, :] += column_sum(cot)


def attention_forward(lengths_ref, x_ref, vec_ref, q_ref, k_ref, v_ref, wo_ref, mixed_ref, lse_ref, resid_ref, n2_ref):
    tile = pl.program_id(0)
    rows = q_ref.shape[0]
    slots = lengths_ref.shape[1]
    bias = mask_bias(lengths_ref, tile, slots, rows)
    lane = lax.broadcasted_iota(jnp.int32, (rows, LANES), 1)
    lse = jnp.zeros((rows, LANES), F32)

    def at(pair):
        return pl.ds(pair * LANES, LANES)

    def scores_of(pair):
        qp, kp = q_ref[:, at(pair)], k_ref[:, at(pair)]
        return [dot_nt(half_of(qp, side), kp) for side in range(2)]

    def softmax_of(scores):
        scores = scores + bias
        top = jnp.max(scores, axis=-1, keepdims=True)
        weights = jnp.exp(scores - top)
        sums = jnp.sum(weights, axis=-1, keepdims=True)
        return (weights * (1.0 / sums)).astype(BF16), top + jnp.log(sums)

    raw = {}
    probs = {}
    for turn in range(PAIRS + 2):
        if turn < PAIRS:
            raw[turn] = scores_of(turn)
        if 0 <= turn - 1 < PAIRS:
            both = [softmax_of(scores) for scores in raw.pop(turn - 1)]
            for side in range(2):
                lse = jnp.where(lane == 2 * (turn - 1) + side, both[side][1], lse)
            probs[turn - 1] = [pair[0] for pair in both]
        if turn >= 2:
            vp = v_ref[:, at(turn - 2)]
            parts = [dot_nn(probs[turn - 2][side], half_of(vp, side)) for side in range(2)]
            mixed_ref[:, at(turn - 2)] = (parts[0] + parts[1]).astype(BF16)
    lse_ref[...] = lse
    resid = x_ref[...].astype(F32) + (dot_nn(mixed_ref[...], wo_ref[...]) + vec_ref[4:5, :])
    resid_ref[...] = resid
    hat, _ = normalize(resid)
    n2_ref[...] = (hat * vec_ref[5:6, :] + vec_ref[6:7, :]).astype(BF16)


def spread(me, rows, put):
    layer, plane = me >> 3, (me >> 1) & 3
    each = rows.shape[0] // CHIPS
    for chip in range(CHIPS):
        put((chip & 3) ^ plane, (chip >> 2) ^ layer, rows[chip * each : (chip + 1) * each].astype(BF16))


def fetch_hidden(me, sources, wup_ref, wdown_ref, sem):
    if len(sources) == 2:
        for number in range(wup_ref.shape[0]):
            pltpu.make_async_copy(sources[0].at[number], wup_ref.at[number], sem.at[number]).start()
        pltpu.make_async_copy(sources[1], wdown_ref, sem.at[wup_ref.shape[0]]).start()
        return
    core, chip = me & 1, me >> 1
    planes = (0, 1 + core, 2 - core, 3)
    blocks, width = wup_ref.shape[:2]
    each, deep = width // CHIPS, wdown_ref.shape[0] // CHIPS
    for layer in range(4):
        for index, plane in enumerate(planes):
            owner = chip ^ (4 * layer + plane)
            rows = pl.ds(pl.multiple_of(owner * each, 16), each)
            side = sources[index].shape[2]
            for part in range(sources[index].shape[1] // each):
                number, cols = part * side // width, pl.ds(part * side % width, side)
                pltpu.make_async_copy(
                    sources[index].at[layer, pl.ds(part * each, each), :], wup_ref.at[number, rows, cols], sem.at[number]
                ).start()
            rows = pl.ds(pl.multiple_of(owner * deep, 16), deep)
            source = sources[4 + layer // 2].at[2 * index + layer % 2]
            pltpu.make_async_copy(source, wdown_ref.at[rows, :], sem.at[blocks]).start()


def mlp(sets, count, me_ref, *refs):
    n2_hbm, cot_hbm = refs[:sets], refs[sets : 2 * sets]
    bup_ref = refs[2 * sets]
    sources = refs[2 * sets + 1 : 2 * sets + 1 + count]
    refs = refs[2 * sets + 1 + count :]
    act_hbm, gtwo_hbm, refs = refs[:sets], refs[sets : 2 * sets], refs[2 * sets :]
    down_own, down_send, up_own, up_send, wdown_hbm, dbu_ref = refs[:6]
    n2_ref, cot_ref, gacc, act_ref, gup_ref, low_ref, gdown_ref, gupw_ref = refs[6:14]
    wup_all, wdown_all, in_sem, act_sem, out_sem, grad_sem, weight_sem = refs[14:]
    step = pl.program_id(0)
    last = pl.num_programs(0) - 1
    me = me_ref[0]
    rows = n2_ref.shape[0] // sets

    def rows_of(index):
        return pl.ds(pl.multiple_of(index * rows, rows), rows)

    blocks, width = wup_all.shape[:2]

    @pl.when(step == 0)
    def _():
        fetch_hidden(me, sources, wup_all, wdown_all, weight_sem)
        for index in range(sets):
            at = pl.ds(index * rows, rows)
            pltpu.make_async_copy(n2_hbm[index], n2_ref.at[at, :], in_sem.at[0, index]).start()
            pltpu.make_async_copy(cot_hbm[index], cot_ref.at[at, :], in_sem.at[1, index]).start()

    pltpu.make_async_copy(wup_all.at[step], wup_all.at[step], weight_sem.at[step]).wait()
    write_down = pltpu.make_async_copy(wdown_all, wdown_hbm, weight_sem.at[blocks])

    @pl.when(step == 0)
    def _():
        pltpu.make_async_copy(wdown_all, wdown_all, weight_sem.at[blocks]).wait()
        write_down.start()

    wup = wup_all[step]
    wdown = wdown_all[pl.ds(pl.multiple_of(step * width, width), width), :]
    dbu_ref[...] = jnp.zeros_like(dbu_ref)
    slot = lax.rem(step, 2)

    @pl.loop(0, sets)
    def _(index):
        at = rows_of(index)

        @pl.when(step == 0)
        def _():
            pltpu.make_async_copy(n2_ref.at[at, :], n2_ref.at[at, :], in_sem.at[0, index]).wait()
            pltpu.make_async_copy(cot_ref.at[at, :], cot_ref.at[at, :], in_sem.at[1, index]).wait()

        pre = dot_nn(n2_ref[at, :], wup) + bup_ref[...]
        grad_act = dot_nt(cot_ref[at, :], wdown)
        square = pre * pre
        tanh = jnp.tanh(pre * (GELU_C + (GELU_C * GELU_A) * square))
        half = 0.5 + 0.5 * tanh
        inner = GELU_C + (3.0 * GELU_C * GELU_A) * square
        act_ref[slot, at, :] = (pre * half).astype(BF16)
        gup = (grad_act * (half + (0.5 * pre) * (1.0 - tanh * tanh) * inner)).astype(BF16)
        gup_ref[at, :] = gup
        dbu_ref[...] += column_sum(gup.astype(F32))

    @pl.when(step == 0)
    def _():
        @pl.loop(0, sets)
        def _(index):
            at = rows_of(index)
            gacc[at, :] = dot_nt(gup_ref[at, :], wup)

    @pl.when((step > 0) & (step < last))
    def _():
        @pl.loop(0, sets)
        def _(index):
            at = rows_of(index)
            gacc[at, :] += dot_nt(gup_ref[at, :], wup)

    def results():
        for index in range(sets):
            at = pl.ds(index * rows, rows)
            source = low_ref.at[at, :] if index else gacc.at[at, :]
            yield pltpu.make_async_copy(source, gtwo_hbm[index], out_sem.at[index])

    def activations(number):
        for index in range(sets):
            source = act_ref.at[number, pl.ds(index * rows, rows), :]
            cols = pl.ds(number * width, width)
            yield pltpu.make_async_copy(source, act_hbm[index].at[:, cols], act_sem.at[number, index])

    for number in range(act_ref.shape[0]):

        @pl.when(step == number)
        def _():
            for copy in activations(number):
                copy.start()

    @pl.when(step == last)
    def _():
        @pl.loop(0, sets)
        def _(index):
            at = rows_of(index)
            total = gacc[at, :] + dot_nt(gup_ref[at, :], wup)
            gacc[at, :] = total
            low_ref[at, :] = total.astype(BF16)

        for copy in results():
            copy.start()

    gdown_ref[slot] = dot_tn(act_ref[slot], cot_ref[...]).astype(BF16)
    deep = down_own.shape[2]
    count = gdown_ref.shape[1] // deep
    for index in range(count):
        chip = step * count + index
        source = gdown_ref.at[slot, pl.ds(index * deep, deep), :]
        keep_or_send(me, chip & 3, (chip >> 2) ^ (me >> 3), source, down_own, down_send, grad_sem, 0)

    gupw_ref[slot] = dot_tn(n2_ref[...], gup_ref[...]).astype(BF16)
    each = gupw_ref.shape[1] // CHIPS
    for chip in range(CHIPS):
        source = gupw_ref.at[slot, pl.ds(chip * each, each), :]
        keep_or_send(
            me, chip & 3, (chip >> 2) ^ (me >> 3), source, up_own.at[step], up_send.at[step], grad_sem, 2)

    @pl.when(step == last)
    def _():
        for copy in results():
            copy.wait()
        write_down.wait()
        for number in range(act_ref.shape[0]):
            for copy in activations(number):
                copy.wait()
        for number, ref in enumerate((down_own, down_send, up_own, up_send)):
            pltpu.make_async_copy(ref, ref, grad_sem.at[number]).wait()


def keep_or_send(me, plane, layer, source, own_ref, send_ref, sem, number):
    core = me & 1
    relative = plane ^ ((me >> 1) & 3)
    mine = (relative == 0) | (relative == 2 - core)

    @pl.when(mine)
    def _():
        pltpu.make_async_copy(source, own_ref.at[layer, jnp.where(relative == 0, 0, 1)], sem.at[number]).start()

    @pl.when(jnp.logical_not(mine))
    def _():
        pltpu.make_async_copy(source, send_ref.at[layer, jnp.where(relative == 3, 1, 0)], sem.at[number + 1]).start()


def mlp_out_other(me_ref, act_ref, wdown_ref, out_ref):
    out_ref[...] = dot_nn(act_ref[...], wdown_ref[...]).astype(BF16)


def mlp_out_own(me_ref, resid_ref, vec_ref, act_ref, take_ref, wdown_ref, out_ref):
    half = dot_nn(act_ref[...], wdown_ref[...]) + take_ref[...].astype(F32)
    out_ref[...] = (resid_ref[...] + (half + vec_ref[7:8, :])).astype(BF16)


def attention_backward(lengths_ref, q_ref, k_ref, v_ref, lse_ref, cot_ref, resid_ref, gtwo_ref, gother_ref, vec_ref, wo_ref,
                       grads_ref, gresid_ref, dsum_ref, gmix_ref):
    tile = pl.program_id(0)
    rows = q_ref.shape[0]

    @pl.when(tile == 0)
    def _():
        dsum_ref[...] = jnp.zeros_like(dsum_ref)

    hat, inverse = normalize(resid_ref[...])
    grad_two = gtwo_ref[...] + gother_ref[...].astype(F32)
    gresid = cot_ref[...].astype(F32) + norm_back(grad_two, vec_ref[5:6, :], hat, inverse)
    gresid_ref[...] = gresid
    gattn = gresid.astype(BF16)
    grads_ref[3] = gattn
    dsum_ref[2:3, :] += column_sum(gattn.astype(F32))
    dsum_ref[3:4, :] += column_sum(grad_two * hat)
    dsum_ref[4:5, :] += column_sum(grad_two)
    gmix_ref[...] = dot_nt(gattn, wo_ref[...]).astype(BF16)
    bias = mask_bias(lengths_ref, tile, lengths_ref.shape[1], rows)

    def load(pair):
        cols = pl.ds(pair * LANES, LANES)
        return q_ref[:, cols], k_ref[:, cols], v_ref[:, cols], gmix_ref[:, cols]

    def products_of(pair):
        qp, kp, vp, gp = load(pair)
        return [(dot_nt(half_of(qp, side), kp), dot_nt(half_of(gp, side), vp)) for side in range(2)]

    def softmax_back(pair, products):
        results = []
        for side, (scores, grad_probs) in enumerate(products):
            head = 2 * pair + side
            probs = jnp.exp(scores + bias - lse_ref[:, head : head + 1])
            weighted = probs * grad_probs
            dot = jnp.sum(weighted, axis=-1, keepdims=True)
            results.append((probs.astype(BF16), (weighted - probs * dot).astype(BF16)))
        return results

    def store(pair, results):
        qp, kp, vp, gp = load(pair)
        dq = sum(dot_nn(results[side][1], half_of(kp, side)) for side in range(2))
        dk = sum(dot_tn(results[side][1], half_of(qp, side)) for side in range(2))
        dv = sum(dot_tn(results[side][0], half_of(gp, side)) for side in range(2))
        cols = pl.ds(pair * LANES, LANES)
        grads_ref[0, :, cols] = (dq * SCALE).astype(BF16)
        grads_ref[1, :, cols] = dk.astype(BF16)
        grads_ref[2, :, cols] = dv.astype(BF16)

    raw = {}
    done = {}
    for turn in range(PAIRS + 2):
        if turn < PAIRS:
            raw[turn] = products_of(turn)
        if 0 <= turn - 1 < PAIRS:
            done[turn - 1] = softmax_back(turn - 1, raw.pop(turn - 1))
        if turn >= 2:
            store(turn - 2, done.pop(turn - 2))

    dsum_ref[0:1, :] += column_sum(grads_ref[0].astype(F32))
    dsum_ref[1:2, :] += column_sum(grads_ref[2].astype(F32))


def weight_grads(me_ref, n1_ref, mixed_ref, columns_ref, sum_back_ref, sum_down_ref, sum_up_ref, send_ref, keep_ref):
    step = pl.program_id(0)
    me = me_ref[0]
    first = (me & 1) == 0
    side = send_ref.shape[3]
    each = n1_ref.shape[1] // CHIPS

    def run(left, number):
        result = dot_tn(left, columns_ref[0])
        low, high = result[:, :side], result[:, side:]
        rows_at = pl.ds(pl.multiple_of(number * each, 16), each)

        def put_send(plane, layer, rows):
            send_ref[layer, plane, rows_at, :] = rows

        def put_keep(plane, layer, rows):
            keep_ref[layer, plane, rows_at, :] = rows

        spread(me, jnp.where(first, high, low), put_send)
        spread(me, jnp.where(first, low, high), put_keep)

    @pl.when(step < 3)
    def _():
        run(n1_ref[...], step)

    @pl.when(step == 3)
    def _():
        run(mixed_ref[...], 3)
        nothing = jnp.zeros((2, n1_ref.shape[1]), F32)
        vecs = jnp.concatenate((nothing, sum_back_ref[0:5], sum_down_ref[0:1]), axis=0)
        for chip in range(CHIPS):
            half = chip // (CHIPS // 2)
            block = chip * (sum_up_ref.shape[1] // side) // CHIPS
            last = jnp.broadcast_to(sum_up_ref[:, block * side : (block + 1) * side], (8, side))
            short = vecs[:, half * side : (half + 1) * side]
            at = ((chip >> 2) ^ (me >> 3), (chip & 3) ^ ((me >> 1) & 3))
            keep_ref[at[0], at[1], 4 * each :, :] = jnp.concatenate((short, last), axis=0).astype(BF16)
            send_ref[at[0], at[1], 4 * each :, :] = jnp.concatenate((short, jnp.zeros_like(last)), axis=0).astype(BF16)


def tokens_backward(x_ref, gresid_ref, vec_ref, grads_ref, wq_ref, wk_ref, wv_ref, gtok_ref, dsum_ref):
    @pl.when(pl.program_id(0) == 0)
    def _():
        dsum_ref[...] = jnp.zeros_like(dsum_ref)

    grad_one = dot_nt(grads_ref[0], wq_ref[...]) + dot_nt(grads_ref[1], wk_ref[...]) + dot_nt(grads_ref[2], wv_ref[...])
    hat, inverse = normalize(x_ref[...].astype(F32))
    gtok_ref[...] = (gresid_ref[...] + norm_back(grad_one, vec_ref[0:1, :], hat, inverse)).astype(BF16)
    dsum_ref[0:1, :] += column_sum(grad_one * hat)
    dsum_ref[1:2, :] += column_sum(grad_one)


def rows_spec(block, width):
    return pl.BlockSpec((block, width), lambda i, *me: (i, 0))


def cols_spec(height, block):
    return pl.BlockSpec((height, block), lambda i, *me: (0, i))


def whole_spec(shape):
    return pl.BlockSpec(shape, lambda *i: (0,) * len(shape), pipeline_mode=pl.Buffered(1))


def kept_spec(shape):
    return pl.BlockSpec(shape, lambda *i: (0,) * len(shape))


SMEM = pl.BlockSpec(memory_space=pltpu.SMEM)


def cost(flops):
    return pl.CostEstimate(flops=flops, bytes_accessed=1, transcendentals=0)


def call(kernel, grid, ins, outs, scratch, name, flops, *args):
    out_specs = tuple(spec for spec, _ in outs)
    out_shape = tuple(shape for _, shape in outs)
    return pl.pallas_call(
        kernel,
        grid=grid,
        in_specs=ins,
        out_specs=out_specs,
        out_shape=out_shape,
        scratch_shapes=scratch,
        compiler_params=pltpu.CompilerParams(vmem_limit_bytes=VMEM, dimension_semantics=("arbitrary",) * len(grid)),
        cost_estimate=cost(flops),
        name=name,
    )(*args)


def call_with(me, kernel, steps, ins, outs, scratch, name, flops, *args):
    out_shape = tuple(shape for _, shape in outs)
    return pl.pallas_call(
        kernel,
        grid_spec=pltpu.PrefetchScalarGridSpec(
            num_scalar_prefetch=1, grid=(steps,), in_specs=ins, out_specs=tuple(spec for spec, _ in outs),
            scratch_shapes=scratch),
        out_shape=out_shape,
        compiler_params=pltpu.CompilerParams(vmem_limit_bytes=VMEM, dimension_semantics=("arbitrary",)),
        cost_estimate=cost(0),
        name=name,
    )(me, *args)


def shaped(*shape, dtype=BF16):
    return jax.ShapeDtypeStruct(shape, dtype)


def flipped(count, change):
    pairs = []
    for source in range(count):
        core, chip = source & 1, source >> 1
        core, chip = change(core, chip)
        pairs.append((source, 2 * chip + core))
    return pairs


def swap(array, change):
    return lax.ppermute(array, "dp", flipped(lax.axis_size("dp"), change))


def other_core(core, chip):
    return core ^ 1, chip


def first_plane(core, chip):
    return core, chip ^ (1 + core)


def second_plane(core, chip):
    return core, chip ^ (2 - core)


def other_plane(distance):
    return lambda core, chip: (core, chip ^ distance)


def other_layer(distance):
    return lambda core, chip: (core, chip ^ (4 * distance))


def split_shards(core_ref, q_ref, k_ref, v_ref, o_ref, u_ref, keep_ref, send_ref):
    width = q_ref.shape[1]
    side = width // 2
    first = core_ref[0] == 0

    def put(index, low, high):
        keep_ref[index] = jnp.where(first, low, high).astype(BF16)
        send_ref[index] = jnp.where(first, high, low).astype(BF16)

    for index, ref in enumerate((q_ref, k_ref, v_ref, o_ref)):
        rows = ref[...].astype(F32)
        put(index, rows[:, :side], rows[:, side:])
    up = u_ref[...].astype(F32)
    hidden = up.shape[1]
    deep = hidden // (2 * CHIPS)
    halves = [
        jnp.concatenate([up[:, start : start + deep] for start in range(half * deep, hidden, 2 * deep)], axis=1)
        for half in range(2)
    ]
    for part in range(hidden // width):
        at = slice(part * side, (part + 1) * side)
        put(4 + part, halves[0][:, at], halves[1][:, at])


def join_shards(me_ref, keep_ref, take_ref, *refs):
    vectors, near_ref = refs[:-1], refs[-1]
    me = me_ref[0]
    first = (me & 1) == 0
    parts, own, side = keep_ref.shape
    folds = parts - 4
    keep = keep_ref[...].astype(F32)
    take = take_ref[...].astype(F32)

    def joined(index):
        low = jnp.where(first, keep[index], take[index])
        high = jnp.where(first, take[index], keep[index])
        return jnp.concatenate((low, high), axis=0).astype(BF16)

    for index in range(4):
        near_ref[2 * own * index : 2 * own * (index + 1), :] = joined(index)
    base = 8 * own + 16
    for index in range(folds):
        near_ref[base + 2 * own * index : base + 2 * own * (index + 1), :] = joined(4 + index)
    rows = []
    for ref in vectors:
        flat = ref[...].astype(F32).reshape(1, -1)
        rows.append(jnp.concatenate((flat, jnp.zeros((1, side - flat.shape[1]), F32)), axis=1))
    rows.append(jnp.zeros((16 - len(rows), side), F32))
    rows = jnp.concatenate(rows, axis=0)
    short = pltpu.roll(rows, own * lax.rem(me, side // own), 1)
    long = pltpu.roll(rows, folds * own * lax.rem(me >> 1, side // (folds * own)), 1)
    index = lax.broadcasted_iota(jnp.int32, rows.shape, 0)
    near_ref[8 * own : base, :] = jnp.where(index < 8, short, long).astype(BF16)


def across_layers(shard):
    return jnp.stack([shard] + [swap(shard, other_layer(distance)) for distance in (1, 2, 3)])


def after(arrays, *others):
    return lax.optimization_barrier((arrays, others))[0]


def small_call(kernel, args, outs, name, scratch=(), ins=None, flops=0):
    return pl.pallas_call(
        kernel,
        in_specs=ins,
        out_specs=tuple(spec for spec, _ in outs),
        out_shape=tuple(shape for _, shape in outs),
        scratch_shapes=list(scratch),
        compiler_params=pltpu.CompilerParams(vmem_limit_bytes=VMEM),
        cost_estimate=cost(flops),
        name=name,
    )(*args)


VMEM_SPEC = pl.BlockSpec(memory_space=pltpu.VMEM)
ANY_SPEC = pl.BlockSpec(memory_space=pl.ANY)


def prepare(me, weights, vectors):
    own, width = weights[0].shape
    side = width // 2
    deep = weights[5].shape[0]
    folds = deep // own
    halves = (VMEM_SPEC, shaped(4 + folds, own, side))
    keep, send = small_call(
        split_shards, (me & 1, *weights[:5]), [halves, halves], "split_shards", ins=[SMEM] + [VMEM_SPEC] * 5)
    take = swap(send, other_core)
    return small_call(
        join_shards, (me, keep, take, *vectors), [(VMEM_SPEC, shaped(8 * own + 16 + 2 * deep, side))], "join_shards",
        ins=[SMEM] + [VMEM_SPEC] * (2 + len(vectors)))[0]


def doubled(pieces, change):
    return jnp.concatenate((pieces, swap(pieces, change)))


def gather_down(pieces):
    return doubled(doubled(pieces, first_plane), second_plane)


def gather_plain(weights, vectors):
    squares, up_weight, down_weight = weights[:4], weights[4], weights[5]
    count = lax.axis_size("dp")
    own, width = squares[0].shape
    folds = down_weight.shape[0] // own
    hidden = up_weight.shape[1]
    flat = jnp.concatenate(vectors)
    packed = jnp.concatenate(
        (
            *squares,
            up_weight.reshape(own, folds, width).transpose(1, 0, 2).reshape(own * folds, width),
            down_weight,
            jnp.pad(flat.reshape(1, -1), ((0, 7), (0, width - flat.size))),
        ),
        axis=0,
    )
    whole = lax.all_gather(packed, "dp", axis=0, tiled=True).reshape(count, -1, width)
    square_all = [whole[:, index * own : (index + 1) * own, :].reshape(width, width) for index in range(4)]
    wup = whole[:, 4 * own : (4 + folds) * own, :].reshape(count, folds, own, width).transpose(0, 2, 1, 3)
    wup = wup.reshape(width, 2, CHIPS // 2, 2, -1).transpose(3, 1, 0, 2, 4).reshape(2, 2, width, width)
    wdown = whole[:, (4 + folds) * own : (4 + 2 * folds) * own, :]
    wdown = wdown.reshape(CHIPS, 2, -1, width).transpose(1, 0, 2, 3).reshape(2, hidden // 2, width)
    last = whole[:, (4 + 2 * folds) * own, : flat.size].astype(F32)
    vec = last[:, : 8 * own].reshape(count, 8, own).transpose(1, 0, 2).reshape(8, width)
    bup = last[:, 8 * own :].reshape(CHIPS, 2, -1).transpose(1, 0, 2).reshape(2, 1, -1)
    return (*square_all, (wup, wdown), jnp.pad(vec, ((0, 8), (0, 0))), bup)


def merge_core(core_ref, keep_ref, take_ref, own_ref, send_ref):
    core = core_ref[0]

    def whole(plane):
        return (keep_ref[:, plane].astype(F32) + take_ref[:, plane].astype(F32)).astype(BF16)

    own_ref[:, 0] = whole(0)
    own_ref[:, 1] = whole(2 - core)
    send_ref[:, 0] = whole(1 + core)
    send_ref[:, 1] = whole(3)


def merge_first(*refs):
    pairs, rest_ref, send_ref = refs[:-2], refs[-2], refs[-1]
    base = 0
    for own_ref, take_ref in zip(pairs[::2], pairs[1::2]):
        for part in range(own_ref.shape[0]):
            at = slice(base, base + own_ref.shape[3])
            rest_ref[:, at, :] = own_ref[part, :, 0].astype(F32) + take_ref[part, :, 0].astype(F32)
            send_ref[:, at, :] = (own_ref[part, :, 1].astype(F32) + take_ref[part, :, 1].astype(F32)).astype(BF16)
            base += own_ref.shape[3]


def merge_second(own_ref, take_ref, rest_ref, *send_refs):
    for layer in range(4):
        whole = own_ref[layer] + take_ref[layer].astype(F32)
        if layer == 0:
            rest_ref[...] = whole
        else:
            send_refs[layer - 1][...] = whole.astype(BF16)


def merge_last(deep, core_ref, rest_ref, a_ref, b_ref, c_ref, *refs):
    whole = rest_ref[...] + a_ref[...].astype(F32) + b_ref[...].astype(F32) + c_ref[...].astype(F32)
    first = core_ref[0] == 0
    if deep:
        refs[0][...] = whole[:deep]
        refs = refs[1:]
    keep_ref, send_ref = refs[:2]
    parts, own, _ = keep_ref.shape
    for part in range(parts):
        low = whole[deep + 2 * own * part : deep + 2 * own * part + own]
        high = whole[deep + 2 * own * part + own : deep + 2 * own * (part + 1)]
        keep_ref[part] = jnp.where(first, low, high)
        send_ref[part] = jnp.where(first, high, low)
    if not deep:
        refs[2][...] = whole[2 * own * parts :]


def finish(me_ref, up_keep_ref, up_take_ref, keep_ref, take_ref, flat_ref, late_ref, up_ref, *refs):
    me = me_ref[0]
    first = (me & 1) == 0
    side = keep_ref.shape[2]
    width = 2 * side
    squares, flats = refs[:4], refs[4:]
    own = up_ref.shape[0]
    for number, ref in enumerate(squares):
        keep, take = keep_ref[number], take_ref[number]
        ref[:, :side] = jnp.where(first, keep, take)
        ref[:, side:] = jnp.where(first, take, keep)
    parts = up_keep_ref.shape[0]
    deep = parts * width // CHIPS
    for part in range(parts):
        keep, take = up_keep_ref[part], up_take_ref[part]
        low, high = jnp.where(first, keep, take), jnp.where(first, take, keep)
        pieces = []
        for start in range(0, width, deep):
            pieces += [low[:, start : start + deep], high[:, start : start + deep]]
        up_ref[:, 2 * width * part : 2 * width * (part + 1)] = jnp.concatenate(pieces, axis=1)
    late = jnp.where(me < side // own, late_ref[0:2, :side], late_ref[0:2, side:])
    flat = jnp.concatenate((late, flat_ref[2:]), axis=0)
    long = flats[-1].shape[0]
    short_turn = lax.rem(side - own * lax.rem(me, side // own), side)
    long_turn = lax.rem(side - long * lax.rem(me >> 1, side // long), side)
    short = pltpu.roll(flat, short_turn, 1)
    for number, ref in enumerate(flats[:-1]):
        ref[...] = short[number, :own]
    flats[-1][...] = pltpu.roll(flat, long_turn, 1)[8, :long]


def fenced(function, *args):
    kinds = jax.eval_shape(function, *args)

    def nothing(*_):
        return jax.tree.map(lambda kind: jnp.zeros(kind.shape, kind.dtype), kinds)

    return lax.cond(lax.axis_index("dp") < lax.axis_size("dp"), function, nothing, *args)


def scatter_core(send):
    return swap(send, other_core)


def merge_core_of(core, keep, take):
    shape = keep.shape
    planes, rows, side = shape[-3:]
    keep, take = keep.reshape(-1, planes, rows, side), take.reshape(-1, planes, rows, side)
    count = keep.shape[0]
    steps = MERGE_STEPS
    block = pl.BlockSpec((count // steps, planes, rows, side), lambda i: (i, 0, 0, 0))
    half = (pl.BlockSpec((count // steps, 2, rows, side), lambda i: (i, 0, 0, 0)), shaped(count, 2, rows, side))
    own, send = call(merge_core, (steps,), [SMEM, block, block], [half, half], [], "merge_core", 0, core, keep, take)
    return own.reshape(-1, CHIPS // 4, 2, rows, side), send


def scatter_second(*pairs):
    _, count, _, _, side = pairs[0].shape
    rows = sum(piece.shape[0] * piece.shape[3] for piece in pairs[::2])
    steps = MERGE_STEPS
    ins = [pl.BlockSpec((piece.shape[0], count // steps, *piece.shape[2:]), lambda i: (0, i, 0, 0, 0)) for piece in pairs]
    out = pl.BlockSpec((count // steps, rows, side), lambda i: (i, 0, 0))
    rest, send = call(
        merge_first, (steps,), ins, [(out, shaped(count, rows, side, dtype=F32)), (out, shaped(count, rows, side))], [],
        "merge_first", 0, *pairs)
    return rest, swap(send, second_plane)


def scatter_layers(own, take):
    _, rows, side = own.shape
    out = shaped(rows, side)
    rest, *sends = small_call(
        merge_second, (own, take), [(VMEM_SPEC, shaped(rows, side, dtype=F32))] + [(VMEM_SPEC, out)] * 3,
        "merge_second", ins=[VMEM_SPEC] * 2)
    return [rest] + [swap(piece, other_layer(r + 1)) for r, piece in enumerate(sends)]


def scatter_last(core, pieces, own, parts, deep):
    rows, side = pieces[0].shape
    outs = [(VMEM_SPEC, shaped(parts, own, side, dtype=F32))] * 2
    if deep:
        outs = [(VMEM_SPEC, shaped(deep, side, dtype=F32))] + outs
    else:
        outs.append((VMEM_SPEC, shaped(rows - 2 * own * parts, side, dtype=F32)))
    return small_call(
        functools.partial(merge_last, deep), (core, *pieces), outs, "merge_last", ins=[SMEM] + [VMEM_SPEC] * 4, flops=SHORT if deep else 0)


def reduce_plain(down_pairs, up_pairs, square_pair, flat):
    def scattered(array, axis):
        return lax.psum_scatter(array, "dp", scatter_dimension=axis, tiled=True).astype(F32)

    def planes(own, send, core):
        order = (own[..., 0, :, :], send[..., 0, :, :], own[..., 1, :, :], send[..., 1, :, :])
        if core == 1:
            order = (order[0], order[2], order[1], order[3])
        return jnp.stack(order, axis=-3)

    down = jnp.stack([planes(*pair, core) for core, pair in enumerate(down_pairs)])
    up = jnp.stack([planes(*pair, core) for core, pair in enumerate(up_pairs)])
    width = down.shape[-1]
    each = up.shape[4]
    down = down.transpose(1, 2, 0, 3, 4).reshape(-1, width)
    up = up.reshape(2, 2, CHIPS, each, CHIPS // 2, -1).transpose(2, 3, 1, 4, 0, 5).reshape(CHIPS * each, -1)
    square = jnp.stack(square_pair).transpose(1, 2, 3, 0, 4)[:, :, : 4 * each]
    square = square.reshape(CHIPS, 4, each, width).transpose(1, 0, 2, 3).reshape(4, CHIPS * each, width)
    return (
        scattered(down, 0),
        scattered(up, 0),
        *scattered(square, 1),
        lax.psum_scatter(flat, "dp", scatter_dimension=0, tiled=True).reshape(-1),
    )


def body(tokens, lengths, attn_gain, attn_shift, query_weight, query_bias, key_weight, value_weight, value_bias,
         out_weight, out_bias, mlp_gain, mlp_shift, up_weight, up_bias, down_weight, down_bias, grad_out):
    count = lax.axis_size("dp")
    rows, width = tokens.shape
    tiles = lengths.shape[0]
    tile = rows // tiles
    hidden = up_bias.shape[0] * count
    own = width // count
    folds = hidden // width
    vectors = (attn_gain, attn_shift, query_bias, value_bias, out_bias, mlp_gain, mlp_shift, down_bias, up_bias)
    by_hand = count == 2 * CHIPS
    me = lax.axis_index("dp").astype(jnp.int32).reshape(1) if by_hand else jnp.zeros((1,), jnp.int32)
    core = me & 1
    weights = (query_weight, key_weight, value_weight, out_weight, up_weight, down_weight)

    tile_rows = rows_spec(tile, width)
    square = whole_spec((width, width))
    vec_spec = whole_spec((16, width))
    sums = (kept_spec((8, width)), shaped(8, width, dtype=F32))
    low_rows = (tile_rows, shaped(rows, width))
    lse_spec = rows_spec(tile, LANES)
    mac = 2 * rows * width * width
    kept_square = (kept_spec((width, width)), shaped(width, width))
    kept_vec = (kept_spec((16, width)), shaped(16, width, dtype=F32))
    kept_hidden = (kept_spec((1, hidden // 2)), shaped(1, hidden // 2, dtype=F32))
    side = width // 2

    def masked(*earlier):
        return call(
            mask_grads, (tiles,), [SMEM, tile_rows], [low_rows, sums], [], "mask_grads", 0,
            lengths, after(grad_out, *earlier))

    high_rows = (tile_rows, shaped(rows, width, dtype=F32))

    def attend(q, k, v, vec, wo):
        return call(
            attention_forward, (tiles,), [SMEM, tile_rows, vec_spec, tile_rows, tile_rows, tile_rows, square],
            [low_rows, (lse_spec, shaped(rows, LANES, dtype=F32)), high_rows, low_rows],
            [], "attention_forward", 0, lengths, tokens, vec, q, k, v, wo)

    def gather_near(near):
        cot, sum_down = masked(near)
        cot_other = swap(cot, other_core)
        along = after(swap(near, first_plane), cot)
        across = [swap(near, second_plane), swap(along, second_plane)]
        along, across[0] = after((along, across[0]), *across[:1])
        taken = [swap(near, other_core), swap(along, other_core)]
        across = after(across, taken)
        taken += [swap(piece, other_core) for piece in across]
        return [along, *across, *taken], cot, cot_other, sum_down

    def attend_by_hand(near, up_four):
        up_along = swap(up_four, first_plane)
        n1, q, k, v, wq, wk, wv, wo, vec, bup = call_with(
            me, project, tiles, [tile_rows] + [ANY_SPEC] * 8, [low_rows] * 4 + [kept_square] * 4 + [kept_vec, kept_hidden],
            [pltpu.VMEM((count, 16, side), BF16), pltpu.SemaphoreType.DMA((5,))], "project", 0, tokens, *near)
        up_four, up_along = after((up_four, up_along), n1)
        up = [up_along, swap(up_four, second_plane), swap(up_along, second_plane)]
        mixed, lse, resid, n2 = attend(q, k, v, vec, wo)
        up = after(up, mixed)
        n2_other = swap(after(n2, up), other_core)
        return n1, q, k, v, wq, wk, wv, wo, vec, bup, mixed, lse, resid, n2, n2_other, up

    if by_hand:
        down_two = doubled(down_weight[None], other_layer(1))
        first = prepare(me, weights, vectors)
        moved = [swap(first, other_layer(r)) for r in (1, 2, 3)]
        down_shard = fenced(gather_down, after(down_two, first))
        pieces = [first] + after(moved, down_shard)
        split = 8 * own + 16
        near = jnp.stack([piece[:split] for piece in pieces])
        up_four = jnp.stack([piece[split:] for piece in pieces])
        near, up_four = after((near, up_four))
        down = [down_shard, swap(after(down_shard, near, up_four), other_layer(2))]
        near_moved, cot, cot_other, sum_down = fenced(gather_near, near)
        near = [near] + near_moved
        n1, q, k, v, wq, wk, wv, wo, vec, bup, mixed, lse, resid, n2, n2_other, up = fenced(
            attend_by_hand, near, up_four)
        hidden_weights = [(up_four, *up, *down)]
    else:
        wq, wk, wv, wo, hidden_weights, vec, bup = gather_plain(weights, vectors)
        hidden_weights = list(zip(*hidden_weights))
        cot, sum_down = masked()
        n1, q, k, v = call(
            project_rows, (tiles,), [tile_rows, vec_spec, square, square, square], [low_rows] * 4,
            [], "project", 0, tokens, vec, wq, wk, wv)
        mixed, lse, resid, n2 = attend(q, k, v, vec, wo)

    each = width // CHIPS
    deep = hidden // (2 * CHIPS)
    blocks = hidden // (2 * width)
    full_rows = whole_spec((rows, width))
    hidden_spec = pl.BlockSpec((1, width), lambda i, me: (0, i))
    low_out, high_out = (ANY_SPEC, shaped(rows, width)), (ANY_SPEC, shaped(rows, width, dtype=F32))
    act_out = (ANY_SPEC, shaped(rows, blocks * width))
    down_part = (ANY_SPEC, shaped(4, 2, deep, width))
    up_part = (ANY_SPEC, shaped(blocks, 4, 2, each, width))

    act_spec = pl.BlockSpec((tile, blocks * width), lambda i, *me: (i, 0))
    wide_spec = whole_spec((hidden // 2, width))

    def run_mlp(me, tokens_of, bup, sources):
        sets = len(tokens_of[0])
        low, high = pltpu.VMEM((sets * rows, width), BF16), pltpu.VMEM((sets * rows, width), F32)
        weight = pltpu.VMEM((2, width, width), BF16)
        dma = pltpu.SemaphoreType.DMA((2, sets))
        return call_with(
            me, functools.partial(mlp, sets, len(sources)), blocks,
            [ANY_SPEC] * (2 * sets) + [hidden_spec] + [ANY_SPEC] * len(sources),
            [act_out] * sets + [high_out] + [low_out] * (sets - 1) + [down_part] * 2 + [up_part] * 2
            + [(ANY_SPEC, shaped(hidden // 2, width)), (hidden_spec, shaped(1, hidden // 2, dtype=F32))],
            [low, low, high, pltpu.VMEM((blocks, sets * rows, width), BF16), low, low, weight, weight,
             pltpu.VMEM((blocks, width, width), BF16), pltpu.VMEM((hidden // 2, width), BF16), dma,
             pltpu.SemaphoreType.DMA((blocks, sets)), pltpu.SemaphoreType.DMA((sets,)), pltpu.SemaphoreType.DMA((4,)),
             pltpu.SemaphoreType.DMA((blocks + 1,))],
            "mlp", 0, *tokens_of[0], *tokens_of[1], bup, *sources)

    if by_hand:
        act_own, act_other, gtwo, gtwo_other, down_own, down_send, up_own, up_send, wdown, sum_up = run_mlp(
            me, ((n2, n2_other), (cot, cot_other)), bup, hidden_weights[0])
        gtwo_take = swap(gtwo_other, other_core)
        parts = (-1, CHIPS // 4, 2)
        down_first = [piece.reshape(*parts, deep, width) for piece in (down_own, swap(down_send, first_plane))]
        up_first = [piece.reshape(*parts, each, width) for piece in (up_own, swap(up_send, first_plane))]
    else:
        runs = [run_mlp(me + half, ((n2,), (cot,)), bup[half], hidden_weights[half]) for half in range(2)]
        (act_own, gtwo), (act_other, gtwo_take) = ((run[0], run[1]) for run in runs)
        gtwo_take = gtwo_take.astype(BF16)
        sum_up = jnp.concatenate([run[7] for run in runs], axis=1)
    grads_spec = pl.BlockSpec((4, tile, width), lambda i, *me: (0, i, 0))
    grads, gresid, sum_back = call(
        attention_backward, (tiles,),
        [SMEM, tile_rows, tile_rows, tile_rows, lse_spec, tile_rows, tile_rows, tile_rows, tile_rows, vec_spec, square],
        [(grads_spec, shaped(4, rows, width)), high_rows, sums], [pltpu.VMEM((tile, width), BF16)],
        "attention_backward", 0, lengths, q, k, v, lse, cot, resid, gtwo, gtwo_take, vec, wo)
    sum_spec = whole_spec((8, width))
    pair_shape = (CHIPS // 4, 4, 4 * each + 16, side)
    columns = pl.BlockSpec((1, rows, width), lambda i, me: (i, 0, 0))

    def run_weights(grads):
        return call_with(
            me, weight_grads, 4, [full_rows] * 2 + [columns, sum_spec, sum_spec, whole_spec((1, sum_up.shape[1]))],
            [(kept_spec(pair_shape), shaped(*pair_shape))] * 2, [], "weight_grads", 0,
            n1, mixed, grads, sum_back, sum_down, sum_up)

    def run_tokens(gresid):
        return call(
            tokens_backward, (tiles,), [tile_rows, tile_rows, vec_spec, grads_spec, square, square, square],
            [low_rows, sums], [], "tokens_backward", MIDDLE, tokens, gresid, vec, grads, wq, wk, wv)

    if by_hand:
        (out_other,) = call_with(
            me, mlp_out_other, tiles, [act_spec, wide_spec], [low_rows], [], "mlp_out_other", 0, after(act_other, grads), wdown)
        down_first, up_first = after((down_first, up_first), out_other)
        hidden_rest, hidden_take = scatter_second(*down_first, *up_first)

        def weights_of_chip(grads):
            square_send, square_keep = run_weights(grads)
            return merge_core_of(core, square_keep, scatter_core(square_send))

        square_own, square_send = fenced(weights_of_chip, after(grads, hidden_rest))
        square_take = swap(square_send, first_plane).reshape(square_own.shape)
        hidden_rest, hidden_take = after((hidden_rest, hidden_take), square_own)
        hidden_layers = scatter_layers(hidden_rest, hidden_take)
        gtok, late = run_tokens(after(gresid, hidden_layers[0]))
        square_take = after(square_take, late)
        late = late + swap(late, other_core)
        square_second = scatter_second(square_own, square_take)
        late = after(late, square_second[0])
        out_take = after(swap(out_other, other_core), square_second[0])
        (out,) = call_with(
            me, mlp_out_own, tiles, [tile_rows, vec_spec, act_spec, tile_rows, wide_spec], [low_rows], [],
            "mlp_out_own", 0, resid, vec, act_own, out_take, wdown)
        late = late + after(swap(late, other_layer(1)), out)
        hidden_layers = after(hidden_layers, late)
        g_down, up_keep, up_send = scatter_last(core, hidden_layers, own, blocks, deep)
        up_take = scatter_core(up_send)
        late = late + after(swap(late, other_layer(2)), g_down)
        square_second = after(square_second, g_down, late)
        square_layers = scatter_layers(*square_second)
        late = late + after(swap(late, other_plane(1)), square_layers[0])
        late = late + swap(late, other_plane(2))
        square_layers = after(square_layers, late)
        square_keep, square_send, flat = scatter_last(core, square_layers, own, 4, 0)
        square_take = scatter_core(square_send)
        outs = [(VMEM_SPEC, shaped(own, hidden, dtype=F32))] + [(VMEM_SPEC, shaped(own, width, dtype=F32))] * 4
        outs += [(VMEM_SPEC, shaped(own, dtype=F32))] * 8 + [(VMEM_SPEC, shaped(folds * own, dtype=F32))]
        g_up, g_q, g_k, g_v, g_o, *g_flat, g_ub = small_call(
            finish, (me, up_keep, up_take, square_keep, square_take, flat, late), outs, "finish",
            ins=[SMEM] + [VMEM_SPEC] * 6)
    else:
        square_send, square_keep = run_weights(grads)
        gtok, sum_one = run_tokens(gresid)
        flat = jnp.concatenate((sum_one[0:2], sum_back[0:5], sum_down[0:1]), axis=0)
        flat = flat.reshape(8, count, own).transpose(1, 0, 2).reshape(count, 8 * own)
        hidden_sums = sum_up.reshape(2, CHIPS, deep).transpose(1, 0, 2).reshape(count, folds * own)
        flat = jnp.concatenate((flat, hidden_sums), axis=1)
        g_down, g_up, g_q, g_k, g_v, g_o, flat = reduce_plain(
            [run[2:4] for run in runs], [run[4:6] for run in runs], (square_keep, square_send), flat)
        (out_other,) = call_with(
            me + 1, mlp_out_other, tiles, [act_spec, wide_spec], [low_rows], [], "mlp_out_other", 0, act_other, runs[1][6])
        (out,) = call_with(
            me, mlp_out_own, tiles, [tile_rows, vec_spec, act_spec, tile_rows, wide_spec], [low_rows], [],
            "mlp_out_own", 0, resid, vec, act_own, out_other, runs[0][6])
        g_flat = [flat[index * own : (index + 1) * own] for index in range(8)]
        g_ub = flat[8 * own :]
    g_gain, g_shift, g_qb, g_vb, g_ob, g_mg, g_ms, g_db = g_flat
    return (out, gtok, g_gain, g_shift, g_q, g_qb, g_k, g_v, g_vb, g_o, g_ob, g_mg, g_ms, g_up, g_ub, g_down, g_db)


def solution(mesh):
    rows, flat = P("dp", None), P("dp")
    return jax.shard_map(
        body,
        mesh=mesh,
        in_specs=(rows, rows, flat, flat, rows, flat, rows, rows, flat, rows, flat, flat, flat, rows, flat, rows, flat, rows),
        out_specs=(rows, rows, flat, flat, rows, flat, rows, rows, flat, rows, flat, flat, flat, rows, flat, rows, flat),
        check_vma=False,
    )
```

```python
import functools

import jax
import jax.numpy as jnp
from jax import lax
from jax.experimental import pallas as pl
from jax.experimental.pallas import tpu as pltpu
from jax.sharding import PartitionSpec as P

HEADS = 12
HEAD_DIM = 64
PAIRS = 6
LANES = 128
CHIPS = 16
MERGE_STEPS = 2
LONG = 10**11
SHORT = 6 * 10**9
MIDDLE = 115 * 10**8
LATER = 9 * 10**9
EPS = 1e-06
MASKED = -1e30
SCALE = HEAD_DIM**-0.5
GELU_C = 0.7978845608028654
GELU_A = 0.044715
VMEM = 64 * 1024 * 1024 - 65536
F32 = jnp.float32
BF16 = jnp.bfloat16


def dot_nn(left, right):
    return lax.dot_general(left, right, (((1,), (0,)), ((), ())), preferred_element_type=F32)


def dot_nt(left, right):
    return lax.dot_general(left, right, (((1,), (1,)), ((), ())), preferred_element_type=F32)


def dot_tn(left, right):
    return lax.dot_general(left, right, (((0,), (0,)), ((), ())), preferred_element_type=F32)


def normalize(rows):
    centered = rows - jnp.mean(rows, axis=-1, keepdims=True)
    inverse = lax.rsqrt(jnp.mean(centered * centered, axis=-1, keepdims=True) + EPS)
    return centered * inverse, inverse


def norm_back(grads, gain, hat, inverse):
    scaled = grads * gain
    mean = jnp.mean(scaled, axis=-1, keepdims=True)
    mean_hat = jnp.mean(scaled * hat, axis=-1, keepdims=True)
    return inverse * (scaled - mean - hat * mean_hat)


def column_sum(rows):
    return jnp.sum(rows, axis=0, keepdims=True)


def segments(lengths_ref, tile, slots, rows, axis):
    shape = (rows, 1) if axis == 0 else (1, rows)
    index = lax.broadcasted_iota(jnp.int32, shape, axis)
    segment = jnp.zeros(shape, jnp.int32)
    bound = 0
    for slot in range(slots):
        bound = bound + lengths_ref[tile, slot]
        segment = segment + (index >= bound).astype(jnp.int32)
    return segment


def mask_bias(lengths_ref, tile, slots, rows):
    same = segments(lengths_ref, tile, slots, rows, 0) == segments(lengths_ref, tile, slots, rows, 1)
    return jnp.where(same, 0.0, MASKED).astype(F32)


def half_of(pair, side):
    lane = lax.broadcasted_iota(jnp.int32, pair.shape, 1)
    keep = lane < HEAD_DIM if side == 0 else lane >= HEAD_DIM
    return jnp.where(keep, pair, jnp.zeros_like(pair))


def fetch_weights(me, sources, stage_ref, sem):
    core, chip = me & 1, me >> 1
    side = sources[0].shape[3]
    for index, source in enumerate(sources):
        half = core if index < 4 else 1 - core
        plane = (0, 1 + half, 2 - half, 3)[index % 4]
        cols = pl.ds(pl.multiple_of(half * side, LANES), side)
        for layer in range(4):
            owner = chip ^ (4 * layer + plane)
            pltpu.make_async_copy(source.at[layer], stage_ref.at[owner, :, :, cols], sem.at[0]).start()


def project(me_ref, x_ref, *refs):
    sources = refs[:8]
    n1_ref, q_ref, k_ref, v_ref = refs[8:12]
    outs, (vec_ref, bup_ref, weights_ref, stage_ref, sem, out_sem) = refs[12:16], refs[16:]
    step = pl.program_id(0)
    core = me_ref[0] & 1
    weights = [weights_ref.at[number] for number in range(4)]

    def write(number):
        return pltpu.make_async_copy(weights[number], outs[number], out_sem.at[number])

    @pl.when(step == 0)
    def _():
        fetch_weights(me_ref[0], sources, stage_ref, sem)
        pltpu.make_async_copy(stage_ref, stage_ref, sem.at[0]).wait()
        width = stage_ref.shape[3]
        side = width // 2
        blocks = width // (16 * CHIPS)
        for number in range(4):
            weights[number][...] = stage_ref[:, number * blocks : (number + 1) * blocks].reshape(width, width)
            write(number).start()
        parts = [stage_ref[chip, 4 * blocks].astype(F32) for chip in range(CHIPS)]
        halves = []
        for half in range(2):
            group = parts[half * CHIPS // 2 : (half + 1) * CHIPS // 2]
            halves.append(sum(part[:, :side] + part[:, side:] for part in group))
        vec_ref[...] = jnp.concatenate(halves, axis=1)
        blocks = bup_ref.shape[1] // side
        group = CHIPS // blocks
        for block in range(blocks):
            rows = sum(parts[block * group : (block + 1) * group])
            bup_ref[:, block * side : (block + 1) * side] = jnp.where(core == 0, rows[8:9, :side], rows[8:9, side:])

    project_rows(x_ref, vec_ref, *weights[:3], n1_ref, q_ref, k_ref, v_ref)

    @pl.when(step == pl.num_programs(0) - 1)
    def _():
        for number in range(4):
            write(number).wait()


def project_rows(x_ref, vec_ref, wq_ref, wk_ref, wv_ref, n1_ref, q_ref, k_ref, v_ref):
    hat, _ = normalize(x_ref[...].astype(F32))
    n1 = (hat * vec_ref[0:1, :] + vec_ref[1:2, :]).astype(BF16)
    n1_ref[...] = n1
    q_ref[...] = (dot_nn(n1, wq_ref[...]) + vec_ref[2:3, :]).astype(BF16) * jnp.asarray(SCALE, BF16)
    k_ref[...] = dot_nn(n1, wk_ref[...]).astype(BF16)
    v_ref[...] = (dot_nn(n1, wv_ref[...]) + vec_ref[3:4, :]).astype(BF16)


def mask_grads(lengths_ref, grad_ref, cot_ref, dsum_ref):
    tile = pl.program_id(0)
    slots = lengths_ref.shape[1]
    valid = segments(lengths_ref, tile, slots, grad_ref.shape[0], 0) < slots
    cot = jnp.where(valid, grad_ref[...].astype(F32), 0.0)
    cot_ref[...] = cot.astype(BF16)

    @pl.when(tile == 0)
    def _():
        dsum_ref[...] = jnp.zeros_like(dsum_ref)

    dsum_ref[0:1, :] += column_sum(cot)


def attention_forward(lengths_ref, x_ref, vec_ref, q_ref, k_ref, v_ref, wo_ref, mixed_ref, lse_ref, resid_ref, n2_ref):
    tile = pl.program_id(0)
    rows = q_ref.shape[0]
    slots = lengths_ref.shape[1]
    bias = mask_bias(lengths_ref, tile, slots, rows)
    lane = lax.broadcasted_iota(jnp.int32, (rows, LANES), 1)
    lse = jnp.zeros((rows, LANES), F32)

    def at(pair):
        return pl.ds(pair * LANES, LANES)

    def scores_of(pair):
        qp, kp = q_ref[:, at(pair)], k_ref[:, at(pair)]
        return [dot_nt(half_of(qp, side), kp) for side in range(2)]

    def softmax_of(scores):
        scores = scores + bias
        top = jnp.max(scores, axis=-1, keepdims=True)
        weights = jnp.exp(scores - top)
        sums = jnp.sum(weights, axis=-1, keepdims=True)
        return (weights * (1.0 / sums)).astype(BF16), top + jnp.log(sums)

    raw = {}
    probs = {}
    for turn in range(PAIRS + 2):
        if turn < PAIRS:
            raw[turn] = scores_of(turn)
        if 0 <= turn - 1 < PAIRS:
            both = [softmax_of(scores) for scores in raw.pop(turn - 1)]
            for side in range(2):
                lse = jnp.where(lane == 2 * (turn - 1) + side, both[side][1], lse)
            probs[turn - 1] = [pair[0] for pair in both]
        if turn >= 2:
            vp = v_ref[:, at(turn - 2)]
            parts = [dot_nn(probs[turn - 2][side], half_of(vp, side)) for side in range(2)]
            mixed_ref[:, at(turn - 2)] = (parts[0] + parts[1]).astype(BF16)
    lse_ref[...] = lse
    resid = x_ref[...].astype(F32) + (dot_nn(mixed_ref[...], wo_ref[...]) + vec_ref[4:5, :])
    resid_ref[...] = resid
    hat, _ = normalize(resid)
    n2_ref[...] = (hat * vec_ref[5:6, :] + vec_ref[6:7, :]).astype(BF16)


def spread(me, rows, put):
    layer, plane = me >> 3, (me >> 1) & 3
    each = rows.shape[0] // CHIPS
    for chip in range(CHIPS):
        put((chip & 3) ^ plane, (chip >> 2) ^ layer, rows[chip * each : (chip + 1) * each].astype(BF16))


def fetch_hidden(me, sources, wup_ref, wdown_ref, sem):
    if len(sources) == 2:
        for number in range(wup_ref.shape[0]):
            pltpu.make_async_copy(sources[0].at[number], wup_ref.at[number], sem.at[number]).start()
        pltpu.make_async_copy(sources[1], wdown_ref, sem.at[wup_ref.shape[0]]).start()
        return
    core, chip = me & 1, me >> 1
    planes = (0, 1 + core, 2 - core, 3)
    blocks, width = wup_ref.shape[:2]
    each, deep = width // CHIPS, wdown_ref.shape[0] // CHIPS
    for layer in range(4):
        for index, plane in enumerate(planes):
            owner = chip ^ (4 * layer + plane)
            rows = pl.ds(pl.multiple_of(owner * each, 16), each)
            side = sources[index].shape[2]
            for part in range(sources[index].shape[1] // each):
                number, cols = part * side // width, pl.ds(part * side % width, side)
                pltpu.make_async_copy(
                    sources[index].at[layer, pl.ds(part * each, each), :], wup_ref.at[number, rows, cols], sem.at[number]
                ).start()
            source = sources[4 + layer // 2].at[2 * index + layer % 2]
            rows = pl.ds(pl.multiple_of(owner * deep, 16), source.shape[0])
            pltpu.make_async_copy(source, wdown_ref.at[rows, :], sem.at[blocks]).start()
            rest = deep - source.shape[0]
            rows = pl.ds(pl.multiple_of(owner * deep + source.shape[0], 16), rest)
            for part in range(width // side):
                at = pl.ds(sources[index].shape[1] - (width // side - part) * rest, rest)
                pltpu.make_async_copy(
                    sources[index].at[layer, at, :], wdown_ref.at[rows, pl.ds(part * side, side)], sem.at[blocks]
                ).start()


def mlp(sets, count, me_ref, *refs):
    n2_hbm, cot_hbm = refs[:sets], refs[sets : 2 * sets]
    bup_ref = refs[2 * sets]
    sources = refs[2 * sets + 1 : 2 * sets + 1 + count]
    refs = refs[2 * sets + 1 + count :]
    act_hbm, gtwo_hbm, refs = refs[:sets], refs[sets : 2 * sets], refs[2 * sets :]
    down_own, down_send, up_own, up_send, wdown_hbm, dbu_ref = refs[:6]
    n2_ref, cot_ref, gacc, act_ref, gup_ref, low_ref, gdown_ref, gupw_ref = refs[6:14]
    wup_all, wdown_all, in_sem, act_sem, out_sem, grad_sem, weight_sem = refs[14:]
    step = pl.program_id(0)
    last = pl.num_programs(0) - 1
    me = me_ref[0]
    rows = n2_ref.shape[0] // sets

    def rows_of(index):
        return pl.ds(pl.multiple_of(index * rows, rows), rows)

    blocks, width = wup_all.shape[:2]

    @pl.when(step == 0)
    def _():
        fetch_hidden(me, sources, wup_all, wdown_all, weight_sem)
        for index in range(sets):
            at = pl.ds(index * rows, rows)
            pltpu.make_async_copy(n2_hbm[index], n2_ref.at[at, :], in_sem.at[0, index]).start()
            pltpu.make_async_copy(cot_hbm[index], cot_ref.at[at, :], in_sem.at[1, index]).start()

    pltpu.make_async_copy(wup_all.at[step], wup_all.at[step], weight_sem.at[step]).wait()
    write_down = pltpu.make_async_copy(wdown_all, wdown_hbm, weight_sem.at[blocks])

    @pl.when(step == 0)
    def _():
        pltpu.make_async_copy(wdown_all, wdown_all, weight_sem.at[blocks]).wait()
        write_down.start()

    wup = wup_all[step]
    wdown = wdown_all[pl.ds(pl.multiple_of(step * width, width), width), :]
    dbu_ref[...] = jnp.zeros_like(dbu_ref)
    slot = lax.rem(step, 2)

    @pl.loop(0, sets)
    def _(index):
        at = rows_of(index)

        @pl.when(step == 0)
        def _():
            pltpu.make_async_copy(n2_ref.at[at, :], n2_ref.at[at, :], in_sem.at[0, index]).wait()
            pltpu.make_async_copy(cot_ref.at[at, :], cot_ref.at[at, :], in_sem.at[1, index]).wait()

        pre = dot_nn(n2_ref[at, :], wup) + bup_ref[...]
        grad_act = dot_nt(cot_ref[at, :], wdown)
        square = pre * pre
        tanh = jnp.tanh(pre * (GELU_C + (GELU_C * GELU_A) * square))
        half = 0.5 + 0.5 * tanh
        inner = GELU_C + (3.0 * GELU_C * GELU_A) * square
        act_ref[slot, at, :] = (pre * half).astype(BF16)
        gup = (grad_act * (half + (0.5 * pre) * (1.0 - tanh * tanh) * inner)).astype(BF16)
        gup_ref[at, :] = gup
        dbu_ref[...] += column_sum(gup.astype(F32))

    @pl.when(step == 0)
    def _():
        @pl.loop(0, sets)
        def _(index):
            at = rows_of(index)
            gacc[at, :] = dot_nt(gup_ref[at, :], wup)

    @pl.when((step > 0) & (step < last))
    def _():
        @pl.loop(0, sets)
        def _(index):
            at = rows_of(index)
            gacc[at, :] += dot_nt(gup_ref[at, :], wup)

    def results():
        for index in range(sets):
            at = pl.ds(index * rows, rows)
            source = low_ref.at[at, :] if index else gacc.at[at, :]
            yield pltpu.make_async_copy(source, gtwo_hbm[index], out_sem.at[index])

    def activations(number):
        for index in range(sets):
            source = act_ref.at[number, pl.ds(index * rows, rows), :]
            cols = pl.ds(number * width, width)
            yield pltpu.make_async_copy(source, act_hbm[index].at[:, cols], act_sem.at[number, index])

    for number in range(act_ref.shape[0]):

        @pl.when(step == number)
        def _():
            for copy in activations(number):
                copy.start()

    @pl.when(step == last)
    def _():
        @pl.loop(0, sets)
        def _(index):
            at = rows_of(index)
            total = gacc[at, :] + dot_nt(gup_ref[at, :], wup)
            gacc[at, :] = total
            low_ref[at, :] = total.astype(BF16)

        for copy in results():
            copy.start()

    gdown_ref[slot] = dot_tn(act_ref[slot], cot_ref[...]).astype(BF16)
    deep = down_own.shape[2]
    count = gdown_ref.shape[1] // deep
    for index in range(count):
        chip = step * count + index
        source = gdown_ref.at[slot, pl.ds(index * deep, deep), :]
        keep_or_send(me, chip & 3, (chip >> 2) ^ (me >> 3), source, down_own, down_send, grad_sem, 0)

    gupw_ref[slot] = dot_tn(n2_ref[...], gup_ref[...]).astype(BF16)
    each = gupw_ref.shape[1] // CHIPS
    for chip in range(CHIPS):
        source = gupw_ref.at[slot, pl.ds(chip * each, each), :]
        keep_or_send(
            me, chip & 3, (chip >> 2) ^ (me >> 3), source, up_own.at[step], up_send.at[step], grad_sem, 2)

    @pl.when(step == last)
    def _():
        for copy in results():
            copy.wait()
        write_down.wait()
        for number in range(act_ref.shape[0]):
            for copy in activations(number):
                copy.wait()
        for number, ref in enumerate((down_own, down_send, up_own, up_send)):
            pltpu.make_async_copy(ref, ref, grad_sem.at[number]).wait()


def keep_or_send(me, plane, layer, source, own_ref, send_ref, sem, number):
    core = me & 1
    relative = plane ^ ((me >> 1) & 3)
    mine = (relative == 0) | (relative == 2 - core)

    @pl.when(mine)
    def _():
        pltpu.make_async_copy(source, own_ref.at[layer, jnp.where(relative == 0, 0, 1)], sem.at[number]).start()

    @pl.when(jnp.logical_not(mine))
    def _():
        pltpu.make_async_copy(source, send_ref.at[layer, jnp.where(relative == 3, 1, 0)], sem.at[number + 1]).start()


def mlp_out_other(me_ref, act_ref, wdown_ref, out_ref):
    out_ref[...] = dot_nn(act_ref[...], wdown_ref[...]).astype(BF16)


def mlp_out_own(me_ref, resid_ref, vec_ref, act_ref, take_ref, wdown_ref, out_ref):
    half = dot_nn(act_ref[...], wdown_ref[...]) + take_ref[...].astype(F32)
    out_ref[...] = (resid_ref[...] + (half + vec_ref[7:8, :])).astype(BF16)


def attention_backward(lengths_ref, q_ref, k_ref, v_ref, lse_ref, cot_ref, resid_ref, gtwo_ref, gother_ref, vec_ref, wo_ref,
                       grads_ref, gresid_ref, dsum_ref, gmix_ref):
    tile = pl.program_id(0)
    rows = q_ref.shape[0]

    @pl.when(tile == 0)
    def _():
        dsum_ref[...] = jnp.zeros_like(dsum_ref)

    hat, inverse = normalize(resid_ref[...])
    grad_two = gtwo_ref[...] + gother_ref[...].astype(F32)
    gresid = cot_ref[...].astype(F32) + norm_back(grad_two, vec_ref[5:6, :], hat, inverse)
    gresid_ref[...] = gresid
    gattn = gresid.astype(BF16)
    grads_ref[3] = gattn
    dsum_ref[2:3, :] += column_sum(gattn.astype(F32))
    dsum_ref[3:4, :] += column_sum(grad_two * hat)
    dsum_ref[4:5, :] += column_sum(grad_two)
    gmix_ref[...] = dot_nt(gattn, wo_ref[...]).astype(BF16)
    bias = mask_bias(lengths_ref, tile, lengths_ref.shape[1], rows)

    def load(pair):
        cols = pl.ds(pair * LANES, LANES)
        return q_ref[:, cols], k_ref[:, cols], v_ref[:, cols], gmix_ref[:, cols]

    def products_of(pair):
        qp, kp, vp, gp = load(pair)
        return [(dot_nt(half_of(qp, side), kp), dot_nt(half_of(gp, side), vp)) for side in range(2)]

    def softmax_back(pair, products):
        results = []
        for side, (scores, grad_probs) in enumerate(products):
            head = 2 * pair + side
            probs = jnp.exp(scores + bias - lse_ref[:, head : head + 1])
            weighted = probs * grad_probs
            dot = jnp.sum(weighted, axis=-1, keepdims=True)
            results.append((probs.astype(BF16), (weighted - probs * dot).astype(BF16)))
        return results

    def store(pair, results):
        qp, kp, vp, gp = load(pair)
        dq = sum(dot_nn(results[side][1], half_of(kp, side)) for side in range(2))
        dk = sum(dot_tn(results[side][1], half_of(qp, side)) for side in range(2))
        dv = sum(dot_tn(results[side][0], half_of(gp, side)) for side in range(2))
        cols = pl.ds(pair * LANES, LANES)
        grads_ref[0, :, cols] = (dq * SCALE).astype(BF16)
        grads_ref[1, :, cols] = dk.astype(BF16)
        grads_ref[2, :, cols] = dv.astype(BF16)

    raw = {}
    done = {}
    for turn in range(PAIRS + 2):
        if turn < PAIRS:
            raw[turn] = products_of(turn)
        if 0 <= turn - 1 < PAIRS:
            done[turn - 1] = softmax_back(turn - 1, raw.pop(turn - 1))
        if turn >= 2:
            store(turn - 2, done.pop(turn - 2))

    dsum_ref[0:1, :] += column_sum(grads_ref[0].astype(F32))
    dsum_ref[1:2, :] += column_sum(grads_ref[2].astype(F32))


def weight_grads(me_ref, n1_ref, mixed_hbm, columns_ref, sum_back_ref, sum_down_ref, sum_up_ref, send_hbm, keep_hbm,
                 send_ref, keep_ref, mixed_ref, in_sem, out_sem):
    step = pl.program_id(0)
    me = me_ref[0]
    first = (me & 1) == 0
    side = send_ref.shape[3]
    each = n1_ref.shape[1] // CHIPS
    load = pltpu.make_async_copy(mixed_hbm, mixed_ref, in_sem.at[0])

    def writes(number):
        rows = pl.ds(number * each, each if number < 4 else 16)
        for index, (ref, out) in enumerate(((send_ref, send_hbm), (keep_ref, keep_hbm))):
            yield pltpu.make_async_copy(ref.at[:, :, rows, :], out.at[:, :, rows, :], out_sem.at[index, number])

    @pl.when(step == 0)
    def _():
        load.start()

    def run(left, number):
        result = dot_tn(left, columns_ref[0])
        low, high = result[:, :side], result[:, side:]
        rows_at = pl.ds(pl.multiple_of(number * each, 16), each)

        def put_send(plane, layer, rows):
            send_ref[layer, plane, rows_at, :] = rows

        def put_keep(plane, layer, rows):
            keep_ref[layer, plane, rows_at, :] = rows

        spread(me, jnp.where(first, high, low), put_send)
        spread(me, jnp.where(first, low, high), put_keep)

    @pl.when(step < 3)
    def _():
        run(n1_ref[...], step)

    for number in range(3):

        @pl.when(step == number)
        def _():
            for copy in writes(number):
                copy.start()

    @pl.when(step == 3)
    def _():
        nothing = jnp.zeros((2, n1_ref.shape[1]), F32)
        vecs = jnp.concatenate((nothing, sum_back_ref[0:5], sum_down_ref[0:1]), axis=0)
        for chip in range(CHIPS):
            half = chip // (CHIPS // 2)
            block = chip * (sum_up_ref.shape[1] // side) // CHIPS
            last = jnp.broadcast_to(sum_up_ref[:, block * side : (block + 1) * side], (8, side))
            short = vecs[:, half * side : (half + 1) * side]
            at = ((chip >> 2) ^ (me >> 3), (chip & 3) ^ ((me >> 1) & 3))
            keep_ref[at[0], at[1], 4 * each :, :] = jnp.concatenate((short, last), axis=0).astype(BF16)
            send_ref[at[0], at[1], 4 * each :, :] = jnp.concatenate((short, jnp.zeros_like(last)), axis=0).astype(BF16)
        for copy in writes(4):
            copy.start()
        load.wait()
        run(mixed_ref[...], 3)
        for copy in writes(3):
            copy.start()
        for number in range(5):
            for copy in writes(number):
                copy.wait()


def tokens_backward(x_ref, gresid_ref, vec_ref, grads_ref, wq_ref, wk_ref, wv_ref, gtok_ref, dsum_ref):
    @pl.when(pl.program_id(0) == 0)
    def _():
        dsum_ref[...] = jnp.zeros_like(dsum_ref)

    grad_one = dot_nt(grads_ref[0], wq_ref[...]) + dot_nt(grads_ref[1], wk_ref[...]) + dot_nt(grads_ref[2], wv_ref[...])
    hat, inverse = normalize(x_ref[...].astype(F32))
    gtok_ref[...] = (gresid_ref[...] + norm_back(grad_one, vec_ref[0:1, :], hat, inverse)).astype(BF16)
    dsum_ref[0:1, :] += column_sum(grad_one * hat)
    dsum_ref[1:2, :] += column_sum(grad_one)


def rows_spec(block, width):
    return pl.BlockSpec((block, width), lambda i, *me: (i, 0))


def cols_spec(height, block):
    return pl.BlockSpec((height, block), lambda i, *me: (0, i))


def whole_spec(shape):
    return pl.BlockSpec(shape, lambda *i: (0,) * len(shape), pipeline_mode=pl.Buffered(1))


def kept_spec(shape):
    return pl.BlockSpec(shape, lambda *i: (0,) * len(shape))


SMEM = pl.BlockSpec(memory_space=pltpu.SMEM)


def cost(flops):
    return pl.CostEstimate(flops=flops, bytes_accessed=1, transcendentals=0)


def call(kernel, grid, ins, outs, scratch, name, flops, *args):
    out_specs = tuple(spec for spec, _ in outs)
    out_shape = tuple(shape for _, shape in outs)
    return pl.pallas_call(
        kernel,
        grid=grid,
        in_specs=ins,
        out_specs=out_specs,
        out_shape=out_shape,
        scratch_shapes=scratch,
        compiler_params=pltpu.CompilerParams(vmem_limit_bytes=VMEM, dimension_semantics=("arbitrary",) * len(grid)),
        cost_estimate=cost(flops),
        name=name,
    )(*args)


def call_with(me, kernel, steps, ins, outs, scratch, name, flops, *args):
    out_shape = tuple(shape for _, shape in outs)
    return pl.pallas_call(
        kernel,
        grid_spec=pltpu.PrefetchScalarGridSpec(
            num_scalar_prefetch=1, grid=(steps,), in_specs=ins, out_specs=tuple(spec for spec, _ in outs),
            scratch_shapes=scratch),
        out_shape=out_shape,
        compiler_params=pltpu.CompilerParams(vmem_limit_bytes=VMEM, dimension_semantics=("arbitrary",)),
        cost_estimate=cost(flops),
        name=name,
    )(me, *args)


def shaped(*shape, dtype=BF16):
    return jax.ShapeDtypeStruct(shape, dtype)


def flipped(count, change):
    pairs = []
    for source in range(count):
        core, chip = source & 1, source >> 1
        core, chip = change(core, chip)
        pairs.append((source, 2 * chip + core))
    return pairs


def swap(array, change):
    return lax.ppermute(array, "dp", flipped(lax.axis_size("dp"), change))


def other_core(core, chip):
    return core ^ 1, chip


def first_plane(core, chip):
    return core, chip ^ (1 + core)


def second_plane(core, chip):
    return core, chip ^ (2 - core)


def other_plane(distance):
    return lambda core, chip: (core, chip ^ distance)


def other_layer(distance):
    return lambda core, chip: (core, chip ^ (4 * distance))


def split_shards(core_ref, q_ref, k_ref, v_ref, o_ref, u_ref, keep_ref, send_ref):
    width = q_ref.shape[1]
    side = width // 2
    first = core_ref[0] == 0

    def put(index, low, high):
        keep_ref[index] = jnp.where(first, low, high).astype(BF16)
        send_ref[index] = jnp.where(first, high, low).astype(BF16)

    for index, ref in enumerate((q_ref, k_ref, v_ref, o_ref)):
        rows = ref[...].astype(F32)
        put(index, rows[:, :side], rows[:, side:])
    up = u_ref[...].astype(F32)
    hidden = up.shape[1]
    deep = hidden // (2 * CHIPS)
    halves = [
        jnp.concatenate([up[:, start : start + deep] for start in range(half * deep, hidden, 2 * deep)], axis=1)
        for half in range(2)
    ]
    for part in range(hidden // width):
        at = slice(part * side, (part + 1) * side)
        put(4 + part, halves[0][:, at], halves[1][:, at])


def join_shards(me_ref, keep_ref, take_ref, down_ref, *refs):
    vectors, (near_ref, up_ref) = refs[:-2], refs[-2:]
    me = me_ref[0]
    first = (me & 1) == 0
    parts, own, side = keep_ref.shape
    folds = parts - 4
    keep = keep_ref[...].astype(F32)
    take = take_ref[...].astype(F32)

    def joined(index):
        low = jnp.where(first, keep[index], take[index])
        high = jnp.where(first, take[index], keep[index])
        return jnp.concatenate((low, high), axis=0).astype(BF16)

    for index in range(4):
        near_ref[2 * own * index : 2 * own * (index + 1), :] = joined(index)
    for index in range(folds):
        up_ref[2 * own * index : 2 * own * (index + 1), :] = joined(4 + index)
    base = 2 * own * folds
    up_ref[base : base + 16, :] = down_ref[-16:, :side]
    up_ref[base + 16 :, :] = down_ref[-16:, side:]
    rows = []
    for ref in vectors:
        flat = ref[...].astype(F32).reshape(1, -1)
        rows.append(jnp.concatenate((flat, jnp.zeros((1, side - flat.shape[1]), F32)), axis=1))
    rows.append(jnp.zeros((16 - len(rows), side), F32))
    rows = jnp.concatenate(rows, axis=0)
    short = pltpu.roll(rows, own * lax.rem(me, side // own), 1)
    long = pltpu.roll(rows, folds * own * lax.rem(me >> 1, side // (folds * own)), 1)
    index = lax.broadcasted_iota(jnp.int32, rows.shape, 0)
    near_ref[8 * own :, :] = jnp.where(index < 8, short, long).astype(BF16)


def across_layers(shard):
    return jnp.stack([shard] + [swap(shard, other_layer(distance)) for distance in (1, 2, 3)])


def after(arrays, *others):
    return lax.optimization_barrier((arrays, others))[0]


def small_call(kernel, args, outs, name, scratch=(), ins=None, flops=0):
    return pl.pallas_call(
        kernel,
        in_specs=ins,
        out_specs=tuple(spec for spec, _ in outs),
        out_shape=tuple(shape for _, shape in outs),
        scratch_shapes=list(scratch),
        compiler_params=pltpu.CompilerParams(vmem_limit_bytes=VMEM),
        cost_estimate=cost(flops),
        name=name,
    )(*args)


VMEM_SPEC = pl.BlockSpec(memory_space=pltpu.VMEM)
ANY_SPEC = pl.BlockSpec(memory_space=pl.ANY)


def prepare(me, weights, vectors):
    own, width = weights[0].shape
    side = width // 2
    deep = weights[5].shape[0]
    folds = deep // own
    halves = (VMEM_SPEC, shaped(4 + folds, own, side))
    keep, send = small_call(
        split_shards, (me & 1, *weights[:5]), [halves, halves], "split_shards", ins=[SMEM] + [VMEM_SPEC] * 5)
    take = swap(send, other_core)
    return small_call(
        join_shards, (me, keep, take, weights[5], *vectors),
        [(VMEM_SPEC, shaped(8 * own + 16, side)), (VMEM_SPEC, shaped(2 * deep + 32, side))], "join_shards",
        ins=[SMEM] + [VMEM_SPEC] * (3 + len(vectors)))


def doubled(pieces, change):
    return jnp.concatenate((pieces, swap(pieces, change)))


def gather_down(pieces):
    return doubled(doubled(pieces, first_plane), second_plane)


def gather_plain(weights, vectors):
    squares, up_weight, down_weight = weights[:4], weights[4], weights[5]
    count = lax.axis_size("dp")
    own, width = squares[0].shape
    folds = down_weight.shape[0] // own
    hidden = up_weight.shape[1]
    flat = jnp.concatenate(vectors)
    packed = jnp.concatenate(
        (
            *squares,
            up_weight.reshape(own, folds, width).transpose(1, 0, 2).reshape(own * folds, width),
            down_weight,
            jnp.pad(flat.reshape(1, -1), ((0, 7), (0, width - flat.size))),
        ),
        axis=0,
    )
    whole = lax.all_gather(packed, "dp", axis=0, tiled=True).reshape(count, -1, width)
    square_all = [whole[:, index * own : (index + 1) * own, :].reshape(width, width) for index in range(4)]
    wup = whole[:, 4 * own : (4 + folds) * own, :].reshape(count, folds, own, width).transpose(0, 2, 1, 3)
    wup = wup.reshape(width, 2, CHIPS // 2, 2, -1).transpose(3, 1, 0, 2, 4).reshape(2, 2, width, width)
    wdown = whole[:, (4 + folds) * own : (4 + 2 * folds) * own, :]
    wdown = wdown.reshape(CHIPS, 2, -1, width).transpose(1, 0, 2, 3).reshape(2, hidden // 2, width)
    last = whole[:, (4 + 2 * folds) * own, : flat.size].astype(F32)
    vec = last[:, : 8 * own].reshape(count, 8, own).transpose(1, 0, 2).reshape(8, width)
    bup = last[:, 8 * own :].reshape(CHIPS, 2, -1).transpose(1, 0, 2).reshape(2, 1, -1)
    return (*square_all, (wup, wdown), jnp.pad(vec, ((0, 8), (0, 0))), bup)


def merge_core(core_ref, keep_ref, take_ref, own_ref, send_ref):
    core = core_ref[0]

    def whole(plane):
        return (keep_ref[:, plane].astype(F32) + take_ref[:, plane].astype(F32)).astype(BF16)

    own_ref[:, 0] = whole(0)
    own_ref[:, 1] = whole(2 - core)
    send_ref[:, 0] = whole(1 + core)
    send_ref[:, 1] = whole(3)


def merge_first(*refs):
    pairs, rest_ref, send_ref = refs[:-2], refs[-2], refs[-1]
    base = 0
    for own_ref, take_ref in zip(pairs[::2], pairs[1::2]):
        for part in range(own_ref.shape[0]):
            at = slice(base, base + own_ref.shape[3])
            rest_ref[:, at, :] = (own_ref[part, :, 0].astype(F32) + take_ref[part, :, 0].astype(F32)).astype(BF16)
            send_ref[:, at, :] = (own_ref[part, :, 1].astype(F32) + take_ref[part, :, 1].astype(F32)).astype(BF16)
            base += own_ref.shape[3]


def merge_second(own_ref, take_ref, rest_ref, *send_refs):
    for layer in range(4):
        whole = own_ref[layer].astype(F32) + take_ref[layer].astype(F32)
        if layer == 0:
            rest_ref[...] = whole
        else:
            send_refs[layer - 1][...] = whole.astype(BF16)


def merge_last(deep, core_ref, rest_ref, a_ref, b_ref, c_ref, *refs):
    whole = rest_ref[...] + a_ref[...].astype(F32) + b_ref[...].astype(F32) + c_ref[...].astype(F32)
    first = core_ref[0] == 0
    if deep:
        refs[0][...] = whole[:deep]
        refs = refs[1:]
    keep_ref, send_ref = refs[:2]
    parts, own, _ = keep_ref.shape
    for part in range(parts):
        low = whole[deep + 2 * own * part : deep + 2 * own * part + own]
        high = whole[deep + 2 * own * part + own : deep + 2 * own * (part + 1)]
        keep_ref[part] = jnp.where(first, low, high)
        send_ref[part] = jnp.where(first, high, low)
    if not deep:
        refs[2][...] = whole[2 * own * parts :]


def finish(me_ref, up_keep_ref, up_take_ref, keep_ref, take_ref, flat_ref, late_ref, up_ref, *refs):
    me = me_ref[0]
    first = (me & 1) == 0
    side = keep_ref.shape[2]
    width = 2 * side
    squares, flats = refs[:4], refs[4:]
    own = up_ref.shape[0]
    for number, ref in enumerate(squares):
        keep, take = keep_ref[number], take_ref[number]
        ref[:, :side] = jnp.where(first, keep, take)
        ref[:, side:] = jnp.where(first, take, keep)
    parts = up_keep_ref.shape[0]
    deep = parts * width // CHIPS
    for part in range(parts):
        keep, take = up_keep_ref[part], up_take_ref[part]
        low, high = jnp.where(first, keep, take), jnp.where(first, take, keep)
        pieces = []
        for start in range(0, width, deep):
            pieces += [low[:, start : start + deep], high[:, start : start + deep]]
        up_ref[:, 2 * width * part : 2 * width * (part + 1)] = jnp.concatenate(pieces, axis=1)
    late = jnp.where(me < side // own, late_ref[0:2, :side], late_ref[0:2, side:])
    flat = jnp.concatenate((late, flat_ref[2:]), axis=0)
    long = flats[-1].shape[0]
    short_turn = lax.rem(side - own * lax.rem(me, side // own), side)
    long_turn = lax.rem(side - long * lax.rem(me >> 1, side // long), side)
    short = pltpu.roll(flat, short_turn, 1)
    for number, ref in enumerate(flats[:-1]):
        ref[...] = short[number, :own]
    flats[-1][...] = pltpu.roll(flat, long_turn, 1)[8, :long]


def fenced(function, *args):
    kinds = jax.eval_shape(function, *args)

    def nothing(*_):
        return jax.tree.map(lambda kind: jnp.zeros(kind.shape, kind.dtype), kinds)

    return lax.cond(lax.axis_index("dp") < lax.axis_size("dp"), function, nothing, *args)


def scatter_core(send):
    return swap(send, other_core)


def merge_core_of(core, keep, take):
    shape = keep.shape
    planes, rows, side = shape[-3:]
    keep, take = keep.reshape(-1, planes, rows, side), take.reshape(-1, planes, rows, side)
    count = keep.shape[0]
    steps = MERGE_STEPS
    block = pl.BlockSpec((count // steps, planes, rows, side), lambda i: (i, 0, 0, 0))
    half = (pl.BlockSpec((count // steps, 2, rows, side), lambda i: (i, 0, 0, 0)), shaped(count, 2, rows, side))
    own, send = call(merge_core, (steps,), [SMEM, block, block], [half, half], [], "merge_core", 0, core, keep, take)
    return own.reshape(-1, CHIPS // 4, 2, rows, side), send


def scatter_second(*pairs):
    _, count, _, _, side = pairs[0].shape
    rows = sum(piece.shape[0] * piece.shape[3] for piece in pairs[::2])
    steps = MERGE_STEPS
    ins = [pl.BlockSpec((piece.shape[0], count // steps, *piece.shape[2:]), lambda i: (0, i, 0, 0, 0)) for piece in pairs]
    out = pl.BlockSpec((count // steps, rows, side), lambda i: (i, 0, 0))
    rest, send = call(
        merge_first, (steps,), ins, [(out, shaped(count, rows, side))] * 2, [],
        "merge_first", 0, *pairs)
    return rest, swap(send, second_plane)


def merge_layers_of(own, take):
    _, rows, side = own.shape
    out = shaped(rows, side)
    return small_call(
        merge_second, (own, take), [(VMEM_SPEC, shaped(rows, side, dtype=F32))] + [(VMEM_SPEC, out)] * 3,
        "merge_second", ins=[VMEM_SPEC] * 2)


def scatter_layers(own, take):
    rest, *sends = merge_layers_of(own, take)
    return [rest] + [swap(piece, other_layer(r + 1)) for r, piece in enumerate(sends)]


def scatter_last(core, pieces, own, parts, deep):
    rows, side = pieces[0].shape
    outs = [(VMEM_SPEC, shaped(parts, own, side, dtype=F32))] * 2
    if deep:
        outs = [(VMEM_SPEC, shaped(deep, side, dtype=F32))] + outs
    else:
        outs.append((VMEM_SPEC, shaped(rows - 2 * own * parts, side, dtype=F32)))
    return small_call(
        functools.partial(merge_last, deep), (core, *pieces), outs, "merge_last", ins=[SMEM] + [VMEM_SPEC] * 4, flops=SHORT if deep else 0)


def reduce_plain(down_pairs, up_pairs, square_pair, flat):
    def scattered(array, axis):
        return lax.psum_scatter(array, "dp", scatter_dimension=axis, tiled=True).astype(F32)

    def planes(own, send, core):
        order = (own[..., 0, :, :], send[..., 0, :, :], own[..., 1, :, :], send[..., 1, :, :])
        if core == 1:
            order = (order[0], order[2], order[1], order[3])
        return jnp.stack(order, axis=-3)

    down = jnp.stack([planes(*pair, core) for core, pair in enumerate(down_pairs)])
    up = jnp.stack([planes(*pair, core) for core, pair in enumerate(up_pairs)])
    width = down.shape[-1]
    each = up.shape[4]
    down = down.transpose(1, 2, 0, 3, 4).reshape(-1, width)
    up = up.reshape(2, 2, CHIPS, each, CHIPS // 2, -1).transpose(2, 3, 1, 4, 0, 5).reshape(CHIPS * each, -1)
    square = jnp.stack(square_pair).transpose(1, 2, 3, 0, 4)[:, :, : 4 * each]
    square = square.reshape(CHIPS, 4, each, width).transpose(1, 0, 2, 3).reshape(4, CHIPS * each, width)
    return (
        scattered(down, 0),
        scattered(up, 0),
        *scattered(square, 1),
        lax.psum_scatter(flat, "dp", scatter_dimension=0, tiled=True).reshape(-1),
    )


def body(tokens, lengths, attn_gain, attn_shift, query_weight, query_bias, key_weight, value_weight, value_bias,
         out_weight, out_bias, mlp_gain, mlp_shift, up_weight, up_bias, down_weight, down_bias, grad_out):
    count = lax.axis_size("dp")
    rows, width = tokens.shape
    tiles = lengths.shape[0]
    tile = rows // tiles
    hidden = up_bias.shape[0] * count
    own = width // count
    folds = hidden // width
    vectors = (attn_gain, attn_shift, query_bias, value_bias, out_bias, mlp_gain, mlp_shift, down_bias, up_bias)
    by_hand = count == 2 * CHIPS
    me = lax.axis_index("dp").astype(jnp.int32).reshape(1) if by_hand else jnp.zeros((1,), jnp.int32)
    core = me & 1
    weights = (query_weight, key_weight, value_weight, out_weight, up_weight, down_weight)

    tile_rows = rows_spec(tile, width)
    square = whole_spec((width, width))
    vec_spec = whole_spec((16, width))
    sums = (kept_spec((8, width)), shaped(8, width, dtype=F32))
    low_rows = (tile_rows, shaped(rows, width))
    fold = 2 if tiles % 2 == 0 else 1
    wide_rows = rows_spec(fold * tile, width)
    wide_low = (wide_rows, shaped(rows, width))
    lse_spec = rows_spec(tile, LANES)
    mac = 2 * rows * width * width
    kept_vec = (kept_spec((16, width)), shaped(16, width, dtype=F32))
    kept_hidden = (kept_spec((1, hidden // 2)), shaped(1, hidden // 2, dtype=F32))
    side = width // 2

    def masked(*earlier):
        return call(
            mask_grads, (tiles,), [SMEM, tile_rows], [low_rows, sums], [], "mask_grads", 0,
            lengths, after(grad_out, *earlier))

    high_rows = (tile_rows, shaped(rows, width, dtype=F32))

    def attend(q, k, v, vec, wo):
        return call(
            attention_forward, (tiles,), [SMEM, tile_rows, vec_spec, tile_rows, tile_rows, tile_rows, square],
            [low_rows, (lse_spec, shaped(rows, LANES, dtype=F32)), high_rows, low_rows],
            [], "attention_forward", 0, lengths, tokens, vec, q, k, v, wo)

    def gather_first(near):
        cot, sum_down = masked(near)
        along = after(swap(near, first_plane), cot)
        return along, swap(near, second_plane), cot, sum_down

    def gather_second(near, along, across, cot, up_two, up_taken):
        cot_other = swap(cot, other_core)
        corner = swap(along, second_plane)
        taken = [swap(near, other_core), swap(along, other_core)]
        across, corner_out = after((across, corner), taken)
        taken += [swap(across, other_core), swap(corner_out, other_core)]
        return corner, taken, cot_other, jnp.concatenate((up_two, up_taken))

    def attend_by_hand(q, k, v, vec, wo, up_four, up_along):
        up = [swap(up_four, second_plane), swap(up_along, second_plane)]
        mixed, lse, resid, n2 = attend(q, k, v, vec, wo)
        up = after(up, mixed)
        n2_other = swap(after(n2, up), other_core)
        return mixed, lse, resid, n2, n2_other, up

    if by_hand:
        down_two = doubled(down_weight[None, :-16], other_layer(1))
        near, up = prepare(me, weights, vectors)
        near_moved = [swap(near, other_layer(r)) for r in (1, 2, 3)]
        up_moved = swap(up, other_layer(1))
        down_shard = fenced(gather_down, after(down_two, near))
        near_moved, up_moved = after((near_moved, up_moved), down_shard)
        near = jnp.stack([near] + near_moved)
        up_two = jnp.stack((up, up_moved))
        near, up_two = after((near, up_two))
        up_moved = swap(up_two, other_layer(2))
        along, across, cot, sum_down = fenced(gather_first, near)
        up_taken = after(up_moved, along)
        down = [down_shard, swap(after(down_shard, along), other_layer(2))]
        corner, taken, cot_other, up_four = fenced(gather_second, near, along, across, cot, up_two, up_taken)
        near = [near, along, across, corner] + taken
        up_along = swap(up_four, first_plane)
        n1, q, k, v, wq, wk, wv, wo, vec, bup = call_with(
            me, project, tiles, [tile_rows] + [ANY_SPEC] * 8,
            [low_rows] * 4 + [(ANY_SPEC, shaped(width, width))] * 4 + [kept_vec, kept_hidden],
            [pltpu.VMEM((4, width, width), BF16), pltpu.VMEM((CHIPS, width // (4 * CHIPS) + 1, 16, width), BF16),
             pltpu.SemaphoreType.DMA((1,)), pltpu.SemaphoreType.DMA((4,))],
            "project", LATER, tokens, *[piece.reshape(4, -1, 16, side) for piece in near])
        up_along = after(up_along, n1)
        mixed, lse, resid, n2, n2_other, up_moved = fenced(attend_by_hand, q, k, v, vec, wo, up_four, up_along)
        up = [up_along] + up_moved
        hidden_weights = [(up_four, *up, *down)]
    else:
        wq, wk, wv, wo, hidden_weights, vec, bup = gather_plain(weights, vectors)
        hidden_weights = list(zip(*hidden_weights))
        cot, sum_down = masked()
        n1, q, k, v = call(
            project_rows, (tiles,), [tile_rows, vec_spec, square, square, square], [low_rows] * 4,
            [], "project", 0, tokens, vec, wq, wk, wv)
        mixed, lse, resid, n2 = attend(q, k, v, vec, wo)

    each = width // CHIPS
    deep = hidden // (2 * CHIPS)
    blocks = hidden // (2 * width)
    full_rows = whole_spec((rows, width))
    hidden_spec = pl.BlockSpec((1, width), lambda i, me: (0, i))
    low_out, high_out = (ANY_SPEC, shaped(rows, width)), (ANY_SPEC, shaped(rows, width, dtype=F32))
    act_out = (ANY_SPEC, shaped(rows, blocks * width))
    down_part = (ANY_SPEC, shaped(4, 2, deep, width))
    up_part = (ANY_SPEC, shaped(blocks, 4, 2, each, width))

    act_spec = pl.BlockSpec((fold * tile, blocks * width), lambda i, *me: (i, 0))
    wide_spec = whole_spec((hidden // 2, width))

    def run_mlp(me, tokens_of, bup, sources):
        sets = len(tokens_of[0])
        low, high = pltpu.VMEM((sets * rows, width), BF16), pltpu.VMEM((sets * rows, width), F32)
        weight = pltpu.VMEM((2, width, width), BF16)
        dma = pltpu.SemaphoreType.DMA((2, sets))
        return call_with(
            me, functools.partial(mlp, sets, len(sources)), blocks,
            [ANY_SPEC] * (2 * sets) + [hidden_spec] + [ANY_SPEC] * len(sources),
            [act_out] * sets + [high_out] + [low_out] * (sets - 1) + [down_part] * 2 + [up_part] * 2
            + [(ANY_SPEC, shaped(hidden // 2, width)), (hidden_spec, shaped(1, hidden // 2, dtype=F32))],
            [low, low, high, pltpu.VMEM((blocks, sets * rows, width), BF16), low, low, weight, weight,
             pltpu.VMEM((blocks, width, width), BF16), pltpu.VMEM((hidden // 2, width), BF16), dma,
             pltpu.SemaphoreType.DMA((blocks, sets)), pltpu.SemaphoreType.DMA((sets,)), pltpu.SemaphoreType.DMA((4,)),
             pltpu.SemaphoreType.DMA((blocks + 1,))],
            "mlp", 0, *tokens_of[0], *tokens_of[1], bup, *sources)

    if by_hand:
        act_own, act_other, gtwo, gtwo_other, down_own, down_send, up_own, up_send, wdown, sum_up = run_mlp(
            me, ((n2, n2_other), (cot, cot_other)), bup, hidden_weights[0])
        gtwo_take = swap(gtwo_other, other_core)
        parts = (-1, CHIPS // 4, 2)
        down_first = [piece.reshape(*parts, deep, width) for piece in (down_own, swap(down_send, first_plane))]
        up_first = [piece.reshape(*parts, each, width) for piece in (up_own, swap(up_send, first_plane))]
    else:
        runs = [run_mlp(me + half, ((n2,), (cot,)), bup[half], hidden_weights[half]) for half in range(2)]
        (act_own, gtwo), (act_other, gtwo_take) = ((run[0], run[1]) for run in runs)
        gtwo_take = gtwo_take.astype(BF16)
        sum_up = jnp.concatenate([run[7] for run in runs], axis=1)
    grads_spec = pl.BlockSpec((4, tile, width), lambda i, *me: (0, i, 0))
    grads, gresid, sum_back = call(
        attention_backward, (tiles,),
        [SMEM, tile_rows, tile_rows, tile_rows, lse_spec, tile_rows, tile_rows, tile_rows, tile_rows, vec_spec, square],
        [(grads_spec, shaped(4, rows, width)), high_rows, sums], [pltpu.VMEM((tile, width), BF16)],
        "attention_backward", 0, lengths, q, k, v, lse, cot, resid, gtwo, gtwo_take, vec, wo)
    sum_spec = whole_spec((8, width))
    pair_shape = (CHIPS // 4, 4, 4 * each + 16, side)
    columns = pl.BlockSpec((1, rows, width), lambda i, me: (i, 0, 0))

    def run_weights(grads):
        return call_with(
            me, weight_grads, 4, [full_rows, ANY_SPEC, columns, sum_spec, sum_spec, whole_spec((1, sum_up.shape[1]))],
            [(ANY_SPEC, shaped(*pair_shape))] * 2,
            [pltpu.VMEM(pair_shape, BF16)] * 2
            + [pltpu.VMEM((rows, width), BF16), pltpu.SemaphoreType.DMA((1,)), pltpu.SemaphoreType.DMA((2, 5))],
            "weight_grads", 0,
            n1, mixed, grads, sum_back, sum_down, sum_up)

    def run_tokens(gresid):
        return call(
            tokens_backward, (tiles // fold,),
            [wide_rows, wide_rows, vec_spec, pl.BlockSpec((4, fold * tile, width), lambda i: (0, i, 0)), square, square, square],
            [wide_low, sums], [], "tokens_backward", MIDDLE, tokens, gresid, vec, grads, wq, wk, wv)

    if by_hand:
        (out_other,) = call_with(
            me, mlp_out_other, tiles // fold, [act_spec, wide_spec], [wide_low], [], "mlp_out_other", 0, after(act_other, grads), wdown)
        down_first, up_first = after((down_first, up_first), out_other)
        hidden_rest, hidden_take = scatter_second(*down_first, *up_first)

        def weights_of_chip(grads, out_take):
            square_send, square_keep = run_weights(grads)
            (out,) = call_with(
                me, mlp_out_own, tiles // fold, [wide_rows, vec_spec, act_spec, wide_rows, wide_spec], [wide_low], [],
                "mlp_out_own", 0, resid, vec, act_own, after(out_take, square_send), wdown)
            square_take = after(scatter_core(square_send), out)
            return *merge_core_of(core, square_keep, square_take), out

        out_take = swap(out_other, other_core)
        square_own, square_send, out = fenced(weights_of_chip, after(grads, hidden_rest), out_take)
        square_take = swap(square_send, first_plane).reshape(square_own.shape)
        hidden_rest, hidden_take = after((hidden_rest, hidden_take), square_own)
        hidden_layers = scatter_layers(hidden_rest, hidden_take)
        gtok, late = run_tokens(after(gresid, hidden_layers[0]))
        square_take = after(square_take, late)
        late = late + swap(late, other_core)
        square_second = scatter_second(square_own, square_take)
        late = after(late, square_second[0])
        late = late + swap(late, other_layer(1))
        hidden_layers = after(hidden_layers, late)
        g_down, up_keep, up_send = scatter_last(core, hidden_layers, own, blocks, deep)
        up_take = scatter_core(up_send)
        late_take = after(swap(late, other_layer(2)), g_down)
        square_second = after(square_second, g_down)
        rest, *sends = merge_layers_of(*square_second)
        rest, sends, late_take = after((rest, sends, late_take))
        square_layers = [rest] + [swap(piece, other_layer(r + 1)) for r, piece in enumerate(sends)]
        late = late + late_take
        late = late + after(swap(late, other_plane(1)), rest)
        late = late + swap(late, other_plane(2))
        square_layers = after(square_layers, late)
        square_keep, square_send, flat = scatter_last(core, square_layers, own, 4, 0)
        square_take = scatter_core(square_send)
        outs = [(VMEM_SPEC, shaped(own, hidden, dtype=F32))] + [(VMEM_SPEC, shaped(own, width, dtype=F32))] * 4
        outs += [(VMEM_SPEC, shaped(own, dtype=F32))] * 8 + [(VMEM_SPEC, shaped(folds * own, dtype=F32))]
        g_up, g_q, g_k, g_v, g_o, *g_flat, g_ub = small_call(
            finish, (me, up_keep, up_take, square_keep, square_take, flat, late), outs, "finish",
            ins=[SMEM] + [VMEM_SPEC] * 6)
    else:
        square_send, square_keep = run_weights(grads)
        gtok, sum_one = run_tokens(gresid)
        flat = jnp.concatenate((sum_one[0:2], sum_back[0:5], sum_down[0:1]), axis=0)
        flat = flat.reshape(8, count, own).transpose(1, 0, 2).reshape(count, 8 * own)
        hidden_sums = sum_up.reshape(2, CHIPS, deep).transpose(1, 0, 2).reshape(count, folds * own)
        flat = jnp.concatenate((flat, hidden_sums), axis=1)
        g_down, g_up, g_q, g_k, g_v, g_o, flat = reduce_plain(
            [run[2:4] for run in runs], [run[4:6] for run in runs], (square_keep, square_send), flat)
        (out_other,) = call_with(
            me + 1, mlp_out_other, tiles // fold, [act_spec, wide_spec], [wide_low], [], "mlp_out_other", 0, act_other, runs[1][6])
        (out,) = call_with(
            me, mlp_out_own, tiles // fold, [wide_rows, vec_spec, act_spec, wide_rows, wide_spec], [wide_low], [],
            "mlp_out_own", 0, resid, vec, act_own, out_other, runs[0][6])
        g_flat = [flat[index * own : (index + 1) * own] for index in range(8)]
        g_ub = flat[8 * own :]
    g_gain, g_shift, g_qb, g_vb, g_ob, g_mg, g_ms, g_db = g_flat
    return (out, gtok, g_gain, g_shift, g_q, g_qb, g_k, g_v, g_vb, g_o, g_ob, g_mg, g_ms, g_up, g_ub, g_down, g_db)


def solution(mesh):
    rows, flat = P("dp", None), P("dp")
    return jax.shard_map(
        body,
        mesh=mesh,
        in_specs=(rows, rows, flat, flat, rows, flat, rows, rows, flat, rows, flat, flat, flat, rows, flat, rows, flat, rows),
        out_specs=(rows, rows, flat, flat, rows, flat, rows, rows, flat, rows, flat, flat, flat, rows, flat, rows, flat),
        check_vma=False,
    )
```

```python
import functools

import jax
import jax.numpy as jnp
from jax import lax
from jax.experimental import pallas as pl
from jax.experimental.pallas import tpu as pltpu
from jax.sharding import PartitionSpec as P

HEADS = 12
HEAD_DIM = 64
PAIRS = 6
LANES = 128
CHIPS = 16
PARTS = 2
MERGE_STEPS = 2
LONG = 10**11
SHORT = 6 * 10**9
MIDDLE = 115 * 10**8
LATER = 9 * 10**9
EPS = 1e-06
MASKED = -1e30
SCALE = HEAD_DIM**-0.5
GELU_C = 0.7978845608028654
GELU_A = 0.044715
VMEM = 64 * 1024 * 1024 - 65536
F32 = jnp.float32
BF16 = jnp.bfloat16


def dot_nn(left, right):
    return lax.dot_general(left, right, (((1,), (0,)), ((), ())), preferred_element_type=F32)


def dot_nt(left, right):
    return lax.dot_general(left, right, (((1,), (1,)), ((), ())), preferred_element_type=F32)


def dot_tn(left, right):
    return lax.dot_general(left, right, (((0,), (0,)), ((), ())), preferred_element_type=F32)


def normalize(rows):
    centered = rows - jnp.mean(rows, axis=-1, keepdims=True)
    inverse = lax.rsqrt(jnp.mean(centered * centered, axis=-1, keepdims=True) + EPS)
    return centered * inverse, inverse


def norm_back(grads, gain, hat, inverse):
    scaled = grads * gain
    mean = jnp.mean(scaled, axis=-1, keepdims=True)
    mean_hat = jnp.mean(scaled * hat, axis=-1, keepdims=True)
    return inverse * (scaled - mean - hat * mean_hat)


def column_sum(rows):
    return jnp.sum(rows, axis=0, keepdims=True)


def segments(lengths_ref, tile, slots, rows, axis):
    shape = (rows, 1) if axis == 0 else (1, rows)
    index = lax.broadcasted_iota(jnp.int32, shape, axis)
    segment = jnp.zeros(shape, jnp.int32)
    bound = 0
    for slot in range(slots):
        bound = bound + lengths_ref[tile, slot]
        segment = segment + (index >= bound).astype(jnp.int32)
    return segment


def mask_bias(lengths_ref, tile, slots, rows):
    same = segments(lengths_ref, tile, slots, rows, 0) == segments(lengths_ref, tile, slots, rows, 1)
    return jnp.where(same, 0.0, MASKED).astype(F32)


def half_of(pair, side):
    lane = lax.broadcasted_iota(jnp.int32, pair.shape, 1)
    keep = lane < HEAD_DIM if side == 0 else lane >= HEAD_DIM
    return jnp.where(keep, pair, jnp.zeros_like(pair))


def fetch_weights(me, sources, stage_ref, sem):
    core, chip = me & 1, me >> 1
    side = sources[0].shape[3]
    for index, source in enumerate(sources):
        half = core if index < 4 else 1 - core
        plane = (0, 1 + half, 2 - half, 3)[index % 4]
        cols = pl.ds(pl.multiple_of(half * side, LANES), side)
        for layer in range(4):
            owner = chip ^ (4 * layer + plane)
            pltpu.make_async_copy(source.at[layer], stage_ref.at[owner, :, :, cols], sem.at[0]).start()


def project(me_ref, x_ref, *refs):
    sources = refs[:8]
    n1_ref, q_ref, k_ref, v_ref = refs[8:12]
    outs, (vec_ref, bup_ref, weights_ref, stage_ref, sem, out_sem) = refs[12:16], refs[16:]
    step = pl.program_id(0)
    core = me_ref[0] & 1
    weights = [weights_ref.at[number] for number in range(4)]

    def write(number):
        return pltpu.make_async_copy(weights[number], outs[number], out_sem.at[number])

    @pl.when(step == 0)
    def _():
        fetch_weights(me_ref[0], sources, stage_ref, sem)
        pltpu.make_async_copy(stage_ref, stage_ref, sem.at[0]).wait()
        width = stage_ref.shape[3]
        side = width // 2
        blocks = width // (16 * CHIPS)
        for number in range(4):
            weights[number][...] = stage_ref[:, number * blocks : (number + 1) * blocks].reshape(width, width)
            write(number).start()
        parts = [stage_ref[chip, 4 * blocks].astype(F32) for chip in range(CHIPS)]
        halves = []
        for half in range(2):
            group = parts[half * CHIPS // 2 : (half + 1) * CHIPS // 2]
            halves.append(sum(part[:, :side] + part[:, side:] for part in group))
        vec_ref[...] = jnp.concatenate(halves, axis=1)
        blocks = bup_ref.shape[1] // side
        group = CHIPS // blocks
        for block in range(blocks):
            rows = sum(parts[block * group : (block + 1) * group])
            bup_ref[:, block * side : (block + 1) * side] = jnp.where(core == 0, rows[8:9, :side], rows[8:9, side:])

    project_rows(x_ref, vec_ref, *weights[:3], n1_ref, q_ref, k_ref, v_ref)

    @pl.when(step == pl.num_programs(0) - 1)
    def _():
        for number in range(4):
            write(number).wait()


def project_rows(x_ref, vec_ref, wq_ref, wk_ref, wv_ref, n1_ref, q_ref, k_ref, v_ref):
    hat, _ = normalize(x_ref[...].astype(F32))
    n1 = (hat * vec_ref[0:1, :] + vec_ref[1:2, :]).astype(BF16)
    n1_ref[...] = n1
    q_ref[...] = (dot_nn(n1, wq_ref[...]) + vec_ref[2:3, :]).astype(BF16) * jnp.asarray(SCALE, BF16)
    k_ref[...] = dot_nn(n1, wk_ref[...]).astype(BF16)
    v_ref[...] = (dot_nn(n1, wv_ref[...]) + vec_ref[3:4, :]).astype(BF16)


def mask_grads(lengths_ref, grad_ref, cot_ref, dsum_ref):
    tile = pl.program_id(0)
    slots = lengths_ref.shape[1]
    valid = segments(lengths_ref, tile, slots, grad_ref.shape[0], 0) < slots
    cot = jnp.where(valid, grad_ref[...].astype(F32), 0.0)
    cot_ref[...] = cot.astype(BF16)

    @pl.when(tile == 0)
    def _():
        dsum_ref[...] = jnp.zeros_like(dsum_ref)

    dsum_ref[0:1, :] += column_sum(cot)


def attention_forward(lengths_ref, x_ref, vec_ref, q_ref, k_ref, v_ref, wo_ref, mixed_ref, lse_ref, resid_ref, *n2_refs):
    tile = pl.program_id(0)
    rows = q_ref.shape[0]
    slots = lengths_ref.shape[1]
    bias = mask_bias(lengths_ref, tile, slots, rows)
    lane = lax.broadcasted_iota(jnp.int32, (rows, LANES), 1)
    lse = jnp.zeros((rows, LANES), F32)

    def at(pair):
        return pl.ds(pair * LANES, LANES)

    def scores_of(pair):
        qp, kp = q_ref[:, at(pair)], k_ref[:, at(pair)]
        return [dot_nt(half_of(qp, side), kp) for side in range(2)]

    def softmax_of(scores):
        scores = scores + bias
        top = jnp.max(scores, axis=-1, keepdims=True)
        weights = jnp.exp(scores - top)
        sums = jnp.sum(weights, axis=-1, keepdims=True)
        return (weights * (1.0 / sums)).astype(BF16), top + jnp.log(sums)

    raw = {}
    probs = {}
    for turn in range(PAIRS + 2):
        if turn < PAIRS:
            raw[turn] = scores_of(turn)
        if 0 <= turn - 1 < PAIRS:
            both = [softmax_of(scores) for scores in raw.pop(turn - 1)]
            for side in range(2):
                lse = jnp.where(lane == 2 * (turn - 1) + side, both[side][1], lse)
            probs[turn - 1] = [pair[0] for pair in both]
        if turn >= 2:
            vp = v_ref[:, at(turn - 2)]
            parts = [dot_nn(probs[turn - 2][side], half_of(vp, side)) for side in range(2)]
            mixed_ref[:, at(turn - 2)] = (parts[0] + parts[1]).astype(BF16)
    lse_ref[...] = lse
    resid = x_ref[...].astype(F32) + (dot_nn(mixed_ref[...], wo_ref[...]) + vec_ref[4:5, :])
    resid_ref[...] = resid
    hat, _ = normalize(resid)
    normed = (hat * vec_ref[5:6, :] + vec_ref[6:7, :]).astype(BF16)
    share = pl.num_programs(0) // len(n2_refs)
    for number, ref in enumerate(n2_refs):

        @pl.when(tile // share == number)
        def _():
            ref[...] = normed


def spread(me, rows, put):
    layer, plane = me >> 3, (me >> 1) & 3
    each = rows.shape[0] // CHIPS
    for chip in range(CHIPS):
        put((chip & 3) ^ plane, (chip >> 2) ^ layer, rows[chip * each : (chip + 1) * each].astype(BF16))


def fetch_hidden(me, sources, wup_ref, wdown_ref, sem):
    if len(sources) == 2:
        for number in range(wup_ref.shape[0]):
            pltpu.make_async_copy(sources[0].at[number], wup_ref.at[number], sem.at[number]).start()
        pltpu.make_async_copy(sources[1], wdown_ref, sem.at[wup_ref.shape[0]]).start()
        return
    core, chip = me & 1, me >> 1
    planes = (0, 1 + core, 2 - core, 3)
    blocks, width = wup_ref.shape[:2]
    each, deep = width // CHIPS, wdown_ref.shape[0] // CHIPS
    for layer in range(4):
        for index, plane in enumerate(planes):
            owner = chip ^ (4 * layer + plane)
            ref, at_layer = sources[min(index, 2)], layer + 4 * max(index - 2, 0)
            rows = pl.ds(pl.multiple_of(owner * each, 16), each)
            side = ref.shape[2]
            for part in range(ref.shape[1] // each):
                number, cols = part * side // width, pl.ds(part * side % width, side)
                pltpu.make_async_copy(
                    ref.at[at_layer, pl.ds(part * each, each), :], wup_ref.at[number, rows, cols], sem.at[number]
                ).start()
            source = sources[3 + layer // 2].at[2 * index + layer % 2]
            rows = pl.ds(pl.multiple_of(owner * deep, 16), source.shape[0])
            pltpu.make_async_copy(source, wdown_ref.at[rows, :], sem.at[blocks]).start()
            rest = deep - source.shape[0]
            rows = pl.ds(pl.multiple_of(owner * deep + source.shape[0], 16), rest)
            for part in range(width // side):
                at = pl.ds(ref.shape[1] - (width // side - part) * rest, rest)
                pltpu.make_async_copy(
                    ref.at[at_layer, at, :], wdown_ref.at[rows, pl.ds(part * side, side)], sem.at[blocks]
                ).start()


def mlp(sets, count, me_ref, *refs):
    n2_hbm, refs = [refs[:PARTS], refs[PARTS : 2 * PARTS]][:sets], refs[PARTS * sets :]
    cot_hbm, bup_ref = refs[:sets], refs[sets]
    sources = refs[sets + 1 : sets + 1 + count]
    refs = refs[sets + 1 + count :]
    act_hbm, gtwo_hbm, refs = refs[:sets], refs[sets : 2 * sets], refs[2 * sets :]
    down_own, down_send, up_own, up_send, wdown_hbm, dbu_ref = refs[:6]
    n2_ref, cot_ref, gacc, act_ref, gup_ref, low_ref, gdown_ref, gupw_ref = refs[6:14]
    wup_all, wdown_all, in_sem, act_sem, out_sem, grad_sem, weight_sem = refs[14:]
    step = pl.program_id(0)
    last = pl.num_programs(0) - 1
    me = me_ref[0]
    rows = n2_ref.shape[0] // sets

    def rows_of(index):
        return pl.ds(pl.multiple_of(index * rows, rows), rows)

    blocks, width = wup_all.shape[:2]

    @pl.when(step == 0)
    def _():
        fetch_hidden(me, sources, wup_all, wdown_all, weight_sem)
        for index in range(sets):
            at = pl.ds(index * rows, rows)
            part = rows // len(n2_hbm[index])
            for number, ref in enumerate(n2_hbm[index]):
                piece = pl.ds(index * rows + number * part, part)
                pltpu.make_async_copy(ref, n2_ref.at[piece, :], in_sem.at[0, index]).start()
            pltpu.make_async_copy(cot_hbm[index], cot_ref.at[at, :], in_sem.at[1, index]).start()

    pltpu.make_async_copy(wup_all.at[step], wup_all.at[step], weight_sem.at[step]).wait()
    write_down = pltpu.make_async_copy(wdown_all, wdown_hbm, weight_sem.at[blocks])

    @pl.when(step == 0)
    def _():
        pltpu.make_async_copy(wdown_all, wdown_all, weight_sem.at[blocks]).wait()
        write_down.start()

    wup = wup_all[step]
    wdown = wdown_all[pl.ds(pl.multiple_of(step * width, width), width), :]
    dbu_ref[...] = jnp.zeros_like(dbu_ref)
    slot = lax.rem(step, 2)

    @pl.loop(0, sets)
    def _(index):
        at = rows_of(index)

        @pl.when(step == 0)
        def _():
            pltpu.make_async_copy(n2_ref.at[at, :], n2_ref.at[at, :], in_sem.at[0, index]).wait()
            pltpu.make_async_copy(cot_ref.at[at, :], cot_ref.at[at, :], in_sem.at[1, index]).wait()

        pre = dot_nn(n2_ref[at, :], wup) + bup_ref[...]
        grad_act = dot_nt(cot_ref[at, :], wdown)
        square = pre * pre
        tanh = jnp.tanh(pre * (GELU_C + (GELU_C * GELU_A) * square))
        half = 0.5 + 0.5 * tanh
        inner = GELU_C + (3.0 * GELU_C * GELU_A) * square
        act_ref[slot, at, :] = (pre * half).astype(BF16)
        gup = (grad_act * (half + (0.5 * pre) * (1.0 - tanh * tanh) * inner)).astype(BF16)
        gup_ref[at, :] = gup
        dbu_ref[...] += column_sum(gup.astype(F32))

    @pl.when(step == 0)
    def _():
        @pl.loop(0, sets)
        def _(index):
            at = rows_of(index)
            gacc[at, :] = dot_nt(gup_ref[at, :], wup)

    @pl.when((step > 0) & (step < last))
    def _():
        @pl.loop(0, sets)
        def _(index):
            at = rows_of(index)
            gacc[at, :] += dot_nt(gup_ref[at, :], wup)

    def results():
        for index in range(sets):
            at = pl.ds(index * rows, rows)
            source = low_ref.at[at, :] if index else gacc.at[at, :]
            yield pltpu.make_async_copy(source, gtwo_hbm[index], out_sem.at[index])

    def activations(number):
        for index in range(sets):
            source = act_ref.at[number, pl.ds(index * rows, rows), :]
            cols = pl.ds(number * width, width)
            yield pltpu.make_async_copy(source, act_hbm[index].at[:, cols], act_sem.at[number, index])

    for number in range(act_ref.shape[0]):

        @pl.when(step == number)
        def _():
            for copy in activations(number):
                copy.start()

    @pl.when(step == last)
    def _():
        @pl.loop(0, sets)
        def _(index):
            at = rows_of(index)
            total = gacc[at, :] + dot_nt(gup_ref[at, :], wup)
            gacc[at, :] = total
            low_ref[at, :] = total.astype(BF16)

        for copy in results():
            copy.start()

    gdown_ref[slot] = dot_tn(act_ref[slot], cot_ref[...]).astype(BF16)
    deep = down_own.shape[2]
    count = gdown_ref.shape[1] // deep
    for index in range(count):
        chip = step * count + index
        source = gdown_ref.at[slot, pl.ds(index * deep, deep), :]
        keep_or_send(me, chip & 3, (chip >> 2) ^ (me >> 3), source, down_own, down_send, grad_sem, 0)

    gupw_ref[slot] = dot_tn(n2_ref[...], gup_ref[...]).astype(BF16)
    each = gupw_ref.shape[1] // CHIPS
    for chip in range(CHIPS):
        source = gupw_ref.at[slot, pl.ds(chip * each, each), :]
        keep_or_send(
            me, chip & 3, (chip >> 2) ^ (me >> 3), source, up_own.at[step], up_send.at[step], grad_sem, 2)

    @pl.when(step == last)
    def _():
        for copy in results():
            copy.wait()
        write_down.wait()
        for number in range(act_ref.shape[0]):
            for copy in activations(number):
                copy.wait()
        for number, ref in enumerate((down_own, down_send, up_own, up_send)):
            pltpu.make_async_copy(ref, ref, grad_sem.at[number]).wait()


def keep_or_send(me, plane, layer, source, own_ref, send_ref, sem, number):
    core = me & 1
    relative = plane ^ ((me >> 1) & 3)
    mine = (relative == 0) | (relative == 2 - core)

    @pl.when(mine)
    def _():
        pltpu.make_async_copy(source, own_ref.at[layer, jnp.where(relative == 0, 0, 1)], sem.at[number]).start()

    @pl.when(jnp.logical_not(mine))
    def _():
        pltpu.make_async_copy(source, send_ref.at[layer, jnp.where(relative == 3, 1, 0)], sem.at[number + 1]).start()


def mlp_out_other(me_ref, act_ref, wdown_ref, out_ref):
    out_ref[...] = dot_nn(act_ref[...], wdown_ref[...]).astype(BF16)


def mlp_out_own(me_ref, resid_ref, vec_ref, act_ref, take_ref, wdown_ref, out_ref):
    half = dot_nn(act_ref[...], wdown_ref[...]) + take_ref[...].astype(F32)
    out_ref[...] = (resid_ref[...] + (half + vec_ref[7:8, :])).astype(BF16)


def attention_backward(lengths_ref, q_ref, k_ref, v_ref, lse_ref, cot_ref, resid_ref, gtwo_ref, gother_ref, vec_ref, wo_ref,
                       grads_ref, gresid_ref, dsum_ref, gmix_ref):
    tile = pl.program_id(0)
    rows = q_ref.shape[0]

    @pl.when(tile == 0)
    def _():
        dsum_ref[...] = jnp.zeros_like(dsum_ref)

    hat, inverse = normalize(resid_ref[...])
    grad_two = gtwo_ref[...] + gother_ref[...].astype(F32)
    gresid = cot_ref[...].astype(F32) + norm_back(grad_two, vec_ref[5:6, :], hat, inverse)
    gresid_ref[...] = gresid
    gattn = gresid.astype(BF16)
    grads_ref[3] = gattn
    dsum_ref[2:3, :] += column_sum(gattn.astype(F32))
    dsum_ref[3:4, :] += column_sum(grad_two * hat)
    dsum_ref[4:5, :] += column_sum(grad_two)
    gmix_ref[...] = dot_nt(gattn, wo_ref[...]).astype(BF16)
    bias = mask_bias(lengths_ref, tile, lengths_ref.shape[1], rows)

    def load(pair):
        cols = pl.ds(pair * LANES, LANES)
        return q_ref[:, cols], k_ref[:, cols], v_ref[:, cols], gmix_ref[:, cols]

    def products_of(pair):
        qp, kp, vp, gp = load(pair)
        return [(dot_nt(half_of(qp, side), kp), dot_nt(half_of(gp, side), vp)) for side in range(2)]

    def softmax_back(pair, products):
        results = []
        for side, (scores, grad_probs) in enumerate(products):
            head = 2 * pair + side
            probs = jnp.exp(scores + bias - lse_ref[:, head : head + 1])
            weighted = probs * grad_probs
            dot = jnp.sum(weighted, axis=-1, keepdims=True)
            results.append((probs.astype(BF16), (weighted - probs * dot).astype(BF16)))
        return results

    def store(pair, results):
        qp, kp, vp, gp = load(pair)
        dq = sum(dot_nn(results[side][1], half_of(kp, side)) for side in range(2))
        dk = sum(dot_tn(results[side][1], half_of(qp, side)) for side in range(2))
        dv = sum(dot_tn(results[side][0], half_of(gp, side)) for side in range(2))
        cols = pl.ds(pair * LANES, LANES)
        grads_ref[0, :, cols] = (dq * SCALE).astype(BF16)
        grads_ref[1, :, cols] = dk.astype(BF16)
        grads_ref[2, :, cols] = dv.astype(BF16)

    raw = {}
    done = {}
    for turn in range(PAIRS + 2):
        if turn < PAIRS:
            raw[turn] = products_of(turn)
        if 0 <= turn - 1 < PAIRS:
            done[turn - 1] = softmax_back(turn - 1, raw.pop(turn - 1))
        if turn >= 2:
            store(turn - 2, done.pop(turn - 2))

    dsum_ref[0:1, :] += column_sum(grads_ref[0].astype(F32))
    dsum_ref[1:2, :] += column_sum(grads_ref[2].astype(F32))


def weight_grads(me_ref, n1_ref, mixed_hbm, columns_ref, sum_back_ref, sum_down_ref, sum_up_ref, send_hbm, keep_hbm,
                 send_ref, keep_ref, mixed_ref, in_sem, out_sem):
    step = pl.program_id(0)
    me = me_ref[0]
    first = (me & 1) == 0
    side = send_ref.shape[3]
    each = n1_ref.shape[1] // CHIPS
    load = pltpu.make_async_copy(mixed_hbm, mixed_ref, in_sem.at[0])

    def writes(number):
        rows = pl.ds(number * each, each if number < 4 else 16)
        for index, (ref, out) in enumerate(((send_ref, send_hbm), (keep_ref, keep_hbm))):
            yield pltpu.make_async_copy(ref.at[:, :, rows, :], out.at[:, :, rows, :], out_sem.at[index, number])

    @pl.when(step == 0)
    def _():
        load.start()

    def run(left, number):
        result = dot_tn(left, columns_ref[0])
        low, high = result[:, :side], result[:, side:]
        rows_at = pl.ds(pl.multiple_of(number * each, 16), each)

        def put_send(plane, layer, rows):
            send_ref[layer, plane, rows_at, :] = rows

        def put_keep(plane, layer, rows):
            keep_ref[layer, plane, rows_at, :] = rows

        spread(me, jnp.where(first, high, low), put_send)
        spread(me, jnp.where(first, low, high), put_keep)

    @pl.when(step < 3)
    def _():
        run(n1_ref[...], step)

    for number in range(3):

        @pl.when(step == number)
        def _():
            for copy in writes(number):
                copy.start()

    @pl.when(step == 3)
    def _():
        nothing = jnp.zeros((2, n1_ref.shape[1]), F32)
        vecs = jnp.concatenate((nothing, sum_back_ref[0:5], sum_down_ref[0:1]), axis=0)
        for chip in range(CHIPS):
            half = chip // (CHIPS // 2)
            block = chip * (sum_up_ref.shape[1] // side) // CHIPS
            last = jnp.broadcast_to(sum_up_ref[:, block * side : (block + 1) * side], (8, side))
            short = vecs[:, half * side : (half + 1) * side]
            at = ((chip >> 2) ^ (me >> 3), (chip & 3) ^ ((me >> 1) & 3))
            keep_ref[at[0], at[1], 4 * each :, :] = jnp.concatenate((short, last), axis=0).astype(BF16)
            send_ref[at[0], at[1], 4 * each :, :] = jnp.concatenate((short, jnp.zeros_like(last)), axis=0).astype(BF16)
        for copy in writes(4):
            copy.start()
        load.wait()
        run(mixed_ref[...], 3)
        for copy in writes(3):
            copy.start()
        for number in range(5):
            for copy in writes(number):
                copy.wait()


def tokens_backward(x_ref, gresid_ref, vec_ref, grads_ref, wq_ref, wk_ref, wv_ref, gtok_ref, dsum_ref):
    @pl.when(pl.program_id(0) == 0)
    def _():
        dsum_ref[...] = jnp.zeros_like(dsum_ref)

    grad_one = dot_nt(grads_ref[0], wq_ref[...]) + dot_nt(grads_ref[1], wk_ref[...]) + dot_nt(grads_ref[2], wv_ref[...])
    hat, inverse = normalize(x_ref[...].astype(F32))
    gtok_ref[...] = (gresid_ref[...] + norm_back(grad_one, vec_ref[0:1, :], hat, inverse)).astype(BF16)
    dsum_ref[0:1, :] += column_sum(grad_one * hat)
    dsum_ref[1:2, :] += column_sum(grad_one)


def rows_spec(block, width):
    return pl.BlockSpec((block, width), lambda i, *me: (i, 0))


def cols_spec(height, block):
    return pl.BlockSpec((height, block), lambda i, *me: (0, i))


def whole_spec(shape):
    return pl.BlockSpec(shape, lambda *i: (0,) * len(shape), pipeline_mode=pl.Buffered(1))


def kept_spec(shape):
    return pl.BlockSpec(shape, lambda *i: (0,) * len(shape))


SMEM = pl.BlockSpec(memory_space=pltpu.SMEM)


def cost(flops):
    return pl.CostEstimate(flops=flops, bytes_accessed=1, transcendentals=0)


def call(kernel, grid, ins, outs, scratch, name, flops, *args):
    out_specs = tuple(spec for spec, _ in outs)
    out_shape = tuple(shape for _, shape in outs)
    return pl.pallas_call(
        kernel,
        grid=grid,
        in_specs=ins,
        out_specs=out_specs,
        out_shape=out_shape,
        scratch_shapes=scratch,
        compiler_params=pltpu.CompilerParams(vmem_limit_bytes=VMEM, dimension_semantics=("arbitrary",) * len(grid)),
        cost_estimate=cost(flops),
        name=name,
    )(*args)


def call_with(me, kernel, steps, ins, outs, scratch, name, flops, *args):
    out_shape = tuple(shape for _, shape in outs)
    return pl.pallas_call(
        kernel,
        grid_spec=pltpu.PrefetchScalarGridSpec(
            num_scalar_prefetch=1, grid=(steps,), in_specs=ins, out_specs=tuple(spec for spec, _ in outs),
            scratch_shapes=scratch),
        out_shape=out_shape,
        compiler_params=pltpu.CompilerParams(vmem_limit_bytes=VMEM, dimension_semantics=("arbitrary",)),
        cost_estimate=cost(flops),
        name=name,
    )(me, *args)


def shaped(*shape, dtype=BF16):
    return jax.ShapeDtypeStruct(shape, dtype)


def flipped(count, change):
    pairs = []
    for source in range(count):
        core, chip = source & 1, source >> 1
        core, chip = change(core, chip)
        pairs.append((source, 2 * chip + core))
    return pairs


def swap(array, change):
    return lax.ppermute(array, "dp", flipped(lax.axis_size("dp"), change))


def other_core(core, chip):
    return core ^ 1, chip


def first_plane(core, chip):
    return core, chip ^ (1 + core)


def second_plane(core, chip):
    return core, chip ^ (2 - core)


def other_plane(distance):
    return lambda core, chip: (core, chip ^ distance)


def other_layer(distance):
    return lambda core, chip: (core, chip ^ (4 * distance))


def split_shards(core_ref, q_ref, k_ref, v_ref, o_ref, u_ref, d_ref, keep_ref, send_ref, down_ref):
    down_ref[...] = d_ref[: down_ref.shape[0], :]
    width = q_ref.shape[1]
    side = width // 2
    first = core_ref[0] == 0

    def put(index, low, high):
        keep_ref[index] = jnp.where(first, low, high).astype(BF16)
        send_ref[index] = jnp.where(first, high, low).astype(BF16)

    for index, ref in enumerate((q_ref, k_ref, v_ref, o_ref)):
        rows = ref[...].astype(F32)
        put(index, rows[:, :side], rows[:, side:])
    up = u_ref[...].astype(F32)
    hidden = up.shape[1]
    deep = hidden // (2 * CHIPS)
    halves = [
        jnp.concatenate([up[:, start : start + deep] for start in range(half * deep, hidden, 2 * deep)], axis=1)
        for half in range(2)
    ]
    for part in range(hidden // width):
        at = slice(part * side, (part + 1) * side)
        put(4 + part, halves[0][:, at], halves[1][:, at])


def join_shards(me_ref, keep_ref, take_ref, down_ref, *refs):
    vectors, (near_ref, up_ref) = refs[:-2], refs[-2:]
    me = me_ref[0]
    first = (me & 1) == 0
    parts, own, side = keep_ref.shape
    folds = parts - 4
    keep = keep_ref[...].astype(F32)
    take = take_ref[...].astype(F32)

    def joined(index):
        low = jnp.where(first, keep[index], take[index])
        high = jnp.where(first, take[index], keep[index])
        return jnp.concatenate((low, high), axis=0).astype(BF16)

    for index in range(4):
        near_ref[2 * own * index : 2 * own * (index + 1), :] = joined(index)
    for index in range(folds):
        up_ref[2 * own * index : 2 * own * (index + 1), :] = joined(4 + index)
    base = 2 * own * folds
    up_ref[base : base + 16, :] = down_ref[-16:, :side]
    up_ref[base + 16 :, :] = down_ref[-16:, side:]
    rows = []
    for ref in vectors:
        flat = ref[...].astype(F32).reshape(1, -1)
        rows.append(jnp.concatenate((flat, jnp.zeros((1, side - flat.shape[1]), F32)), axis=1))
    rows.append(jnp.zeros((16 - len(rows), side), F32))
    rows = jnp.concatenate(rows, axis=0)
    short = pltpu.roll(rows, own * lax.rem(me, side // own), 1)
    long = pltpu.roll(rows, folds * own * lax.rem(me >> 1, side // (folds * own)), 1)
    index = lax.broadcasted_iota(jnp.int32, rows.shape, 0)
    near_ref[8 * own :, :] = jnp.where(index < 8, short, long).astype(BF16)


def across_layers(shard):
    return jnp.stack([shard] + [swap(shard, other_layer(distance)) for distance in (1, 2, 3)])


def after(arrays, *others):
    return lax.optimization_barrier((arrays, others))[0]


def small_call(kernel, args, outs, name, scratch=(), ins=None, flops=0):
    return pl.pallas_call(
        kernel,
        in_specs=ins,
        out_specs=tuple(spec for spec, _ in outs),
        out_shape=tuple(shape for _, shape in outs),
        scratch_shapes=list(scratch),
        compiler_params=pltpu.CompilerParams(vmem_limit_bytes=VMEM),
        cost_estimate=cost(flops),
        name=name,
    )(*args)


VMEM_SPEC = pl.BlockSpec(memory_space=pltpu.VMEM)
ANY_SPEC = pl.BlockSpec(memory_space=pl.ANY)


def prepare(me, weights, vectors):
    own, width = weights[0].shape
    side = width // 2
    deep = weights[5].shape[0]
    folds = deep // own
    halves = (VMEM_SPEC, shaped(4 + folds, own, side))
    keep, send, down = small_call(
        split_shards, (me & 1, *weights), [halves, halves, (VMEM_SPEC, shaped(deep - 16, width))], "split_shards",
        ins=[SMEM] + [VMEM_SPEC] * 6)
    take = swap(send, other_core)
    near, up = small_call(
        join_shards, (me, keep, take, weights[5], *vectors),
        [(VMEM_SPEC, shaped(8 * own + 16, side)), (VMEM_SPEC, shaped(2 * deep + 32, side))], "join_shards",
        ins=[SMEM] + [VMEM_SPEC] * (3 + len(vectors)))
    return near, up, down


def doubled(pieces, change):
    return jnp.concatenate((pieces, swap(pieces, change)))


def gather_down(pieces):
    return doubled(doubled(pieces, first_plane), second_plane)


def gather_plain(weights, vectors):
    squares, up_weight, down_weight = weights[:4], weights[4], weights[5]
    count = lax.axis_size("dp")
    own, width = squares[0].shape
    folds = down_weight.shape[0] // own
    hidden = up_weight.shape[1]
    flat = jnp.concatenate(vectors)
    packed = jnp.concatenate(
        (
            *squares,
            up_weight.reshape(own, folds, width).transpose(1, 0, 2).reshape(own * folds, width),
            down_weight,
            jnp.pad(flat.reshape(1, -1), ((0, 7), (0, width - flat.size))),
        ),
        axis=0,
    )
    whole = lax.all_gather(packed, "dp", axis=0, tiled=True).reshape(count, -1, width)
    square_all = [whole[:, index * own : (index + 1) * own, :].reshape(width, width) for index in range(4)]
    wup = whole[:, 4 * own : (4 + folds) * own, :].reshape(count, folds, own, width).transpose(0, 2, 1, 3)
    wup = wup.reshape(width, 2, CHIPS // 2, 2, -1).transpose(3, 1, 0, 2, 4).reshape(2, 2, width, width)
    wdown = whole[:, (4 + folds) * own : (4 + 2 * folds) * own, :]
    wdown = wdown.reshape(CHIPS, 2, -1, width).transpose(1, 0, 2, 3).reshape(2, hidden // 2, width)
    last = whole[:, (4 + 2 * folds) * own, : flat.size].astype(F32)
    vec = last[:, : 8 * own].reshape(count, 8, own).transpose(1, 0, 2).reshape(8, width)
    bup = last[:, 8 * own :].reshape(CHIPS, 2, -1).transpose(1, 0, 2).reshape(2, 1, -1)
    return (*square_all, (wup, wdown), jnp.pad(vec, ((0, 8), (0, 0))), bup)


def merge_core(core_ref, keep_ref, take_ref, own_ref, send_ref):
    core = core_ref[0]

    def whole(plane):
        return (keep_ref[:, plane].astype(F32) + take_ref[:, plane].astype(F32)).astype(BF16)

    own_ref[:, 0] = whole(0)
    own_ref[:, 1] = whole(2 - core)
    send_ref[:, 0] = whole(1 + core)
    send_ref[:, 1] = whole(3)


def merge_first(*refs):
    pairs, rest_ref, send_ref = refs[:-2], refs[-2], refs[-1]
    base = 0
    for own_ref, take_ref in zip(pairs[::2], pairs[1::2]):
        for part in range(own_ref.shape[0]):
            at = slice(base, base + own_ref.shape[3])
            rest_ref[:, at, :] = (own_ref[part, :, 0].astype(F32) + take_ref[part, :, 0].astype(F32)).astype(BF16)
            send_ref[:, at, :] = (own_ref[part, :, 1].astype(F32) + take_ref[part, :, 1].astype(F32)).astype(BF16)
            base += own_ref.shape[3]


def merge_second(own_ref, take_ref, rest_ref, *send_refs):
    for layer in range(4):
        whole = own_ref[layer].astype(F32) + take_ref[layer].astype(F32)
        if layer == 0:
            rest_ref[...] = whole
        else:
            send_refs[layer - 1][...] = whole.astype(BF16)


def merge_last(deep, core_ref, rest_ref, a_ref, b_ref, c_ref, *refs):
    whole = rest_ref[...] + a_ref[...].astype(F32) + b_ref[...].astype(F32) + c_ref[...].astype(F32)
    first = core_ref[0] == 0
    if deep:
        refs[0][...] = whole[:deep]
        refs = refs[1:]
    keep_ref, send_ref = refs[:2]
    parts, own, _ = keep_ref.shape
    for part in range(parts):
        low = whole[deep + 2 * own * part : deep + 2 * own * part + own]
        high = whole[deep + 2 * own * part + own : deep + 2 * own * (part + 1)]
        keep_ref[part] = jnp.where(first, low, high)
        send_ref[part] = jnp.where(first, high, low)
    if not deep:
        refs[2][...] = whole[2 * own * parts :]


def finish(me_ref, up_keep_ref, up_take_ref, keep_ref, take_ref, flat_ref, late_ref, up_ref, *refs):
    me = me_ref[0]
    first = (me & 1) == 0
    side = keep_ref.shape[2]
    width = 2 * side
    squares, flats = refs[:4], refs[4:]
    own = up_ref.shape[0]
    for number, ref in enumerate(squares):
        keep, take = keep_ref[number], take_ref[number]
        ref[:, :side] = jnp.where(first, keep, take)
        ref[:, side:] = jnp.where(first, take, keep)
    parts = up_keep_ref.shape[0]
    deep = parts * width // CHIPS
    for part in range(parts):
        keep, take = up_keep_ref[part], up_take_ref[part]
        low, high = jnp.where(first, keep, take), jnp.where(first, take, keep)
        pieces = []
        for start in range(0, width, deep):
            pieces += [low[:, start : start + deep], high[:, start : start + deep]]
        up_ref[:, 2 * width * part : 2 * width * (part + 1)] = jnp.concatenate(pieces, axis=1)
    late = jnp.where(me < side // own, late_ref[0:2, :side], late_ref[0:2, side:])
    flat = jnp.concatenate((late, flat_ref[2:]), axis=0)
    long = flats[-1].shape[0]
    short_turn = lax.rem(side - own * lax.rem(me, side // own), side)
    long_turn = lax.rem(side - long * lax.rem(me >> 1, side // long), side)
    short = pltpu.roll(flat, short_turn, 1)
    for number, ref in enumerate(flats[:-1]):
        ref[...] = short[number, :own]
    flats[-1][...] = pltpu.roll(flat, long_turn, 1)[8, :long]


def fenced(function, *args):
    kinds = jax.eval_shape(function, *args)

    def nothing(*_):
        return jax.tree.map(lambda kind: jnp.zeros(kind.shape, kind.dtype), kinds)

    return lax.cond(lax.axis_index("dp") < lax.axis_size("dp"), function, nothing, *args)


def scatter_core(send):
    return swap(send, other_core)


def merge_core_of(core, keep, take):
    shape = keep.shape
    planes, rows, side = shape[-3:]
    keep, take = keep.reshape(-1, planes, rows, side), take.reshape(-1, planes, rows, side)
    count = keep.shape[0]
    steps = MERGE_STEPS
    block = pl.BlockSpec((count // steps, planes, rows, side), lambda i: (i, 0, 0, 0))
    half = (pl.BlockSpec((count // steps, 2, rows, side), lambda i: (i, 0, 0, 0)), shaped(count, 2, rows, side))
    own, send = call(merge_core, (steps,), [SMEM, block, block], [half, half], [], "merge_core", 0, core, keep, take)
    return own.reshape(-1, CHIPS // 4, 2, rows, side), send


def scatter_second(*pairs):
    _, count, _, _, side = pairs[0].shape
    rows = sum(piece.shape[0] * piece.shape[3] for piece in pairs[::2])
    steps = MERGE_STEPS
    ins = [pl.BlockSpec((piece.shape[0], count // steps, *piece.shape[2:]), lambda i: (0, i, 0, 0, 0)) for piece in pairs]
    out = pl.BlockSpec((count // steps, rows, side), lambda i: (i, 0, 0))
    rest, send = call(
        merge_first, (steps,), ins, [(out, shaped(count, rows, side))] * 2, [],
        "merge_first", 0, *pairs)
    return rest, swap(send, second_plane)


def merge_layers_of(own, take):
    _, rows, side = own.shape
    out = shaped(rows, side)
    return small_call(
        merge_second, (own, take), [(VMEM_SPEC, shaped(rows, side, dtype=F32))] + [(VMEM_SPEC, out)] * 3,
        "merge_second", ins=[VMEM_SPEC] * 2)


def scatter_layers(own, take):
    rest, *sends = merge_layers_of(own, take)
    return [rest] + [swap(piece, other_layer(r + 1)) for r, piece in enumerate(sends)]


def scatter_last(core, pieces, own, parts, deep):
    rows, side = pieces[0].shape
    outs = [(VMEM_SPEC, shaped(parts, own, side, dtype=F32))] * 2
    if deep:
        outs = [(VMEM_SPEC, shaped(deep, side, dtype=F32))] + outs
    else:
        outs.append((VMEM_SPEC, shaped(rows - 2 * own * parts, side, dtype=F32)))
    return small_call(
        functools.partial(merge_last, deep), (core, *pieces), outs, "merge_last", ins=[SMEM] + [VMEM_SPEC] * 4, flops=SHORT if deep else 0)


def reduce_plain(down_pairs, up_pairs, square_pair, flat):
    def scattered(array, axis):
        return lax.psum_scatter(array, "dp", scatter_dimension=axis, tiled=True).astype(F32)

    def planes(own, send, core):
        order = (own[..., 0, :, :], send[..., 0, :, :], own[..., 1, :, :], send[..., 1, :, :])
        if core == 1:
            order = (order[0], order[2], order[1], order[3])
        return jnp.stack(order, axis=-3)

    down = jnp.stack([planes(*pair, core) for core, pair in enumerate(down_pairs)])
    up = jnp.stack([planes(*pair, core) for core, pair in enumerate(up_pairs)])
    width = down.shape[-1]
    each = up.shape[4]
    down = down.transpose(1, 2, 0, 3, 4).reshape(-1, width)
    up = up.reshape(2, 2, CHIPS, each, CHIPS // 2, -1).transpose(2, 3, 1, 4, 0, 5).reshape(CHIPS * each, -1)
    square = jnp.stack(square_pair).transpose(1, 2, 3, 0, 4)[:, :, : 4 * each]
    square = square.reshape(CHIPS, 4, each, width).transpose(1, 0, 2, 3).reshape(4, CHIPS * each, width)
    return (
        scattered(down, 0),
        scattered(up, 0),
        *scattered(square, 1),
        lax.psum_scatter(flat, "dp", scatter_dimension=0, tiled=True).reshape(-1),
    )


def body(tokens, lengths, attn_gain, attn_shift, query_weight, query_bias, key_weight, value_weight, value_bias,
         out_weight, out_bias, mlp_gain, mlp_shift, up_weight, up_bias, down_weight, down_bias, grad_out):
    count = lax.axis_size("dp")
    rows, width = tokens.shape
    tiles = lengths.shape[0]
    tile = rows // tiles
    hidden = up_bias.shape[0] * count
    own = width // count
    folds = hidden // width
    vectors = (attn_gain, attn_shift, query_bias, value_bias, out_bias, mlp_gain, mlp_shift, down_bias, up_bias)
    by_hand = count == 2 * CHIPS
    me = lax.axis_index("dp").astype(jnp.int32).reshape(1) if by_hand else jnp.zeros((1,), jnp.int32)
    core = me & 1
    weights = (query_weight, key_weight, value_weight, out_weight, up_weight, down_weight)

    tile_rows = rows_spec(tile, width)
    square = whole_spec((width, width))
    vec_spec = whole_spec((16, width))
    sums = (kept_spec((8, width)), shaped(8, width, dtype=F32))
    low_rows = (tile_rows, shaped(rows, width))
    fold = 2 if tiles % 2 == 0 else 1
    wide_rows = rows_spec(fold * tile, width)
    wide_low = (wide_rows, shaped(rows, width))
    lse_spec = rows_spec(tile, LANES)
    mac = 2 * rows * width * width
    kept_vec = (kept_spec((16, width)), shaped(16, width, dtype=F32))
    kept_hidden = (kept_spec((1, hidden // 2)), shaped(1, hidden // 2, dtype=F32))
    side = width // 2

    def masked(*earlier):
        return call(
            mask_grads, (tiles,), [SMEM, tile_rows], [low_rows, sums], [], "mask_grads", 0,
            lengths, after(grad_out, *earlier))

    high_rows = (tile_rows, shaped(rows, width, dtype=F32))

    share = tiles // PARTS
    normed_outs = [
        (pl.BlockSpec((tile, width), lambda i, part=part: (jnp.clip(i - part * share, 0, share - 1), 0)),
         shaped(share * tile, width))
        for part in range(PARTS)
    ]

    def attend(q, k, v, vec, wo):
        return call(
            attention_forward, (tiles,), [SMEM, tile_rows, vec_spec, tile_rows, tile_rows, tile_rows, square],
            [low_rows, (lse_spec, shaped(rows, LANES, dtype=F32)), high_rows] + normed_outs,
            [], "attention_forward", 0, lengths, tokens, vec, q, k, v, wo)

    def gather_first(near):
        cot, sum_down = masked(near)
        along = after(swap(near, first_plane), cot)
        return along, swap(near, second_plane), cot, sum_down

    def gather_second(near, along, across, cot, up_two, up_taken):
        cot_other = swap(cot, other_core)
        corner = swap(along, second_plane)
        taken = [swap(near, other_core), swap(along, other_core)]
        across, corner_out = after((across, corner), taken)
        taken += [swap(across, other_core), swap(corner_out, other_core)]
        return corner, taken, cot_other, jnp.concatenate((up_two, up_taken))

    def attend_by_hand(q, k, v, vec, wo, up_four, up_along):
        up = swap(jnp.concatenate((up_four, up_along)), second_plane)
        mixed, lse, resid, *n2 = attend(q, k, v, vec, wo)
        n2_other = [swap(piece, other_core) for piece in n2]
        return mixed, lse, resid, n2, n2_other, up

    if by_hand:
        near, up, down = prepare(me, weights, vectors)
        down = after(down, near)[None]
        down_two = doubled(down, other_layer(1))
        near_moved = [swap(near, other_layer(r)) for r in (1, 2, 3)]
        up_moved = swap(up, other_layer(1))
        down_shard = fenced(gather_down, after(down_two, near))
        near_moved, up_moved = after((near_moved, up_moved), down_shard)
        near = jnp.stack([near] + near_moved)
        up_two = jnp.stack((up, up_moved))
        near, up_two = after((near, up_two))
        up_moved = swap(up_two, other_layer(2))
        along, across, cot, sum_down = fenced(gather_first, near)
        up_taken = after(up_moved, along)
        down = [down_shard, swap(after(down_shard, up_taken), other_layer(2))]
        corner, taken, cot_other, up_four = fenced(gather_second, near, along, across, cot, up_two, up_taken)
        near = [near, along, across, corner] + taken
        up_along = swap(up_four, first_plane)
        n1, q, k, v, wq, wk, wv, wo, vec, bup = call_with(
            me, project, tiles, [tile_rows] + [ANY_SPEC] * 8,
            [low_rows] * 4 + [(ANY_SPEC, shaped(width, width))] * 4 + [kept_vec, kept_hidden],
            [pltpu.VMEM((4, width, width), BF16), pltpu.VMEM((CHIPS, width // (4 * CHIPS) + 1, 16, width), BF16),
             pltpu.SemaphoreType.DMA((1,)), pltpu.SemaphoreType.DMA((4,))],
            "project", LATER, tokens, *[piece.reshape(4, -1, 16, side) for piece in after(near)])
        up_along = after(up_along, n1)
        mixed, lse, resid, n2, n2_other, up_moved = fenced(attend_by_hand, q, k, v, vec, wo, up_four, up_along)
        up = [up_along, up_moved]
        hidden_weights = [(up_four, *up, *down)]
    else:
        wq, wk, wv, wo, hidden_weights, vec, bup = gather_plain(weights, vectors)
        hidden_weights = list(zip(*hidden_weights))
        cot, sum_down = masked()
        n1, q, k, v = call(
            project_rows, (tiles,), [tile_rows, vec_spec, square, square, square], [low_rows] * 4,
            [], "project", 0, tokens, vec, wq, wk, wv)
        mixed, lse, resid, *n2 = attend(q, k, v, vec, wo)

    each = width // CHIPS
    deep = hidden // (2 * CHIPS)
    blocks = hidden // (2 * width)
    full_rows = whole_spec((rows, width))
    hidden_spec = pl.BlockSpec((1, width), lambda i, me: (0, i))
    low_out, high_out = (ANY_SPEC, shaped(rows, width)), (ANY_SPEC, shaped(rows, width, dtype=F32))
    act_out = (ANY_SPEC, shaped(rows, blocks * width))
    down_part = (ANY_SPEC, shaped(4, 2, deep, width))
    up_part = (ANY_SPEC, shaped(blocks, 4, 2, each, width))

    act_spec = pl.BlockSpec((fold * tile, blocks * width), lambda i, *me: (i, 0))
    wide_spec = whole_spec((hidden // 2, width))

    def run_mlp(me, tokens_of, bup, sources):
        sets = len(tokens_of[1])
        low, high = pltpu.VMEM((sets * rows, width), BF16), pltpu.VMEM((sets * rows, width), F32)
        weight = pltpu.VMEM((2, width, width), BF16)
        dma = pltpu.SemaphoreType.DMA((2, sets))
        return call_with(
            me, functools.partial(mlp, sets, len(sources)), blocks,
            [ANY_SPEC] * (PARTS * sets + sets) + [hidden_spec] + [ANY_SPEC] * len(sources),
            [act_out] * sets + [high_out] + [low_out] * (sets - 1) + [down_part] * 2 + [up_part] * 2
            + [(ANY_SPEC, shaped(hidden // 2, width)), (hidden_spec, shaped(1, hidden // 2, dtype=F32))],
            [low, low, high, pltpu.VMEM((blocks, sets * rows, width), BF16), low, low, weight, weight,
             pltpu.VMEM((blocks, width, width), BF16), pltpu.VMEM((hidden // 2, width), BF16), dma,
             pltpu.SemaphoreType.DMA((blocks, sets)), pltpu.SemaphoreType.DMA((sets,)), pltpu.SemaphoreType.DMA((4,)),
             pltpu.SemaphoreType.DMA((blocks + 1,))],
            "mlp", 0, *tokens_of[0], *tokens_of[1], bup, *sources)

    if by_hand:
        act_own, act_other, gtwo, gtwo_other, down_own, down_send, up_own, up_send, wdown, sum_up = run_mlp(
            me, ((*n2, *n2_other), (cot, cot_other)), bup, hidden_weights[0])
        gtwo_take = swap(gtwo_other, other_core)
        parts = (-1, CHIPS // 4, 2)
        down_first = [piece.reshape(*parts, deep, width) for piece in (down_own, swap(down_send, first_plane))]
        up_first = [piece.reshape(*parts, each, width) for piece in (up_own, swap(up_send, first_plane))]
    else:
        runs = [run_mlp(me + half, (n2, (cot,)), bup[half], hidden_weights[half]) for half in range(2)]
        (act_own, gtwo), (act_other, gtwo_take) = ((run[0], run[1]) for run in runs)
        gtwo_take = gtwo_take.astype(BF16)
        sum_up = jnp.concatenate([run[7] for run in runs], axis=1)
    grads_spec = pl.BlockSpec((4, tile, width), lambda i, *me: (0, i, 0))
    grads, gresid, sum_back = call(
        attention_backward, (tiles,),
        [SMEM, tile_rows, tile_rows, tile_rows, lse_spec, tile_rows, tile_rows, tile_rows, tile_rows, vec_spec, square],
        [(grads_spec, shaped(4, rows, width)), high_rows, sums], [pltpu.VMEM((tile, width), BF16)],
        "attention_backward", 0, lengths, q, k, v, lse, cot, resid, gtwo, gtwo_take, vec, wo)
    sum_spec = whole_spec((8, width))
    pair_shape = (CHIPS // 4, 4, 4 * each + 16, side)
    columns = pl.BlockSpec((1, rows, width), lambda i, me: (i, 0, 0))

    def run_weights(grads):
        return call_with(
            me, weight_grads, 4, [full_rows, ANY_SPEC, columns, sum_spec, sum_spec, whole_spec((1, sum_up.shape[1]))],
            [(ANY_SPEC, shaped(*pair_shape))] * 2,
            [pltpu.VMEM(pair_shape, BF16)] * 2
            + [pltpu.VMEM((rows, width), BF16), pltpu.SemaphoreType.DMA((1,)), pltpu.SemaphoreType.DMA((2, 5))],
            "weight_grads", 0,
            n1, mixed, grads, sum_back, sum_down, sum_up)

    def run_tokens(gresid):
        return call(
            tokens_backward, (tiles // fold,),
            [wide_rows, wide_rows, vec_spec, pl.BlockSpec((4, fold * tile, width), lambda i: (0, i, 0)), square, square, square],
            [wide_low, sums], [], "tokens_backward", MIDDLE, tokens, gresid, vec, grads, wq, wk, wv)

    if by_hand:
        (out_other,) = call_with(
            me, mlp_out_other, tiles // fold, [act_spec, wide_spec], [wide_low], [], "mlp_out_other", 0, after(act_other, grads), wdown)
        down_first, up_first = after((down_first, up_first), out_other)
        hidden_rest, hidden_take = scatter_second(*down_first, *up_first)

        def weights_of_chip(grads, out_take):
            square_send, square_keep = run_weights(grads)
            (out,) = call_with(
                me, mlp_out_own, tiles // fold, [wide_rows, vec_spec, act_spec, wide_rows, wide_spec], [wide_low], [],
                "mlp_out_own", 0, resid, vec, act_own, after(out_take, square_send), wdown)
            square_take = after(scatter_core(square_send), out)
            return *merge_core_of(core, square_keep, square_take), out

        out_take = swap(out_other, other_core)
        square_own, square_send, out = fenced(weights_of_chip, after(grads, hidden_rest), out_take)
        square_take = swap(square_send, first_plane).reshape(square_own.shape)
        hidden_rest, hidden_take = after((hidden_rest, hidden_take), square_own)
        hidden_layers = scatter_layers(hidden_rest, hidden_take)
        gtok, late = run_tokens(after(gresid, hidden_layers[0]))
        square_take = after(square_take, late)
        late = late + swap(late, other_core)
        square_second = scatter_second(square_own, square_take)
        late = after(late, square_second[0])
        late = late + swap(late, other_layer(1))
        hidden_layers = after(hidden_layers, late)
        g_down, up_keep, up_send = scatter_last(core, hidden_layers, own, blocks, deep)
        up_take = scatter_core(up_send)
        late_take = after(swap(late, other_layer(2)), g_down)
        square_second = after(square_second, g_down)
        rest, *sends = merge_layers_of(*square_second)
        late_take = after(late_take, rest)
        sends = after(sends, late_take)
        square_layers = [rest] + [swap(piece, other_layer(r + 1)) for r, piece in enumerate(sends)]
        late = late + late_take
        late = late + after(swap(late, other_plane(1)), rest)
        late = late + swap(late, other_plane(2))
        square_layers = after(square_layers, late)
        square_keep, square_send, flat = scatter_last(core, square_layers, own, 4, 0)
        square_take = scatter_core(square_send)
        outs = [(VMEM_SPEC, shaped(own, hidden, dtype=F32))] + [(VMEM_SPEC, shaped(own, width, dtype=F32))] * 4
        outs += [(VMEM_SPEC, shaped(own, dtype=F32))] * 8 + [(VMEM_SPEC, shaped(folds * own, dtype=F32))]
        g_up, g_q, g_k, g_v, g_o, *g_flat, g_ub = small_call(
            finish, (me, up_keep, up_take, square_keep, square_take, flat, late), outs, "finish",
            ins=[SMEM] + [VMEM_SPEC] * 6)
    else:
        square_send, square_keep = run_weights(grads)
        gtok, sum_one = run_tokens(gresid)
        flat = jnp.concatenate((sum_one[0:2], sum_back[0:5], sum_down[0:1]), axis=0)
        flat = flat.reshape(8, count, own).transpose(1, 0, 2).reshape(count, 8 * own)
        hidden_sums = sum_up.reshape(2, CHIPS, deep).transpose(1, 0, 2).reshape(count, folds * own)
        flat = jnp.concatenate((flat, hidden_sums), axis=1)
        g_down, g_up, g_q, g_k, g_v, g_o, flat = reduce_plain(
            [run[2:4] for run in runs], [run[4:6] for run in runs], (square_keep, square_send), flat)
        (out_other,) = call_with(
            me + 1, mlp_out_other, tiles // fold, [act_spec, wide_spec], [wide_low], [], "mlp_out_other", 0, act_other, runs[1][6])
        (out,) = call_with(
            me, mlp_out_own, tiles // fold, [wide_rows, vec_spec, act_spec, wide_rows, wide_spec], [wide_low], [],
            "mlp_out_own", 0, resid, vec, act_own, out_other, runs[0][6])
        g_flat = [flat[index * own : (index + 1) * own] for index in range(8)]
        g_ub = flat[8 * own :]
    g_gain, g_shift, g_qb, g_vb, g_ob, g_mg, g_ms, g_db = g_flat
    return (out, gtok, g_gain, g_shift, g_q, g_qb, g_k, g_v, g_vb, g_o, g_ob, g_mg, g_ms, g_up, g_ub, g_down, g_db)


def solution(mesh):
    rows, flat = P("dp", None), P("dp")
    return jax.shard_map(
        body,
        mesh=mesh,
        in_specs=(rows, rows, flat, flat, rows, flat, rows, rows, flat, rows, flat, flat, flat, rows, flat, rows, flat, rows),
        out_specs=(rows, rows, flat, flat, rows, flat, rows, rows, flat, rows, flat, flat, flat, rows, flat, rows, flat),
        check_vma=False,
    )
```

```python
import functools

import jax
import jax.numpy as jnp
from jax import lax
from jax.experimental import pallas as pl
from jax.experimental.pallas import tpu as pltpu
from jax.sharding import PartitionSpec as P

HEADS = 12
HEAD_DIM = 64
PAIRS = 6
LANES = 128
CHIPS = 16
MERGE_STEPS = 2
LONG = 10**11
SHORT = 6 * 10**9
MIDDLE = 115 * 10**8
LATER = 9 * 10**9
EPS = 1e-06
MASKED = -1e30
SCALE = HEAD_DIM**-0.5
GELU_C = 0.7978845608028654
GELU_A = 0.044715
VMEM = 64 * 1024 * 1024 - 65536
F32 = jnp.float32
BF16 = jnp.bfloat16


def dot_nn(left, right):
    return lax.dot_general(left, right, (((1,), (0,)), ((), ())), preferred_element_type=F32)


def dot_nt(left, right):
    return lax.dot_general(left, right, (((1,), (1,)), ((), ())), preferred_element_type=F32)


def dot_tn(left, right):
    return lax.dot_general(left, right, (((0,), (0,)), ((), ())), preferred_element_type=F32)


def normalize(rows):
    centered = rows - jnp.mean(rows, axis=-1, keepdims=True)
    inverse = lax.rsqrt(jnp.mean(centered * centered, axis=-1, keepdims=True) + EPS)
    return centered * inverse, inverse


def norm_back(grads, gain, hat, inverse):
    scaled = grads * gain
    mean = jnp.mean(scaled, axis=-1, keepdims=True)
    mean_hat = jnp.mean(scaled * hat, axis=-1, keepdims=True)
    return inverse * (scaled - mean - hat * mean_hat)


def column_sum(rows):
    return jnp.sum(rows, axis=0, keepdims=True)


def segments(lengths_ref, tile, slots, rows, axis):
    shape = (rows, 1) if axis == 0 else (1, rows)
    index = lax.broadcasted_iota(jnp.int32, shape, axis)
    segment = jnp.zeros(shape, jnp.int32)
    bound = 0
    for slot in range(slots):
        bound = bound + lengths_ref[tile, slot]
        segment = segment + (index >= bound).astype(jnp.int32)
    return segment


def mask_bias(lengths_ref, tile, slots, rows):
    same = segments(lengths_ref, tile, slots, rows, 0) == segments(lengths_ref, tile, slots, rows, 1)
    return jnp.where(same, 0.0, MASKED).astype(F32)


def half_of(pair, side):
    lane = lax.broadcasted_iota(jnp.int32, pair.shape, 1)
    keep = lane < HEAD_DIM if side == 0 else lane >= HEAD_DIM
    return jnp.where(keep, pair, jnp.zeros_like(pair))


def fetch_weights(me, sources, stage_ref, sem):
    core, chip = me & 1, me >> 1
    side = sources[0].shape[3]
    for index, source in enumerate(sources):
        half = core if index < 4 else 1 - core
        plane = (0, 1 + half, 2 - half, 3)[index % 4]
        cols = pl.ds(pl.multiple_of(half * side, LANES), side)
        for layer in range(4):
            owner = chip ^ (4 * layer + plane)
            pltpu.make_async_copy(source.at[layer], stage_ref.at[owner, :, :, cols], sem.at[0]).start()


def project(me_ref, x_ref, *refs):
    sources = refs[:8]
    n1_ref, q_ref, k_ref, v_ref = refs[8:12]
    outs, (vec_ref, bup_ref, weights_ref, stage_ref, sem, out_sem) = refs[12:16], refs[16:]
    step = pl.program_id(0)
    core = me_ref[0] & 1
    weights = [weights_ref.at[number] for number in range(4)]

    def write(number):
        return pltpu.make_async_copy(weights[number], outs[number], out_sem.at[number])

    @pl.when(step == 0)
    def _():
        fetch_weights(me_ref[0], sources, stage_ref, sem)
        pltpu.make_async_copy(stage_ref, stage_ref, sem.at[0]).wait()
        width = stage_ref.shape[3]
        side = width // 2
        blocks = width // (16 * CHIPS)
        for number in range(4):
            weights[number][...] = stage_ref[:, number * blocks : (number + 1) * blocks].reshape(width, width)
            write(number).start()
        parts = [stage_ref[chip, 4 * blocks].astype(F32) for chip in range(CHIPS)]
        halves = []
        for half in range(2):
            group = parts[half * CHIPS // 2 : (half + 1) * CHIPS // 2]
            halves.append(sum(part[:, :side] + part[:, side:] for part in group))
        vec_ref[...] = jnp.concatenate(halves, axis=1)
        blocks = bup_ref.shape[1] // side
        group = CHIPS // blocks
        for block in range(blocks):
            rows = sum(parts[block * group : (block + 1) * group])
            bup_ref[:, block * side : (block + 1) * side] = jnp.where(core == 0, rows[8:9, :side], rows[8:9, side:])

    project_rows(x_ref, vec_ref, *weights[:3], n1_ref, q_ref, k_ref, v_ref)

    @pl.when(step == pl.num_programs(0) - 1)
    def _():
        for number in range(4):
            write(number).wait()


def project_rows(x_ref, vec_ref, wq_ref, wk_ref, wv_ref, n1_ref, q_ref, k_ref, v_ref):
    hat, _ = normalize(x_ref[...].astype(F32))
    n1 = (hat * vec_ref[0:1, :] + vec_ref[1:2, :]).astype(BF16)
    n1_ref[...] = n1
    q_ref[...] = (dot_nn(n1, wq_ref[...]) + vec_ref[2:3, :]).astype(BF16) * jnp.asarray(SCALE, BF16)
    k_ref[...] = dot_nn(n1, wk_ref[...]).astype(BF16)
    v_ref[...] = (dot_nn(n1, wv_ref[...]) + vec_ref[3:4, :]).astype(BF16)


def mask_grads(lengths_ref, grad_ref, cot_ref, dsum_ref):
    tile = pl.program_id(0)
    slots = lengths_ref.shape[1]
    valid = segments(lengths_ref, tile, slots, grad_ref.shape[0], 0) < slots
    cot = jnp.where(valid, grad_ref[...].astype(F32), 0.0)
    cot_ref[...] = cot.astype(BF16)

    @pl.when(tile == 0)
    def _():
        dsum_ref[...] = jnp.zeros_like(dsum_ref)

    dsum_ref[0:1, :] += column_sum(cot)


def attention_forward(lengths_ref, x_ref, vec_ref, q_ref, k_ref, v_ref, wo_ref, mixed_ref, lse_ref, resid_ref, n2_ref):
    tile = pl.program_id(0)
    rows = q_ref.shape[0]
    slots = lengths_ref.shape[1]
    bias = mask_bias(lengths_ref, tile, slots, rows)
    lane = lax.broadcasted_iota(jnp.int32, (rows, LANES), 1)
    lse = jnp.zeros((rows, LANES), F32)

    def at(pair):
        return pl.ds(pair * LANES, LANES)

    def scores_of(pair):
        qp, kp = q_ref[:, at(pair)], k_ref[:, at(pair)]
        return [dot_nt(half_of(qp, side), kp) for side in range(2)]

    def softmax_of(scores):
        scores = scores + bias
        top = jnp.max(scores, axis=-1, keepdims=True)
        weights = jnp.exp(scores - top)
        sums = jnp.sum(weights, axis=-1, keepdims=True)
        return (weights * (1.0 / sums)).astype(BF16), top + jnp.log(sums)

    raw = {}
    probs = {}
    for turn in range(PAIRS + 2):
        if turn < PAIRS:
            raw[turn] = scores_of(turn)
        if 0 <= turn - 1 < PAIRS:
            both = [softmax_of(scores) for scores in raw.pop(turn - 1)]
            for side in range(2):
                lse = jnp.where(lane == 2 * (turn - 1) + side, both[side][1], lse)
            probs[turn - 1] = [pair[0] for pair in both]
        if turn >= 2:
            vp = v_ref[:, at(turn - 2)]
            parts = [dot_nn(probs[turn - 2][side], half_of(vp, side)) for side in range(2)]
            mixed_ref[:, at(turn - 2)] = (parts[0] + parts[1]).astype(BF16)
    lse_ref[...] = lse
    resid = x_ref[...].astype(F32) + (dot_nn(mixed_ref[...], wo_ref[...]) + vec_ref[4:5, :])
    resid_ref[...] = resid
    hat, _ = normalize(resid)
    n2_ref[...] = (hat * vec_ref[5:6, :] + vec_ref[6:7, :]).astype(BF16)


def spread(me, rows, put):
    layer, plane = me >> 3, (me >> 1) & 3
    each = rows.shape[0] // CHIPS
    for chip in range(CHIPS):
        put((chip & 3) ^ plane, (chip >> 2) ^ layer, rows[chip * each : (chip + 1) * each].astype(BF16))


def fetch_hidden(me, sources, wup_ref, wdown_ref, sem):
    if len(sources) == 2:
        for number in range(wup_ref.shape[0]):
            pltpu.make_async_copy(sources[0].at[number], wup_ref.at[number], sem.at[number]).start()
        pltpu.make_async_copy(sources[1], wdown_ref, sem.at[wup_ref.shape[0]]).start()
        return
    core, chip = me & 1, me >> 1
    planes = (0, 1 + core, 2 - core, 3)
    blocks, width = wup_ref.shape[:2]
    each, deep = width // CHIPS, wdown_ref.shape[0] // CHIPS
    for layer in range(4):
        for index, plane in enumerate(planes):
            owner = chip ^ (4 * layer + plane)
            rows = pl.ds(pl.multiple_of(owner * each, 16), each)
            side = sources[index].shape[2]
            for part in range(sources[index].shape[1] // each):
                number, cols = part * side // width, pl.ds(part * side % width, side)
                pltpu.make_async_copy(
                    sources[index].at[layer, pl.ds(part * each, each), :], wup_ref.at[number, rows, cols], sem.at[number]
                ).start()
            source = sources[4 + layer // 2].at[2 * index + layer % 2]
            rows = pl.ds(pl.multiple_of(owner * deep, 16), source.shape[0])
            pltpu.make_async_copy(source, wdown_ref.at[rows, :], sem.at[blocks]).start()
            rest = deep - source.shape[0]
            rows = pl.ds(pl.multiple_of(owner * deep + source.shape[0], 16), rest)
            for part in range(width // side):
                at = pl.ds(sources[index].shape[1] - (width // side - part) * rest, rest)
                pltpu.make_async_copy(
                    sources[index].at[layer, at, :], wdown_ref.at[rows, pl.ds(part * side, side)], sem.at[blocks]
                ).start()


def mlp(sets, count, me_ref, *refs):
    n2_hbm, cot_hbm = refs[:sets], refs[sets : 2 * sets]
    bup_ref = refs[2 * sets]
    sources = refs[2 * sets + 1 : 2 * sets + 1 + count]
    refs = refs[2 * sets + 1 + count :]
    act_hbm, gtwo_hbm, refs = refs[:sets], refs[sets : 2 * sets], refs[2 * sets :]
    down_own, down_send, up_own, up_send, wdown_hbm, dbu_ref = refs[:6]
    n2_ref, cot_ref, gacc, act_ref, gup_ref, low_ref, gdown_ref, gupw_ref = refs[6:14]
    wup_all, wdown_all, in_sem, act_sem, out_sem, grad_sem, weight_sem = refs[14:]
    step = pl.program_id(0)
    last = pl.num_programs(0) - 1
    me = me_ref[0]
    rows = n2_ref.shape[0] // sets

    def rows_of(index):
        return pl.ds(pl.multiple_of(index * rows, rows), rows)

    blocks, width = wup_all.shape[:2]

    @pl.when(step == 0)
    def _():
        fetch_hidden(me, sources, wup_all, wdown_all, weight_sem)
        for index in range(sets):
            at = pl.ds(index * rows, rows)
            pltpu.make_async_copy(n2_hbm[index], n2_ref.at[at, :], in_sem.at[0, index]).start()
            pltpu.make_async_copy(cot_hbm[index], cot_ref.at[at, :], in_sem.at[1, index]).start()

    pltpu.make_async_copy(wup_all.at[step], wup_all.at[step], weight_sem.at[step]).wait()
    write_down = pltpu.make_async_copy(wdown_all, wdown_hbm, weight_sem.at[blocks])

    @pl.when(step == 0)
    def _():
        pltpu.make_async_copy(wdown_all, wdown_all, weight_sem.at[blocks]).wait()
        write_down.start()

    wup = wup_all[step]
    wdown = wdown_all[pl.ds(pl.multiple_of(step * width, width), width), :]
    dbu_ref[...] = jnp.zeros_like(dbu_ref)
    slot = lax.rem(step, 2)

    @pl.loop(0, sets)
    def _(index):
        at = rows_of(index)

        @pl.when(step == 0)
        def _():
            pltpu.make_async_copy(n2_ref.at[at, :], n2_ref.at[at, :], in_sem.at[0, index]).wait()
            pltpu.make_async_copy(cot_ref.at[at, :], cot_ref.at[at, :], in_sem.at[1, index]).wait()

        pre = dot_nn(n2_ref[at, :], wup) + bup_ref[...]
        grad_act = dot_nt(cot_ref[at, :], wdown)
        square = pre * pre
        tanh = jnp.tanh(pre * (GELU_C + (GELU_C * GELU_A) * square))
        half = 0.5 + 0.5 * tanh
        inner = GELU_C + (3.0 * GELU_C * GELU_A) * square
        act_ref[slot, at, :] = (pre * half).astype(BF16)
        gup = (grad_act * (half + (0.5 * pre) * (1.0 - tanh * tanh) * inner)).astype(BF16)
        gup_ref[at, :] = gup
        dbu_ref[...] += column_sum(gup.astype(F32))

    @pl.when(step == 0)
    def _():
        @pl.loop(0, sets)
        def _(index):
            at = rows_of(index)
            gacc[at, :] = dot_nt(gup_ref[at, :], wup)

    @pl.when((step > 0) & (step < last))
    def _():
        @pl.loop(0, sets)
        def _(index):
            at = rows_of(index)
            gacc[at, :] += dot_nt(gup_ref[at, :], wup)

    def results():
        for index in range(sets):
            at = pl.ds(index * rows, rows)
            source = low_ref.at[at, :] if index else gacc.at[at, :]
            yield pltpu.make_async_copy(source, gtwo_hbm[index], out_sem.at[index])

    def activations(number):
        for index in range(sets):
            source = act_ref.at[number, pl.ds(index * rows, rows), :]
            cols = pl.ds(number * width, width)
            yield pltpu.make_async_copy(source, act_hbm[index].at[:, cols], act_sem.at[number, index])

    for number in range(act_ref.shape[0]):

        @pl.when(step == number)
        def _():
            for copy in activations(number):
                copy.start()

    @pl.when(step == last)
    def _():
        @pl.loop(0, sets)
        def _(index):
            at = rows_of(index)
            total = gacc[at, :] + dot_nt(gup_ref[at, :], wup)
            gacc[at, :] = total
            low_ref[at, :] = total.astype(BF16)

        for copy in results():
            copy.start()

    gdown_ref[slot] = dot_tn(act_ref[slot], cot_ref[...]).astype(BF16)
    deep = down_own.shape[2]
    count = gdown_ref.shape[1] // deep
    for index in range(count):
        chip = step * count + index
        source = gdown_ref.at[slot, pl.ds(index * deep, deep), :]
        keep_or_send(me, chip & 3, (chip >> 2) ^ (me >> 3), source, down_own, down_send, grad_sem, 0)

    gupw_ref[slot] = dot_tn(n2_ref[...], gup_ref[...]).astype(BF16)
    each = gupw_ref.shape[1] // CHIPS
    for chip in range(CHIPS):
        source = gupw_ref.at[slot, pl.ds(chip * each, each), :]
        keep_or_send(
            me, chip & 3, (chip >> 2) ^ (me >> 3), source, up_own.at[step], up_send.at[step], grad_sem, 2)

    @pl.when(step == last)
    def _():
        for copy in results():
            copy.wait()
        write_down.wait()
        for number in range(act_ref.shape[0]):
            for copy in activations(number):
                copy.wait()
        for number, ref in enumerate((down_own, down_send, up_own, up_send)):
            pltpu.make_async_copy(ref, ref, grad_sem.at[number]).wait()


def keep_or_send(me, plane, layer, source, own_ref, send_ref, sem, number):
    core = me & 1
    relative = plane ^ ((me >> 1) & 3)
    mine = (relative == 0) | (relative == 2 - core)

    @pl.when(mine)
    def _():
        pltpu.make_async_copy(source, own_ref.at[layer, jnp.where(relative == 0, 0, 1)], sem.at[number]).start()

    @pl.when(jnp.logical_not(mine))
    def _():
        pltpu.make_async_copy(source, send_ref.at[layer, jnp.where(relative == 3, 1, 0)], sem.at[number + 1]).start()


def mlp_out_other(me_ref, act_ref, wdown_ref, out_ref):
    out_ref[...] = dot_nn(act_ref[...], wdown_ref[...]).astype(BF16)


def mlp_out_own(me_ref, resid_ref, vec_ref, act_ref, take_ref, wdown_ref, out_ref):
    half = dot_nn(act_ref[...], wdown_ref[...]) + take_ref[...].astype(F32)
    out_ref[...] = (resid_ref[...] + (half + vec_ref[7:8, :])).astype(BF16)


def attention_backward(lengths_ref, q_ref, k_ref, v_ref, lse_ref, cot_ref, resid_ref, gtwo_ref, gother_ref, vec_ref, wo_ref,
                       grads_ref, gresid_ref, dsum_ref, gmix_ref):
    tile = pl.program_id(0)
    rows = q_ref.shape[0]

    @pl.when(tile == 0)
    def _():
        dsum_ref[...] = jnp.zeros_like(dsum_ref)

    hat, inverse = normalize(resid_ref[...])
    grad_two = gtwo_ref[...] + gother_ref[...].astype(F32)
    gresid = cot_ref[...].astype(F32) + norm_back(grad_two, vec_ref[5:6, :], hat, inverse)
    gresid_ref[...] = gresid
    gattn = gresid.astype(BF16)
    grads_ref[3] = gattn
    dsum_ref[2:3, :] += column_sum(gattn.astype(F32))
    dsum_ref[3:4, :] += column_sum(grad_two * hat)
    dsum_ref[4:5, :] += column_sum(grad_two)
    gmix_ref[...] = dot_nt(gattn, wo_ref[...]).astype(BF16)
    bias = mask_bias(lengths_ref, tile, lengths_ref.shape[1], rows)

    def load(pair):
        cols = pl.ds(pair * LANES, LANES)
        return q_ref[:, cols], k_ref[:, cols], v_ref[:, cols], gmix_ref[:, cols]

    def products_of(pair):
        qp, kp, vp, gp = load(pair)
        return [(dot_nt(half_of(qp, side), kp), dot_nt(half_of(gp, side), vp)) for side in range(2)]

    def softmax_back(pair, products):
        results = []
        for side, (scores, grad_probs) in enumerate(products):
            head = 2 * pair + side
            probs = jnp.exp(scores + bias - lse_ref[:, head : head + 1])
            weighted = probs * grad_probs
            dot = jnp.sum(weighted, axis=-1, keepdims=True)
            results.append((probs.astype(BF16), (weighted - probs * dot).astype(BF16)))
        return results

    def store(pair, results):
        qp, kp, vp, gp = load(pair)
        dq = sum(dot_nn(results[side][1], half_of(kp, side)) for side in range(2))
        dk = sum(dot_tn(results[side][1], half_of(qp, side)) for side in range(2))
        dv = sum(dot_tn(results[side][0], half_of(gp, side)) for side in range(2))
        cols = pl.ds(pair * LANES, LANES)
        grads_ref[0, :, cols] = (dq * SCALE).astype(BF16)
        grads_ref[1, :, cols] = dk.astype(BF16)
        grads_ref[2, :, cols] = dv.astype(BF16)

    raw = {}
    done = {}
    for turn in range(PAIRS + 2):
        if turn < PAIRS:
            raw[turn] = products_of(turn)
        if 0 <= turn - 1 < PAIRS:
            done[turn - 1] = softmax_back(turn - 1, raw.pop(turn - 1))
        if turn >= 2:
            store(turn - 2, done.pop(turn - 2))

    dsum_ref[0:1, :] += column_sum(grads_ref[0].astype(F32))
    dsum_ref[1:2, :] += column_sum(grads_ref[2].astype(F32))


def weight_grads(me_ref, n1_ref, mixed_hbm, columns_ref, sum_back_ref, sum_down_ref, sum_up_ref, send_hbm, keep_hbm,
                 send_ref, keep_ref, mixed_ref, in_sem, out_sem):
    step = pl.program_id(0)
    me = me_ref[0]
    first = (me & 1) == 0
    side = send_ref.shape[3]
    each = n1_ref.shape[1] // CHIPS
    load = pltpu.make_async_copy(mixed_hbm, mixed_ref, in_sem.at[0])

    def writes(number):
        rows = pl.ds(number * each, each if number < 4 else 16)
        for index, (ref, out) in enumerate(((send_ref, send_hbm), (keep_ref, keep_hbm))):
            yield pltpu.make_async_copy(ref.at[:, :, rows, :], out.at[:, :, rows, :], out_sem.at[index, number])

    @pl.when(step == 0)
    def _():
        load.start()

    def run(left, number):
        result = dot_tn(left, columns_ref[0])
        low, high = result[:, :side], result[:, side:]
        rows_at = pl.ds(pl.multiple_of(number * each, 16), each)

        def put_send(plane, layer, rows):
            send_ref[layer, plane, rows_at, :] = rows

        def put_keep(plane, layer, rows):
            keep_ref[layer, plane, rows_at, :] = rows

        spread(me, jnp.where(first, high, low), put_send)
        spread(me, jnp.where(first, low, high), put_keep)

    @pl.when(step < 3)
    def _():
        run(n1_ref[...], step)

    for number in range(3):

        @pl.when(step == number)
        def _():
            for copy in writes(number):
                copy.start()

    @pl.when(step == 3)
    def _():
        nothing = jnp.zeros((2, n1_ref.shape[1]), F32)
        vecs = jnp.concatenate((nothing, sum_back_ref[0:5], sum_down_ref[0:1]), axis=0)
        for chip in range(CHIPS):
            half = chip // (CHIPS // 2)
            block = chip * (sum_up_ref.shape[1] // side) // CHIPS
            last = jnp.broadcast_to(sum_up_ref[:, block * side : (block + 1) * side], (8, side))
            short = vecs[:, half * side : (half + 1) * side]
            at = ((chip >> 2) ^ (me >> 3), (chip & 3) ^ ((me >> 1) & 3))
            keep_ref[at[0], at[1], 4 * each :, :] = jnp.concatenate((short, last), axis=0).astype(BF16)
            send_ref[at[0], at[1], 4 * each :, :] = jnp.concatenate((short, jnp.zeros_like(last)), axis=0).astype(BF16)
        for copy in writes(4):
            copy.start()
        load.wait()
        run(mixed_ref[...], 3)
        for copy in writes(3):
            copy.start()
        for number in range(5):
            for copy in writes(number):
                copy.wait()


def tokens_backward(x_ref, gresid_ref, vec_ref, grads_ref, wq_ref, wk_ref, wv_ref, gtok_ref, dsum_ref):
    @pl.when(pl.program_id(0) == 0)
    def _():
        dsum_ref[...] = jnp.zeros_like(dsum_ref)

    grad_one = dot_nt(grads_ref[0], wq_ref[...]) + dot_nt(grads_ref[1], wk_ref[...]) + dot_nt(grads_ref[2], wv_ref[...])
    hat, inverse = normalize(x_ref[...].astype(F32))
    gtok_ref[...] = (gresid_ref[...] + norm_back(grad_one, vec_ref[0:1, :], hat, inverse)).astype(BF16)
    dsum_ref[0:1, :] += column_sum(grad_one * hat)
    dsum_ref[1:2, :] += column_sum(grad_one)


def rows_spec(block, width):
    return pl.BlockSpec((block, width), lambda i, *me: (i, 0))


def cols_spec(height, block):
    return pl.BlockSpec((height, block), lambda i, *me: (0, i))


def whole_spec(shape):
    return pl.BlockSpec(shape, lambda *i: (0,) * len(shape), pipeline_mode=pl.Buffered(1))


def kept_spec(shape):
    return pl.BlockSpec(shape, lambda *i: (0,) * len(shape))


SMEM = pl.BlockSpec(memory_space=pltpu.SMEM)


def cost(flops):
    return pl.CostEstimate(flops=flops, bytes_accessed=1, transcendentals=0)


def call(kernel, grid, ins, outs, scratch, name, flops, *args):
    out_specs = tuple(spec for spec, _ in outs)
    out_shape = tuple(shape for _, shape in outs)
    return pl.pallas_call(
        kernel,
        grid=grid,
        in_specs=ins,
        out_specs=out_specs,
        out_shape=out_shape,
        scratch_shapes=scratch,
        compiler_params=pltpu.CompilerParams(vmem_limit_bytes=VMEM, dimension_semantics=("arbitrary",) * len(grid)),
        cost_estimate=cost(flops),
        name=name,
    )(*args)


def call_with(me, kernel, steps, ins, outs, scratch, name, flops, *args):
    out_shape = tuple(shape for _, shape in outs)
    return pl.pallas_call(
        kernel,
        grid_spec=pltpu.PrefetchScalarGridSpec(
            num_scalar_prefetch=1, grid=(steps,), in_specs=ins, out_specs=tuple(spec for spec, _ in outs),
            scratch_shapes=scratch),
        out_shape=out_shape,
        compiler_params=pltpu.CompilerParams(vmem_limit_bytes=VMEM, dimension_semantics=("arbitrary",)),
        cost_estimate=cost(flops),
        name=name,
    )(me, *args)


def shaped(*shape, dtype=BF16):
    return jax.ShapeDtypeStruct(shape, dtype)


def flipped(count, change):
    pairs = []
    for source in range(count):
        core, chip = source & 1, source >> 1
        core, chip = change(core, chip)
        pairs.append((source, 2 * chip + core))
    return pairs


def swap(array, change):
    return lax.ppermute(array, "dp", flipped(lax.axis_size("dp"), change))


def other_core(core, chip):
    return core ^ 1, chip


def first_plane(core, chip):
    return core, chip ^ (1 + core)


def second_plane(core, chip):
    return core, chip ^ (2 - core)


def other_plane(distance):
    return lambda core, chip: (core, chip ^ distance)


def other_layer(distance):
    return lambda core, chip: (core, chip ^ (4 * distance))


def split_shards(core_ref, q_ref, k_ref, v_ref, o_ref, u_ref, d_ref, keep_ref, send_ref, down_ref):
    down_ref[...] = d_ref[: down_ref.shape[0], :]
    width = q_ref.shape[1]
    side = width // 2
    first = core_ref[0] == 0

    def put(index, low, high):
        keep_ref[index] = jnp.where(first, low, high).astype(BF16)
        send_ref[index] = jnp.where(first, high, low).astype(BF16)

    for index, ref in enumerate((q_ref, k_ref, v_ref, o_ref)):
        rows = ref[...].astype(F32)
        put(index, rows[:, :side], rows[:, side:])
    up = u_ref[...].astype(F32)
    hidden = up.shape[1]
    deep = hidden // (2 * CHIPS)
    halves = [
        jnp.concatenate([up[:, start : start + deep] for start in range(half * deep, hidden, 2 * deep)], axis=1)
        for half in range(2)
    ]
    for part in range(hidden // width):
        at = slice(part * side, (part + 1) * side)
        put(4 + part, halves[0][:, at], halves[1][:, at])


def join_shards(me_ref, keep_ref, take_ref, down_ref, *refs):
    vectors, (near_ref, up_ref) = refs[:-2], refs[-2:]
    me = me_ref[0]
    first = (me & 1) == 0
    parts, own, side = keep_ref.shape
    folds = parts - 4
    keep = keep_ref[...].astype(F32)
    take = take_ref[...].astype(F32)

    def joined(index):
        low = jnp.where(first, keep[index], take[index])
        high = jnp.where(first, take[index], keep[index])
        return jnp.concatenate((low, high), axis=0).astype(BF16)

    for index in range(4):
        near_ref[2 * own * index : 2 * own * (index + 1), :] = joined(index)
    for index in range(folds):
        up_ref[2 * own * index : 2 * own * (index + 1), :] = joined(4 + index)
    base = 2 * own * folds
    up_ref[base : base + 16, :] = down_ref[-16:, :side]
    up_ref[base + 16 :, :] = down_ref[-16:, side:]
    rows = []
    for ref in vectors:
        flat = ref[...].astype(F32).reshape(1, -1)
        rows.append(jnp.concatenate((flat, jnp.zeros((1, side - flat.shape[1]), F32)), axis=1))
    rows.append(jnp.zeros((16 - len(rows), side), F32))
    rows = jnp.concatenate(rows, axis=0)
    short = pltpu.roll(rows, own * lax.rem(me, side // own), 1)
    long = pltpu.roll(rows, folds * own * lax.rem(me >> 1, side // (folds * own)), 1)
    index = lax.broadcasted_iota(jnp.int32, rows.shape, 0)
    near_ref[8 * own :, :] = jnp.where(index < 8, short, long).astype(BF16)


def across_layers(shard):
    return jnp.stack([shard] + [swap(shard, other_layer(distance)) for distance in (1, 2, 3)])


def after(arrays, *others):
    return lax.optimization_barrier((arrays, others))[0]


def small_call(kernel, args, outs, name, scratch=(), ins=None, flops=0):
    return pl.pallas_call(
        kernel,
        in_specs=ins,
        out_specs=tuple(spec for spec, _ in outs),
        out_shape=tuple(shape for _, shape in outs),
        scratch_shapes=list(scratch),
        compiler_params=pltpu.CompilerParams(vmem_limit_bytes=VMEM),
        cost_estimate=cost(flops),
        name=name,
    )(*args)


VMEM_SPEC = pl.BlockSpec(memory_space=pltpu.VMEM)
ANY_SPEC = pl.BlockSpec(memory_space=pl.ANY)


def prepare(me, weights, vectors):
    own, width = weights[0].shape
    side = width // 2
    deep = weights[5].shape[0]
    folds = deep // own
    halves = (VMEM_SPEC, shaped(4 + folds, own, side))
    keep, send, down = small_call(
        split_shards, (me & 1, *weights), [halves, halves, (VMEM_SPEC, shaped(deep - 16, width))], "split_shards",
        ins=[SMEM] + [VMEM_SPEC] * 6)
    take = swap(send, other_core)
    near, up = small_call(
        join_shards, (me, keep, take, weights[5], *vectors),
        [(VMEM_SPEC, shaped(8 * own + 16, side)), (VMEM_SPEC, shaped(2 * deep + 32, side))], "join_shards",
        ins=[SMEM] + [VMEM_SPEC] * (3 + len(vectors)))
    return near, up, down


def doubled(pieces, change):
    return jnp.concatenate((pieces, swap(pieces, change)))


def gather_down(pieces):
    return doubled(doubled(pieces, first_plane), second_plane)


def gather_plain(weights, vectors):
    squares, up_weight, down_weight = weights[:4], weights[4], weights[5]
    count = lax.axis_size("dp")
    own, width = squares[0].shape
    folds = down_weight.shape[0] // own
    hidden = up_weight.shape[1]
    flat = jnp.concatenate(vectors)
    packed = jnp.concatenate(
        (
            *squares,
            up_weight.reshape(own, folds, width).transpose(1, 0, 2).reshape(own * folds, width),
            down_weight,
            jnp.pad(flat.reshape(1, -1), ((0, 7), (0, width - flat.size))),
        ),
        axis=0,
    )
    whole = lax.all_gather(packed, "dp", axis=0, tiled=True).reshape(count, -1, width)
    square_all = [whole[:, index * own : (index + 1) * own, :].reshape(width, width) for index in range(4)]
    wup = whole[:, 4 * own : (4 + folds) * own, :].reshape(count, folds, own, width).transpose(0, 2, 1, 3)
    wup = wup.reshape(width, 2, CHIPS // 2, 2, -1).transpose(3, 1, 0, 2, 4).reshape(2, 2, width, width)
    wdown = whole[:, (4 + folds) * own : (4 + 2 * folds) * own, :]
    wdown = wdown.reshape(CHIPS, 2, -1, width).transpose(1, 0, 2, 3).reshape(2, hidden // 2, width)
    last = whole[:, (4 + 2 * folds) * own, : flat.size].astype(F32)
    vec = last[:, : 8 * own].reshape(count, 8, own).transpose(1, 0, 2).reshape(8, width)
    bup = last[:, 8 * own :].reshape(CHIPS, 2, -1).transpose(1, 0, 2).reshape(2, 1, -1)
    return (*square_all, (wup, wdown), jnp.pad(vec, ((0, 8), (0, 0))), bup)


def merge_core(core_ref, keep_ref, take_ref, own_ref, send_ref):
    core = core_ref[0]

    def whole(plane):
        return (keep_ref[:, plane].astype(F32) + take_ref[:, plane].astype(F32)).astype(BF16)

    own_ref[:, 0] = whole(0)
    own_ref[:, 1] = whole(2 - core)
    send_ref[:, 0] = whole(1 + core)
    send_ref[:, 1] = whole(3)


def merge_first(*refs):
    pairs, rest_ref, send_ref = refs[:-2], refs[-2], refs[-1]
    base = 0
    for own_ref, take_ref in zip(pairs[::2], pairs[1::2]):
        for part in range(own_ref.shape[0]):
            at = slice(base, base + own_ref.shape[3])
            rest_ref[:, at, :] = (own_ref[part, :, 0].astype(F32) + take_ref[part, :, 0].astype(F32)).astype(BF16)
            send_ref[:, at, :] = (own_ref[part, :, 1].astype(F32) + take_ref[part, :, 1].astype(F32)).astype(BF16)
            base += own_ref.shape[3]


def merge_second(own_ref, take_ref, rest_ref, *send_refs):
    for layer in range(4):
        whole = own_ref[layer].astype(F32) + take_ref[layer].astype(F32)
        if layer == 0:
            rest_ref[...] = whole
        else:
            send_refs[layer - 1][...] = whole.astype(BF16)


def merge_last(deep, core_ref, rest_ref, a_ref, b_ref, c_ref, *refs):
    whole = rest_ref[...] + a_ref[...].astype(F32) + b_ref[...].astype(F32) + c_ref[...].astype(F32)
    first = core_ref[0] == 0
    if deep:
        refs[0][...] = whole[:deep]
        refs = refs[1:]
    keep_ref, send_ref = refs[:2]
    parts, own, _ = keep_ref.shape
    for part in range(parts):
        low = whole[deep + 2 * own * part : deep + 2 * own * part + own]
        high = whole[deep + 2 * own * part + own : deep + 2 * own * (part + 1)]
        keep_ref[part] = jnp.where(first, low, high)
        send_ref[part] = jnp.where(first, high, low)
    if not deep:
        refs[2][...] = whole[2 * own * parts :]


def finish(me_ref, up_keep_ref, up_take_ref, keep_ref, take_ref, flat_ref, late_ref, up_ref, *refs):
    me = me_ref[0]
    first = (me & 1) == 0
    side = keep_ref.shape[2]
    width = 2 * side
    squares, flats = refs[:4], refs[4:]
    own = up_ref.shape[0]
    for number, ref in enumerate(squares):
        keep, take = keep_ref[number], take_ref[number]
        ref[:, :side] = jnp.where(first, keep, take)
        ref[:, side:] = jnp.where(first, take, keep)
    parts = up_keep_ref.shape[0]
    deep = parts * width // CHIPS
    for part in range(parts):
        keep, take = up_keep_ref[part], up_take_ref[part]
        low, high = jnp.where(first, keep, take), jnp.where(first, take, keep)
        pieces = []
        for start in range(0, width, deep):
            pieces += [low[:, start : start + deep], high[:, start : start + deep]]
        up_ref[:, 2 * width * part : 2 * width * (part + 1)] = jnp.concatenate(pieces, axis=1)
    late = jnp.where(me < side // own, late_ref[0:2, :side], late_ref[0:2, side:])
    flat = jnp.concatenate((late, flat_ref[2:]), axis=0)
    long = flats[-1].shape[0]
    short_turn = lax.rem(side - own * lax.rem(me, side // own), side)
    long_turn = lax.rem(side - long * lax.rem(me >> 1, side // long), side)
    short = pltpu.roll(flat, short_turn, 1)
    for number, ref in enumerate(flats[:-1]):
        ref[...] = short[number, :own]
    flats[-1][...] = pltpu.roll(flat, long_turn, 1)[8, :long]


def fenced(function, *args):
    kinds = jax.eval_shape(function, *args)

    def nothing(*_):
        return jax.tree.map(lambda kind: jnp.zeros(kind.shape, kind.dtype), kinds)

    return lax.cond(lax.axis_index("dp") < lax.axis_size("dp"), function, nothing, *args)


def scatter_core(send):
    return swap(send, other_core)


def merge_core_of(core, keep, take):
    shape = keep.shape
    planes, rows, side = shape[-3:]
    keep, take = keep.reshape(-1, planes, rows, side), take.reshape(-1, planes, rows, side)
    count = keep.shape[0]
    steps = MERGE_STEPS
    block = pl.BlockSpec((count // steps, planes, rows, side), lambda i: (i, 0, 0, 0))
    half = (pl.BlockSpec((count // steps, 2, rows, side), lambda i: (i, 0, 0, 0)), shaped(count, 2, rows, side))
    own, send = call(merge_core, (steps,), [SMEM, block, block], [half, half], [], "merge_core", 0, core, keep, take)
    return own.reshape(-1, CHIPS // 4, 2, rows, side), send


def scatter_second(*pairs):
    _, count, _, _, side = pairs[0].shape
    rows = sum(piece.shape[0] * piece.shape[3] for piece in pairs[::2])
    steps = MERGE_STEPS
    ins = [pl.BlockSpec((piece.shape[0], count // steps, *piece.shape[2:]), lambda i: (0, i, 0, 0, 0)) for piece in pairs]
    out = pl.BlockSpec((count // steps, rows, side), lambda i: (i, 0, 0))
    rest, send = call(
        merge_first, (steps,), ins, [(out, shaped(count, rows, side))] * 2, [],
        "merge_first", 0, *pairs)
    return rest, swap(send, second_plane)


def merge_layers_of(own, take):
    _, rows, side = own.shape
    out = shaped(rows, side)
    return small_call(
        merge_second, (own, take), [(VMEM_SPEC, shaped(rows, side, dtype=F32))] + [(VMEM_SPEC, out)] * 3,
        "merge_second", ins=[VMEM_SPEC] * 2)


def scatter_layers(own, take):
    rest, *sends = merge_layers_of(own, take)
    return [rest] + [swap(piece, other_layer(r + 1)) for r, piece in enumerate(sends)]


def scatter_last(core, pieces, own, parts, deep):
    rows, side = pieces[0].shape
    outs = [(VMEM_SPEC, shaped(parts, own, side, dtype=F32))] * 2
    if deep:
        outs = [(VMEM_SPEC, shaped(deep, side, dtype=F32))] + outs
    else:
        outs.append((VMEM_SPEC, shaped(rows - 2 * own * parts, side, dtype=F32)))
    return small_call(
        functools.partial(merge_last, deep), (core, *pieces), outs, "merge_last", ins=[SMEM] + [VMEM_SPEC] * 4, flops=SHORT if deep else 0)


def reduce_plain(down_pairs, up_pairs, square_pair, flat):
    def scattered(array, axis):
        return lax.psum_scatter(array, "dp", scatter_dimension=axis, tiled=True).astype(F32)

    def planes(own, send, core):
        order = (own[..., 0, :, :], send[..., 0, :, :], own[..., 1, :, :], send[..., 1, :, :])
        if core == 1:
            order = (order[0], order[2], order[1], order[3])
        return jnp.stack(order, axis=-3)

    down = jnp.stack([planes(*pair, core) for core, pair in enumerate(down_pairs)])
    up = jnp.stack([planes(*pair, core) for core, pair in enumerate(up_pairs)])
    width = down.shape[-1]
    each = up.shape[4]
    down = down.transpose(1, 2, 0, 3, 4).reshape(-1, width)
    up = up.reshape(2, 2, CHIPS, each, CHIPS // 2, -1).transpose(2, 3, 1, 4, 0, 5).reshape(CHIPS * each, -1)
    square = jnp.stack(square_pair).transpose(1, 2, 3, 0, 4)[:, :, : 4 * each]
    square = square.reshape(CHIPS, 4, each, width).transpose(1, 0, 2, 3).reshape(4, CHIPS * each, width)
    return (
        scattered(down, 0),
        scattered(up, 0),
        *scattered(square, 1),
        lax.psum_scatter(flat, "dp", scatter_dimension=0, tiled=True).reshape(-1),
    )


def body(tokens, lengths, attn_gain, attn_shift, query_weight, query_bias, key_weight, value_weight, value_bias,
         out_weight, out_bias, mlp_gain, mlp_shift, up_weight, up_bias, down_weight, down_bias, grad_out):
    count = lax.axis_size("dp")
    rows, width = tokens.shape
    tiles = lengths.shape[0]
    tile = rows // tiles
    hidden = up_bias.shape[0] * count
    own = width // count
    folds = hidden // width
    vectors = (attn_gain, attn_shift, query_bias, value_bias, out_bias, mlp_gain, mlp_shift, down_bias, up_bias)
    by_hand = count == 2 * CHIPS
    me = lax.axis_index("dp").astype(jnp.int32).reshape(1) if by_hand else jnp.zeros((1,), jnp.int32)
    core = me & 1
    weights = (query_weight, key_weight, value_weight, out_weight, up_weight, down_weight)

    tile_rows = rows_spec(tile, width)
    square = whole_spec((width, width))
    vec_spec = whole_spec((16, width))
    sums = (kept_spec((8, width)), shaped(8, width, dtype=F32))
    low_rows = (tile_rows, shaped(rows, width))
    fold = 2 if tiles % 2 == 0 else 1
    wide_rows = rows_spec(fold * tile, width)
    wide_low = (wide_rows, shaped(rows, width))
    lse_spec = rows_spec(tile, LANES)
    mac = 2 * rows * width * width
    kept_vec = (kept_spec((16, width)), shaped(16, width, dtype=F32))
    kept_hidden = (kept_spec((1, hidden // 2)), shaped(1, hidden // 2, dtype=F32))
    side = width // 2

    def masked(*earlier):
        return call(
            mask_grads, (tiles,), [SMEM, tile_rows], [low_rows, sums], [], "mask_grads", 0,
            lengths, after(grad_out, *earlier))

    high_rows = (tile_rows, shaped(rows, width, dtype=F32))

    def attend(q, k, v, vec, wo):
        return call(
            attention_forward, (tiles,), [SMEM, tile_rows, vec_spec, tile_rows, tile_rows, tile_rows, square],
            [low_rows, (lse_spec, shaped(rows, LANES, dtype=F32)), high_rows, low_rows],
            [], "attention_forward", 0, lengths, tokens, vec, q, k, v, wo)

    def gather_first(near):
        cot, sum_down = masked(near)
        along = after(swap(near, first_plane), cot)
        return along, swap(near, second_plane), cot, sum_down

    def gather_second(near, along, across, cot, up_two, up_taken):
        cot_other = swap(cot, other_core)
        corner = swap(along, second_plane)
        taken = [swap(near, other_core), swap(along, other_core)]
        across, corner_out = after((across, corner), taken)
        taken += [swap(across, other_core), swap(corner_out, other_core)]
        return corner, taken, cot_other, jnp.concatenate((up_two, up_taken))

    def attend_by_hand(q, k, v, vec, wo, up_four, up_along):
        up = [swap(up_four, second_plane), swap(up_along, second_plane)]
        mixed, lse, resid, n2 = attend(q, k, v, vec, wo)
        n2_other = fenced(scatter_core, n2)
        up = after(up, n2_other)
        return mixed, lse, resid, n2, n2_other, up

    if by_hand:
        near, up, down = prepare(me, weights, vectors)
        down = after(down, near)[None]
        down_two = doubled(down, other_layer(1))
        near_moved = [swap(near, other_layer(r)) for r in (1, 2, 3)]
        up_moved = swap(up, other_layer(1))
        down_shard = fenced(gather_down, after(down_two, near))
        near_moved, up_moved = after((near_moved, up_moved), down_shard)
        near = jnp.stack([near] + near_moved)
        up_two = jnp.stack((up, up_moved))
        near, up_two = after((near, up_two))
        up_moved = swap(up_two, other_layer(2))
        along, across, cot, sum_down = fenced(gather_first, near)
        up_taken = after(up_moved, along)
        down = [down_shard, swap(after(down_shard, up_taken), other_layer(2))]
        corner, taken, cot_other, up_four = fenced(gather_second, near, along, across, cot, up_two, up_taken)
        near = [near, along, across, corner] + taken
        up_along = swap(up_four, first_plane)
        n1, q, k, v, wq, wk, wv, wo, vec, bup = call_with(
            me, project, tiles, [tile_rows] + [ANY_SPEC] * 8,
            [low_rows] * 4 + [(ANY_SPEC, shaped(width, width))] * 4 + [kept_vec, kept_hidden],
            [pltpu.VMEM((4, width, width), BF16), pltpu.VMEM((CHIPS, width // (4 * CHIPS) + 1, 16, width), BF16),
             pltpu.SemaphoreType.DMA((1,)), pltpu.SemaphoreType.DMA((4,))],
            "project", LATER, tokens, *[piece.reshape(4, -1, 16, side) for piece in after(near)])
        up_along = after(up_along, n1)
        mixed, lse, resid, n2, n2_other, up_moved = fenced(attend_by_hand, q, k, v, vec, wo, up_four, up_along)
        up = [up_along] + up_moved
        hidden_weights = [(up_four, *up, *down)]
    else:
        wq, wk, wv, wo, hidden_weights, vec, bup = gather_plain(weights, vectors)
        hidden_weights = list(zip(*hidden_weights))
        cot, sum_down = masked()
        n1, q, k, v = call(
            project_rows, (tiles,), [tile_rows, vec_spec, square, square, square], [low_rows] * 4,
            [], "project", 0, tokens, vec, wq, wk, wv)
        mixed, lse, resid, n2 = attend(q, k, v, vec, wo)

    each = width // CHIPS
    deep = hidden // (2 * CHIPS)
    blocks = hidden // (2 * width)
    full_rows = whole_spec((rows, width))
    hidden_spec = pl.BlockSpec((1, width), lambda i, me: (0, i))
    low_out, high_out = (ANY_SPEC, shaped(rows, width)), (ANY_SPEC, shaped(rows, width, dtype=F32))
    act_out = (ANY_SPEC, shaped(rows, blocks * width))
    down_part = (ANY_SPEC, shaped(4, 2, deep, width))
    up_part = (ANY_SPEC, shaped(blocks, 4, 2, each, width))

    act_spec = pl.BlockSpec((fold * tile, blocks * width), lambda i, *me: (i, 0))
    wide_spec = whole_spec((hidden // 2, width))

    def run_mlp(me, tokens_of, bup, sources):
        sets = len(tokens_of[0])
        low, high = pltpu.VMEM((sets * rows, width), BF16), pltpu.VMEM((sets * rows, width), F32)
        weight = pltpu.VMEM((2, width, width), BF16)
        dma = pltpu.SemaphoreType.DMA((2, sets))
        return call_with(
            me, functools.partial(mlp, sets, len(sources)), blocks,
            [ANY_SPEC] * (2 * sets) + [hidden_spec] + [ANY_SPEC] * len(sources),
            [act_out] * sets + [high_out] + [low_out] * (sets - 1) + [down_part] * 2 + [up_part] * 2
            + [(ANY_SPEC, shaped(hidden // 2, width)), (hidden_spec, shaped(1, hidden // 2, dtype=F32))],
            [low, low, high, pltpu.VMEM((blocks, sets * rows, width), BF16), low, low, weight, weight,
             pltpu.VMEM((blocks, width, width), BF16), pltpu.VMEM((hidden // 2, width), BF16), dma,
             pltpu.SemaphoreType.DMA((blocks, sets)), pltpu.SemaphoreType.DMA((sets,)), pltpu.SemaphoreType.DMA((4,)),
             pltpu.SemaphoreType.DMA((blocks + 1,))],
            "mlp", 0, *tokens_of[0], *tokens_of[1], bup, *sources)

    if by_hand:
        act_own, act_other, gtwo, gtwo_other, down_own, down_send, up_own, up_send, wdown, sum_up = run_mlp(
            me, ((n2, n2_other), (cot, cot_other)), bup, hidden_weights[0])
        gtwo_take = swap(gtwo_other, other_core)
        parts = (-1, CHIPS // 4, 2)
        down_first = [piece.reshape(*parts, deep, width) for piece in (down_own, swap(down_send, first_plane))]
        up_first = [piece.reshape(*parts, each, width) for piece in (up_own, swap(up_send, first_plane))]
    else:
        runs = [run_mlp(me + half, ((n2,), (cot,)), bup[half], hidden_weights[half]) for half in range(2)]
        (act_own, gtwo), (act_other, gtwo_take) = ((run[0], run[1]) for run in runs)
        gtwo_take = gtwo_take.astype(BF16)
        sum_up = jnp.concatenate([run[7] for run in runs], axis=1)
    grads_spec = pl.BlockSpec((4, tile, width), lambda i, *me: (0, i, 0))
    grads, gresid, sum_back = call(
        attention_backward, (tiles,),
        [SMEM, tile_rows, tile_rows, tile_rows, lse_spec, tile_rows, tile_rows, tile_rows, tile_rows, vec_spec, square],
        [(grads_spec, shaped(4, rows, width)), high_rows, sums], [pltpu.VMEM((tile, width), BF16)],
        "attention_backward", 0, lengths, q, k, v, lse, cot, resid, gtwo, gtwo_take, vec, wo)
    sum_spec = whole_spec((8, width))
    pair_shape = (CHIPS // 4, 4, 4 * each + 16, side)
    columns = pl.BlockSpec((1, rows, width), lambda i, me: (i, 0, 0))

    def run_weights(grads):
        return call_with(
            me, weight_grads, 4, [full_rows, ANY_SPEC, columns, sum_spec, sum_spec, whole_spec((1, sum_up.shape[1]))],
            [(ANY_SPEC, shaped(*pair_shape))] * 2,
            [pltpu.VMEM(pair_shape, BF16)] * 2
            + [pltpu.VMEM((rows, width), BF16), pltpu.SemaphoreType.DMA((1,)), pltpu.SemaphoreType.DMA((2, 5))],
            "weight_grads", 0,
            n1, mixed, grads, sum_back, sum_down, sum_up)

    def run_tokens(gresid):
        return call(
            tokens_backward, (tiles // fold,),
            [wide_rows, wide_rows, vec_spec, pl.BlockSpec((4, fold * tile, width), lambda i: (0, i, 0)), square, square, square],
            [wide_low, sums], [], "tokens_backward", MIDDLE, tokens, gresid, vec, grads, wq, wk, wv)

    if by_hand:
        (out_other,) = call_with(
            me, mlp_out_other, tiles // fold, [act_spec, wide_spec], [wide_low], [], "mlp_out_other", 0, after(act_other, grads), wdown)
        down_first, up_first = after((down_first, up_first), out_other)
        hidden_rest, hidden_take = scatter_second(*down_first, *up_first)

        def weights_of_chip(grads, out_take):
            square_send, square_keep = run_weights(grads)
            (out,) = call_with(
                me, mlp_out_own, tiles // fold, [wide_rows, vec_spec, act_spec, wide_rows, wide_spec], [wide_low], [],
                "mlp_out_own", 0, resid, vec, act_own, after(out_take, square_send), wdown)
            square_take = after(scatter_core(square_send), out)
            return *merge_core_of(core, square_keep, square_take), out

        out_take = swap(out_other, other_core)
        square_own, square_send, out = fenced(weights_of_chip, after(grads, hidden_rest), out_take)
        square_take = swap(square_send, first_plane).reshape(square_own.shape)
        hidden_rest, hidden_take = after((hidden_rest, hidden_take), square_own)
        hidden_layers = scatter_layers(hidden_rest, hidden_take)
        gtok, late = run_tokens(after(gresid, hidden_layers[0]))
        square_take = after(square_take, late)
        late = late + swap(late, other_core)
        square_second = scatter_second(square_own, square_take)
        late = after(late, square_second[0])
        late = late + swap(late, other_layer(1))
        hidden_layers = after(hidden_layers, late)
        g_down, up_keep, up_send = scatter_last(core, hidden_layers, own, blocks, deep)
        up_take = scatter_core(up_send)
        late_take = after(swap(late, other_layer(2)), g_down)
        square_second = after(square_second, g_down)
        rest, *sends = merge_layers_of(*square_second)
        late_take = after(late_take, rest)
        sends = after(sends, late_take)
        square_layers = [rest] + [swap(piece, other_layer(r + 1)) for r, piece in enumerate(sends)]
        late = late + late_take
        late = late + after(swap(late, other_plane(1)), rest)
        late = late + swap(late, other_plane(2))
        square_layers = after(square_layers, late)
        square_keep, square_send, flat = scatter_last(core, square_layers, own, 4, 0)
        square_take = scatter_core(square_send)
        outs = [(VMEM_SPEC, shaped(own, hidden, dtype=F32))] + [(VMEM_SPEC, shaped(own, width, dtype=F32))] * 4
        outs += [(VMEM_SPEC, shaped(own, dtype=F32))] * 8 + [(VMEM_SPEC, shaped(folds * own, dtype=F32))]
        g_up, g_q, g_k, g_v, g_o, *g_flat, g_ub = small_call(
            finish, (me, up_keep, up_take, square_keep, square_take, flat, late), outs, "finish",
            ins=[SMEM] + [VMEM_SPEC] * 6)
    else:
        square_send, square_keep = run_weights(grads)
        gtok, sum_one = run_tokens(gresid)
        flat = jnp.concatenate((sum_one[0:2], sum_back[0:5], sum_down[0:1]), axis=0)
        flat = flat.reshape(8, count, own).transpose(1, 0, 2).reshape(count, 8 * own)
        hidden_sums = sum_up.reshape(2, CHIPS, deep).transpose(1, 0, 2).reshape(count, folds * own)
        flat = jnp.concatenate((flat, hidden_sums), axis=1)
        g_down, g_up, g_q, g_k, g_v, g_o, flat = reduce_plain(
            [run[2:4] for run in runs], [run[4:6] for run in runs], (square_keep, square_send), flat)
        (out_other,) = call_with(
            me + 1, mlp_out_other, tiles // fold, [act_spec, wide_spec], [wide_low], [], "mlp_out_other", 0, act_other, runs[1][6])
        (out,) = call_with(
            me, mlp_out_own, tiles // fold, [wide_rows, vec_spec, act_spec, wide_rows, wide_spec], [wide_low], [],
            "mlp_out_own", 0, resid, vec, act_own, out_other, runs[0][6])
        g_flat = [flat[index * own : (index + 1) * own] for index in range(8)]
        g_ub = flat[8 * own :]
    g_gain, g_shift, g_qb, g_vb, g_ob, g_mg, g_ms, g_db = g_flat
    return (out, gtok, g_gain, g_shift, g_q, g_qb, g_k, g_v, g_vb, g_o, g_ob, g_mg, g_ms, g_up, g_ub, g_down, g_db)


def solution(mesh):
    rows, flat = P("dp", None), P("dp")
    return jax.shard_map(
        body,
        mesh=mesh,
        in_specs=(rows, rows, flat, flat, rows, flat, rows, rows, flat, rows, flat, flat, flat, rows, flat, rows, flat, rows),
        out_specs=(rows, rows, flat, flat, rows, flat, rows, rows, flat, rows, flat, flat, flat, rows, flat, rows, flat),
        check_vma=False,
    )
```

```python
import functools

import jax
import jax.numpy as jnp
from jax import lax
from jax.experimental import pallas as pl
from jax.experimental.pallas import tpu as pltpu
from jax.sharding import PartitionSpec as P

HEADS = 12
HEAD_DIM = 64
PAIRS = 6
LANES = 128
CHIPS = 16
MERGE_STEPS = 2
LONG = 10**11
SHORT = 6 * 10**9
MIDDLE = 115 * 10**8
LATER = 9 * 10**9
EPS = 1e-06
MASKED = -1e30
SCALE = HEAD_DIM**-0.5
GELU_C = 0.7978845608028654
GELU_A = 0.044715
VMEM = 64 * 1024 * 1024 - 65536
F32 = jnp.float32
BF16 = jnp.bfloat16


def dot_nn(left, right):
    return lax.dot_general(left, right, (((1,), (0,)), ((), ())), preferred_element_type=F32)


def dot_nt(left, right):
    return lax.dot_general(left, right, (((1,), (1,)), ((), ())), preferred_element_type=F32)


def dot_tn(left, right):
    return lax.dot_general(left, right, (((0,), (0,)), ((), ())), preferred_element_type=F32)


def normalize(rows):
    centered = rows - jnp.mean(rows, axis=-1, keepdims=True)
    inverse = lax.rsqrt(jnp.mean(centered * centered, axis=-1, keepdims=True) + EPS)
    return centered * inverse, inverse


def norm_back(grads, gain, hat, inverse):
    scaled = grads * gain
    mean = jnp.mean(scaled, axis=-1, keepdims=True)
    mean_hat = jnp.mean(scaled * hat, axis=-1, keepdims=True)
    return inverse * (scaled - mean - hat * mean_hat)


def column_sum(rows):
    return jnp.sum(rows, axis=0, keepdims=True)


def segments(lengths_ref, tile, slots, rows, axis):
    shape = (rows, 1) if axis == 0 else (1, rows)
    index = lax.broadcasted_iota(jnp.int32, shape, axis)
    segment = jnp.zeros(shape, jnp.int32)
    bound = 0
    for slot in range(slots):
        bound = bound + lengths_ref[tile, slot]
        segment = segment + (index >= bound).astype(jnp.int32)
    return segment


def mask_bias(lengths_ref, tile, slots, rows):
    same = segments(lengths_ref, tile, slots, rows, 0) == segments(lengths_ref, tile, slots, rows, 1)
    return jnp.where(same, 0.0, MASKED).astype(F32)


def half_of(pair, side):
    lane = lax.broadcasted_iota(jnp.int32, pair.shape, 1)
    keep = lane < HEAD_DIM if side == 0 else lane >= HEAD_DIM
    return jnp.where(keep, pair, jnp.zeros_like(pair))


def fetch_weights(me, sources, stage_ref, sem):
    core, chip = me & 1, me >> 1
    side = sources[0].shape[3]
    for index, source in enumerate(sources):
        half = core if index < 4 else 1 - core
        plane = (0, 1 + half, 2 - half, 3)[index % 4]
        cols = pl.ds(pl.multiple_of(half * side, LANES), side)
        for layer in range(4):
            owner = chip ^ (4 * layer + plane)
            pltpu.make_async_copy(source.at[layer], stage_ref.at[owner, :, :, cols], sem.at[0]).start()


def project(me_ref, x_ref, *refs):
    sources = refs[:8]
    n1_ref, q_ref, k_ref, v_ref = refs[8:12]
    outs, (vec_ref, bup_ref, weights_ref, stage_ref, sem, out_sem) = refs[12:16], refs[16:]
    step = pl.program_id(0)
    core = me_ref[0] & 1
    weights = [weights_ref.at[number] for number in range(4)]

    def write(number):
        return pltpu.make_async_copy(weights[number], outs[number], out_sem.at[number])

    @pl.when(step == 0)
    def _():
        fetch_weights(me_ref[0], sources, stage_ref, sem)
        pltpu.make_async_copy(stage_ref, stage_ref, sem.at[0]).wait()
        width = stage_ref.shape[3]
        side = width // 2
        blocks = width // (16 * CHIPS)
        for number in range(4):
            weights[number][...] = stage_ref[:, number * blocks : (number + 1) * blocks].reshape(width, width)
            write(number).start()
        parts = [stage_ref[chip, 4 * blocks].astype(F32) for chip in range(CHIPS)]
        halves = []
        for half in range(2):
            group = parts[half * CHIPS // 2 : (half + 1) * CHIPS // 2]
            halves.append(sum(part[:, :side] + part[:, side:] for part in group))
        vec_ref[...] = jnp.concatenate(halves, axis=1)
        blocks = bup_ref.shape[1] // side
        group = CHIPS // blocks
        for block in range(blocks):
            rows = sum(parts[block * group : (block + 1) * group])
            bup_ref[:, block * side : (block + 1) * side] = jnp.where(core == 0, rows[8:9, :side], rows[8:9, side:])

    project_rows(x_ref, vec_ref, *weights[:3], n1_ref, q_ref, k_ref, v_ref)

    @pl.when(step == pl.num_programs(0) - 1)
    def _():
        for number in range(4):
            write(number).wait()


def project_rows(x_ref, vec_ref, wq_ref, wk_ref, wv_ref, n1_ref, q_ref, k_ref, v_ref):
    hat, _ = normalize(x_ref[...].astype(F32))
    n1 = (hat * vec_ref[0:1, :] + vec_ref[1:2, :]).astype(BF16)
    n1_ref[...] = n1
    q_ref[...] = (dot_nn(n1, wq_ref[...]) + vec_ref[2:3, :]).astype(BF16) * jnp.asarray(SCALE, BF16)
    k_ref[...] = dot_nn(n1, wk_ref[...]).astype(BF16)
    v_ref[...] = (dot_nn(n1, wv_ref[...]) + vec_ref[3:4, :]).astype(BF16)


def mask_grads(lengths_ref, grad_ref, cot_ref, dsum_ref):
    tile = pl.program_id(0)
    slots = lengths_ref.shape[1]
    valid = segments(lengths_ref, tile, slots, grad_ref.shape[0], 0) < slots
    cot = jnp.where(valid, grad_ref[...].astype(F32), 0.0)
    cot_ref[...] = cot.astype(BF16)

    @pl.when(tile == 0)
    def _():
        dsum_ref[...] = jnp.zeros_like(dsum_ref)

    dsum_ref[0:1, :] += column_sum(cot)


def attention_forward(lengths_ref, x_ref, vec_ref, q_ref, k_ref, v_ref, wo_ref, mixed_ref, lse_ref, resid_ref, n2_ref):
    tile = pl.program_id(0)
    rows = q_ref.shape[0]
    slots = lengths_ref.shape[1]
    bias = mask_bias(lengths_ref, tile, slots, rows)
    lane = lax.broadcasted_iota(jnp.int32, (rows, LANES), 1)
    lse = jnp.zeros((rows, LANES), F32)

    def at(pair):
        return pl.ds(pair * LANES, LANES)

    def scores_of(pair):
        qp, kp = q_ref[:, at(pair)], k_ref[:, at(pair)]
        return [dot_nt(half_of(qp, side), kp) for side in range(2)]

    def softmax_of(scores):
        scores = scores + bias
        top = jnp.max(scores, axis=-1, keepdims=True)
        weights = jnp.exp(scores - top)
        sums = jnp.sum(weights, axis=-1, keepdims=True)
        return (weights.astype(BF16), 1.0 / sums), top + jnp.log(sums)

    raw = {}
    probs = {}
    for turn in range(PAIRS + 2):
        if turn < PAIRS:
            raw[turn] = scores_of(turn)
        if 0 <= turn - 1 < PAIRS:
            both = [softmax_of(scores) for scores in raw.pop(turn - 1)]
            for side in range(2):
                lse = jnp.where(lane == 2 * (turn - 1) + side, both[side][1], lse)
            probs[turn - 1] = [pair[0] for pair in both]
        if turn >= 2:
            vp = v_ref[:, at(turn - 2)]
            parts = [dot_nn(probs[turn - 2][side][0], half_of(vp, side)) * probs[turn - 2][side][1] for side in range(2)]
            mixed_ref[:, at(turn - 2)] = (parts[0] + parts[1]).astype(BF16)
    lse_ref[...] = lse
    resid = x_ref[...].astype(F32) + (dot_nn(mixed_ref[...], wo_ref[...]) + vec_ref[4:5, :])
    resid_ref[...] = resid
    hat, _ = normalize(resid)
    n2_ref[...] = (hat * vec_ref[5:6, :] + vec_ref[6:7, :]).astype(BF16)


def spread(me, rows, put):
    layer, plane = me >> 3, (me >> 1) & 3
    each = rows.shape[0] // CHIPS
    for chip in range(CHIPS):
        put((chip & 3) ^ plane, (chip >> 2) ^ layer, rows[chip * each : (chip + 1) * each].astype(BF16))


def fetch_hidden(me, sources, wup_ref, wdown_ref, sem):
    if len(sources) == 2:
        for number in range(wup_ref.shape[0]):
            pltpu.make_async_copy(sources[0].at[number], wup_ref.at[number], sem.at[number]).start()
        pltpu.make_async_copy(sources[1], wdown_ref, sem.at[wup_ref.shape[0]]).start()
        return
    core, chip = me & 1, me >> 1
    planes = (0, 1 + core, 2 - core, 3)
    blocks, width = wup_ref.shape[:2]
    each, deep = width // CHIPS, wdown_ref.shape[0] // CHIPS
    for layer in range(4):
        for index, plane in enumerate(planes):
            owner = chip ^ (4 * layer + plane)
            rows = pl.ds(pl.multiple_of(owner * each, 16), each)
            side = sources[index].shape[2]
            for part in range(sources[index].shape[1] // each):
                number, cols = part * side // width, pl.ds(part * side % width, side)
                pltpu.make_async_copy(
                    sources[index].at[layer, pl.ds(part * each, each), :], wup_ref.at[number, rows, cols], sem.at[number]
                ).start()
            source = sources[4 + layer // 2].at[2 * index + layer % 2]
            rows = pl.ds(pl.multiple_of(owner * deep, 16), source.shape[0])
            pltpu.make_async_copy(source, wdown_ref.at[rows, :], sem.at[blocks]).start()
            rest = deep - source.shape[0]
            rows = pl.ds(pl.multiple_of(owner * deep + source.shape[0], 16), rest)
            for part in range(width // side):
                at = pl.ds(sources[index].shape[1] - (width // side - part) * rest, rest)
                pltpu.make_async_copy(
                    sources[index].at[layer, at, :], wdown_ref.at[rows, pl.ds(part * side, side)], sem.at[blocks]
                ).start()


def mlp(sets, count, me_ref, *refs):
    n2_hbm, cot_hbm = refs[:sets], refs[sets : 2 * sets]
    bup_ref = refs[2 * sets]
    sources = refs[2 * sets + 1 : 2 * sets + 1 + count]
    refs = refs[2 * sets + 1 + count :]
    act_hbm, gtwo_hbm, refs = refs[:sets], refs[sets : 2 * sets], refs[2 * sets :]
    down_own, down_send, up_own, up_send, wdown_hbm, dbu_ref = refs[:6]
    n2_ref, cot_ref, gacc, act_ref, gup_ref, low_ref, gdown_ref, gupw_ref = refs[6:14]
    wup_all, wdown_all, in_sem, act_sem, out_sem, grad_sem, weight_sem = refs[14:]
    step = pl.program_id(0)
    last = pl.num_programs(0) - 1
    me = me_ref[0]
    rows = n2_ref.shape[0] // sets

    def rows_of(index):
        return pl.ds(pl.multiple_of(index * rows, rows), rows)

    blocks, width = wup_all.shape[:2]

    @pl.when(step == 0)
    def _():
        fetch_hidden(me, sources, wup_all, wdown_all, weight_sem)
        for index in range(sets):
            at = pl.ds(index * rows, rows)
            pltpu.make_async_copy(n2_hbm[index], n2_ref.at[at, :], in_sem.at[0, index]).start()
            pltpu.make_async_copy(cot_hbm[index], cot_ref.at[at, :], in_sem.at[1, index]).start()

    pltpu.make_async_copy(wup_all.at[step], wup_all.at[step], weight_sem.at[step]).wait()
    write_down = pltpu.make_async_copy(wdown_all, wdown_hbm, weight_sem.at[blocks])

    @pl.when(step == 0)
    def _():
        pltpu.make_async_copy(wdown_all, wdown_all, weight_sem.at[blocks]).wait()
        write_down.start()

    wup = wup_all[step]
    wdown = wdown_all[pl.ds(pl.multiple_of(step * width, width), width), :]
    dbu_ref[...] = jnp.zeros_like(dbu_ref)
    slot = lax.rem(step, 2)

    @pl.loop(0, sets)
    def _(index):
        at = rows_of(index)

        @pl.when(step == 0)
        def _():
            pltpu.make_async_copy(n2_ref.at[at, :], n2_ref.at[at, :], in_sem.at[0, index]).wait()
            pltpu.make_async_copy(cot_ref.at[at, :], cot_ref.at[at, :], in_sem.at[1, index]).wait()

        pre = dot_nn(n2_ref[at, :], wup) + bup_ref[...]
        grad_act = dot_nt(cot_ref[at, :], wdown)
        square = pre * pre
        tanh = jnp.tanh(pre * (GELU_C + (GELU_C * GELU_A) * square))
        half = 0.5 + 0.5 * tanh
        inner = GELU_C + (3.0 * GELU_C * GELU_A) * square
        act_ref[slot, at, :] = (pre * half).astype(BF16)
        gup = (grad_act * (half + (0.5 * pre) * (1.0 - tanh * tanh) * inner)).astype(BF16)
        gup_ref[at, :] = gup
        dbu_ref[...] += column_sum(gup.astype(F32))

    @pl.when(step == 0)
    def _():
        @pl.loop(0, sets)
        def _(index):
            at = rows_of(index)
            gacc[at, :] = dot_nt(gup_ref[at, :], wup)

    @pl.when((step > 0) & (step < last))
    def _():
        @pl.loop(0, sets)
        def _(index):
            at = rows_of(index)
            gacc[at, :] += dot_nt(gup_ref[at, :], wup)

    def results():
        for index in range(sets):
            at = pl.ds(index * rows, rows)
            source = low_ref.at[at, :] if index else gacc.at[at, :]
            yield pltpu.make_async_copy(source, gtwo_hbm[index], out_sem.at[index])

    def activations(number):
        for index in range(sets):
            source = act_ref.at[number, pl.ds(index * rows, rows), :]
            cols = pl.ds(number * width, width)
            yield pltpu.make_async_copy(source, act_hbm[index].at[:, cols], act_sem.at[number, index])

    for number in range(act_ref.shape[0]):

        @pl.when(step == number)
        def _():
            for copy in activations(number):
                copy.start()

    @pl.when(step == last)
    def _():
        @pl.loop(0, sets)
        def _(index):
            at = rows_of(index)
            total = gacc[at, :] + dot_nt(gup_ref[at, :], wup)
            gacc[at, :] = total
            low_ref[at, :] = total.astype(BF16)

        for copy in results():
            copy.start()

    gdown_ref[slot] = dot_tn(act_ref[slot], cot_ref[...]).astype(BF16)
    deep = down_own.shape[2]
    count = gdown_ref.shape[1] // deep
    for index in range(count):
        chip = step * count + index
        source = gdown_ref.at[slot, pl.ds(index * deep, deep), :]
        keep_or_send(me, chip & 3, (chip >> 2) ^ (me >> 3), source, down_own, down_send, grad_sem, 0)

    gupw_ref[slot] = dot_tn(n2_ref[...], gup_ref[...]).astype(BF16)
    each = gupw_ref.shape[1] // CHIPS
    for chip in range(CHIPS):
        source = gupw_ref.at[slot, pl.ds(chip * each, each), :]
        keep_or_send(
            me, chip & 3, (chip >> 2) ^ (me >> 3), source, up_own.at[step], up_send.at[step], grad_sem, 2)

    @pl.when(step == last)
    def _():
        for copy in results():
            copy.wait()
        write_down.wait()
        for number in range(act_ref.shape[0]):
            for copy in activations(number):
                copy.wait()
        for number, ref in enumerate((down_own, down_send, up_own, up_send)):
            pltpu.make_async_copy(ref, ref, grad_sem.at[number]).wait()


def keep_or_send(me, plane, layer, source, own_ref, send_ref, sem, number):
    core = me & 1
    relative = plane ^ ((me >> 1) & 3)
    mine = (relative == 0) | (relative == 2 - core)

    @pl.when(mine)
    def _():
        pltpu.make_async_copy(source, own_ref.at[layer, jnp.where(relative == 0, 0, 1)], sem.at[number]).start()

    @pl.when(jnp.logical_not(mine))
    def _():
        pltpu.make_async_copy(source, send_ref.at[layer, jnp.where(relative == 3, 1, 0)], sem.at[number + 1]).start()


def mlp_out_other(me_ref, act_ref, wdown_ref, out_ref):
    out_ref[...] = dot_nn(act_ref[...], wdown_ref[...]).astype(BF16)


def mlp_out_own(me_ref, resid_ref, vec_ref, act_ref, take_ref, wdown_ref, out_ref):
    half = dot_nn(act_ref[...], wdown_ref[...]) + take_ref[...].astype(F32)
    out_ref[...] = (resid_ref[...] + (half + vec_ref[7:8, :])).astype(BF16)


def attention_backward(lengths_ref, q_ref, k_ref, v_ref, lse_ref, cot_ref, resid_ref, gtwo_ref, gother_ref, vec_ref, wo_ref,
                       grads_ref, gresid_ref, dsum_ref, gmix_ref):
    tile = pl.program_id(0)
    rows = q_ref.shape[0]

    @pl.when(tile == 0)
    def _():
        dsum_ref[...] = jnp.zeros_like(dsum_ref)

    hat, inverse = normalize(resid_ref[...])
    grad_two = gtwo_ref[...] + gother_ref[...].astype(F32)
    gresid = cot_ref[...].astype(F32) + norm_back(grad_two, vec_ref[5:6, :], hat, inverse)
    gresid_ref[...] = gresid
    gattn = gresid.astype(BF16)
    grads_ref[3] = gattn
    dsum_ref[2:3, :] += column_sum(gattn.astype(F32))
    dsum_ref[3:4, :] += column_sum(grad_two * hat)
    dsum_ref[4:5, :] += column_sum(grad_two)
    gmix_ref[...] = dot_nt(gattn, wo_ref[...]).astype(BF16)
    bias = mask_bias(lengths_ref, tile, lengths_ref.shape[1], rows)

    def load(pair):
        cols = pl.ds(pair * LANES, LANES)
        return q_ref[:, cols], k_ref[:, cols], v_ref[:, cols], gmix_ref[:, cols]

    def products_of(pair):
        qp, kp, vp, gp = load(pair)
        return [(dot_nt(half_of(qp, side), kp), dot_nt(half_of(gp, side), vp)) for side in range(2)]

    def softmax_back(pair, products):
        results = []
        for side, (scores, grad_probs) in enumerate(products):
            head = 2 * pair + side
            probs = jnp.exp(scores + bias - lse_ref[:, head : head + 1])
            weighted = probs * grad_probs
            dot = jnp.sum(weighted, axis=-1, keepdims=True)
            results.append((probs.astype(BF16), (weighted - probs * dot).astype(BF16)))
        return results

    def store(pair, results):
        qp, kp, vp, gp = load(pair)
        dq = sum(dot_nn(results[side][1], half_of(kp, side)) for side in range(2))
        dk = sum(dot_tn(results[side][1], half_of(qp, side)) for side in range(2))
        dv = sum(dot_tn(results[side][0], half_of(gp, side)) for side in range(2))
        cols = pl.ds(pair * LANES, LANES)
        grads_ref[0, :, cols] = (dq * SCALE).astype(BF16)
        grads_ref[1, :, cols] = dk.astype(BF16)
        grads_ref[2, :, cols] = dv.astype(BF16)

    raw = {}
    done = {}
    for turn in range(PAIRS + 2):
        if turn < PAIRS:
            raw[turn] = products_of(turn)
        if 0 <= turn - 1 < PAIRS:
            done[turn - 1] = softmax_back(turn - 1, raw.pop(turn - 1))
        if turn >= 2:
            store(turn - 2, done.pop(turn - 2))

    dsum_ref[0:1, :] += column_sum(grads_ref[0].astype(F32))
    dsum_ref[1:2, :] += column_sum(grads_ref[2].astype(F32))


def weight_grads(me_ref, n1_ref, mixed_hbm, columns_ref, sum_back_ref, sum_down_ref, sum_up_ref, send_hbm, keep_hbm,
                 send_ref, keep_ref, mixed_ref, in_sem, out_sem):
    step = pl.program_id(0)
    me = me_ref[0]
    first = (me & 1) == 0
    side = send_ref.shape[3]
    each = n1_ref.shape[1] // CHIPS
    load = pltpu.make_async_copy(mixed_hbm, mixed_ref, in_sem.at[0])

    def writes(number):
        rows = pl.ds(number * each, each if number < 4 else 16)
        for index, (ref, out) in enumerate(((send_ref, send_hbm), (keep_ref, keep_hbm))):
            yield pltpu.make_async_copy(ref.at[:, :, rows, :], out.at[:, :, rows, :], out_sem.at[index, number])

    @pl.when(step == 0)
    def _():
        load.start()

    def run(left, number):
        result = dot_tn(left, columns_ref[0])
        low, high = result[:, :side], result[:, side:]
        rows_at = pl.ds(pl.multiple_of(number * each, 16), each)

        def put_send(plane, layer, rows):
            send_ref[layer, plane, rows_at, :] = rows

        def put_keep(plane, layer, rows):
            keep_ref[layer, plane, rows_at, :] = rows

        spread(me, jnp.where(first, high, low), put_send)
        spread(me, jnp.where(first, low, high), put_keep)

    @pl.when(step < 3)
    def _():
        run(n1_ref[...], step)

    for number in range(3):

        @pl.when(step == number)
        def _():
            for copy in writes(number):
                copy.start()

    @pl.when(step == 3)
    def _():
        nothing = jnp.zeros((2, n1_ref.shape[1]), F32)
        vecs = jnp.concatenate((nothing, sum_back_ref[0:5], sum_down_ref[0:1]), axis=0)
        for chip in range(CHIPS):
            half = chip // (CHIPS // 2)
            block = chip * (sum_up_ref.shape[1] // side) // CHIPS
            last = jnp.broadcast_to(sum_up_ref[:, block * side : (block + 1) * side], (8, side))
            short = vecs[:, half * side : (half + 1) * side]
            at = ((chip >> 2) ^ (me >> 3), (chip & 3) ^ ((me >> 1) & 3))
            keep_ref[at[0], at[1], 4 * each :, :] = jnp.concatenate((short, last), axis=0).astype(BF16)
            send_ref[at[0], at[1], 4 * each :, :] = jnp.concatenate((short, jnp.zeros_like(last)), axis=0).astype(BF16)
        for copy in writes(4):
            copy.start()
        load.wait()
        run(mixed_ref[...], 3)
        for copy in writes(3):
            copy.start()
        for number in range(5):
            for copy in writes(number):
                copy.wait()


def tokens_backward(x_ref, gresid_ref, vec_ref, grads_ref, wq_ref, wk_ref, wv_ref, gtok_ref, dsum_ref):
    @pl.when(pl.program_id(0) == 0)
    def _():
        dsum_ref[...] = jnp.zeros_like(dsum_ref)

    grad_one = dot_nt(grads_ref[0], wq_ref[...]) + dot_nt(grads_ref[1], wk_ref[...]) + dot_nt(grads_ref[2], wv_ref[...])
    hat, inverse = normalize(x_ref[...].astype(F32))
    gtok_ref[...] = (gresid_ref[...] + norm_back(grad_one, vec_ref[0:1, :], hat, inverse)).astype(BF16)
    dsum_ref[0:1, :] += column_sum(grad_one * hat)
    dsum_ref[1:2, :] += column_sum(grad_one)


def rows_spec(block, width):
    return pl.BlockSpec((block, width), lambda i, *me: (i, 0))


def cols_spec(height, block):
    return pl.BlockSpec((height, block), lambda i, *me: (0, i))


def whole_spec(shape):
    return pl.BlockSpec(shape, lambda *i: (0,) * len(shape), pipeline_mode=pl.Buffered(1))


def kept_spec(shape):
    return pl.BlockSpec(shape, lambda *i: (0,) * len(shape))


SMEM = pl.BlockSpec(memory_space=pltpu.SMEM)


def cost(flops):
    return pl.CostEstimate(flops=flops, bytes_accessed=1, transcendentals=0)


def call(kernel, grid, ins, outs, scratch, name, flops, *args):
    out_specs = tuple(spec for spec, _ in outs)
    out_shape = tuple(shape for _, shape in outs)
    return pl.pallas_call(
        kernel,
        grid=grid,
        in_specs=ins,
        out_specs=out_specs,
        out_shape=out_shape,
        scratch_shapes=scratch,
        compiler_params=pltpu.CompilerParams(vmem_limit_bytes=VMEM, dimension_semantics=("arbitrary",) * len(grid)),
        cost_estimate=cost(flops),
        name=name,
    )(*args)


def call_with(me, kernel, steps, ins, outs, scratch, name, flops, *args):
    out_shape = tuple(shape for _, shape in outs)
    return pl.pallas_call(
        kernel,
        grid_spec=pltpu.PrefetchScalarGridSpec(
            num_scalar_prefetch=1, grid=(steps,), in_specs=ins, out_specs=tuple(spec for spec, _ in outs),
            scratch_shapes=scratch),
        out_shape=out_shape,
        compiler_params=pltpu.CompilerParams(vmem_limit_bytes=VMEM, dimension_semantics=("arbitrary",)),
        cost_estimate=cost(flops),
        name=name,
    )(me, *args)


def shaped(*shape, dtype=BF16):
    return jax.ShapeDtypeStruct(shape, dtype)


def flipped(count, change):
    pairs = []
    for source in range(count):
        core, chip = source & 1, source >> 1
        core, chip = change(core, chip)
        pairs.append((source, 2 * chip + core))
    return pairs


def swap(array, change):
    return lax.ppermute(array, "dp", flipped(lax.axis_size("dp"), change))


def other_core(core, chip):
    return core ^ 1, chip


def first_plane(core, chip):
    return core, chip ^ (1 + core)


def second_plane(core, chip):
    return core, chip ^ (2 - core)


def other_plane(distance):
    return lambda core, chip: (core, chip ^ distance)


def other_layer(distance):
    return lambda core, chip: (core, chip ^ (4 * distance))


def split_shards(core_ref, q_ref, k_ref, v_ref, o_ref, u_ref, d_ref, keep_ref, send_ref, down_ref):
    down_ref[...] = d_ref[: down_ref.shape[0], :]
    width = q_ref.shape[1]
    side = width // 2
    first = core_ref[0] == 0

    def put(index, low, high):
        keep_ref[index] = jnp.where(first, low, high).astype(BF16)
        send_ref[index] = jnp.where(first, high, low).astype(BF16)

    for index, ref in enumerate((q_ref, k_ref, v_ref, o_ref)):
        rows = ref[...].astype(F32)
        put(index, rows[:, :side], rows[:, side:])
    up = u_ref[...].astype(F32)
    hidden = up.shape[1]
    deep = hidden // (2 * CHIPS)
    halves = [
        jnp.concatenate([up[:, start : start + deep] for start in range(half * deep, hidden, 2 * deep)], axis=1)
        for half in range(2)
    ]
    for part in range(hidden // width):
        at = slice(part * side, (part + 1) * side)
        put(4 + part, halves[0][:, at], halves[1][:, at])


def join_shards(me_ref, keep_ref, take_ref, down_ref, *refs):
    vectors, (near_ref, up_ref) = refs[:-2], refs[-2:]
    me = me_ref[0]
    first = (me & 1) == 0
    parts, own, side = keep_ref.shape
    folds = parts - 4
    keep = keep_ref[...].astype(F32)
    take = take_ref[...].astype(F32)

    def joined(index):
        low = jnp.where(first, keep[index], take[index])
        high = jnp.where(first, take[index], keep[index])
        return jnp.concatenate((low, high), axis=0).astype(BF16)

    for index in range(4):
        near_ref[2 * own * index : 2 * own * (index + 1), :] = joined(index)
    for index in range(folds):
        up_ref[2 * own * index : 2 * own * (index + 1), :] = joined(4 + index)
    base = 2 * own * folds
    up_ref[base : base + 16, :] = down_ref[-16:, :side]
    up_ref[base + 16 :, :] = down_ref[-16:, side:]
    rows = []
    for ref in vectors:
        flat = ref[...].astype(F32).reshape(1, -1)
        rows.append(jnp.concatenate((flat, jnp.zeros((1, side - flat.shape[1]), F32)), axis=1))
    rows.append(jnp.zeros((16 - len(rows), side), F32))
    rows = jnp.concatenate(rows, axis=0)
    short = pltpu.roll(rows, own * lax.rem(me, side // own), 1)
    long = pltpu.roll(rows, folds * own * lax.rem(me >> 1, side // (folds * own)), 1)
    index = lax.broadcasted_iota(jnp.int32, rows.shape, 0)
    near_ref[8 * own :, :] = jnp.where(index < 8, short, long).astype(BF16)


def across_layers(shard):
    return jnp.stack([shard] + [swap(shard, other_layer(distance)) for distance in (1, 2, 3)])


def after(arrays, *others):
    return lax.optimization_barrier((arrays, others))[0]


def small_call(kernel, args, outs, name, scratch=(), ins=None, flops=0):
    return pl.pallas_call(
        kernel,
        in_specs=ins,
        out_specs=tuple(spec for spec, _ in outs),
        out_shape=tuple(shape for _, shape in outs),
        scratch_shapes=list(scratch),
        compiler_params=pltpu.CompilerParams(vmem_limit_bytes=VMEM),
        cost_estimate=cost(flops),
        name=name,
    )(*args)


VMEM_SPEC = pl.BlockSpec(memory_space=pltpu.VMEM)
ANY_SPEC = pl.BlockSpec(memory_space=pl.ANY)


def prepare(me, weights, vectors):
    own, width = weights[0].shape
    side = width // 2
    deep = weights[5].shape[0]
    folds = deep // own
    halves = (VMEM_SPEC, shaped(4 + folds, own, side))
    keep, send, down = small_call(
        split_shards, (me & 1, *weights), [halves, halves, (VMEM_SPEC, shaped(deep - 16, width))], "split_shards",
        ins=[SMEM] + [VMEM_SPEC] * 6)
    take = swap(send, other_core)
    near, up = small_call(
        join_shards, (me, keep, take, weights[5], *vectors),
        [(VMEM_SPEC, shaped(8 * own + 16, side)), (VMEM_SPEC, shaped(2 * deep + 32, side))], "join_shards",
        ins=[SMEM] + [VMEM_SPEC] * (3 + len(vectors)))
    return near, up, down


def doubled(pieces, change):
    return jnp.concatenate((pieces, swap(pieces, change)))


def gather_down(pieces):
    return doubled(doubled(pieces, first_plane), second_plane)


def gather_plain(weights, vectors):
    squares, up_weight, down_weight = weights[:4], weights[4], weights[5]
    count = lax.axis_size("dp")
    own, width = squares[0].shape
    folds = down_weight.shape[0] // own
    hidden = up_weight.shape[1]
    flat = jnp.concatenate(vectors)
    packed = jnp.concatenate(
        (
            *squares,
            up_weight.reshape(own, folds, width).transpose(1, 0, 2).reshape(own * folds, width),
            down_weight,
            jnp.pad(flat.reshape(1, -1), ((0, 7), (0, width - flat.size))),
        ),
        axis=0,
    )
    whole = lax.all_gather(packed, "dp", axis=0, tiled=True).reshape(count, -1, width)
    square_all = [whole[:, index * own : (index + 1) * own, :].reshape(width, width) for index in range(4)]
    wup = whole[:, 4 * own : (4 + folds) * own, :].reshape(count, folds, own, width).transpose(0, 2, 1, 3)
    wup = wup.reshape(width, 2, CHIPS // 2, 2, -1).transpose(3, 1, 0, 2, 4).reshape(2, 2, width, width)
    wdown = whole[:, (4 + folds) * own : (4 + 2 * folds) * own, :]
    wdown = wdown.reshape(CHIPS, 2, -1, width).transpose(1, 0, 2, 3).reshape(2, hidden // 2, width)
    last = whole[:, (4 + 2 * folds) * own, : flat.size].astype(F32)
    vec = last[:, : 8 * own].reshape(count, 8, own).transpose(1, 0, 2).reshape(8, width)
    bup = last[:, 8 * own :].reshape(CHIPS, 2, -1).transpose(1, 0, 2).reshape(2, 1, -1)
    return (*square_all, (wup, wdown), jnp.pad(vec, ((0, 8), (0, 0))), bup)


def merge_core(core_ref, keep_ref, take_ref, own_ref, send_ref):
    core = core_ref[0]

    def whole(plane):
        return (keep_ref[:, plane].astype(F32) + take_ref[:, plane].astype(F32)).astype(BF16)

    own_ref[:, 0] = whole(0)
    own_ref[:, 1] = whole(2 - core)
    send_ref[:, 0] = whole(1 + core)
    send_ref[:, 1] = whole(3)


def merge_first(*refs):
    pairs, rest_ref, send_ref = refs[:-2], refs[-2], refs[-1]
    base = 0
    for own_ref, take_ref in zip(pairs[::2], pairs[1::2]):
        for part in range(own_ref.shape[0]):
            at = slice(base, base + own_ref.shape[3])
            rest_ref[:, at, :] = (own_ref[part, :, 0].astype(F32) + take_ref[part, :, 0].astype(F32)).astype(BF16)
            send_ref[:, at, :] = (own_ref[part, :, 1].astype(F32) + take_ref[part, :, 1].astype(F32)).astype(BF16)
            base += own_ref.shape[3]


def merge_second(own_ref, take_ref, rest_ref, *send_refs):
    for layer in range(4):
        whole = own_ref[layer].astype(F32) + take_ref[layer].astype(F32)
        if layer == 0:
            rest_ref[...] = whole
        else:
            send_refs[layer - 1][...] = whole.astype(BF16)


def merge_last(deep, core_ref, rest_ref, a_ref, b_ref, c_ref, *refs):
    whole = rest_ref[...] + a_ref[...].astype(F32) + b_ref[...].astype(F32) + c_ref[...].astype(F32)
    first = core_ref[0] == 0
    if deep:
        refs[0][...] = whole[:deep]
        refs = refs[1:]
    keep_ref, send_ref = refs[:2]
    parts, own, _ = keep_ref.shape
    for part in range(parts):
        low = whole[deep + 2 * own * part : deep + 2 * own * part + own]
        high = whole[deep + 2 * own * part + own : deep + 2 * own * (part + 1)]
        keep_ref[part] = jnp.where(first, low, high)
        send_ref[part] = jnp.where(first, high, low)
    if not deep:
        refs[2][...] = whole[2 * own * parts :]


def finish(me_ref, up_keep_ref, up_take_ref, keep_ref, take_ref, flat_ref, late_ref, up_ref, *refs):
    me = me_ref[0]
    first = (me & 1) == 0
    side = keep_ref.shape[2]
    width = 2 * side
    squares, flats = refs[:4], refs[4:]
    own = up_ref.shape[0]
    for number, ref in enumerate(squares):
        keep, take = keep_ref[number], take_ref[number]
        ref[:, :side] = jnp.where(first, keep, take)
        ref[:, side:] = jnp.where(first, take, keep)
    parts = up_keep_ref.shape[0]
    deep = parts * width // CHIPS
    for part in range(parts):
        keep, take = up_keep_ref[part], up_take_ref[part]
        low, high = jnp.where(first, keep, take), jnp.where(first, take, keep)
        pieces = []
        for start in range(0, width, deep):
            pieces += [low[:, start : start + deep], high[:, start : start + deep]]
        up_ref[:, 2 * width * part : 2 * width * (part + 1)] = jnp.concatenate(pieces, axis=1)
    late = jnp.where(me < side // own, late_ref[0:2, :side], late_ref[0:2, side:])
    flat = jnp.concatenate((late, flat_ref[2:]), axis=0)
    long = flats[-1].shape[0]
    short_turn = lax.rem(side - own * lax.rem(me, side // own), side)
    long_turn = lax.rem(side - long * lax.rem(me >> 1, side // long), side)
    short = pltpu.roll(flat, short_turn, 1)
    for number, ref in enumerate(flats[:-1]):
        ref[...] = short[number, :own]
    flats[-1][...] = pltpu.roll(flat, long_turn, 1)[8, :long]


def fenced(function, *args):
    kinds = jax.eval_shape(function, *args)

    def nothing(*_):
        return jax.tree.map(lambda kind: jnp.zeros(kind.shape, kind.dtype), kinds)

    return lax.cond(lax.axis_index("dp") < lax.axis_size("dp"), function, nothing, *args)


def scatter_core(send):
    return swap(send, other_core)


def merge_core_of(core, keep, take):
    shape = keep.shape
    planes, rows, side = shape[-3:]
    keep, take = keep.reshape(-1, planes, rows, side), take.reshape(-1, planes, rows, side)
    count = keep.shape[0]
    steps = MERGE_STEPS
    block = pl.BlockSpec((count // steps, planes, rows, side), lambda i: (i, 0, 0, 0))
    half = (pl.BlockSpec((count // steps, 2, rows, side), lambda i: (i, 0, 0, 0)), shaped(count, 2, rows, side))
    own, send = call(merge_core, (steps,), [SMEM, block, block], [half, half], [], "merge_core", 0, core, keep, take)
    return own.reshape(-1, CHIPS // 4, 2, rows, side), send


def scatter_second(*pairs):
    _, count, _, _, side = pairs[0].shape
    rows = sum(piece.shape[0] * piece.shape[3] for piece in pairs[::2])
    steps = MERGE_STEPS
    ins = [pl.BlockSpec((piece.shape[0], count // steps, *piece.shape[2:]), lambda i: (0, i, 0, 0, 0)) for piece in pairs]
    out = pl.BlockSpec((count // steps, rows, side), lambda i: (i, 0, 0))
    rest, send = call(
        merge_first, (steps,), ins, [(out, shaped(count, rows, side))] * 2, [],
        "merge_first", 0, *pairs)
    return rest, swap(send, second_plane)


def merge_layers_of(own, take):
    _, rows, side = own.shape
    out = shaped(rows, side)
    return small_call(
        merge_second, (own, take), [(VMEM_SPEC, shaped(rows, side, dtype=F32))] + [(VMEM_SPEC, out)] * 3,
        "merge_second", ins=[VMEM_SPEC] * 2)


def scatter_layers(own, take):
    rest, *sends = merge_layers_of(own, take)
    return [rest] + [swap(piece, other_layer(r + 1)) for r, piece in enumerate(sends)]


def scatter_last(core, pieces, own, parts, deep):
    rows, side = pieces[0].shape
    outs = [(VMEM_SPEC, shaped(parts, own, side, dtype=F32))] * 2
    if deep:
        outs = [(VMEM_SPEC, shaped(deep, side, dtype=F32))] + outs
    else:
        outs.append((VMEM_SPEC, shaped(rows - 2 * own * parts, side, dtype=F32)))
    return small_call(
        functools.partial(merge_last, deep), (core, *pieces), outs, "merge_last", ins=[SMEM] + [VMEM_SPEC] * 4, flops=SHORT if deep else 0)


def reduce_plain(down_pairs, up_pairs, square_pair, flat):
    def scattered(array, axis):
        return lax.psum_scatter(array, "dp", scatter_dimension=axis, tiled=True).astype(F32)

    def planes(own, send, core):
        order = (own[..., 0, :, :], send[..., 0, :, :], own[..., 1, :, :], send[..., 1, :, :])
        if core == 1:
            order = (order[0], order[2], order[1], order[3])
        return jnp.stack(order, axis=-3)

    down = jnp.stack([planes(*pair, core) for core, pair in enumerate(down_pairs)])
    up = jnp.stack([planes(*pair, core) for core, pair in enumerate(up_pairs)])
    width = down.shape[-1]
    each = up.shape[4]
    down = down.transpose(1, 2, 0, 3, 4).reshape(-1, width)
    up = up.reshape(2, 2, CHIPS, each, CHIPS // 2, -1).transpose(2, 3, 1, 4, 0, 5).reshape(CHIPS * each, -1)
    square = jnp.stack(square_pair).transpose(1, 2, 3, 0, 4)[:, :, : 4 * each]
    square = square.reshape(CHIPS, 4, each, width).transpose(1, 0, 2, 3).reshape(4, CHIPS * each, width)
    return (
        scattered(down, 0),
        scattered(up, 0),
        *scattered(square, 1),
        lax.psum_scatter(flat, "dp", scatter_dimension=0, tiled=True).reshape(-1),
    )


def body(tokens, lengths, attn_gain, attn_shift, query_weight, query_bias, key_weight, value_weight, value_bias,
         out_weight, out_bias, mlp_gain, mlp_shift, up_weight, up_bias, down_weight, down_bias, grad_out):
    count = lax.axis_size("dp")
    rows, width = tokens.shape
    tiles = lengths.shape[0]
    tile = rows // tiles
    hidden = up_bias.shape[0] * count
    own = width // count
    folds = hidden // width
    vectors = (attn_gain, attn_shift, query_bias, value_bias, out_bias, mlp_gain, mlp_shift, down_bias, up_bias)
    by_hand = count == 2 * CHIPS
    me = lax.axis_index("dp").astype(jnp.int32).reshape(1) if by_hand else jnp.zeros((1,), jnp.int32)
    core = me & 1
    weights = (query_weight, key_weight, value_weight, out_weight, up_weight, down_weight)

    tile_rows = rows_spec(tile, width)
    square = whole_spec((width, width))
    vec_spec = whole_spec((16, width))
    sums = (kept_spec((8, width)), shaped(8, width, dtype=F32))
    low_rows = (tile_rows, shaped(rows, width))
    fold = 2 if tiles % 2 == 0 else 1
    wide_rows = rows_spec(fold * tile, width)
    wide_low = (wide_rows, shaped(rows, width))
    lse_spec = rows_spec(tile, LANES)
    mac = 2 * rows * width * width
    kept_vec = (kept_spec((16, width)), shaped(16, width, dtype=F32))
    kept_hidden = (kept_spec((1, hidden // 2)), shaped(1, hidden // 2, dtype=F32))
    side = width // 2

    def masked(*earlier):
        return call(
            mask_grads, (tiles,), [SMEM, tile_rows], [low_rows, sums], [], "mask_grads", 0,
            lengths, after(grad_out, *earlier))

    high_rows = (tile_rows, shaped(rows, width, dtype=F32))

    def attend(q, k, v, vec, wo):
        return call(
            attention_forward, (tiles,), [SMEM, tile_rows, vec_spec, tile_rows, tile_rows, tile_rows, square],
            [low_rows, (lse_spec, shaped(rows, LANES, dtype=F32)), high_rows, low_rows],
            [], "attention_forward", 0, lengths, tokens, vec, q, k, v, wo)

    def gather_first(near):
        cot, sum_down = masked(near)
        along = after(swap(near, first_plane), cot)
        return along, swap(near, second_plane), cot, sum_down

    def gather_second(near, along, across, cot, up_two, up_taken):
        cot_other = swap(cot, other_core)
        corner = swap(along, second_plane)
        taken = [swap(near, other_core), swap(along, other_core)]
        across, corner_out = after((across, corner), taken)
        taken += [swap(across, other_core), swap(corner_out, other_core)]
        return corner, taken, cot_other, jnp.concatenate((up_two, up_taken))

    def attend_by_hand(q, k, v, vec, wo, up_four, up_along):
        up = [swap(up_four, second_plane), swap(up_along, second_plane)]
        mixed, lse, resid, n2 = attend(q, k, v, vec, wo)
        n2_other = fenced(scatter_core, n2)
        up = after(up, n2_other)
        return mixed, lse, resid, n2, n2_other, up

    if by_hand:
        near, up, down = prepare(me, weights, vectors)
        down = after(down, near)[None]
        down_two = doubled(down, other_layer(1))
        near_moved = [swap(near, other_layer(r)) for r in (1, 2, 3)]
        up_moved = swap(up, other_layer(1))
        down_shard = fenced(gather_down, after(down_two, near))
        near_moved, up_moved = after((near_moved, up_moved), down_shard)
        near = jnp.stack([near] + near_moved)
        up_two = jnp.stack((up, up_moved))
        near, up_two = after((near, up_two))
        up_moved = swap(up_two, other_layer(2))
        along, across, cot, sum_down = fenced(gather_first, near)
        up_taken = after(up_moved, along)
        down = [down_shard, swap(after(down_shard, up_taken), other_layer(2))]
        corner, taken, cot_other, up_four = fenced(gather_second, near, along, across, cot, up_two, up_taken)
        near = [near, along, across, corner] + taken
        up_along = swap(up_four, first_plane)
        n1, q, k, v, wq, wk, wv, wo, vec, bup = call_with(
            me, project, tiles, [tile_rows] + [ANY_SPEC] * 8,
            [low_rows] * 4 + [(ANY_SPEC, shaped(width, width))] * 4 + [kept_vec, kept_hidden],
            [pltpu.VMEM((4, width, width), BF16), pltpu.VMEM((CHIPS, width // (4 * CHIPS) + 1, 16, width), BF16),
             pltpu.SemaphoreType.DMA((1,)), pltpu.SemaphoreType.DMA((4,))],
            "project", LATER, tokens, *[piece.reshape(4, -1, 16, side) for piece in after(near)])
        up_along = after(up_along, n1)
        mixed, lse, resid, n2, n2_other, up_moved = fenced(attend_by_hand, q, k, v, vec, wo, up_four, up_along)
        up = [up_along] + up_moved
        hidden_weights = [(up_four, *up, *down)]
    else:
        wq, wk, wv, wo, hidden_weights, vec, bup = gather_plain(weights, vectors)
        hidden_weights = list(zip(*hidden_weights))
        cot, sum_down = masked()
        n1, q, k, v = call(
            project_rows, (tiles,), [tile_rows, vec_spec, square, square, square], [low_rows] * 4,
            [], "project", 0, tokens, vec, wq, wk, wv)
        mixed, lse, resid, n2 = attend(q, k, v, vec, wo)

    each = width // CHIPS
    deep = hidden // (2 * CHIPS)
    blocks = hidden // (2 * width)
    full_rows = whole_spec((rows, width))
    hidden_spec = pl.BlockSpec((1, width), lambda i, me: (0, i))
    low_out, high_out = (ANY_SPEC, shaped(rows, width)), (ANY_SPEC, shaped(rows, width, dtype=F32))
    act_out = (ANY_SPEC, shaped(rows, blocks * width))
    down_part = (ANY_SPEC, shaped(4, 2, deep, width))
    up_part = (ANY_SPEC, shaped(blocks, 4, 2, each, width))

    act_spec = pl.BlockSpec((fold * tile, blocks * width), lambda i, *me: (i, 0))
    wide_spec = whole_spec((hidden // 2, width))

    def run_mlp(me, tokens_of, bup, sources):
        sets = len(tokens_of[0])
        low, high = pltpu.VMEM((sets * rows, width), BF16), pltpu.VMEM((sets * rows, width), F32)
        weight = pltpu.VMEM((2, width, width), BF16)
        dma = pltpu.SemaphoreType.DMA((2, sets))
        return call_with(
            me, functools.partial(mlp, sets, len(sources)), blocks,
            [ANY_SPEC] * (2 * sets) + [hidden_spec] + [ANY_SPEC] * len(sources),
            [act_out] * sets + [high_out] + [low_out] * (sets - 1) + [down_part] * 2 + [up_part] * 2
            + [(ANY_SPEC, shaped(hidden // 2, width)), (hidden_spec, shaped(1, hidden // 2, dtype=F32))],
            [low, low, high, pltpu.VMEM((blocks, sets * rows, width), BF16), low, low, weight, weight,
             pltpu.VMEM((blocks, width, width), BF16), pltpu.VMEM((hidden // 2, width), BF16), dma,
             pltpu.SemaphoreType.DMA((blocks, sets)), pltpu.SemaphoreType.DMA((sets,)), pltpu.SemaphoreType.DMA((4,)),
             pltpu.SemaphoreType.DMA((blocks + 1,))],
            "mlp", 0, *tokens_of[0], *tokens_of[1], bup, *sources)

    if by_hand:
        act_own, act_other, gtwo, gtwo_other, down_own, down_send, up_own, up_send, wdown, sum_up = run_mlp(
            me, ((n2, n2_other), (cot, cot_other)), bup, hidden_weights[0])
        gtwo_take = swap(gtwo_other, other_core)
        parts = (-1, CHIPS // 4, 2)
        down_first = [piece.reshape(*parts, deep, width) for piece in (down_own, swap(down_send, first_plane))]
        up_first = [piece.reshape(*parts, each, width) for piece in (up_own, swap(up_send, first_plane))]
    else:
        runs = [run_mlp(me + half, ((n2,), (cot,)), bup[half], hidden_weights[half]) for half in range(2)]
        (act_own, gtwo), (act_other, gtwo_take) = ((run[0], run[1]) for run in runs)
        gtwo_take = gtwo_take.astype(BF16)
        sum_up = jnp.concatenate([run[7] for run in runs], axis=1)
    grads_spec = pl.BlockSpec((4, tile, width), lambda i, *me: (0, i, 0))
    grads, gresid, sum_back = call(
        attention_backward, (tiles,),
        [SMEM, tile_rows, tile_rows, tile_rows, lse_spec, tile_rows, tile_rows, tile_rows, tile_rows, vec_spec, square],
        [(grads_spec, shaped(4, rows, width)), high_rows, sums], [pltpu.VMEM((tile, width), BF16)],
        "attention_backward", 0, lengths, q, k, v, lse, cot, resid, gtwo, gtwo_take, vec, wo)
    sum_spec = whole_spec((8, width))
    pair_shape = (CHIPS // 4, 4, 4 * each + 16, side)
    columns = pl.BlockSpec((1, rows, width), lambda i, me: (i, 0, 0))

    def run_weights(grads):
        return call_with(
            me, weight_grads, 4, [full_rows, ANY_SPEC, columns, sum_spec, sum_spec, whole_spec((1, sum_up.shape[1]))],
            [(ANY_SPEC, shaped(*pair_shape))] * 2,
            [pltpu.VMEM(pair_shape, BF16)] * 2
            + [pltpu.VMEM((rows, width), BF16), pltpu.SemaphoreType.DMA((1,)), pltpu.SemaphoreType.DMA((2, 5))],
            "weight_grads", 0,
            n1, mixed, grads, sum_back, sum_down, sum_up)

    def run_tokens(gresid):
        return call(
            tokens_backward, (tiles // fold,),
            [wide_rows, wide_rows, vec_spec, pl.BlockSpec((4, fold * tile, width), lambda i: (0, i, 0)), square, square, square],
            [wide_low, sums], [], "tokens_backward", MIDDLE, tokens, gresid, vec, grads, wq, wk, wv)

    if by_hand:
        (out_other,) = call_with(
            me, mlp_out_other, tiles // fold, [act_spec, wide_spec], [wide_low], [], "mlp_out_other", 0, after(act_other, grads), wdown)
        down_first, up_first = after((down_first, up_first), out_other)
        hidden_rest, hidden_take = scatter_second(*down_first, *up_first)

        def weights_of_chip(grads, out_take):
            square_send, square_keep = run_weights(grads)
            (out,) = call_with(
                me, mlp_out_own, tiles // fold, [wide_rows, vec_spec, act_spec, wide_rows, wide_spec], [wide_low], [],
                "mlp_out_own", 0, resid, vec, act_own, after(out_take, square_send), wdown)
            square_take = after(scatter_core(square_send), out)
            return *merge_core_of(core, square_keep, square_take), out

        out_take = swap(out_other, other_core)
        square_own, square_send, out = fenced(weights_of_chip, after(grads, hidden_rest), out_take)
        square_take = swap(square_send, first_plane).reshape(square_own.shape)
        hidden_rest, hidden_take = after((hidden_rest, hidden_take), square_own)
        hidden_layers = scatter_layers(hidden_rest, hidden_take)
        gtok, late = run_tokens(after(gresid, hidden_layers[0]))
        square_take = after(square_take, late)
        late = late + swap(late, other_core)
        square_second = scatter_second(square_own, square_take)
        late = after(late, square_second[0])
        late = late + swap(late, other_layer(1))
        hidden_layers = after(hidden_layers, late)
        g_down, up_keep, up_send = scatter_last(core, hidden_layers, own, blocks, deep)
        up_take = scatter_core(up_send)
        late_take = after(swap(late, other_layer(2)), g_down)
        square_second = after(square_second, g_down)
        rest, *sends = merge_layers_of(*square_second)
        late_take = after(late_take, rest)
        sends = after(sends, late_take)
        square_layers = [rest] + [swap(piece, other_layer(r + 1)) for r, piece in enumerate(sends)]
        late = late + late_take
        late = late + after(swap(late, other_plane(1)), rest)
        late = late + swap(late, other_plane(2))
        square_layers = after(square_layers, late)
        square_keep, square_send, flat = scatter_last(core, square_layers, own, 4, 0)
        square_take = scatter_core(square_send)
        outs = [(VMEM_SPEC, shaped(own, hidden, dtype=F32))] + [(VMEM_SPEC, shaped(own, width, dtype=F32))] * 4
        outs += [(VMEM_SPEC, shaped(own, dtype=F32))] * 8 + [(VMEM_SPEC, shaped(folds * own, dtype=F32))]
        g_up, g_q, g_k, g_v, g_o, *g_flat, g_ub = small_call(
            finish, (me, up_keep, up_take, square_keep, square_take, flat, late), outs, "finish",
            ins=[SMEM] + [VMEM_SPEC] * 6)
    else:
        square_send, square_keep = run_weights(grads)
        gtok, sum_one = run_tokens(gresid)
        flat = jnp.concatenate((sum_one[0:2], sum_back[0:5], sum_down[0:1]), axis=0)
        flat = flat.reshape(8, count, own).transpose(1, 0, 2).reshape(count, 8 * own)
        hidden_sums = sum_up.reshape(2, CHIPS, deep).transpose(1, 0, 2).reshape(count, folds * own)
        flat = jnp.concatenate((flat, hidden_sums), axis=1)
        g_down, g_up, g_q, g_k, g_v, g_o, flat = reduce_plain(
            [run[2:4] for run in runs], [run[4:6] for run in runs], (square_keep, square_send), flat)
        (out_other,) = call_with(
            me + 1, mlp_out_other, tiles // fold, [act_spec, wide_spec], [wide_low], [], "mlp_out_other", 0, act_other, runs[1][6])
        (out,) = call_with(
            me, mlp_out_own, tiles // fold, [wide_rows, vec_spec, act_spec, wide_rows, wide_spec], [wide_low], [],
            "mlp_out_own", 0, resid, vec, act_own, out_other, runs[0][6])
        g_flat = [flat[index * own : (index + 1) * own] for index in range(8)]
        g_ub = flat[8 * own :]
    g_gain, g_shift, g_qb, g_vb, g_ob, g_mg, g_ms, g_db = g_flat
    return (out, gtok, g_gain, g_shift, g_q, g_qb, g_k, g_v, g_vb, g_o, g_ob, g_mg, g_ms, g_up, g_ub, g_down, g_db)


def solution(mesh):
    rows, flat = P("dp", None), P("dp")
    return jax.shard_map(
        body,
        mesh=mesh,
        in_specs=(rows, rows, flat, flat, rows, flat, rows, rows, flat, rows, flat, flat, flat, rows, flat, rows, flat, rows),
        out_specs=(rows, rows, flat, flat, rows, flat, rows, rows, flat, rows, flat, flat, flat, rows, flat, rows, flat),
        check_vma=False,
    )
```

```python
import functools

import jax
import jax.numpy as jnp
from jax import lax
from jax.experimental import pallas as pl
from jax.experimental.pallas import tpu as pltpu
from jax.sharding import PartitionSpec as P

HEADS = 12
HEAD_DIM = 64
PAIRS = 6
LANES = 128
CHIPS = 16
MERGE_STEPS = 2
LONG = 10**11
SHORT = 6 * 10**9
MIDDLE = 115 * 10**8
LATER = 9 * 10**9
EPS = 1e-06
MASKED = -1e30
SCALE = HEAD_DIM**-0.5
GELU_C = 0.7978845608028654
GELU_A = 0.044715
VMEM = 64 * 1024 * 1024 - 65536
F32 = jnp.float32
BF16 = jnp.bfloat16


def dot_nn(left, right):
    return lax.dot_general(left, right, (((1,), (0,)), ((), ())), preferred_element_type=F32)


def dot_nt(left, right):
    return lax.dot_general(left, right, (((1,), (1,)), ((), ())), preferred_element_type=F32)


def dot_tn(left, right):
    return lax.dot_general(left, right, (((0,), (0,)), ((), ())), preferred_element_type=F32)


def normalize(rows):
    centered = rows - jnp.mean(rows, axis=-1, keepdims=True)
    inverse = lax.rsqrt(jnp.mean(centered * centered, axis=-1, keepdims=True) + EPS)
    return centered * inverse, inverse


def norm_back(grads, gain, hat, inverse):
    scaled = grads * gain
    mean = jnp.mean(scaled, axis=-1, keepdims=True)
    mean_hat = jnp.mean(scaled * hat, axis=-1, keepdims=True)
    return inverse * (scaled - mean - hat * mean_hat)


def column_sum(rows):
    return jnp.sum(rows, axis=0, keepdims=True)


def segments(lengths_ref, tile, slots, rows, axis):
    shape = (rows, 1) if axis == 0 else (1, rows)
    index = lax.broadcasted_iota(jnp.int32, shape, axis)
    segment = jnp.zeros(shape, jnp.int32)
    bound = 0
    for slot in range(slots):
        bound = bound + lengths_ref[tile, slot]
        segment = segment + (index >= bound).astype(jnp.int32)
    return segment


def mask_bias(lengths_ref, tile, slots, rows):
    same = segments(lengths_ref, tile, slots, rows, 0) == segments(lengths_ref, tile, slots, rows, 1)
    return jnp.where(same, 0.0, MASKED).astype(F32)


def half_of(pair, side):
    lane = lax.broadcasted_iota(jnp.int32, pair.shape, 1)
    keep = lane < HEAD_DIM if side == 0 else lane >= HEAD_DIM
    return jnp.where(keep, pair, jnp.zeros_like(pair))


def fetch_weights(me, sources, stage_ref, sem):
    core, chip = me & 1, me >> 1
    side = sources[0].shape[3]
    for index, source in enumerate(sources):
        half = core if index < 4 else 1 - core
        plane = (0, 1 + half, 2 - half, 3)[index % 4]
        cols = pl.ds(pl.multiple_of(half * side, LANES), side)
        for layer in range(4):
            owner = chip ^ (4 * layer + plane)
            pltpu.make_async_copy(source.at[layer], stage_ref.at[owner, :, :, cols], sem.at[0]).start()


def project(me_ref, x_ref, *refs):
    sources = refs[:8]
    n1_ref, q_ref, k_ref, v_ref = refs[8:12]
    outs, (vec_ref, bup_ref, weights_ref, stage_ref, sem, out_sem) = refs[12:16], refs[16:]
    step = pl.program_id(0)
    core = me_ref[0] & 1
    weights = [weights_ref.at[number] for number in range(4)]

    def write(number):
        return pltpu.make_async_copy(weights[number], outs[number], out_sem.at[number])

    @pl.when(step == 0)
    def _():
        fetch_weights(me_ref[0], sources, stage_ref, sem)
        pltpu.make_async_copy(stage_ref, stage_ref, sem.at[0]).wait()
        width = stage_ref.shape[3]
        side = width // 2
        blocks = width // (16 * CHIPS)
        for number in range(4):
            weights[number][...] = stage_ref[:, number * blocks : (number + 1) * blocks].reshape(width, width)
            write(number).start()
        parts = [stage_ref[chip, 4 * blocks].astype(F32) for chip in range(CHIPS)]
        halves = []
        for half in range(2):
            group = parts[half * CHIPS // 2 : (half + 1) * CHIPS // 2]
            halves.append(sum(part[:, :side] + part[:, side:] for part in group))
        vec_ref[...] = jnp.concatenate(halves, axis=1)
        blocks = bup_ref.shape[1] // side
        group = CHIPS // blocks
        for block in range(blocks):
            rows = sum(parts[block * group : (block + 1) * group])
            bup_ref[:, block * side : (block + 1) * side] = jnp.where(core == 0, rows[8:9, :side], rows[8:9, side:])

    project_rows(x_ref, vec_ref, *weights[:3], n1_ref, q_ref, k_ref, v_ref)

    @pl.when(step == pl.num_programs(0) - 1)
    def _():
        for number in range(4):
            write(number).wait()


def project_rows(x_ref, vec_ref, wq_ref, wk_ref, wv_ref, n1_ref, q_ref, k_ref, v_ref):
    hat, _ = normalize(x_ref[...].astype(F32))
    n1 = (hat * vec_ref[0:1, :] + vec_ref[1:2, :]).astype(BF16)
    n1_ref[...] = n1
    q_ref[...] = (dot_nn(n1, wq_ref[...]) + vec_ref[2:3, :]).astype(BF16) * jnp.asarray(SCALE, BF16)
    k_ref[...] = dot_nn(n1, wk_ref[...]).astype(BF16)
    v_ref[...] = (dot_nn(n1, wv_ref[...]) + vec_ref[3:4, :]).astype(BF16)


def mask_grads(lengths_ref, grad_ref, cot_ref, dsum_ref):
    tile = pl.program_id(0)
    slots = lengths_ref.shape[1]
    valid = segments(lengths_ref, tile, slots, grad_ref.shape[0], 0) < slots
    cot = jnp.where(valid, grad_ref[...].astype(F32), 0.0)
    cot_ref[...] = cot.astype(BF16)

    @pl.when(tile == 0)
    def _():
        dsum_ref[...] = jnp.zeros_like(dsum_ref)

    dsum_ref[0:1, :] += column_sum(cot)


def attention_forward(lengths_ref, x_ref, vec_ref, q_ref, k_ref, v_ref, wo_ref, mixed_ref, lse_ref, resid_ref, n2_ref):
    tile = pl.program_id(0)
    rows = q_ref.shape[0]
    slots = lengths_ref.shape[1]
    bias = mask_bias(lengths_ref, tile, slots, rows)
    lane = lax.broadcasted_iota(jnp.int32, (rows, LANES), 1)
    lse = jnp.zeros((rows, LANES), F32)

    def at(pair):
        return pl.ds(pair * LANES, LANES)

    def scores_of(pair):
        qp, kp = q_ref[:, at(pair)], k_ref[:, at(pair)]
        return [dot_nt(half_of(qp, side), kp) for side in range(2)]

    def softmax_of(scores):
        scores = scores + bias
        top = jnp.max(scores, axis=-1, keepdims=True)
        weights = jnp.exp(scores - top)
        sums = jnp.sum(weights, axis=-1, keepdims=True)
        return (weights.astype(BF16), 1.0 / sums), top + jnp.log(sums)

    raw = {}
    probs = {}
    for turn in range(PAIRS + 2):
        if turn < PAIRS:
            raw[turn] = scores_of(turn)
        if 0 <= turn - 1 < PAIRS:
            both = [softmax_of(scores) for scores in raw.pop(turn - 1)]
            for side in range(2):
                lse = jnp.where(lane == 2 * (turn - 1) + side, both[side][1], lse)
            probs[turn - 1] = [pair[0] for pair in both]
        if turn >= 2:
            vp = v_ref[:, at(turn - 2)]
            parts = [dot_nn(probs[turn - 2][side][0], half_of(vp, side)) * probs[turn - 2][side][1] for side in range(2)]
            mixed_ref[:, at(turn - 2)] = (parts[0] + parts[1]).astype(BF16)
    lse_ref[...] = lse
    resid = x_ref[...].astype(F32) + (dot_nn(mixed_ref[...], wo_ref[...]) + vec_ref[4:5, :])
    resid_ref[...] = resid
    hat, _ = normalize(resid)
    n2_ref[...] = (hat * vec_ref[5:6, :] + vec_ref[6:7, :]).astype(BF16)


def spread(me, rows, put):
    layer, plane = me >> 3, (me >> 1) & 3
    each = rows.shape[0] // CHIPS
    for chip in range(CHIPS):
        put((chip & 3) ^ plane, (chip >> 2) ^ layer, rows[chip * each : (chip + 1) * each].astype(BF16))


def fetch_hidden(me, sources, wup_ref, wdown_ref, sem):
    if len(sources) == 2:
        for number in range(wup_ref.shape[0]):
            pltpu.make_async_copy(sources[0].at[number], wup_ref.at[number], sem.at[number]).start()
        pltpu.make_async_copy(sources[1], wdown_ref, sem.at[wup_ref.shape[0]]).start()
        return
    core, chip = me & 1, me >> 1
    planes = (0, 1 + core, 2 - core, 3)
    blocks, width = wup_ref.shape[:2]
    each, deep = width // CHIPS, wdown_ref.shape[0] // CHIPS
    for layer in range(4):
        for index, plane in enumerate(planes):
            owner = chip ^ (4 * layer + plane)
            rows = pl.ds(pl.multiple_of(owner * each, 16), each)
            side = sources[index].shape[2]
            for part in range(sources[index].shape[1] // each):
                number, cols = part * side // width, pl.ds(part * side % width, side)
                pltpu.make_async_copy(
                    sources[index].at[layer, pl.ds(part * each, each), :], wup_ref.at[number, rows, cols], sem.at[number]
                ).start()
            source = sources[4 + layer // 2].at[2 * index + layer % 2]
            rows = pl.ds(pl.multiple_of(owner * deep, 16), source.shape[0])
            pltpu.make_async_copy(source, wdown_ref.at[rows, :], sem.at[blocks]).start()
            rest = deep - source.shape[0]
            rows = pl.ds(pl.multiple_of(owner * deep + source.shape[0], 16), rest)
            for part in range(width // side):
                at = pl.ds(sources[index].shape[1] - (width // side - part) * rest, rest)
                pltpu.make_async_copy(
                    sources[index].at[layer, at, :], wdown_ref.at[rows, pl.ds(part * side, side)], sem.at[blocks]
                ).start()


def mlp(sets, count, me_ref, *refs):
    n2_hbm, cot_hbm = refs[:sets], refs[sets : 2 * sets]
    bup_ref = refs[2 * sets]
    sources = refs[2 * sets + 1 : 2 * sets + 1 + count]
    refs = refs[2 * sets + 1 + count :]
    act_hbm, gtwo_hbm, refs = refs[:sets], refs[sets : 2 * sets], refs[2 * sets :]
    down_own, down_send, up_own, up_send, wdown_hbm, dbu_ref = refs[:6]
    n2_ref, cot_ref, gacc, act_ref, gup_ref, low_ref, gdown_ref, gupw_ref = refs[6:14]
    wup_all, wdown_all, in_sem, act_sem, out_sem, grad_sem, weight_sem = refs[14:]
    step = pl.program_id(0)
    last = pl.num_programs(0) - 1
    me = me_ref[0]
    rows = n2_ref.shape[0] // sets

    def rows_of(index):
        return pl.ds(pl.multiple_of(index * rows, rows), rows)

    blocks, width = wup_all.shape[:2]

    @pl.when(step == 0)
    def _():
        fetch_hidden(me, sources, wup_all, wdown_all, weight_sem)
        for index in range(sets):
            at = pl.ds(index * rows, rows)
            pltpu.make_async_copy(n2_hbm[index], n2_ref.at[at, :], in_sem.at[0, index]).start()
            pltpu.make_async_copy(cot_hbm[index], cot_ref.at[at, :], in_sem.at[1, index]).start()

    pltpu.make_async_copy(wup_all.at[step], wup_all.at[step], weight_sem.at[step]).wait()
    write_down = pltpu.make_async_copy(wdown_all, wdown_hbm, weight_sem.at[blocks])

    @pl.when(step == 0)
    def _():
        pltpu.make_async_copy(wdown_all, wdown_all, weight_sem.at[blocks]).wait()
        write_down.start()

    wup = wup_all[step]
    wdown = wdown_all[pl.ds(pl.multiple_of(step * width, width), width), :]
    dbu_ref[...] = jnp.zeros_like(dbu_ref)
    slot = lax.rem(step, 2)

    @pl.loop(0, sets)
    def _(index):
        at = rows_of(index)

        @pl.when(step == 0)
        def _():
            pltpu.make_async_copy(n2_ref.at[at, :], n2_ref.at[at, :], in_sem.at[0, index]).wait()
            pltpu.make_async_copy(cot_ref.at[at, :], cot_ref.at[at, :], in_sem.at[1, index]).wait()

        pre = dot_nn(n2_ref[at, :], wup) + bup_ref[...]
        grad_act = dot_nt(cot_ref[at, :], wdown)
        square = pre * pre
        tanh = jnp.tanh(pre * (GELU_C + (GELU_C * GELU_A) * square))
        half = 0.5 + 0.5 * tanh
        inner = GELU_C + (3.0 * GELU_C * GELU_A) * square
        act_ref[slot, at, :] = (pre * half).astype(BF16)
        gup = (grad_act * (half + (0.5 * pre) * (1.0 - tanh * tanh) * inner)).astype(BF16)
        gup_ref[at, :] = gup
        dbu_ref[...] += column_sum(gup.astype(F32))

    @pl.when(step == 0)
    def _():
        @pl.loop(0, sets)
        def _(index):
            at = rows_of(index)
            gacc[at, :] = dot_nt(gup_ref[at, :], wup)

    @pl.when((step > 0) & (step < last))
    def _():
        @pl.loop(0, sets)
        def _(index):
            at = rows_of(index)
            gacc[at, :] += dot_nt(gup_ref[at, :], wup)

    def results():
        for index in range(sets):
            at = pl.ds(index * rows, rows)
            source = low_ref.at[at, :] if index else gacc.at[at, :]
            yield pltpu.make_async_copy(source, gtwo_hbm[index], out_sem.at[index])

    def activations(number):
        for index in range(sets):
            source = act_ref.at[number, pl.ds(index * rows, rows), :]
            cols = pl.ds(number * width, width)
            yield pltpu.make_async_copy(source, act_hbm[index].at[:, cols], act_sem.at[number, index])

    for number in range(act_ref.shape[0]):

        @pl.when(step == number)
        def _():
            for copy in activations(number):
                copy.start()

    @pl.when(step == last)
    def _():
        @pl.loop(0, sets)
        def _(index):
            at = rows_of(index)
            total = gacc[at, :] + dot_nt(gup_ref[at, :], wup)
            gacc[at, :] = total
            low_ref[at, :] = total.astype(BF16)

        for copy in results():
            copy.start()

    gdown_ref[slot] = dot_tn(act_ref[slot], cot_ref[...]).astype(BF16)
    deep = down_own.shape[2]
    count = gdown_ref.shape[1] // deep
    for index in range(count):
        chip = step * count + index
        source = gdown_ref.at[slot, pl.ds(index * deep, deep), :]
        keep_or_send(me, chip & 3, (chip >> 2) ^ (me >> 3), source, down_own, down_send, grad_sem, 0)

    gupw_ref[slot] = dot_tn(n2_ref[...], gup_ref[...]).astype(BF16)
    each = gupw_ref.shape[1] // CHIPS
    for chip in range(CHIPS):
        source = gupw_ref.at[slot, pl.ds(chip * each, each), :]
        keep_or_send(
            me, chip & 3, (chip >> 2) ^ (me >> 3), source, up_own.at[step], up_send.at[step], grad_sem, 2)

    @pl.when(step == last)
    def _():
        for copy in results():
            copy.wait()
        write_down.wait()
        for number in range(act_ref.shape[0]):
            for copy in activations(number):
                copy.wait()
        for number, ref in enumerate((down_own, down_send, up_own, up_send)):
            pltpu.make_async_copy(ref, ref, grad_sem.at[number]).wait()


def keep_or_send(me, plane, layer, source, own_ref, send_ref, sem, number):
    core = me & 1
    relative = plane ^ ((me >> 1) & 3)
    mine = (relative == 0) | (relative == 2 - core)

    @pl.when(mine)
    def _():
        pltpu.make_async_copy(source, own_ref.at[layer, jnp.where(relative == 0, 0, 1)], sem.at[number]).start()

    @pl.when(jnp.logical_not(mine))
    def _():
        pltpu.make_async_copy(source, send_ref.at[layer, jnp.where(relative == 3, 1, 0)], sem.at[number + 1]).start()


def mlp_out_other(me_ref, act_ref, wdown_ref, out_ref):
    out_ref[...] = dot_nn(act_ref[...], wdown_ref[...]).astype(BF16)


def mlp_out_own(me_ref, resid_ref, vec_ref, act_ref, take_ref, wdown_ref, out_ref):
    half = dot_nn(act_ref[...], wdown_ref[...]) + take_ref[...].astype(F32)
    out_ref[...] = (resid_ref[...] + (half + vec_ref[7:8, :])).astype(BF16)


def attention_backward(lengths_ref, q_ref, k_ref, v_ref, lse_ref, cot_ref, resid_ref, gtwo_ref, gother_ref, vec_ref, wo_ref,
                       grads_ref, gresid_ref, dsum_ref, gmix_ref):
    tile = pl.program_id(0)
    rows = q_ref.shape[0]

    @pl.when(tile == 0)
    def _():
        dsum_ref[...] = jnp.zeros_like(dsum_ref)

    hat, inverse = normalize(resid_ref[...])
    grad_two = gtwo_ref[...] + gother_ref[...].astype(F32)
    gresid = cot_ref[...].astype(F32) + norm_back(grad_two, vec_ref[5:6, :], hat, inverse)
    gresid_ref[...] = gresid
    gattn = gresid.astype(BF16)
    grads_ref[3] = gattn
    dsum_ref[2:3, :] += column_sum(gattn.astype(F32))
    dsum_ref[3:4, :] += column_sum(grad_two * hat)
    dsum_ref[4:5, :] += column_sum(grad_two)
    gmix_ref[...] = dot_nt(gattn, wo_ref[...]).astype(BF16)
    bias = mask_bias(lengths_ref, tile, lengths_ref.shape[1], rows)

    def load(pair):
        cols = pl.ds(pair * LANES, LANES)
        return q_ref[:, cols], k_ref[:, cols], v_ref[:, cols], gmix_ref[:, cols]

    def products_of(pair):
        qp, kp, vp, gp = load(pair)
        return [(dot_nt(half_of(qp, side), kp), dot_nt(half_of(gp, side), vp)) for side in range(2)]

    def softmax_back(pair, products):
        results = []
        for side, (scores, grad_probs) in enumerate(products):
            head = 2 * pair + side
            probs = jnp.exp(scores + bias - lse_ref[:, head : head + 1])
            weighted = probs * grad_probs
            dot = jnp.sum(weighted, axis=-1, keepdims=True)
            results.append((probs.astype(BF16), (weighted - probs * dot).astype(BF16)))
        return results

    def store(pair, results):
        qp, kp, vp, gp = load(pair)
        dq = sum(dot_nn(results[side][1], half_of(kp, side)) for side in range(2))
        dk = sum(dot_tn(results[side][1], half_of(qp, side)) for side in range(2))
        dv = sum(dot_tn(results[side][0], half_of(gp, side)) for side in range(2))
        cols = pl.ds(pair * LANES, LANES)
        grads_ref[0, :, cols] = (dq * SCALE).astype(BF16)
        grads_ref[1, :, cols] = dk.astype(BF16)
        grads_ref[2, :, cols] = dv.astype(BF16)

    raw = {}
    done = {}
    for turn in range(PAIRS + 2):
        if turn < PAIRS:
            raw[turn] = products_of(turn)
        if 0 <= turn - 1 < PAIRS:
            done[turn - 1] = softmax_back(turn - 1, raw.pop(turn - 1))
        if turn >= 2:
            store(turn - 2, done.pop(turn - 2))

    dsum_ref[0:1, :] += column_sum(grads_ref[0].astype(F32))
    dsum_ref[1:2, :] += column_sum(grads_ref[2].astype(F32))


def weight_grads(me_ref, n1_ref, mixed_hbm, columns_ref, sum_back_ref, sum_down_ref, sum_up_ref, send_hbm, keep_hbm,
                 send_ref, keep_ref, mixed_ref, in_sem, out_sem):
    step = pl.program_id(0)
    me = me_ref[0]
    first = (me & 1) == 0
    side = send_ref.shape[3]
    each = n1_ref.shape[1] // CHIPS
    load = pltpu.make_async_copy(mixed_hbm, mixed_ref, in_sem.at[0])

    def writes(number):
        rows = pl.ds(number * each, each if number < 4 else 16)
        for index, (ref, out) in enumerate(((send_ref, send_hbm), (keep_ref, keep_hbm))):
            yield pltpu.make_async_copy(ref.at[:, :, rows, :], out.at[:, :, rows, :], out_sem.at[index, number])

    @pl.when(step == 0)
    def _():
        load.start()

    def run(left, number):
        result = dot_tn(left, columns_ref[0])
        low, high = result[:, :side], result[:, side:]
        rows_at = pl.ds(pl.multiple_of(number * each, 16), each)

        def put_send(plane, layer, rows):
            send_ref[layer, plane, rows_at, :] = rows

        def put_keep(plane, layer, rows):
            keep_ref[layer, plane, rows_at, :] = rows

        spread(me, jnp.where(first, high, low), put_send)
        spread(me, jnp.where(first, low, high), put_keep)

    @pl.when(step < 3)
    def _():
        run(n1_ref[...], step)

    for number in range(3):

        @pl.when(step == number)
        def _():
            for copy in writes(number):
                copy.start()

    @pl.when(step == 3)
    def _():
        nothing = jnp.zeros((2, n1_ref.shape[1]), F32)
        vecs = jnp.concatenate((nothing, sum_back_ref[0:5], sum_down_ref[0:1]), axis=0)
        for chip in range(CHIPS):
            half = chip // (CHIPS // 2)
            block = chip * (sum_up_ref.shape[1] // side) // CHIPS
            last = jnp.broadcast_to(sum_up_ref[:, block * side : (block + 1) * side], (8, side))
            short = vecs[:, half * side : (half + 1) * side]
            at = ((chip >> 2) ^ (me >> 3), (chip & 3) ^ ((me >> 1) & 3))
            keep_ref[at[0], at[1], 4 * each :, :] = jnp.concatenate((short, last), axis=0).astype(BF16)
            send_ref[at[0], at[1], 4 * each :, :] = jnp.concatenate((short, jnp.zeros_like(last)), axis=0).astype(BF16)
        for copy in writes(4):
            copy.start()
        load.wait()
        run(mixed_ref[...], 3)
        for copy in writes(3):
            copy.start()
        for number in range(5):
            for copy in writes(number):
                copy.wait()


def tokens_backward(x_ref, gresid_ref, vec_ref, grads_ref, wq_ref, wk_ref, wv_ref, gtok_ref, dsum_ref):
    @pl.when(pl.program_id(0) == 0)
    def _():
        dsum_ref[...] = jnp.zeros_like(dsum_ref)

    grad_one = dot_nt(grads_ref[0], wq_ref[...]) + dot_nt(grads_ref[1], wk_ref[...]) + dot_nt(grads_ref[2], wv_ref[...])
    hat, inverse = normalize(x_ref[...].astype(F32))
    gtok_ref[...] = (gresid_ref[...] + norm_back(grad_one, vec_ref[0:1, :], hat, inverse)).astype(BF16)
    dsum_ref[0:1, :] += column_sum(grad_one * hat)
    dsum_ref[1:2, :] += column_sum(grad_one)


def rows_spec(block, width):
    return pl.BlockSpec((block, width), lambda i, *me: (i, 0))


def cols_spec(height, block):
    return pl.BlockSpec((height, block), lambda i, *me: (0, i))


def whole_spec(shape):
    return pl.BlockSpec(shape, lambda *i: (0,) * len(shape), pipeline_mode=pl.Buffered(1))


def kept_spec(shape):
    return pl.BlockSpec(shape, lambda *i: (0,) * len(shape))


SMEM = pl.BlockSpec(memory_space=pltpu.SMEM)


def cost(flops):
    return pl.CostEstimate(flops=flops, bytes_accessed=1, transcendentals=0)


def call(kernel, grid, ins, outs, scratch, name, flops, *args):
    out_specs = tuple(spec for spec, _ in outs)
    out_shape = tuple(shape for _, shape in outs)
    return pl.pallas_call(
        kernel,
        grid=grid,
        in_specs=ins,
        out_specs=out_specs,
        out_shape=out_shape,
        scratch_shapes=scratch,
        compiler_params=pltpu.CompilerParams(vmem_limit_bytes=VMEM, dimension_semantics=("arbitrary",) * len(grid)),
        cost_estimate=cost(flops),
        name=name,
    )(*args)


def call_with(me, kernel, steps, ins, outs, scratch, name, flops, *args):
    out_shape = tuple(shape for _, shape in outs)
    return pl.pallas_call(
        kernel,
        grid_spec=pltpu.PrefetchScalarGridSpec(
            num_scalar_prefetch=1, grid=(steps,), in_specs=ins, out_specs=tuple(spec for spec, _ in outs),
            scratch_shapes=scratch),
        out_shape=out_shape,
        compiler_params=pltpu.CompilerParams(vmem_limit_bytes=VMEM, dimension_semantics=("arbitrary",)),
        cost_estimate=cost(flops),
        name=name,
    )(me, *args)


def shaped(*shape, dtype=BF16):
    return jax.ShapeDtypeStruct(shape, dtype)


def flipped(count, change):
    pairs = []
    for source in range(count):
        core, chip = source & 1, source >> 1
        core, chip = change(core, chip)
        pairs.append((source, 2 * chip + core))
    return pairs


def swap(array, change):
    return lax.ppermute(array, "dp", flipped(lax.axis_size("dp"), change))


def other_core(core, chip):
    return core ^ 1, chip


def first_plane(core, chip):
    return core, chip ^ (1 + core)


def second_plane(core, chip):
    return core, chip ^ (2 - core)


def other_plane(distance):
    return lambda core, chip: (core, chip ^ distance)


def other_layer(distance):
    return lambda core, chip: (core, chip ^ (4 * distance))


def split_shards(core_ref, q_ref, k_ref, v_ref, o_ref, u_ref, d_ref, keep_ref, send_ref, down_ref):
    down_ref[...] = d_ref[: down_ref.shape[0], :]
    width = q_ref.shape[1]
    side = width // 2
    first = core_ref[0] == 0

    def put(index, low, high):
        keep_ref[index] = jnp.where(first, low, high).astype(BF16)
        send_ref[index] = jnp.where(first, high, low).astype(BF16)

    for index, ref in enumerate((q_ref, k_ref, v_ref, o_ref)):
        rows = ref[...].astype(F32)
        put(index, rows[:, :side], rows[:, side:])
    up = u_ref[...].astype(F32)
    hidden = up.shape[1]
    deep = hidden // (2 * CHIPS)
    halves = [
        jnp.concatenate([up[:, start : start + deep] for start in range(half * deep, hidden, 2 * deep)], axis=1)
        for half in range(2)
    ]
    for part in range(hidden // width):
        at = slice(part * side, (part + 1) * side)
        put(4 + part, halves[0][:, at], halves[1][:, at])


def join_shards(me_ref, keep_ref, take_ref, down_ref, *refs):
    vectors, (near_ref, up_ref) = refs[:-2], refs[-2:]
    me = me_ref[0]
    first = (me & 1) == 0
    parts, own, side = keep_ref.shape
    folds = parts - 4
    keep = keep_ref[...].astype(F32)
    take = take_ref[...].astype(F32)

    def joined(index):
        low = jnp.where(first, keep[index], take[index])
        high = jnp.where(first, take[index], keep[index])
        return jnp.concatenate((low, high), axis=0).astype(BF16)

    for index in range(4):
        near_ref[2 * own * index : 2 * own * (index + 1), :] = joined(index)
    for index in range(folds):
        up_ref[2 * own * index : 2 * own * (index + 1), :] = joined(4 + index)
    base = 2 * own * folds
    up_ref[base : base + 16, :] = down_ref[-16:, :side]
    up_ref[base + 16 :, :] = down_ref[-16:, side:]
    rows = []
    for ref in vectors:
        flat = ref[...].astype(F32).reshape(1, -1)
        rows.append(jnp.concatenate((flat, jnp.zeros((1, side - flat.shape[1]), F32)), axis=1))
    rows.append(jnp.zeros((16 - len(rows), side), F32))
    rows = jnp.concatenate(rows, axis=0)
    short = pltpu.roll(rows, own * lax.rem(me, side // own), 1)
    long = pltpu.roll(rows, folds * own * lax.rem(me >> 1, side // (folds * own)), 1)
    index = lax.broadcasted_iota(jnp.int32, rows.shape, 0)
    near_ref[8 * own :, :] = jnp.where(index < 8, short, long).astype(BF16)


def across_layers(shard):
    return jnp.stack([shard] + [swap(shard, other_layer(distance)) for distance in (1, 2, 3)])


def after(arrays, *others):
    return lax.optimization_barrier((arrays, others))[0]


def small_call(kernel, args, outs, name, scratch=(), ins=None, flops=0):
    return pl.pallas_call(
        kernel,
        in_specs=ins,
        out_specs=tuple(spec for spec, _ in outs),
        out_shape=tuple(shape for _, shape in outs),
        scratch_shapes=list(scratch),
        compiler_params=pltpu.CompilerParams(vmem_limit_bytes=VMEM),
        cost_estimate=cost(flops),
        name=name,
    )(*args)


VMEM_SPEC = pl.BlockSpec(memory_space=pltpu.VMEM)
ANY_SPEC = pl.BlockSpec(memory_space=pl.ANY)


def prepare(me, weights, vectors):
    own, width = weights[0].shape
    side = width // 2
    deep = weights[5].shape[0]
    folds = deep // own
    halves = (VMEM_SPEC, shaped(4 + folds, own, side))
    keep, send, down = small_call(
        split_shards, (me & 1, *weights), [halves, halves, (VMEM_SPEC, shaped(deep - 16, width))], "split_shards",
        ins=[SMEM] + [VMEM_SPEC] * 6)
    take = swap(send, other_core)
    near, up = small_call(
        join_shards, (me, keep, take, weights[5], *vectors),
        [(VMEM_SPEC, shaped(8 * own + 16, side)), (VMEM_SPEC, shaped(2 * deep + 32, side))], "join_shards",
        ins=[SMEM] + [VMEM_SPEC] * (3 + len(vectors)))
    return near, up, down


def doubled(pieces, change):
    return jnp.concatenate((pieces, swap(pieces, change)))


def gather_down(pieces):
    return doubled(doubled(pieces, first_plane), second_plane)


def gather_plain(weights, vectors):
    squares, up_weight, down_weight = weights[:4], weights[4], weights[5]
    count = lax.axis_size("dp")
    own, width = squares[0].shape
    folds = down_weight.shape[0] // own
    hidden = up_weight.shape[1]
    flat = jnp.concatenate(vectors)
    packed = jnp.concatenate(
        (
            *squares,
            up_weight.reshape(own, folds, width).transpose(1, 0, 2).reshape(own * folds, width),
            down_weight,
            jnp.pad(flat.reshape(1, -1), ((0, 7), (0, width - flat.size))),
        ),
        axis=0,
    )
    whole = lax.all_gather(packed, "dp", axis=0, tiled=True).reshape(count, -1, width)
    square_all = [whole[:, index * own : (index + 1) * own, :].reshape(width, width) for index in range(4)]
    wup = whole[:, 4 * own : (4 + folds) * own, :].reshape(count, folds, own, width).transpose(0, 2, 1, 3)
    wup = wup.reshape(width, 2, CHIPS // 2, 2, -1).transpose(3, 1, 0, 2, 4).reshape(2, 2, width, width)
    wdown = whole[:, (4 + folds) * own : (4 + 2 * folds) * own, :]
    wdown = wdown.reshape(CHIPS, 2, -1, width).transpose(1, 0, 2, 3).reshape(2, hidden // 2, width)
    last = whole[:, (4 + 2 * folds) * own, : flat.size].astype(F32)
    vec = last[:, : 8 * own].reshape(count, 8, own).transpose(1, 0, 2).reshape(8, width)
    bup = last[:, 8 * own :].reshape(CHIPS, 2, -1).transpose(1, 0, 2).reshape(2, 1, -1)
    return (*square_all, (wup, wdown), jnp.pad(vec, ((0, 8), (0, 0))), bup)


def merge_core(core_ref, keep_ref, take_ref, own_ref, send_ref):
    core = core_ref[0]

    def whole(plane):
        return (keep_ref[:, plane].astype(F32) + take_ref[:, plane].astype(F32)).astype(BF16)

    own_ref[:, 0] = whole(0)
    own_ref[:, 1] = whole(2 - core)
    send_ref[:, 0] = whole(1 + core)
    send_ref[:, 1] = whole(3)


def merge_first(*refs):
    pairs, rest_ref, send_ref = refs[:-2], refs[-2], refs[-1]
    base = 0
    for own_ref, take_ref in zip(pairs[::2], pairs[1::2]):
        for part in range(own_ref.shape[0]):
            at = slice(base, base + own_ref.shape[3])
            rest_ref[:, at, :] = (own_ref[part, :, 0].astype(F32) + take_ref[part, :, 0].astype(F32)).astype(BF16)
            send_ref[:, at, :] = (own_ref[part, :, 1].astype(F32) + take_ref[part, :, 1].astype(F32)).astype(BF16)
            base += own_ref.shape[3]


def merge_second(own_ref, take_ref, rest_ref, *send_refs):
    for layer in range(4):
        whole = own_ref[layer].astype(F32) + take_ref[layer].astype(F32)
        if layer == 0:
            rest_ref[...] = whole
        else:
            send_refs[layer - 1][...] = whole.astype(BF16)


def merge_last(deep, core_ref, rest_ref, a_ref, b_ref, c_ref, *refs):
    whole = rest_ref[...] + a_ref[...].astype(F32) + b_ref[...].astype(F32) + c_ref[...].astype(F32)
    first = core_ref[0] == 0
    if deep:
        refs[0][...] = whole[:deep]
        refs = refs[1:]
    keep_ref, send_ref = refs[:2]
    parts, own, _ = keep_ref.shape
    for part in range(parts):
        low = whole[deep + 2 * own * part : deep + 2 * own * part + own]
        high = whole[deep + 2 * own * part + own : deep + 2 * own * (part + 1)]
        keep_ref[part] = jnp.where(first, low, high)
        send_ref[part] = jnp.where(first, high, low)
    if not deep:
        refs[2][...] = whole[2 * own * parts :]


def finish(me_ref, up_keep_ref, up_take_ref, keep_ref, take_ref, flat_ref, late_ref, up_ref, *refs):
    me = me_ref[0]
    first = (me & 1) == 0
    side = keep_ref.shape[2]
    width = 2 * side
    squares, flats = refs[:4], refs[4:]
    own = up_ref.shape[0]
    for number, ref in enumerate(squares):
        keep, take = keep_ref[number], take_ref[number]
        ref[:, :side] = jnp.where(first, keep, take)
        ref[:, side:] = jnp.where(first, take, keep)
    parts = up_keep_ref.shape[0]
    deep = parts * width // CHIPS
    for part in range(parts):
        keep, take = up_keep_ref[part], up_take_ref[part]
        low, high = jnp.where(first, keep, take), jnp.where(first, take, keep)
        pieces = []
        for start in range(0, width, deep):
            pieces += [low[:, start : start + deep], high[:, start : start + deep]]
        up_ref[:, 2 * width * part : 2 * width * (part + 1)] = jnp.concatenate(pieces, axis=1)
    late = jnp.where(me < side // own, late_ref[0:2, :side], late_ref[0:2, side:])
    flat = jnp.concatenate((late, flat_ref[2:]), axis=0)
    long = flats[-1].shape[0]
    short_turn = lax.rem(side - own * lax.rem(me, side // own), side)
    long_turn = lax.rem(side - long * lax.rem(me >> 1, side // long), side)
    short = pltpu.roll(flat, short_turn, 1)
    for number, ref in enumerate(flats[:-1]):
        ref[...] = short[number, :own]
    flats[-1][...] = pltpu.roll(flat, long_turn, 1)[8, :long]


def fenced(function, *args):
    kinds = jax.eval_shape(function, *args)

    def nothing(*_):
        return jax.tree.map(lambda kind: jnp.zeros(kind.shape, kind.dtype), kinds)

    return lax.cond(lax.axis_index("dp") < lax.axis_size("dp"), function, nothing, *args)


def scatter_core(send):
    return swap(send, other_core)


def merge_core_of(core, keep, take):
    shape = keep.shape
    planes, rows, side = shape[-3:]
    keep, take = keep.reshape(-1, planes, rows, side), take.reshape(-1, planes, rows, side)
    count = keep.shape[0]
    steps = MERGE_STEPS
    block = pl.BlockSpec((count // steps, planes, rows, side), lambda i: (i, 0, 0, 0))
    half = (pl.BlockSpec((count // steps, 2, rows, side), lambda i: (i, 0, 0, 0)), shaped(count, 2, rows, side))
    own, send = call(merge_core, (steps,), [SMEM, block, block], [half, half], [], "merge_core", 0, core, keep, take)
    return own.reshape(-1, CHIPS // 4, 2, rows, side), send


def scatter_second(*pairs):
    _, count, _, _, side = pairs[0].shape
    rows = sum(piece.shape[0] * piece.shape[3] for piece in pairs[::2])
    steps = MERGE_STEPS
    ins = [pl.BlockSpec((piece.shape[0], count // steps, *piece.shape[2:]), lambda i: (0, i, 0, 0, 0)) for piece in pairs]
    out = pl.BlockSpec((count // steps, rows, side), lambda i: (i, 0, 0))
    rest, send = call(
        merge_first, (steps,), ins, [(out, shaped(count, rows, side))] * 2, [],
        "merge_first", 0, *pairs)
    return rest, swap(send, second_plane)


def merge_layers_of(own, take):
    _, rows, side = own.shape
    out = shaped(rows, side)
    return small_call(
        merge_second, (own, take), [(VMEM_SPEC, shaped(rows, side, dtype=F32))] + [(VMEM_SPEC, out)] * 3,
        "merge_second", ins=[VMEM_SPEC] * 2)


def scatter_layers(own, take):
    rest, *sends = merge_layers_of(own, take)
    return [rest] + [swap(piece, other_layer(r + 1)) for r, piece in enumerate(sends)]


def scatter_last(core, pieces, own, parts, deep):
    rows, side = pieces[0].shape
    outs = [(VMEM_SPEC, shaped(parts, own, side, dtype=F32))] * 2
    if deep:
        outs = [(VMEM_SPEC, shaped(deep, side, dtype=F32))] + outs
    else:
        outs.append((VMEM_SPEC, shaped(rows - 2 * own * parts, side, dtype=F32)))
    return small_call(
        functools.partial(merge_last, deep), (core, *pieces), outs, "merge_last", ins=[SMEM] + [VMEM_SPEC] * 4, flops=SHORT if deep else 0)


def reduce_plain(down_pairs, up_pairs, square_pair, flat):
    def scattered(array, axis):
        return lax.psum_scatter(array, "dp", scatter_dimension=axis, tiled=True).astype(F32)

    def planes(own, send, core):
        order = (own[..., 0, :, :], send[..., 0, :, :], own[..., 1, :, :], send[..., 1, :, :])
        if core == 1:
            order = (order[0], order[2], order[1], order[3])
        return jnp.stack(order, axis=-3)

    down = jnp.stack([planes(*pair, core) for core, pair in enumerate(down_pairs)])
    up = jnp.stack([planes(*pair, core) for core, pair in enumerate(up_pairs)])
    width = down.shape[-1]
    each = up.shape[4]
    down = down.transpose(1, 2, 0, 3, 4).reshape(-1, width)
    up = up.reshape(2, 2, CHIPS, each, CHIPS // 2, -1).transpose(2, 3, 1, 4, 0, 5).reshape(CHIPS * each, -1)
    square = jnp.stack(square_pair).transpose(1, 2, 3, 0, 4)[:, :, : 4 * each]
    square = square.reshape(CHIPS, 4, each, width).transpose(1, 0, 2, 3).reshape(4, CHIPS * each, width)
    return (
        scattered(down, 0),
        scattered(up, 0),
        *scattered(square, 1),
        lax.psum_scatter(flat, "dp", scatter_dimension=0, tiled=True).reshape(-1),
    )


def body(tokens, lengths, attn_gain, attn_shift, query_weight, query_bias, key_weight, value_weight, value_bias,
         out_weight, out_bias, mlp_gain, mlp_shift, up_weight, up_bias, down_weight, down_bias, grad_out):
    count = lax.axis_size("dp")
    rows, width = tokens.shape
    tiles = lengths.shape[0]
    tile = rows // tiles
    hidden = up_bias.shape[0] * count
    own = width // count
    folds = hidden // width
    vectors = (attn_gain, attn_shift, query_bias, value_bias, out_bias, mlp_gain, mlp_shift, down_bias, up_bias)
    by_hand = count == 2 * CHIPS
    me = lax.axis_index("dp").astype(jnp.int32).reshape(1) if by_hand else jnp.zeros((1,), jnp.int32)
    core = me & 1
    weights = (query_weight, key_weight, value_weight, out_weight, up_weight, down_weight)

    tile_rows = rows_spec(tile, width)
    square = whole_spec((width, width))
    vec_spec = whole_spec((16, width))
    sums = (kept_spec((8, width)), shaped(8, width, dtype=F32))
    low_rows = (tile_rows, shaped(rows, width))
    fold = 2 if tiles % 2 == 0 else 1
    wide_rows = rows_spec(fold * tile, width)
    wide_low = (wide_rows, shaped(rows, width))
    lse_spec = rows_spec(tile, LANES)
    mac = 2 * rows * width * width
    kept_vec = (kept_spec((16, width)), shaped(16, width, dtype=F32))
    kept_hidden = (kept_spec((1, hidden // 2)), shaped(1, hidden // 2, dtype=F32))
    side = width // 2

    def masked(*earlier):
        return call(
            mask_grads, (tiles,), [SMEM, tile_rows], [low_rows, sums], [], "mask_grads", 0,
            lengths, after(grad_out, *earlier))

    high_rows = (tile_rows, shaped(rows, width, dtype=F32))

    def attend(q, k, v, vec, wo):
        return call(
            attention_forward, (tiles,), [SMEM, tile_rows, vec_spec, tile_rows, tile_rows, tile_rows, square],
            [low_rows, (lse_spec, shaped(rows, LANES, dtype=F32)), high_rows, low_rows],
            [], "attention_forward", 0, lengths, tokens, vec, q, k, v, wo)

    def gather_first(near):
        cot, sum_down = masked(near)
        along = after(swap(near, first_plane), cot)
        return along, swap(near, second_plane), cot, sum_down

    def gather_second(near, along, across, cot, up_two, up_taken):
        cot_other = swap(cot, other_core)
        corner = swap(along, second_plane)
        taken = [swap(near, other_core), swap(along, other_core)]
        across, corner_out = after((across, corner), taken)
        taken += [swap(across, other_core), swap(corner_out, other_core)]
        return corner, taken, cot_other, jnp.concatenate((up_two, up_taken))

    def attend_by_hand(q, k, v, vec, wo, up_four, up_along):
        up = [swap(up_four, second_plane), swap(up_along, second_plane)]
        mixed, lse, resid, n2 = attend(q, k, v, vec, wo)
        n2_other = fenced(scatter_core, n2)
        up = after(up, n2_other)
        return mixed, lse, resid, n2, n2_other, up

    if by_hand:
        near, up, down = prepare(me, weights, vectors)
        down = after(down, near)[None]
        down_two = doubled(down, other_layer(1))
        near_moved = [swap(near, other_layer(r)) for r in (1, 2, 3)]
        up_moved = swap(up, other_layer(1))
        down_shard = fenced(gather_down, after(down_two, near))
        near_moved, up_moved = after((near_moved, up_moved), down_shard)
        near = jnp.stack([near] + near_moved)
        up_two = jnp.stack((up, up_moved))
        near, up_two = after((near, up_two))
        up_moved = swap(up_two, other_layer(2))
        along, across, cot, sum_down = fenced(gather_first, near)
        up_taken = after(up_moved, along)
        down = [down_shard, swap(after(down_shard, up_taken), other_layer(2))]
        corner, taken, cot_other, up_four = fenced(gather_second, near, along, across, cot, up_two, up_taken)
        near = [near, along, across, corner] + taken
        up_along = swap(up_four, first_plane)
        n1, q, k, v, wq, wk, wv, wo, vec, bup = call_with(
            me, project, tiles, [tile_rows] + [ANY_SPEC] * 8,
            [low_rows] * 4 + [(ANY_SPEC, shaped(width, width))] * 4 + [kept_vec, kept_hidden],
            [pltpu.VMEM((4, width, width), BF16), pltpu.VMEM((CHIPS, width // (4 * CHIPS) + 1, 16, width), BF16),
             pltpu.SemaphoreType.DMA((1,)), pltpu.SemaphoreType.DMA((4,))],
            "project", LATER, tokens, *[piece.reshape(4, -1, 16, side) for piece in after(near)])
        up_along = after(up_along, n1)
        mixed, lse, resid, n2, n2_other, up_moved = fenced(attend_by_hand, q, k, v, vec, wo, up_four, up_along)
        up = [up_along] + up_moved
        hidden_weights = [(up_four, *up, *down)]
    else:
        wq, wk, wv, wo, hidden_weights, vec, bup = gather_plain(weights, vectors)
        hidden_weights = list(zip(*hidden_weights))
        cot, sum_down = masked()
        n1, q, k, v = call(
            project_rows, (tiles,), [tile_rows, vec_spec, square, square, square], [low_rows] * 4,
            [], "project", 0, tokens, vec, wq, wk, wv)
        mixed, lse, resid, n2 = attend(q, k, v, vec, wo)

    each = width // CHIPS
    deep = hidden // (2 * CHIPS)
    blocks = hidden // (2 * width)
    full_rows = whole_spec((rows, width))
    hidden_spec = pl.BlockSpec((1, width), lambda i, me: (0, i))
    low_out, high_out = (ANY_SPEC, shaped(rows, width)), (ANY_SPEC, shaped(rows, width, dtype=F32))
    act_out = (ANY_SPEC, shaped(rows, blocks * width))
    down_part = (ANY_SPEC, shaped(4, 2, deep, width))
    up_part = (ANY_SPEC, shaped(blocks, 4, 2, each, width))

    act_spec = pl.BlockSpec((fold * tile, blocks * width), lambda i, *me: (i, 0))
    wide_spec = whole_spec((hidden // 2, width))

    def run_mlp(me, tokens_of, bup, sources):
        sets = len(tokens_of[0])
        low, high = pltpu.VMEM((sets * rows, width), BF16), pltpu.VMEM((sets * rows, width), F32)
        weight = pltpu.VMEM((2, width, width), BF16)
        dma = pltpu.SemaphoreType.DMA((2, sets))
        return call_with(
            me, functools.partial(mlp, sets, len(sources)), blocks,
            [ANY_SPEC] * (2 * sets) + [hidden_spec] + [ANY_SPEC] * len(sources),
            [act_out] * sets + [high_out] + [low_out] * (sets - 1) + [down_part] * 2 + [up_part] * 2
            + [(ANY_SPEC, shaped(hidden // 2, width)), (hidden_spec, shaped(1, hidden // 2, dtype=F32))],
            [low, low, high, pltpu.VMEM((blocks, sets * rows, width), BF16), low, low, weight, weight,
             pltpu.VMEM((blocks, width, width), BF16), pltpu.VMEM((hidden // 2, width), BF16), dma,
             pltpu.SemaphoreType.DMA((blocks, sets)), pltpu.SemaphoreType.DMA((sets,)), pltpu.SemaphoreType.DMA((4,)),
             pltpu.SemaphoreType.DMA((blocks + 1,))],
            "mlp", 0, *tokens_of[0], *tokens_of[1], bup, *sources)

    if by_hand:
        act_own, act_other, gtwo, gtwo_other, down_own, down_send, up_own, up_send, wdown, sum_up = run_mlp(
            me, ((n2, n2_other), (cot, cot_other)), bup, hidden_weights[0])
        gtwo_take = swap(gtwo_other, other_core)
        parts = (-1, CHIPS // 4, 2)
        down_first = [piece.reshape(*parts, deep, width) for piece in (down_own, swap(down_send, first_plane))]
        up_first = [piece.reshape(*parts, each, width) for piece in (up_own, swap(up_send, first_plane))]
    else:
        runs = [run_mlp(me + half, ((n2,), (cot,)), bup[half], hidden_weights[half]) for half in range(2)]
        (act_own, gtwo), (act_other, gtwo_take) = ((run[0], run[1]) for run in runs)
        gtwo_take = gtwo_take.astype(BF16)
        sum_up = jnp.concatenate([run[7] for run in runs], axis=1)
    grads_spec = pl.BlockSpec((4, tile, width), lambda i, *me: (0, i, 0))
    grads, gresid, sum_back = call(
        attention_backward, (tiles,),
        [SMEM, tile_rows, tile_rows, tile_rows, lse_spec, tile_rows, tile_rows, tile_rows, tile_rows, vec_spec, square],
        [(grads_spec, shaped(4, rows, width)), high_rows, sums], [pltpu.VMEM((tile, width), BF16)],
        "attention_backward", 0, lengths, q, k, v, lse, cot, resid, gtwo, gtwo_take, vec, wo)
    sum_spec = whole_spec((8, width))
    pair_shape = (CHIPS // 4, 4, 4 * each + 16, side)
    columns = pl.BlockSpec((1, rows, width), lambda i, me: (i, 0, 0))

    def run_weights(grads):
        return call_with(
            me, weight_grads, 4, [full_rows, ANY_SPEC, columns, sum_spec, sum_spec, whole_spec((1, sum_up.shape[1]))],
            [(ANY_SPEC, shaped(*pair_shape))] * 2,
            [pltpu.VMEM(pair_shape, BF16)] * 2
            + [pltpu.VMEM((rows, width), BF16), pltpu.SemaphoreType.DMA((1,)), pltpu.SemaphoreType.DMA((2, 5))],
            "weight_grads", 0,
            n1, mixed, grads, sum_back, sum_down, sum_up)

    def run_tokens(gresid):
        return call(
            tokens_backward, (tiles // fold,),
            [wide_rows, wide_rows, vec_spec, pl.BlockSpec((4, fold * tile, width), lambda i: (0, i, 0)), square, square, square],
            [wide_low, sums], [], "tokens_backward", MIDDLE, tokens, gresid, vec, grads, wq, wk, wv)

    if by_hand:
        (out_other,) = call_with(
            me, mlp_out_other, tiles // fold, [act_spec, wide_spec], [wide_low], [], "mlp_out_other", 0, after(act_other, grads), wdown)
        down_first, up_first = after((down_first, up_first), out_other)
        hidden_rest, hidden_take = scatter_second(*down_first, *up_first)

        def weights_of_chip(grads):
            square_send, square_keep = run_weights(grads)
            return merge_core_of(core, square_keep, scatter_core(square_send))

        out_take = swap(out_other, other_core)
        square_own, square_send = fenced(weights_of_chip, after(grads, hidden_rest))
        square_take = swap(square_send, first_plane).reshape(square_own.shape)
        hidden_rest, hidden_take = after((hidden_rest, hidden_take), square_own)
        hidden_layers = scatter_layers(hidden_rest, hidden_take)
        gtok, late = run_tokens(after(gresid, hidden_layers[0]))
        square_take = after(square_take, late)
        late = late + swap(late, other_core)
        square_second = scatter_second(square_own, square_take)
        late = after(late, square_second[0])
        (out,) = call_with(
            me, mlp_out_own, tiles // fold, [wide_rows, vec_spec, act_spec, wide_rows, wide_spec], [wide_low], [],
            "mlp_out_own", 0, resid, vec, act_own, after(out_take, square_second[0]), wdown)
        late = late + after(swap(late, other_layer(1)), out)
        hidden_layers = after(hidden_layers, late)
        g_down, up_keep, up_send = scatter_last(core, hidden_layers, own, blocks, deep)
        up_take = scatter_core(up_send)
        late_take = after(swap(late, other_layer(2)), g_down)
        square_second = after(square_second, g_down)
        rest, *sends = merge_layers_of(*square_second)
        late_take = after(late_take, rest)
        sends = after(sends, late_take)
        square_layers = [rest] + [swap(piece, other_layer(r + 1)) for r, piece in enumerate(sends)]
        late = late + late_take
        late = late + after(swap(late, other_plane(1)), rest)
        late = late + swap(late, other_plane(2))
        square_layers = after(square_layers, late)
        square_keep, square_send, flat = scatter_last(core, square_layers, own, 4, 0)
        square_take = scatter_core(square_send)
        outs = [(VMEM_SPEC, shaped(own, hidden, dtype=F32))] + [(VMEM_SPEC, shaped(own, width, dtype=F32))] * 4
        outs += [(VMEM_SPEC, shaped(own, dtype=F32))] * 8 + [(VMEM_SPEC, shaped(folds * own, dtype=F32))]
        g_up, g_q, g_k, g_v, g_o, *g_flat, g_ub = small_call(
            finish, (me, up_keep, up_take, square_keep, square_take, flat, late), outs, "finish",
            ins=[SMEM] + [VMEM_SPEC] * 6)
    else:
        square_send, square_keep = run_weights(grads)
        gtok, sum_one = run_tokens(gresid)
        flat = jnp.concatenate((sum_one[0:2], sum_back[0:5], sum_down[0:1]), axis=0)
        flat = flat.reshape(8, count, own).transpose(1, 0, 2).reshape(count, 8 * own)
        hidden_sums = sum_up.reshape(2, CHIPS, deep).transpose(1, 0, 2).reshape(count, folds * own)
        flat = jnp.concatenate((flat, hidden_sums), axis=1)
        g_down, g_up, g_q, g_k, g_v, g_o, flat = reduce_plain(
            [run[2:4] for run in runs], [run[4:6] for run in runs], (square_keep, square_send), flat)
        (out_other,) = call_with(
            me + 1, mlp_out_other, tiles // fold, [act_spec, wide_spec], [wide_low], [], "mlp_out_other", 0, act_other, runs[1][6])
        (out,) = call_with(
            me, mlp_out_own, tiles // fold, [wide_rows, vec_spec, act_spec, wide_rows, wide_spec], [wide_low], [],
            "mlp_out_own", 0, resid, vec, act_own, out_other, runs[0][6])
        g_flat = [flat[index * own : (index + 1) * own] for index in range(8)]
        g_ub = flat[8 * own :]
    g_gain, g_shift, g_qb, g_vb, g_ob, g_mg, g_ms, g_db = g_flat
    return (out, gtok, g_gain, g_shift, g_q, g_qb, g_k, g_v, g_vb, g_o, g_ob, g_mg, g_ms, g_up, g_ub, g_down, g_db)


def solution(mesh):
    rows, flat = P("dp", None), P("dp")
    return jax.shard_map(
        body,
        mesh=mesh,
        in_specs=(rows, rows, flat, flat, rows, flat, rows, rows, flat, rows, flat, flat, flat, rows, flat, rows, flat, rows),
        out_specs=(rows, rows, flat, flat, rows, flat, rows, rows, flat, rows, flat, flat, flat, rows, flat, rows, flat),
        check_vma=False,
    )
```
